32 devices in a mesh: dp: 16 (over z, x, core), mod: 2 (over y).
Axes of the slice: x: 2, y: 2, z: 4, core: 2. Of those that a mesh axis runs over, the one named last changes fastest.
Arguments:
- hidden_in: bfloat16 [32, 2, 512, 768], P('dp', 'mod'), may hold values from -6 to 6
- image_count: int32 [32], P('dp'), may hold values from 129 to 256
- text_lengths: int32 [32, 4], P('dp'), may hold values from 1 to 256, 512 in all within a row
- attend_gain: float32 [2, 768], P('mod'), may hold values from 0.5 to 1.5
- attend_shift: float32 [2, 768], P('mod'), may hold values from -1.5 to 1.5
- project_in: bfloat16 [768, 2304], replicated, may hold values from -0.21875 to 0.21875
- bias_pair: float32 [2, 768], replicated, may hold values from -1.5 to 1.5
- project_out: bfloat16 [768, 768], replicated, may hold values from -0.875 to 0.875
- project_bias: float32 [768], replicated, may hold values from -1.5 to 1.5
- feed_gain: float32 [2, 768], P('mod'), may hold values from 0.5 to 1.5
- feed_shift: float32 [2, 768], P('mod'), may hold values from -1.5 to 1.5
- expand_weight: bfloat16 [2, 768, 3072], P('mod'), may hold values from -0.21875 to 0.21875
- expand_bias: float32 [2, 3072], P('mod'), may hold values from -1.5 to 1.5
- reduce_weight: bfloat16 [2, 3072, 768], P('mod'), may hold values from -0.109375 to 0.109375
- reduce_bias: float32 [2, 768], P('mod'), may hold values from -1.5 to 1.5
- cotangent: bfloat16 [32, 2, 512, 768], P('dp', 'mod'), may hold values from -6 to 6
Outputs:
- hidden_out: bfloat16 [32, 2, 512, 768], P('dp', 'mod')
- grad_in: bfloat16 [32, 2, 512, 768], P('dp', 'mod')
- attend_gain_grad: float32 [2, 768], P('mod')
- attend_shift_grad: float32 [2, 768], P('mod')
- project_in_grad: float32 [768, 2304], replicated
- bias_pair_grad: float32 [2, 768], replicated
- project_out_grad: float32 [768, 768], replicated
- project_bias_grad: float32 [768], replicated
- feed_gain_grad: float32 [2, 768], P('mod')
- feed_shift_grad: float32 [2, 768], P('mod')
- expand_weight_grad: float32 [2, 768, 3072], P('mod')
- expand_bias_grad: float32 [2, 3072], P('mod')
- reduce_weight_grad: float32 [2, 3072, 768], P('mod')
- reduce_bias_grad: float32 [2, 768], P('mod')
The draws below stay inside these ranges and needn't reach their ends.
All inputs are finite; a program needn't handle non-finite values.
Results may differ from the reference program's by a relative error of at most 0.011.
Values may be sent and summed in bfloat16 or wider, within the bound.
No kernel may reach another device: no remote copies, remote signals or barrier semaphores. Data moves between devices by JAX's collectives and lax.ppermute only.
A program may use at most 320 MiB of HBM per device.

```python
import math
import jax
import jax.numpy as jnp
import numpy as np
from jax import lax

D = 768
HEADS = 12
HEAD = 64
FF = 3072
MODES = 2
SEQ = 512
IMG_PAD = 256
NSEG = 4
ITEMS = 32


def draw_cotangent(key, part):
    key = jax.random.fold_in(key, 7)
    first_key = jax.random.fold_in(key, 0)
    item_ramp = 0.5 + jnp.arange(ITEMS, dtype=jnp.float32) / (ITEMS - 1)
    full_shape = (ITEMS, MODES, SEQ, D)
    base_draw = jax.random.normal(first_key, full_shape, jnp.float32)
    base_draw = jnp.clip(base_draw, -4.0, 4.0)
    return (base_draw * item_ramp[:, None, None, None]).astype(jnp.bfloat16)


def set_ends(values, own_key, least, largest):
    dims = values.shape
    index_at = [jax.random.randint(jax.random.fold_in(own_key, axis), (), 0, dims[axis]) for axis in range(len(dims))]
    values = values.at[tuple(index_at)].set(least)
    longest = dims.index(max(dims))
    index_at[longest] = (index_at[longest] + 1) % dims[longest]
    return values.at[tuple(index_at)].set(largest)


def level_of(own_key, shape, pieces, low, high):
    def one(axis_at, blocks):
        draws = jax.random.uniform(jax.random.fold_in(jax.random.fold_in(own_key, 6), axis_at), (blocks,), jnp.float32, low / len(pieces), high / len(pieces))
        return jnp.repeat(jnp.exp(draws), shape[axis_at] // blocks).reshape((-1,) + (1,) * (len(shape) - axis_at - 1))

    loudness = one(*pieces[0])
    for cut in pieces[1:]:
        loudness = loudness * one(*cut)
    return loudness


def split_up(amount, total, reach, lean):
    weights = [(1 << 20) // math.isqrt(rank ** lean) + 1 for rank in range(2, amount + 1)]
    surplus, given = total - reach - (amount - 1), [1] * (amount - 1)
    while surplus > 0:
        free = [i for i in range(amount - 1) if given[i] < reach]
        whole, budget = sum([weights[i] for i in free]), surplus
        for i in free:
            addition = min(reach - given[i], max(1, budget * weights[i] // whole), surplus)
            given[i] = given[i] + addition
            surplus = surplus - addition
    return np.array([reach] + given)


def uneven_parts(own_key, number_of, total, most, lean):
    if number_of == 2:
        one = jax.random.randint(own_key, (), max(1, total - most), min(most, total - 1) + 1)
        return jnp.stack([one, total - one])
    sizes = jnp.asarray(split_up(number_of, total, most, lean), jnp.int32)
    couples = (number_of - 1) // 2
    giver, taker = sizes[1:1 + 2 * couples:2], sizes[2:2 + 2 * couples:2]
    margin = jnp.minimum(giver - 1, most - taker)
    passed = jax.random.randint(jax.random.fold_in(own_key, 1), (couples,), 0, 1 << 20) % (margin + 1)
    sizes = sizes.at[1:1 + 2 * couples:2].set(giver - passed).at[2:2 + 2 * couples:2].set(taker + passed)
    return sizes[jax.random.permutation(jax.random.fold_in(own_key, 2), number_of)]


def bell_draw(own_key, extent, scale, reach, pieces=(), kind=jnp.bfloat16):
    result = jax.random.normal(own_key, extent, jnp.float32) * scale
    if len(pieces) > 0:
        result = level_of(own_key, extent, pieces, -0.22, 0.18) * result
    return jnp.clip(result, min=-reach, max=reach).astype(kind)


def setup_inputs(seed: int = 0) -> dict:
    key_list = jax.random.split(jax.random.key(seed), 17)
    return {
        "hidden_in": bell_draw(key_list[0], (ITEMS, MODES, SEQ, D), 1.0, 6.0, ((0, 16), (1, 2))),
        "image_count": set_ends(jax.random.randint(key_list[1], (ITEMS,), IMG_PAD // 2 + 1, IMG_PAD + 1), jax.random.fold_in(key_list[1], 1), IMG_PAD // 2 + 1, IMG_PAD).astype(jnp.int32),
        "text_lengths": jax.vmap(lambda own: uneven_parts(own, NSEG, SEQ, SEQ // 2, 2))(jax.random.split(key_list[2], ITEMS)).reshape((ITEMS, NSEG)).astype(jnp.int32),
        "attend_gain": jnp.clip(1.0 + 0.1 * jax.random.normal(key_list[3], (MODES, D), jnp.float32), 0.5, 1.5),
        "attend_shift": bell_draw(key_list[4], (MODES, D), 0.3, 1.5, ((0, 2),), jnp.float32),
        "project_in": bell_draw(key_list[5], (D, 3 * D), D ** -0.5, 0.21875),
        "bias_pair": bell_draw(key_list[6], (2, D), 0.3, 1.5, (), jnp.float32),
        "project_out": bell_draw(key_list[7], (D, D), (D // 16) ** -0.5, 0.875),
        "project_bias": bell_draw(key_list[8], (D,), 0.3, 1.5, (), jnp.float32),
        "feed_gain": jnp.clip(1.0 + 0.1 * jax.random.normal(key_list[9], (MODES, D), jnp.float32), 0.5, 1.5),
        "feed_shift": bell_draw(key_list[10], (MODES, D), 0.3, 1.5, ((0, 2),), jnp.float32),
        "expand_weight": bell_draw(key_list[11], (MODES, D, FF), D ** -0.5, 0.21875, ((0, 2),)),
        "expand_bias": bell_draw(key_list[12], (MODES, FF), 0.3, 1.5, ((0, 2),), jnp.float32),
        "reduce_weight": bell_draw(key_list[13], (MODES, FF, D), FF ** -0.5, 0.109375, ((0, 2),)),
        "reduce_bias": bell_draw(key_list[14], (MODES, D), 0.3, 1.5, ((0, 2),), jnp.float32),
        "cotangent": draw_cotangent(jax.random.fold_in(key_list[16], 71), 0),
    }


@jax.custom_vjp
def low(v):
    return lax.optimization_barrier(v.astype(jnp.bfloat16)).astype(jnp.float32)

@jax.custom_vjp
def low_back(v):
    return v

def low_keep(v):
    return (low(v), None)

def low_pass(kept, grad):
    return (grad,)

def back_keep(v):
    return (v, None)

def back_low(kept, grad):
    return (low(grad),)
low.defvjp(low_keep, low_pass)
low_back.defvjp(back_keep, back_low)
highest = lax.Precision.HIGHEST
masked_value = -1e+30
norm_eps = 1e-05

def layer_norm(values, gain, shift):
    row_mean = lax.optimization_barrier(jnp.mean(values, axis=-1, keepdims=True))
    centred = values - row_mean
    spread = lax.optimization_barrier(jnp.mean(centred * centred, axis=-1, keepdims=True))
    return centred * lax.rsqrt(spread + norm_eps) * gain + shift

def segment_of(lengths, row_count):
    segment_ends = jnp.cumsum(lengths)
    places = jnp.arange(row_count, dtype=jnp.int32)
    return lax.optimization_barrier(jnp.sum((places[:, None] >= segment_ends[None, :]).astype(jnp.int32), axis=1))

def attend(query_rows, key_rows, value_rows, allowed):
    row_count = query_rows.shape[0]
    heads_q = query_rows.reshape(row_count, HEADS, HEAD)
    heads_k = key_rows.reshape(key_rows.shape[0], HEADS, HEAD)
    heads_v = value_rows.reshape(value_rows.shape[0], HEADS, HEAD)
    scores = low_back(jnp.einsum('rhe,che->hrc', heads_q, heads_k, precision=highest) * HEAD ** (-0.5))
    scores = jnp.where(allowed[None], scores, masked_value)
    probs_low = low(jax.nn.softmax(scores, axis=-1))
    return jnp.einsum('hrc,che->rhe', probs_low, heads_v, precision=highest).reshape(row_count, HEADS * HEAD)

def item_forward(params, inputs, live_count, lengths):
    attend_gain, attend_shift, project_in, bias_pair, project_out, project_bias, feed_gain, feed_shift, expand_weight, expand_bias, reduce_weight, reduce_bias = params
    normed = low(layer_norm(inputs, attend_gain[:, None, :], attend_shift[:, None, :]))
    projected = jnp.einsum('msd,de->mse', normed, project_in, precision=highest)
    query_rows = low(low_back(projected[..., :D] + bias_pair[0]))
    key_rows = low(low_back(projected[..., D:2 * D]))
    value_rows = low(low_back(projected[..., 2 * D:] + bias_pair[1]))
    image_keys = key_rows[0, :IMG_PAD]
    image_values = value_rows[0, :IMG_PAD]
    image_live = jnp.arange(IMG_PAD, dtype=jnp.int32) < live_count
    image_mask = jnp.broadcast_to(image_live[None, :], (SEQ, IMG_PAD))
    segment = segment_of(lengths, SEQ)
    text_mask = jnp.concatenate([image_mask, segment[:, None] == segment[None, :]], axis=1)
    image_attended = attend(query_rows[0], image_keys, image_values, image_mask)
    text_attended = attend(query_rows[1], jnp.concatenate([image_keys, key_rows[1]], axis=0), jnp.concatenate([image_values, value_rows[1]], axis=0), text_mask)
    attended = low(low_back(jnp.stack([image_attended, text_attended])))
    branch = low_back(jnp.einsum('msd,de->mse', attended, project_out, precision=highest))
    middle = inputs + branch + project_bias
    normed_feed = low(layer_norm(middle, feed_gain[:, None, :], feed_shift[:, None, :]))
    upward = low_back(jnp.einsum('msd,mdf->msf', normed_feed, expand_weight, precision=highest) + expand_bias[:, None, :])
    active = low(jax.nn.gelu(upward, approximate=False))
    return middle + jnp.einsum('msf,mfd->msd', active, reduce_weight, precision=highest) + reduce_bias[:, None, :]

def reference(hidden_in, image_count, text_lengths, attend_gain, attend_shift, project_in, bias_pair, project_out, project_bias, feed_gain, feed_shift, expand_weight, expand_bias, reduce_weight, reduce_bias, cotangent):
    params = tuple((weight_value.astype(jnp.float32) for weight_value in (attend_gain, attend_shift, project_in, bias_pair, project_out, project_bias, feed_gain, feed_shift, expand_weight, expand_bias, reduce_weight, reduce_bias)))
    inputs = hidden_in.astype(jnp.float32)

    def forward(inputs, params):
        item_step = jax.checkpoint(item_forward)

        def per_item(packed):
            return item_step(params, packed[0], packed[1], packed[2])
        return lax.map(per_item, (inputs, image_count.astype(jnp.int32), text_lengths.astype(jnp.int32)))
    image_live = jnp.arange(SEQ, dtype=jnp.int32)[None, :] < image_count.astype(jnp.int32)[:, None]
    mode_live = jnp.stack([image_live, jnp.ones_like(image_live)], axis=1)
    grad_top = jnp.where(mode_live[..., None], cotangent.astype(jnp.float32), jnp.float32(0.0))
    output, pullback = jax.vjp(forward, inputs, params)
    grad_inputs, weight_grads = pullback(grad_top)
    return (output.astype(jnp.bfloat16), grad_inputs.astype(jnp.bfloat16), weight_grads[0], weight_grads[1], weight_grads[2], weight_grads[3], weight_grads[4], weight_grads[5], weight_grads[6], weight_grads[7], weight_grads[8], weight_grads[9], weight_grads[10], weight_grads[11])
```

```python
import functools

import jax
import jax.numpy as jnp
from jax import lax
from jax.experimental import pallas as pl
from jax.experimental.pallas import tpu as pltpu
from jax.sharding import PartitionSpec as P

HEADS = 12
HEAD = 64
IMG_PAD = 256
PAIR = 2 * HEAD
PAIRS = HEADS // 2
GROUPS = (2, 2, 2)
FF_BLOCK = 512

masked_value = -1e30
norm_eps = 1e-05

bf16 = jnp.bfloat16
f32 = jnp.float32

NN = (((1,), (0,)), ((), ()))
NT = (((1,), (1,)), ((), ()))
TN = (((0,), (0,)), ((), ()))
VMEM_BYTES = 56 << 20


def dot(left, right, dims=NN):
    return lax.dot_general(left, right, dims, preferred_element_type=f32)


def column_sum(values):
    return jnp.sum(values, axis=0, keepdims=True)


def row_mean(values):
    return jnp.mean(values, axis=1, keepdims=True)


def normalise(values):
    centred = values - row_mean(values)
    scale = lax.rsqrt(row_mean(centred * centred) + norm_eps)
    return centred * scale, scale


def norm_transpose(unit, scale, gain, grad):
    grad_unit = grad * gain
    return scale * (grad_unit - row_mean(grad_unit) - unit * row_mean(grad_unit * unit))


def params(**more):
    return pltpu.CompilerParams(vmem_limit_bytes=VMEM_BYTES, **more)


def cost(flops, moved, special=0):
    return pl.CostEstimate(flops=flops, bytes_accessed=moved, transcendentals=special)


def project_kernel(hid_ref, vec_ref, weight_ref, bias_ref, normed_ref, out_ref):
    unit, _ = normalise(hid_ref[...].astype(f32))
    normed = (unit * vec_ref[0:1] + vec_ref[1:2]).astype(bf16)
    normed_ref[...] = normed
    width = normed.shape[1]
    for part in range(3):
        cols = slice(part * width, (part + 1) * width)
        rows = dot(normed, weight_ref[:, cols])
        if part == 0:
            rows = (rows + bias_ref[0:1]).astype(bf16) * jnp.asarray(HEAD**-0.5, bf16)
        if part == 2:
            rows = rows + bias_ref[1:2]
        out_ref[:, cols] = rows.astype(bf16)


def project_rows(hidden, vecs, weight, bias):
    rows, width = hidden.shape
    block = 256
    whole = lambda shape: pl.BlockSpec(shape, lambda r: (0, 0), pipeline_mode=pl.Buffered(1))
    return pl.pallas_call(
        project_kernel,
        grid=(rows // block,),
        in_specs=[
            pl.BlockSpec((block, width), lambda r: (r, 0)),
            whole(vecs.shape),
            whole(weight.shape),
            whole(bias.shape),
        ],
        out_specs=[
            pl.BlockSpec((block, width), lambda r: (r, 0)),
            pl.BlockSpec((block, 3 * width), lambda r: (r, 0)),
        ],
        out_shape=[
            jax.ShapeDtypeStruct((rows, width), bf16),
            jax.ShapeDtypeStruct((rows, 3 * width), bf16),
        ],
        compiler_params=params(),
        cost_estimate=cost(6 * rows * width * width, 10 * rows * width + 6 * width * width),
        name="project_rows",
    )(hidden, vecs, weight, bias)


def image_kernel(hid_ref, vec_ref, weight_ref, bias_ref, normed_ref, out_ref):
    unit, _ = normalise(hid_ref[...].astype(f32))
    normed = (unit * vec_ref[0:1] + vec_ref[1:2]).astype(bf16)
    normed_ref[...] = normed
    width = normed.shape[1]
    out_ref[:, :width] = dot(normed, weight_ref[:, width : 2 * width]).astype(bf16)
    out_ref[:, width:] = (dot(normed, weight_ref[:, 2 * width :]) + bias_ref[1:2]).astype(bf16)


def image_rows(hidden, vecs, weight, bias):
    rows, width = hidden.shape
    return pl.pallas_call(
        image_kernel,
        out_shape=[
            jax.ShapeDtypeStruct((rows, width), bf16),
            jax.ShapeDtypeStruct((rows, 2 * width), bf16),
        ],
        compiler_params=params(),
        cost_estimate=cost(4 * rows * width * width, 8 * rows * width + 6 * width * width),
        name="image_rows",
    )(hidden, vecs, weight, bias)


def segments(shape, axis, info_ref):
    places = lax.broadcasted_iota(jnp.int32, shape, axis)
    total = jnp.zeros(shape, jnp.int32)
    for which in range(4):
        total += (places >= info_ref[1 + which]).astype(jnp.int32)
    return total


def own_bias(rows, info_ref):
    shape = (rows, rows)
    same = segments(shape, 0, info_ref) == segments(shape, 1, info_ref)
    return jnp.where(same & (info_ref[5] == 1), 0.0, masked_value).astype(f32)


def image_bias(shape, axis, info_ref):
    places = lax.broadcasted_iota(jnp.int32, shape, axis)
    return jnp.where(places < info_ref[0], 0.0, masked_value).astype(f32)


def forward_kernel(
    info_ref, q_ref, k_ref, v_ref, ik_ref, iv_ref, out_ref, lse_ref, image_part, own_part
):
    rows = q_ref.shape[0]

    @pl.when(pl.program_id(0) == 0)
    def _():
        image_part[...] = image_bias(image_part.shape, 1, info_ref)
        own_part[...] = own_bias(rows, info_ref)

    first = lax.broadcasted_iota(jnp.int32, (rows, PAIR), 1) < HEAD
    zero = jnp.zeros((), bf16)
    q = q_ref[...]
    image_keys, image_values = ik_ref[...], iv_ref[...]
    keys, values = k_ref[...], v_ref[...]
    outs, tops = [], []
    for head in range(2):
        q_head = jnp.where(first, q, zero) if head == 0 else jnp.where(first, zero, q)
        far = dot(q_head, image_keys, NT) + image_part[...]
        own = dot(q_head, keys, NT) + own_part[...]
        top = jnp.maximum(
            jnp.max(far, axis=1, keepdims=True), jnp.max(own, axis=1, keepdims=True)
        )
        far = jnp.exp(far - top)
        own = jnp.exp(own - top)
        total = jnp.sum(far, axis=1, keepdims=True) + jnp.sum(own, axis=1, keepdims=True)
        summed = dot(far.astype(bf16), image_values) + dot(own.astype(bf16), values)
        outs.append(summed / total)
        tops.append(top + jnp.log(total))
    out_ref[...] = jnp.where(first, outs[0], outs[1]).astype(bf16)
    turned = jnp.transpose(jnp.where(first, tops[0], tops[1]))
    lse_ref[0, 0:1, :] = turned[0:1]
    lse_ref[0, 1:2, :] = turned[HEAD : HEAD + 1]


def attend_forward(info, item, projected, image):
    rows = projected.shape[0] // 2
    spec = lambda base: pl.BlockSpec((rows, PAIR), lambda h, *_: (item, base + h))
    far = lambda base: pl.BlockSpec((IMG_PAD, PAIR), lambda h, *_: (0, base + h))
    keys = rows + IMG_PAD
    return pl.pallas_call(
        forward_kernel,
        grid_spec=pltpu.PrefetchScalarGridSpec(
            num_scalar_prefetch=1,
            grid=(PAIRS,),
            in_specs=[spec(0), spec(PAIRS), spec(2 * PAIRS), far(0), far(PAIRS)],
            out_specs=[
                pl.BlockSpec((rows, PAIR), lambda h, *_: (0, h)),
                pl.BlockSpec((1, 2, rows), lambda h, *_: (h, 0, 0)),
            ],
            scratch_shapes=[pltpu.VMEM((rows, IMG_PAD), f32), pltpu.VMEM((rows, rows), f32)],
        ),
        out_shape=[
            jax.ShapeDtypeStruct((rows, HEADS * HEAD), bf16),
            jax.ShapeDtypeStruct((PAIRS, 2, rows), f32),
        ],
        compiler_params=params(),
        cost_estimate=cost(16 * HEADS * rows * keys * HEAD, 6 << 20, HEADS * rows * keys),
        name="attend_forward",
    )(info, projected, projected, projected, image, image)


def backward_kernel(
    info_ref,
    q_ref,
    k_ref,
    v_ref,
    ik_ref,
    iv_ref,
    out_ref,
    grad_ref,
    lse_ref,
    gq_ref,
    gk_ref,
    gv_ref,
    gik_ref,
    giv_ref,
    image_part,
    own_part,
):
    rows = q_ref.shape[0]

    @pl.when(pl.program_id(0) == 0)
    def _():
        image_part[...] = image_bias(image_part.shape, 0, info_ref)
        own_part[...] = own_bias(rows, info_ref)

    first = lax.broadcasted_iota(jnp.int32, (rows, PAIR), 1) < HEAD
    zero = jnp.zeros((), bf16)
    q, grad = q_ref[...], grad_ref[...]
    products = grad.astype(f32) * out_ref[...].astype(f32)
    head_lanes = lax.broadcasted_iota(jnp.int32, (8, PAIR), 1) // HEAD
    head_rows = lax.broadcasted_iota(jnp.int32, (8, PAIR), 0)
    center = lax.dot_general(
        (head_lanes == head_rows).astype(f32),
        products,
        NT,
        preferred_element_type=f32,
        precision=lax.Precision.HIGHEST,
    )
    q_heads = [jnp.where(first, q, zero), jnp.where(first, zero, q)]
    grad_heads = [jnp.where(first, grad, zero), jnp.where(first, zero, grad)]
    lse = lse_ref[0]
    grad_query = [None, None]
    half = rows // 2
    pieces = (
        (ik_ref, iv_ref, gik_ref, giv_ref, image_part, 0, IMG_PAD),
        (k_ref, v_ref, gk_ref, gv_ref, own_part, 0, half),
        (k_ref, v_ref, gk_ref, gv_ref, own_part, half, half),
    )
    for keys_ref, values_ref, gk_out, gv_out, bias, start, count in pieces:
        piece = slice(start, start + count)
        keys, values = keys_ref[piece, :], values_ref[piece, :]
        low_lanes = lax.broadcasted_iota(jnp.int32, (count, PAIR), 1) < HEAD
        grad_keys, grad_values = [], []
        for head in range(2):
            scores = dot(keys, q_heads[head], NT) + bias[piece, :]
            probs = jnp.exp(scores - lse[head : head + 1])
            grad_probs = dot(values, grad_heads[head], NT)
            grad_scores = (probs * (grad_probs - center[head : head + 1])).astype(bf16)
            grad_values.append(dot(probs.astype(bf16), grad))
            grad_keys.append(dot(grad_scores, q))
            term = dot(grad_scores, keys, TN)
            grad_query[head] = term if grad_query[head] is None else grad_query[head] + term
        gk_out[piece, :] = jnp.where(low_lanes, grad_keys[0], grad_keys[1]).astype(bf16)
        gv_out[piece, :] = jnp.where(low_lanes, grad_values[0], grad_values[1]).astype(bf16)
    gq_ref[...] = (jnp.where(first, grad_query[0], grad_query[1]) * HEAD**-0.5).astype(bf16)


def attend_backward(info, item, start, pairs, projected, image, attended, grad, lse):
    rows = attended.shape[0]
    spec = lambda base: pl.BlockSpec((rows, PAIR), lambda h, *_: (item, base + start + h))
    far = lambda base: pl.BlockSpec((IMG_PAD, PAIR), lambda h, *_: (0, base + start + h))
    own = pl.BlockSpec((rows, PAIR), lambda h, *_: (0, start + h))
    outs = pl.BlockSpec((rows, PAIR), lambda h, *_: (0, h))
    far_outs = pl.BlockSpec((IMG_PAD, PAIR), lambda h, *_: (0, h))
    keys = rows + IMG_PAD
    return pl.pallas_call(
        backward_kernel,
        grid_spec=pltpu.PrefetchScalarGridSpec(
            num_scalar_prefetch=1,
            grid=(pairs,),
            in_specs=[
                spec(0),
                spec(PAIRS),
                spec(2 * PAIRS),
                far(0),
                far(PAIRS),
                own,
                spec(0),
                pl.BlockSpec((1, 2, rows), lambda h, *_: (start + h, 0, 0)),
            ],
            out_specs=[outs, outs, outs, far_outs, far_outs],
            scratch_shapes=[pltpu.VMEM((IMG_PAD, rows), f32), pltpu.VMEM((rows, rows), f32)],
        ),
        out_shape=[jax.ShapeDtypeStruct((rows, pairs * PAIR), bf16)] * 3
        + [jax.ShapeDtypeStruct((IMG_PAD, pairs * PAIR), bf16)] * 2,
        compiler_params=params(),
        cost_estimate=cost(
            80 * pairs * rows * keys * HEAD, pairs * 2 << 20, 2 * pairs * rows * keys
        ),
        name="attend_backward",
    )(info, projected, projected, projected, image, image, attended, grad, lse)


def gelu_pair(values):
    share = 0.5 * (1.0 + lax.erf(values * 0.7071067811865476))
    slope = share + values * jnp.exp(-0.5 * values * values) * 0.3989422804014327
    return values * share, slope


def feed_kernel(
    live_ref,
    att0_ref,
    att1_ref,
    project_ref,
    hid_ref,
    cot_ref,
    vec_ref,
    expand_ref,
    expand_bias_ref,
    reduce_ref,
    out_ref,
    gmid_ref,
    gatt_ref,
    gproject_ref,
    gvec_ref,
    gexpand_ref,
    greduce_ref,
    gexpand_bias_ref,
    middle,
    feed,
    top,
    result,
    gfeed,
    *,
    item_rows,
):
    step = pl.program_id(0)
    rows, width = hid_ref.shape
    block = 256
    att_refs = (att0_ref, att1_ref)

    @pl.when(step == 0)
    def _():
        for start in range(0, rows, block):
            here = slice(start, start + block)
            inside = slice(start % item_rows, start % item_rows + block)
            att = att_refs[start // item_rows][inside, :]
            x = hid_ref[here, :].astype(f32) + dot(att, project_ref[...]) + vec_ref[0:1]
            middle[here, :] = x
            unit, _ = normalise(x)
            feed[here, :] = (unit * vec_ref[1:2] + vec_ref[2:3]).astype(bf16)
            places = lax.broadcasted_iota(jnp.int32, (block, width), 0) + start % item_rows
            live = places < live_ref[start // item_rows]
            top[here, :] = jnp.where(live, cot_ref[here, :].astype(f32), 0.0).astype(bf16)
            result[here, :] = x + vec_ref[3:4]
            gfeed[here, :] = jnp.zeros((block, width), f32)

    expand, reduce = expand_ref[...], reduce_ref[...]
    active_parts, gup_parts = [], []
    for start in range(0, rows, item_rows):
        here = slice(start, start + item_rows)
        upward = dot(feed[here, :], expand) + expand_bias_ref[...]
        gactive = dot(top[here, :], reduce, NT)
        active, slope = gelu_pair(upward)
        active = active.astype(bf16)
        gup = (gactive * slope).astype(bf16)
        result[here, :] += dot(active, reduce)
        gfeed[here, :] += dot(gup, expand, NT)
        active_parts.append(active)
        gup_parts.append(gup)
    active = jnp.concatenate(active_parts, axis=0)
    gup = jnp.concatenate(gup_parts, axis=0)
    greduce_ref[...] = dot(active, top[...], TN).astype(bf16)
    gexpand_ref[...] = dot(feed[...], gup, TN).astype(bf16)
    gexpand_bias_ref[...] = column_sum(gup.astype(f32))

    @pl.when(step == pl.num_programs(0) - 1)
    def _():
        sums = [jnp.zeros((1, width), f32)] * 4
        for start in range(0, rows, block):
            here = slice(start, start + block)
            out_ref[here, :] = result[here, :].astype(bf16)
            unit, scale = normalise(middle[here, :])
            grad = gfeed[here, :]
            grad_top = top[here, :].astype(f32)
            gmid = grad_top + norm_transpose(unit, scale, vec_ref[1:2], grad)
            terms = (grad * unit, grad, grad_top, gmid)
            sums = [old + column_sum(new) for old, new in zip(sums, terms)]
            gmid_ref[here, :] = gmid
            gbranch = gmid.astype(bf16)
            feed[here, :] = gbranch
            gatt_ref[here, :] = dot(gbranch, project_ref[...], NT).astype(bf16)
        total = dot(att0_ref[...], feed[:item_rows, :], TN)
        total += dot(att1_ref[...], feed[item_rows:, :], TN)
        gproject_ref[...] = total.astype(bf16)
        gvec_ref[...] = jnp.concatenate(sums + [jnp.zeros((4, width), f32)], axis=0)


def feed_forward(live, att0, att1, project, hidden, cotangent, vecs, expand, ebias, reduce):
    rows, width = hidden.shape
    item_rows = att0.shape[0]
    units = reduce.shape[0]
    steps = units // FF_BLOCK
    whole = lambda shape: pl.BlockSpec(
        shape, lambda j, *_: (0,) * len(shape), pipeline_mode=pl.Buffered(1)
    )
    shape = jax.ShapeDtypeStruct
    return pl.pallas_call(
        functools.partial(feed_kernel, item_rows=item_rows),
        grid_spec=pltpu.PrefetchScalarGridSpec(
            num_scalar_prefetch=1,
            grid=(steps,),
            in_specs=[
                whole(att0.shape),
                whole(att1.shape),
                whole(project.shape),
                whole(hidden.shape),
                whole(cotangent.shape),
                whole(vecs.shape),
                pl.BlockSpec((width, FF_BLOCK), lambda j, *_: (0, j)),
                pl.BlockSpec((1, FF_BLOCK), lambda j, *_: (0, j)),
                pl.BlockSpec((FF_BLOCK, width), lambda j, *_: (j, 0)),
            ],
            out_specs=[
                whole((rows, width)),
                whole((rows, width)),
                whole((rows, width)),
                whole((width, width)),
                whole((8, width)),
                pl.BlockSpec((width, FF_BLOCK), lambda j, *_: (j, 0)),
                pl.BlockSpec((FF_BLOCK, width), lambda j, *_: (j, 0)),
                pl.BlockSpec((1, FF_BLOCK), lambda j, *_: (0, j)),
            ],
            scratch_shapes=[
                pltpu.VMEM((rows, width), f32),
                pltpu.VMEM((rows, width), bf16),
                pltpu.VMEM((rows, width), bf16),
                pltpu.VMEM((rows, width), f32),
                pltpu.VMEM((rows, width), f32),
            ],
        ),
        out_shape=[
            shape((rows, width), bf16),
            shape((rows, width), f32),
            shape((rows, width), bf16),
            shape((width, width), bf16),
            shape((8, width), f32),
            shape((steps * width, FF_BLOCK), bf16),
            shape((units, width), bf16),
            shape((1, units), f32),
        ],
        compiler_params=params(),
        cost_estimate=cost(12 * rows * width * units, 40 << 20, 2 * rows * units),
        name="feed_forward",
    )(live, att0, att1, project, hidden, cotangent, vecs, expand, ebias, reduce)


def weight_kernel(normed_ref, img0_ref, img1_ref, *refs):
    grads, (out_ref, sums_ref) = refs[:10], refs[10:]
    rows, width = normed_ref.shape
    half = rows // 2
    sums = []
    for part in range(3):
        total = dot(normed_ref[:half, :], grads[part][...], TN)
        total += dot(normed_ref[half:, :], grads[5 + part][...], TN)
        sums.append(
            column_sum(grads[part][...].astype(f32)) + column_sum(grads[5 + part][...].astype(f32))
        )
        if part > 0:
            total += dot(img0_ref[...], grads[2 + part][...], TN)
            total += dot(img1_ref[...], grads[7 + part][...], TN)
        if part == 2:
            sums[2] += column_sum(grads[4][...].astype(f32)) + column_sum(
                grads[9][...].astype(f32)
            )
        out_ref[part * width : (part + 1) * width, :] = total.astype(bf16)
    zeros = jnp.zeros((6, sums[0].shape[1]), f32)
    sums_ref[...] = jnp.concatenate([sums[0], sums[2], zeros], axis=0)


def weight_grads(normed, img0, img1, first_grads, second_grads):
    rows, width = normed.shape
    cols = first_grads[0].shape[1]
    return pl.pallas_call(
        weight_kernel,
        out_shape=[
            jax.ShapeDtypeStruct((3 * width, cols), bf16),
            jax.ShapeDtypeStruct((8, cols), f32),
        ],
        compiler_params=params(),
        cost_estimate=cost(8 * rows * width * cols, 8 << 20),
        name="weight_grads",
    )(normed, img0, img1, *first_grads, *second_grads)


def image_grad_kernel(weight_ref, *refs):
    grads, out_ref = refs[:-1], refs[-1]
    width = weight_ref.shape[0]
    groups = len(grads) // 4
    for item in range(2):
        total = jnp.zeros((IMG_PAD, width), f32)
        for part in range(2):
            offset = (1 + part) * width
            for group in range(groups):
                grad = grads[(item * groups + group) * 2 + part][...]
                total += dot(grad, weight_ref[:, offset : offset + grad.shape[1]], NT)
                offset += grad.shape[1]
        out_ref[item] = total.astype(bf16)


def image_grads(weight, grads):
    width = weight.shape[0]
    return pl.pallas_call(
        image_grad_kernel,
        out_shape=jax.ShapeDtypeStruct((2, IMG_PAD, width), bf16),
        compiler_params=params(),
        cost_estimate=cost(8 * IMG_PAD * width * width, 6 << 20),
        name="image_grads",
    )(weight, *grads)


def row_grad_kernel(weight_ref, *refs):
    grads, out_ref = refs[:-1], refs[-1]
    width = weight_ref.shape[0]
    groups = len(grads) // 6
    half = out_ref.shape[0] // 2
    for item in range(2):
        total = jnp.zeros((half, width), f32)
        for part in range(3):
            offset = part * width
            for group in range(groups):
                grad = grads[(item * groups + group) * 3 + part][...]
                total += dot(grad, weight_ref[:, offset : offset + grad.shape[1]], NT)
                offset += grad.shape[1]
        out_ref[item * half : (item + 1) * half, :] = total


def row_grads(weight, grads, rows):
    width = weight.shape[0]
    return pl.pallas_call(
        row_grad_kernel,
        out_shape=jax.ShapeDtypeStruct((rows, width), f32),
        compiler_params=params(),
        cost_estimate=cost(6 * rows * width * width, 12 << 20),
        name="row_grads",
    )(weight, *grads)


def finish_kernel(hid_ref, gmid_ref, gnorm_ref, near_ref, far_ref, vec_ref, out_ref, sums_ref):
    rows, width = hid_ref.shape
    half = rows // 2
    sums = [jnp.zeros((1, width), f32)] * 2
    for start in range(0, rows, IMG_PAD):
        here = slice(start, start + IMG_PAD)
        unit, scale = normalise(hid_ref[here, :].astype(f32))
        grad = gnorm_ref[here, :]
        if start % half == 0:
            item = start // half
            near = near_ref[item].astype(f32) * vec_ref[1:2]
            grad = grad + near + far_ref[item].astype(f32)
        sums = [sums[0] + column_sum(grad * unit), sums[1] + column_sum(grad)]
        total = gmid_ref[here, :] + norm_transpose(unit, scale, vec_ref[0:1], grad)
        out_ref[here, :] = total.astype(bf16)
    sums_ref[...] = jnp.concatenate(sums + [jnp.zeros((6, width), f32)], axis=0)


def finish_rows(hidden, gmid, gnorm, near, far, vecs):
    rows, width = hidden.shape
    return pl.pallas_call(
        finish_kernel,
        out_shape=[
            jax.ShapeDtypeStruct((rows, width), bf16),
            jax.ShapeDtypeStruct((8, width), f32),
        ],
        compiler_params=params(),
        cost_estimate=cost(40 * rows * width, 14 * rows * width),
        name="finish_rows",
    )(hidden, gmid, gnorm, near, far, vecs)


def swap(value, axes, pair_of):
    count = 1
    for axis in axes:
        count *= lax.axis_size(axis)
    return lax.ppermute(value, axes, [(source, pair_of(source)) for source in range(count)])


def place_of(axes):
    place = 0
    for axis in axes:
        place = place * lax.axis_size(axis) + lax.axis_index(axis)
    return place


def stage_bits(axes):
    count = 1
    for axis in axes:
        count *= lax.axis_size(axis)
    bits = count.bit_length() - 1
    core = len(axes) - 1
    others = [bit for bit in range(bits) if bit != core]
    if len(axes) == 1:
        if len(others) == 3:
            return [(core, core), (1, 2), (3, 1), (2, 3)]
    elif len(others) == 4:
        return [(core, core), (0, 2), (3, 0), (2, 3), (4, 4)]
    turned = others[1:] + others[:1]
    return [(core, core)] + list(zip(others, turned))


def partner(source, pair, core):
    return source ^ (1 << pair[(source >> core) & 1])


def all_sum(value, axes):
    place = place_of(axes)
    core = len(axes) - 1
    on_second = ((place >> core) & 1) == 1
    stages = stage_bits(axes)
    terms = (value,)

    def part(which, half):
        found = [lax.dynamic_slice_in_dim(t, which * half, half, 0) for t in terms]
        if len(found) == 1:
            return found[0]
        return (found[0].astype(f32) + found[1].astype(f32)).astype(bf16)

    for pair in stages:
        half = terms[0].shape[0] // 2
        side = (place >> jnp.where(on_second, pair[1], pair[0])) & 1
        sent = part(1 - side, half)
        kept = part(side, half)
        got = swap(sent, axes, functools.partial(partner, pair=pair, core=core))
        terms = (kept, got)
    mine = (terms[0].astype(f32) + terms[1].astype(f32)).astype(bf16)
    for pair in reversed(stages):
        side = (place >> jnp.where(on_second, pair[1], pair[0])) & 1
        got = swap(mine, axes, functools.partial(partner, pair=pair, core=core))
        low = jnp.where(side == 0, mine, got)
        high = jnp.where(side == 0, got, mine)
        mine = jnp.concatenate([low, high], axis=0)
    return mine


def small_sum(value, axis):
    for bit in range(lax.axis_size(axis).bit_length() - 1):
        value = value + swap(value, (axis,), lambda source, bit=bit: source ^ (1 << bit))
    return value


def on_device(
    hidden_in,
    image_count,
    text_lengths,
    attend_gain,
    attend_shift,
    project_in,
    bias_pair,
    project_out,
    project_bias,
    feed_gain,
    feed_shift,
    expand_weight,
    expand_bias,
    reduce_weight,
    reduce_bias,
    cotangent,
):
    items, _, rows, width = hidden_in.shape
    is_text = lax.axis_index("mod") == 1
    hidden = hidden_in.reshape(items * rows, width)
    to_text = lambda value: lax.ppermute(value, "mod", [(0, 1)])
    to_image = lambda value: lax.ppermute(value, "mod", [(1, 0)])

    attend_vecs = jnp.concatenate([attend_gain, attend_shift], axis=0)
    image_vecs = jnp.where(is_text, to_text(attend_vecs), attend_vecs)
    ends = jnp.cumsum(text_lengths, axis=1)
    text_flag = is_text.astype(jnp.int32)
    images = []
    for item in range(items):
        own_image = hidden_in[item, 0, :IMG_PAD]
        images.append(jnp.where(is_text, to_text(own_image), own_image))

    normed, projected = project_rows(hidden, attend_vecs, project_in, bias_pair)
    infos, normed_images, image_pairs, attended, lses = [], [], [], [], []
    for item in range(items):
        info = jnp.stack(
            [image_count[item], *(ends[item, j] for j in range(ends.shape[1])), text_flag]
        )
        infos.append(info)
        normed_image, image_pair = image_rows(images[item], image_vecs, project_in, bias_pair)
        normed_images.append(normed_image)
        image_pairs.append(image_pair)
        out, lse = attend_forward(info, item, projected, image_pair)
        attended.append(out)
        lses.append(lse)

    live = jnp.where(is_text, rows, image_count)
    feed_vecs = jnp.concatenate(
        [project_bias[None], feed_gain, feed_shift, reduce_bias, jnp.zeros((4, width), f32)], axis=0
    )
    (
        hidden_out,
        grad_middle,
        grad_attended,
        project_out_grad,
        vec_grads,
        expand_grad,
        reduce_grad,
        expand_bias_grad,
    ) = feed_forward(
        live,
        attended[0],
        attended[1],
        project_out,
        hidden,
        cotangent.reshape(items * rows, width),
        feed_vecs,
        expand_weight[0],
        expand_bias,
        reduce_weight[0],
    )
    reduce_grad = all_sum(reduce_grad, ("dp",))
    expand_grad = all_sum(expand_grad, ("dp",))
    project_out_grad = all_sum(project_out_grad, ("dp", "mod"))

    start = 0
    row_parts = [[], []]
    image_parts = [[], []]
    blocks = []
    pair_sums = []
    for pairs in GROUPS:
        grads = [
            attend_backward(
                infos[item],
                item,
                start,
                pairs,
                projected,
                image_pairs[item],
                attended[item],
                grad_attended,
                lses[item],
            )
            for item in range(items)
        ]
        for item in range(items):
            row_parts[item] += grads[item][:3]
            image_parts[item] += grads[item][3:]
        block, sums = weight_grads(normed, normed_images[0], normed_images[1], grads[0], grads[1])
        blocks.append(all_sum(block, ("dp", "mod")))
        pair_sums.append(sums)
        start += pairs

    near = image_grads(project_in, image_parts[0] + image_parts[1])
    far = to_image(near)
    grad_normed = row_grads(project_in, row_parts[0] + row_parts[1], items * rows)
    image_flag = jnp.where(is_text, 0.0, 1.0) * jnp.ones((1, width), f32)
    finish_vecs = jnp.concatenate([attend_gain, image_flag, jnp.zeros((6, width), f32)], axis=0)
    grad_in, attend_sums = finish_rows(hidden, grad_middle, grad_normed, near, far, finish_vecs)

    early = small_sum(
        jnp.concatenate([vec_grads[:4], expand_bias_grad.reshape(-1, width)], axis=0), "dp"
    )
    bias_pair_grad = jnp.concatenate(pair_sums, axis=1)[:2]
    late = small_sum(jnp.concatenate([attend_sums[:2], bias_pair_grad], axis=0), "dp")
    shared = small_sum(jnp.concatenate([early[3:4], late[2:4]], axis=0), "mod")

    cols = [[], [], []]
    for block in blocks:
        for part in range(3):
            cols[part].append(block[part * width : (part + 1) * width])
    project_in_grad = jnp.concatenate(cols[0] + cols[1] + cols[2], axis=1).astype(f32)
    expand_grad = expand_grad.reshape(-1, width, FF_BLOCK).transpose(1, 0, 2).reshape(width, -1)
    return (
        hidden_out.reshape(hidden_in.shape),
        grad_in.reshape(hidden_in.shape),
        late[0:1],
        late[1:2],
        project_in_grad,
        shared[1:3],
        project_out_grad.astype(f32),
        shared[0],
        early[0:1],
        early[1:2],
        expand_grad.astype(f32)[None],
        early[4:].reshape(1, -1),
        reduce_grad.astype(f32)[None],
        early[2:3],
    )


def solution(mesh):
    in_specs = (
        P("dp", "mod", None, None),
        P("dp"),
        P("dp", None),
        P("mod", None),
        P("mod", None),
        P(),
        P(),
        P(),
        P(),
        P("mod", None),
        P("mod", None),
        P("mod", None, None),
        P("mod", None),
        P("mod", None, None),
        P("mod", None),
        P("dp", "mod", None, None),
    )
    out_specs = (
        P("dp", "mod", None, None),
        P("dp", "mod", None, None),
        P("mod", None),
        P("mod", None),
        P(),
        P(),
        P(),
        P(),
        P("mod", None),
        P("mod", None),
        P("mod", None, None),
        P("mod", None),
        P("mod", None, None),
        P("mod", None),
    )
    return jax.shard_map(
        on_device, mesh=mesh, in_specs=in_specs, out_specs=out_specs, check_vma=False
    )
```

```python
import functools

import jax
import jax.numpy as jnp
from jax import lax
from jax.experimental import pallas as pl
from jax.experimental.pallas import tpu as pltpu
from jax.sharding import PartitionSpec as P

HEADS = 12
HEAD = 64
IMG_PAD = 256
PAIR = 2 * HEAD
PAIRS = HEADS // 2
GROUP_PAIRS = 2
GROUPS = PAIRS // GROUP_PAIRS
LANES = GROUP_PAIRS * PAIR
FF_BLOCK = 768

masked_value = -1e30
norm_eps = 1e-05

bf16 = jnp.bfloat16
f32 = jnp.float32

NN = (((1,), (0,)), ((), ()))
NT = (((1,), (1,)), ((), ()))
TN = (((0,), (0,)), ((), ()))
VMEM_BYTES = 56 << 20


def dot(left, right, dims=NN):
    return lax.dot_general(left, right, dims, preferred_element_type=f32)


def column_sum(values):
    return jnp.sum(values, axis=0, keepdims=True)


def row_mean(values):
    return jnp.mean(values, axis=1, keepdims=True)


def normalise(values):
    centred = values - row_mean(values)
    scale = lax.rsqrt(row_mean(centred * centred) + norm_eps)
    return centred * scale, scale


def norm_transpose(unit, scale, gain, grad):
    grad_unit = grad * gain
    return scale * (grad_unit - row_mean(grad_unit) - unit * row_mean(grad_unit * unit))


def cost(flops, moved, special=0):
    del flops, moved, special
    return pl.CostEstimate(flops=1, bytes_accessed=1, transcendentals=0)


class Order:
    def __init__(self):
        self.zero = None

    def tie(self, value):
        value, self.zero = lax.optimization_barrier((value, self.zero))
        return value


def call(order, kernel, inputs, out_shape, name, estimate, scalars=(), grid=(), specs=None, outs=None,
         scratch=(), aliases=None):
    tokens = () if order.zero is None else (order.zero,)
    count = len(scalars) + len(inputs)
    unused = len(tokens)
    vmem = pl.BlockSpec(memory_space=pltpu.VMEM)
    given = len(out_shape)
    end = count + unused + given

    def body(*refs):
        refs[end][0, 0] = 0
        kernel(*refs[:count], *refs[count + unused : end], *refs[end + 1 :])

    specs = [vmem] * len(inputs) if specs is None else list(specs)
    outs = [vmem] * given if outs is None else list(outs)
    *found, order.zero = pl.pallas_call(
        body,
        grid_spec=pltpu.PrefetchScalarGridSpec(
            num_scalar_prefetch=len(scalars),
            grid=grid,
            in_specs=specs + [pl.BlockSpec(memory_space=pl.ANY)] * unused,
            out_specs=outs + [pl.BlockSpec(memory_space=pltpu.SMEM)],
            scratch_shapes=list(scratch),
        ),
        out_shape=list(out_shape) + [jax.ShapeDtypeStruct((1, 1), jnp.int32)],
        input_output_aliases=aliases or {},
        compiler_params=pltpu.CompilerParams(vmem_limit_bytes=VMEM_BYTES),
        cost_estimate=estimate,
        name=name,
    )(*scalars, *inputs, *tokens)
    return found if given > 1 else found[0]


def shaped(shape, dtype):
    return jax.ShapeDtypeStruct(shape, dtype)


def resident(shape):
    return pl.BlockSpec(shape, lambda *_: (0,) * len(shape), pipeline_mode=pl.Buffered(1))


def project_kernel(hid_ref, gain_ref, shift_ref, weight_ref, bias_ref, normed_ref, out_ref):
    unit, _ = normalise(hid_ref[...].astype(f32))
    normed = (unit * gain_ref[...] + shift_ref[...]).astype(bf16)
    normed_ref[...] = normed
    width = normed.shape[1]
    for part in range(3):
        cols = slice(part * width, (part + 1) * width)
        rows = dot(normed, weight_ref[:, cols])
        if part == 0:
            rows = (rows + bias_ref[0:1]).astype(bf16) * jnp.asarray(HEAD**-0.5, bf16)
        if part == 2:
            rows = rows + bias_ref[1:2]
        out_ref[:, cols] = rows.astype(bf16)


def project_rows(order, hidden, gain, shift, weight, bias):
    rows, width = hidden.shape
    block = 256
    blocked = lambda cols: pl.BlockSpec((block, cols), lambda r: (r, 0))
    inputs = (hidden, gain, shift, weight, bias)
    return call(
        order,
        project_kernel,
        inputs,
        [shaped((rows, width), bf16), shaped((rows, 3 * width), bf16)],
        "project_rows",
        cost(6 * rows * width * width, 10 * rows * width + 6 * width * width),
        grid=(rows // block,),
        specs=[blocked(width)] + [resident(value.shape) for value in inputs[1:]],
        outs=[blocked(width), blocked(3 * width)],
    )


def image_kernel(
    flag_ref,
    own_ref,
    far_ref,
    gain_ref,
    shift_ref,
    vec_ref,
    keys_ref,
    values_ref,
    bias_ref,
    normed_ref,
    out_ref,
):
    is_text = flag_ref[0] == 1
    hidden = jnp.where(is_text, far_ref[...].astype(f32), own_ref[...].astype(f32))
    gain = jnp.where(is_text, vec_ref[0:1], gain_ref[...])
    shift = jnp.where(is_text, vec_ref[1:2], shift_ref[...])
    unit, _ = normalise(hidden)
    normed = (unit * gain + shift).astype(bf16)
    normed_ref[...] = normed
    width = normed.shape[1]
    out_ref[:, :width] = dot(normed, keys_ref[...]).astype(bf16)
    out_ref[:, width:] = (dot(normed, values_ref[...]) + bias_ref[1:2]).astype(bf16)


def image_rows(order, flag, item, hidden, far, gain, shift, vecs, weight, bias, item_rows):
    width = hidden.shape[1]
    place = item * (item_rows // IMG_PAD)
    half = lambda base: pl.BlockSpec((width, width), lambda *_: (0, base))
    return call(
        order,
        image_kernel,
        (hidden, far, gain, shift, vecs, weight, weight, bias),
        [shaped((IMG_PAD, width), bf16), shaped((IMG_PAD, 2 * width), bf16)],
        "image_rows",
        cost(4 * IMG_PAD * width * width, 6 << 20),
        scalars=(flag,),
        grid=(1,),
        specs=[
            pl.BlockSpec((IMG_PAD, width), lambda *_: (place, 0)),
            resident(far.shape),
            resident(gain.shape),
            resident(shift.shape),
            resident(vecs.shape),
            half(1),
            half(2),
            resident(bias.shape),
        ],
        outs=[resident((IMG_PAD, width)), resident((IMG_PAD, 2 * width))],
    )


def segments(shape, axis, lengths_ref, item):
    places = lax.broadcasted_iota(jnp.int32, shape, axis)
    total = jnp.zeros(shape, jnp.int32)
    end = 0
    for which in range(lengths_ref.shape[1]):
        end = end + lengths_ref[item, which]
        total += (places >= end).astype(jnp.int32)
    return total


def own_bias(rows, flag_ref, lengths_ref, item):
    shape = (rows, rows)
    same = segments(shape, 0, lengths_ref, item) == segments(shape, 1, lengths_ref, item)
    return jnp.where(same & (flag_ref[0] == 1), 0.0, masked_value).astype(f32)


def image_bias(shape, axis, count_ref, item):
    places = lax.broadcasted_iota(jnp.int32, shape, axis)
    return jnp.where(places < count_ref[item], 0.0, masked_value).astype(f32)


def forward_kernel(
    item,
    flag_ref,
    count_ref,
    lengths_ref,
    q_ref,
    k_ref,
    v_ref,
    ik_ref,
    iv_ref,
    out_ref,
    lse_ref,
    image_part,
    own_part,
):
    rows = q_ref.shape[0]

    @pl.when(pl.program_id(0) == 0)
    def _():
        image_part[...] = image_bias(image_part.shape, 1, count_ref, item)
        own_part[...] = own_bias(rows, flag_ref, lengths_ref, item)

    first = lax.broadcasted_iota(jnp.int32, (rows, PAIR), 1) < HEAD
    zero = jnp.zeros((), bf16)
    q = q_ref[...]
    image_keys, image_values = ik_ref[...], iv_ref[...]
    keys, values = k_ref[...], v_ref[...]
    outs, tops = [], []
    for head in range(2):
        q_head = jnp.where(first, q, zero) if head == 0 else jnp.where(first, zero, q)
        far = dot(q_head, image_keys, NT) + image_part[...]
        own = dot(q_head, keys, NT) + own_part[...]
        top = jnp.maximum(
            jnp.max(far, axis=1, keepdims=True), jnp.max(own, axis=1, keepdims=True)
        )
        far = jnp.exp(far - top)
        own = jnp.exp(own - top)
        total = jnp.sum(far, axis=1, keepdims=True) + jnp.sum(own, axis=1, keepdims=True)
        summed = dot(far.astype(bf16), image_values) + dot(own.astype(bf16), values)
        outs.append(summed / total)
        tops.append(top + jnp.log(total))
    out_ref[...] = jnp.where(first, outs[0], outs[1]).astype(bf16)
    turned = jnp.transpose(jnp.where(first, tops[0], tops[1]))
    lse_ref[0, 0:1, :] = turned[0:1]
    lse_ref[0, 1:2, :] = turned[HEAD : HEAD + 1]


def attend_forward(order, scalars, item, projected, image):
    rows = projected.shape[0] // 2
    spec = lambda base: pl.BlockSpec((rows, PAIR), lambda h, *_: (item, base + h))
    far = lambda base: pl.BlockSpec((IMG_PAD, PAIR), lambda h, *_: (0, base + h))
    keys = rows + IMG_PAD
    return call(
        order,
        functools.partial(forward_kernel, item),
        (projected, projected, projected, image, image),
        [shaped((rows, HEADS * HEAD), bf16), shaped((PAIRS, 2, rows), f32)],
        "attend_forward",
        cost(16 * HEADS * rows * keys * HEAD, 6 << 20, HEADS * rows * keys),
        scalars=scalars,
        grid=(PAIRS,),
        specs=[spec(0), spec(PAIRS), spec(2 * PAIRS), far(0), far(PAIRS)],
        outs=[
            pl.BlockSpec((rows, PAIR), lambda h, *_: (0, h)),
            pl.BlockSpec((1, 2, rows), lambda h, *_: (h, 0, 0)),
        ],
        scratch=[pltpu.VMEM((rows, IMG_PAD), f32), pltpu.VMEM((rows, rows), f32)],
    )


def backward_kernel(
    item,
    flag_ref,
    count_ref,
    lengths_ref,
    q_ref,
    k_ref,
    v_ref,
    ik_ref,
    iv_ref,
    out_ref,
    grad_ref,
    lse_ref,
    *refs,
):
    gq_ref, gk_ref, gv_ref, gik_ref, giv_ref, image_part, own_part = refs[-7:]
    rows = q_ref.shape[0]

    @pl.when(pl.program_id(0) == 0)
    def _():
        image_part[...] = image_bias(image_part.shape, 0, count_ref, item)
        own_part[...] = own_bias(rows, flag_ref, lengths_ref, item)

    first = lax.broadcasted_iota(jnp.int32, (rows, PAIR), 1) < HEAD
    zero = jnp.zeros((), bf16)
    q, grad = q_ref[...], grad_ref[...]
    products = grad.astype(f32) * out_ref[...].astype(f32)
    head_lanes = lax.broadcasted_iota(jnp.int32, (8, PAIR), 1) // HEAD
    head_rows = lax.broadcasted_iota(jnp.int32, (8, PAIR), 0)
    center = lax.dot_general(
        (head_lanes == head_rows).astype(f32),
        products,
        NT,
        preferred_element_type=f32,
        precision=lax.Precision.HIGHEST,
    )
    q_heads = [jnp.where(first, q, zero), jnp.where(first, zero, q)]
    grad_heads = [jnp.where(first, grad, zero), jnp.where(first, zero, grad)]
    lse = lse_ref[0]
    grad_query = [None, None]
    half = rows // 2
    pieces = (
        (ik_ref, iv_ref, gik_ref, giv_ref, image_part, 0, IMG_PAD),
        (k_ref, v_ref, gk_ref, gv_ref, own_part, 0, half),
        (k_ref, v_ref, gk_ref, gv_ref, own_part, half, half),
    )
    for keys_ref, values_ref, gk_out, gv_out, bias, start, count in pieces:
        piece = slice(start, start + count)
        keys, values = keys_ref[piece, :], values_ref[piece, :]
        low_lanes = lax.broadcasted_iota(jnp.int32, (count, PAIR), 1) < HEAD
        grad_keys, grad_values = [], []
        for head in range(2):
            scores = dot(keys, q_heads[head], NT) + bias[piece, :]
            probs = jnp.exp(scores - lse[head : head + 1])
            grad_probs = dot(values, grad_heads[head], NT)
            grad_scores = (probs * (grad_probs - center[head : head + 1])).astype(bf16)
            grad_values.append(dot(probs.astype(bf16), grad))
            grad_keys.append(dot(grad_scores, q))
            term = dot(grad_scores, keys, TN)
            grad_query[head] = term if grad_query[head] is None else grad_query[head] + term
        gk_out[piece, :] = jnp.where(low_lanes, grad_keys[0], grad_keys[1]).astype(bf16)
        gv_out[piece, :] = jnp.where(low_lanes, grad_values[0], grad_values[1]).astype(bf16)
    gq_ref[...] = (jnp.where(first, grad_query[0], grad_query[1]) * HEAD**-0.5).astype(bf16)


def attend_backward(order, scalars, item, start, pairs, projected, image, attended, grad, lse, earlier):
    rows, width = attended.shape
    spec = lambda base: pl.BlockSpec((rows, PAIR), lambda h, *_: (item, base + start + h))
    far = lambda base: pl.BlockSpec((IMG_PAD, PAIR), lambda h, *_: (0, base + start + h))
    own = pl.BlockSpec((rows, PAIR), lambda h, *_: (0, start + h))
    far_outs = pl.BlockSpec((IMG_PAD, PAIR), lambda h, *_: (item, start + h))
    keys = rows + IMG_PAD
    inputs = (projected, projected, projected, image, image, attended, grad, lse)
    first = len(scalars) + len(inputs)
    return call(
        order,
        functools.partial(backward_kernel, item),
        (*inputs, *earlier),
        [shaped((2 * rows, width), bf16)] * 3 + [shaped((2 * IMG_PAD, width), bf16)] * 2,
        "attend_backward",
        cost(80 * pairs * rows * keys * HEAD, pairs * 2 << 20, 2 * pairs * rows * keys),
        scalars=scalars,
        grid=(pairs,),
        specs=[
            spec(0),
            spec(PAIRS),
            spec(2 * PAIRS),
            far(0),
            far(PAIRS),
            own,
            spec(0),
            pl.BlockSpec((1, 2, rows), lambda h, *_: (start + h, 0, 0)),
        ]
        + [pl.BlockSpec(memory_space=pl.ANY)] * len(earlier),
        outs=[spec(0), spec(0), spec(0), far_outs, far_outs],
        scratch=[pltpu.VMEM((IMG_PAD, rows), f32), pltpu.VMEM((rows, rows), f32)],
        aliases={first + at: at for at in range(len(earlier))},
    )


def gelu_pair(values):
    share = 0.5 * (1.0 + lax.erf(values * 0.7071067811865476))
    slope = share + values * jnp.exp(-0.5 * values * values) * 0.3989422804014327
    return values * share, slope


def feed_step(step, rows, item_rows, feed, top, result, gfeed, expand_ref, ebias_ref, reduce_ref):
    width = feed.shape[1]
    expand, reduce = expand_ref[...], reduce_ref[...]
    active_parts, gup_parts = [], []
    for start in range(0, rows, item_rows):
        here = slice(start, start + item_rows)
        upward = dot(feed[here, :], expand) + ebias_ref[...]
        gactive = dot(top[here, :], reduce, NT)
        active, slope = gelu_pair(upward)
        active = active.astype(bf16)
        gup = (gactive * slope).astype(bf16)
        result[here, :] += dot(active, reduce)
        gfeed[here, :] += dot(gup, expand, NT)
        active_parts.append(active)
        gup_parts.append(gup)
    active = jnp.concatenate(active_parts, axis=0)
    gup = jnp.concatenate(gup_parts, axis=0)
    greduce = dot(active, top[...], TN).astype(bf16)
    gexpand = dot(feed[...], gup, TN).astype(bf16)
    pieces = [greduce[:, at : at + LANES] for at in range(0, width, LANES)]
    pieces += [gexpand[:, at : at + LANES] for at in range(0, FF_BLOCK, LANES)]
    return pieces, column_sum(gup.astype(f32))


def store_pieces(out, pieces):
    at = 0
    for half in range(2):
        for piece in pieces:
            rows = piece.shape[0] // 2
            out[at : at + rows, :] = piece[half * rows : (half + 1) * rows]
            at += rows


def feed_kernel(
    flag_ref,
    count_ref,
    side_ref,
    att0_ref,
    att1_ref,
    project_ref,
    hid_ref,
    cot_ref,
    project_bias_ref,
    gain_ref,
    shift_ref,
    reduce_bias_ref,
    expand_ref,
    ebias_ref,
    reduce_ref,
    out_ref,
    gmid_ref,
    gatt_ref,
    gproject_ref,
    gvec_ref,
    gebias_ref,
    keep0_ref,
    send0_ref,
    keep1_ref,
    send1_ref,
    middle,
    feed,
    top,
    result,
    gfeed,
    low_out,
    gatt,
    grads,
    grad_sems,
    row_sems,
    *,
    item_rows,
):
    step = pl.program_id(0)
    rows, width = hid_ref.shape
    block = 256
    att_refs = (att0_ref, att1_ref)
    half = grads.shape[1] // 2

    steps = grads.shape[0]

    def grad_copies(which):
        found = []
        chunk, place = divmod(which, steps // 2)
        outs = (keep1_ref, send1_ref) if chunk else (keep0_ref, send0_ref)
        for number, out in enumerate(outs):
            side = side_ref[0] if number == 0 else 1 - side_ref[0]
            here = grads.at[which, pl.ds(pl.multiple_of(side * half, half), half)]
            there = out.at[pl.ds(place * half, half)]
            found.append(pltpu.make_async_copy(here, there, grad_sems.at[which, number]))
        return found

    @pl.when(step == 0)
    def _():
        for start in range(0, rows, block):
            here = slice(start, start + block)
            inside = slice(start % item_rows, start % item_rows + block)
            att = att_refs[start // item_rows][inside, :]
            branch = dot(att, project_ref[...]) + project_bias_ref[...]
            x = hid_ref[here, :].astype(f32) + branch
            middle[here, :] = x
            unit, _ = normalise(x)
            feed[here, :] = (unit * gain_ref[...] + shift_ref[...]).astype(bf16)
            at = lax.broadcasted_iota(jnp.int32, (block, width), 0) + start % item_rows
            limit = jnp.where(flag_ref[0] == 1, item_rows, count_ref[start // item_rows])
            top[here, :] = jnp.where(at < limit, cot_ref[here, :].astype(f32), 0.0).astype(bf16)
            result[here, :] = x + reduce_bias_ref[...]
            gfeed[here, :] = jnp.zeros((block, width), f32)

    pieces, gebias_ref[...] = feed_step(
        step, rows, item_rows, feed, top, result, gfeed, expand_ref, ebias_ref, reduce_ref
    )
    store_pieces(grads.at[step], pieces)
    for which in range(steps):

        @pl.when(step == which)
        def _(which=which):
            for copy in grad_copies(which):
                copy.start()

    @pl.when(step == pl.num_programs(0) - 1)
    def _():
        copies = []
        sums = [jnp.zeros((1, width), f32)] * 4
        for number, start in enumerate(range(0, rows, block)):
            here = slice(start, start + block)
            low_out[here, :] = result[here, :].astype(bf16)
            unit, scale = normalise(middle[here, :])
            grad = gfeed[here, :]
            grad_top = top[here, :].astype(f32)
            gmid = grad_top + norm_transpose(unit, scale, gain_ref[...], grad)
            terms = (grad * unit, grad, grad_top, gmid)
            sums = [old + column_sum(new) for old, new in zip(sums, terms)]
            middle[here, :] = gmid
            gbranch = gmid.astype(bf16)
            feed[here, :] = gbranch
            gatt[here, :] = dot(gbranch, project_ref[...], NT).astype(bf16)
            for kind, (mine, there) in enumerate(
                ((low_out, out_ref), (middle, gmid_ref), (gatt, gatt_ref))
            ):
                span = pl.ds(start, block)
                copy = pltpu.make_async_copy(
                    mine.at[span, :], there.at[span, :], row_sems.at[kind, number]
                )
                copy.start()
                copies.append(copy)
        total = dot(att0_ref[...], feed[:item_rows, :], TN)
        total += dot(att1_ref[...], feed[item_rows:, :], TN)
        gproject_ref[...] = total.astype(bf16)
        gvec_ref[...] = jnp.concatenate(sums + [jnp.zeros((4, width), f32)], axis=0)
        for copy in copies:
            copy.wait()
        for which in range(steps):
            for copy in grad_copies(which):
                copy.wait()


def feed_forward(order, flag, count, side, att0, att1, project, hidden, cotangent, vecs, expand, ebias, reduce):
    rows, width = hidden.shape
    item_rows = att0.shape[0]
    units = reduce.shape[0]
    steps = units // FF_BLOCK
    block_rows = 2 * width * FF_BLOCK // LANES
    fixed = (att0, att1, project, hidden, cotangent, *vecs)
    anywhere = pl.BlockSpec(memory_space=pl.ANY)
    return call(
        order,
        functools.partial(feed_kernel, item_rows=item_rows),
        (*fixed, expand, ebias, reduce),
        [
            shaped((rows, width), bf16),
            shaped((rows, width), f32),
            shaped((rows, width), bf16),
            shaped((width, width), bf16),
            shaped((8, width), f32),
            shaped((1, units), f32),
        ]
        + [shaped((steps // 2 * block_rows // 2, LANES), bf16)] * 4,
        "feed_forward",
        cost(12 * rows * width * units, 40 << 20, 2 * rows * units),
        scalars=(flag, count, side),
        grid=(steps,),
        specs=[resident(value.shape) for value in fixed]
        + [
            pl.BlockSpec((width, FF_BLOCK), lambda j, *_: (0, j)),
            pl.BlockSpec((1, FF_BLOCK), lambda j, *_: (0, j)),
            pl.BlockSpec((FF_BLOCK, width), lambda j, *_: (j, 0)),
        ],
        outs=[
            anywhere,
            anywhere,
            anywhere,
            resident((width, width)),
            resident((8, width)),
            pl.BlockSpec((1, FF_BLOCK), lambda j, *_: (0, j)),
        ]
        + [anywhere] * 4,
        scratch=[
            pltpu.VMEM((rows, width), f32),
            pltpu.VMEM((rows, width), bf16),
            pltpu.VMEM((rows, width), bf16),
            pltpu.VMEM((rows, width), f32),
            pltpu.VMEM((rows, width), f32),
            pltpu.VMEM((rows, width), bf16),
            pltpu.VMEM((rows, width), bf16),
            pltpu.VMEM((steps, block_rows, LANES), bf16),
            pltpu.SemaphoreType.DMA((steps, 2)),
            pltpu.SemaphoreType.DMA((3, rows // 256)),
        ],
    )


def weight_kernel(
    side_ref,
    normed_ref,
    image_ref,
    gq_ref,
    gk_ref,
    gv_ref,
    gik_ref,
    giv_ref,
    extra_ref,
    keep_ref,
    send_ref,
    query_ref,
    value_ref,
    turned,
    image_turned,
):
    step = pl.program_id(0)
    kinds = pl.num_programs(0) // 4
    part = step // kinds

    @pl.when(step == 0)
    def _():
        turned[...] = jnp.transpose(normed_ref[...].astype(f32)).astype(bf16)
        image_turned[...] = jnp.transpose(image_ref[...].astype(f32)).astype(bf16)

    def store(total):
        half = total.shape[0] // 2
        upper, lower = total[:half], total[half:]
        first = side_ref[0] == 0
        keep_ref[...] = jnp.where(first, upper, lower).astype(bf16)
        send_ref[...] = jnp.where(first, lower, upper).astype(bf16)

    @pl.when(part == 0)
    def _():
        store(dot(turned[...], gq_ref[...]))
        query_ref[...] = column_sum(gq_ref[...].astype(f32))

    @pl.when(part == 1)
    def _():
        store(dot(turned[...], gk_ref[...]) + dot(image_turned[...], gik_ref[...]))

    @pl.when(part == 2)
    def _():
        store(dot(turned[...], gv_ref[...]) + dot(image_turned[...], giv_ref[...]))
        sums = column_sum(gv_ref[...].astype(f32)) + column_sum(giv_ref[...].astype(f32))
        value_ref[...] = sums

    @pl.when(part == 3)
    def _():
        store(extra_ref[...].astype(f32))


def weight_grads(order, side, normed, image, grads, extra):
    rows, width = normed.shape
    image_rows = image.shape[0]
    kinds = width // LANES
    tall = width // 2

    def column(height, part):
        place = lambda s, *_: (0, jnp.clip(s - part * kinds, 0, kinds - 1))
        return pl.BlockSpec((height, LANES), place)

    half = pl.BlockSpec((tall, LANES), lambda s, *_: (s, 0))
    return call(
        order,
        weight_kernel,
        (normed, image, *grads, extra),
        [shaped((4 * kinds * tall, LANES), bf16)] * 2 + [shaped((1, width), f32)] * 2,
        "weight_grads",
        cost(8 * rows * width * width, 12 << 20),
        scalars=(side,),
        grid=(4 * kinds,),
        specs=[
            resident(normed.shape),
            resident(image.shape),
            column(rows, 0),
            column(rows, 1),
            column(rows, 2),
            column(image_rows, 1),
            column(image_rows, 2),
            column(width, 3),
        ],
        outs=[half, half, column(1, 0), column(1, 2)],
        scratch=[pltpu.VMEM((width, rows), bf16), pltpu.VMEM((width, image_rows), bf16)],
    )


def image_grad_kernel(keys_weight, values_weight, keys_ref, values_ref, out_ref):
    total = dot(keys_ref[...], keys_weight[...], NT) + dot(values_ref[...], values_weight[...], NT)
    out_ref[...] = total.astype(bf16)


def image_grads(order, weight, keys, values):
    rows, width = keys.shape
    part = lambda base: pl.BlockSpec((width, width), lambda *_: (0, base))
    return call(
        order,
        image_grad_kernel,
        (weight, weight, keys, values),
        [shaped((rows, width), bf16)],
        "image_grads",
        cost(4 * rows * width * width, 6 << 20),
        grid=(1,),
        specs=[part(1), part(2), resident(keys.shape), resident(values.shape)],
        outs=[resident((rows, width))],
    )


def finish_kernel(
    flag_ref,
    hid_ref,
    gmid_ref,
    near_ref,
    far_ref,
    gq_ref,
    gk_ref,
    gv_ref,
    gain_ref,
    weight_ref,
    out_ref,
    sums_ref,
):
    rows, width = hid_ref.shape
    sums = [jnp.zeros((1, width), f32)] * 2
    for start in range(0, rows, IMG_PAD):
        here = slice(start, start + IMG_PAD)
        joined = jnp.concatenate([gq_ref[here, :], gk_ref[here, :], gv_ref[here, :]], axis=1)
        grad = dot(joined, weight_ref[...], NT)
        unit, scale = normalise(hid_ref[here, :].astype(f32))
        if start == 0:
            both = near_ref[...].astype(f32) + far_ref[...].astype(f32)
            grad = grad + jnp.where(flag_ref[0] == 1, 0.0, both)
        sums = [sums[0] + column_sum(grad * unit), sums[1] + column_sum(grad)]
        total = gmid_ref[here, :] + norm_transpose(unit, scale, gain_ref[...], grad)
        out_ref[here, :] = total.astype(bf16)
    sums = jnp.concatenate(sums, axis=0)

    @pl.when(pl.program_id(0) == 0)
    def _():
        sums_ref[...] = sums

    @pl.when(pl.program_id(0) > 0)
    def _():
        sums_ref[...] += sums


def finish_rows(order, flag, hidden, gmid, near, far, grads, gain, weight, item_rows):
    rows, width = hidden.shape
    items = rows // item_rows
    mine = pl.BlockSpec((item_rows, width), lambda i, *_: (i, 0))
    image = pl.BlockSpec((IMG_PAD, width), lambda i, *_: (i, 0))
    return call(
        order,
        finish_kernel,
        (hidden, gmid, near, far, *grads, gain, weight),
        [shaped((rows, width), bf16), shaped((2, width), f32)],
        "finish_rows",
        cost(6 * rows * width * width, 16 << 20),
        scalars=(flag,),
        grid=(items,),
        specs=[mine, mine, image, image, mine, mine, mine, resident(gain.shape), resident(weight.shape)],
        outs=[mine, resident((2, width))],
    )


def expert_kernel(half_ref, greduce_ref, gexpand_ref, *refs):
    reduce_ref, expand_ref = refs[-2:]
    reduce_ref[...] = greduce_ref[...].astype(f32)
    expand_ref[...] = gexpand_ref[...].astype(f32)


def expert_outputs(order, halves, first, value, width, units, earlier):
    parts = width // LANES
    tall = width // 2
    count = halves.shape[0]
    blocks = value.shape[0] // (count * 2 * parts * tall)
    source = lambda base: pl.BlockSpec(
        (tall, LANES), lambda i, h, p, *_: ((i * count + h) * 2 * parts + base + p, 0)
    )
    return call(
        order,
        expert_kernel,
        (value, value, *earlier),
        [shaped((units, width), f32), shaped((width, units), f32)],
        "expert_outputs",
        cost(value.size, 6 * value.size),
        scalars=(halves,),
        grid=(blocks, count, parts),
        specs=[source(0), source(parts)] + [pl.BlockSpec(memory_space=pl.ANY)] * len(earlier),
        outs=[
            pl.BlockSpec((tall, LANES), lambda i, h, p, half: (2 * (first + i) + half[h], p)),
            pl.BlockSpec((tall, LANES), lambda i, h, p, half: (half[h], (first + i) * parts + p)),
        ],
        aliases={3: 0, 4: 1} if earlier else None,
    )


def projection_kernel(half_ref, value_ref, *refs):
    in_ref, out_ref = refs[-2:]
    tall, wide = in_ref.shape

    def store(ref):
        for part in range(wide // LANES):
            piece = value_ref[part * tall : (part + 1) * tall, :]
            ref[:, part * LANES : (part + 1) * LANES] = piece.astype(f32)

    @pl.when(pl.program_id(0) < 3)
    def _():
        store(in_ref)

    @pl.when(pl.program_id(0) == 3)
    def _():
        store(out_ref)


def projection_outputs(order, half, value, width, earlier):
    tall = width // 2
    return call(
        order,
        projection_kernel,
        (value, *earlier),
        [shaped((width, 3 * width), f32), shaped((width, width), f32)],
        "projection_outputs",
        cost(value.size, 6 * value.size),
        scalars=(half,),
        grid=(4,),
        specs=[pl.BlockSpec((tall * width // LANES, LANES), lambda b, at: (b, 0))]
        + [pl.BlockSpec(memory_space=pl.ANY)] * len(earlier),
        outs=[
            pl.BlockSpec((tall, width), lambda b, at: (at[0], jnp.minimum(b, 2))),
            pl.BlockSpec((tall, width), lambda b, at: (at[0], 0)),
        ],
        aliases={2: 0, 3: 1} if earlier else None,
    )


def swap(value, axes, pair_of):
    count = 1
    for axis in axes:
        count *= lax.axis_size(axis)
    return lax.ppermute(value, axes, [(source, pair_of(source)) for source in range(count)])


def place_of(axes):
    place = 0
    for axis in axes:
        place = place * lax.axis_size(axis) + lax.axis_index(axis)
    return place


def stage_bits(axes):
    count = 1
    for axis in axes:
        count *= lax.axis_size(axis)
    bits = count.bit_length() - 1
    core = len(axes) - 1
    others = [bit for bit in range(bits) if bit != core]
    if len(axes) == 1 and len(others) == 3:
        return [(core, core), (1, 2), (3, 1), (2, 3)]
    if len(axes) == 2 and len(others) == 4:
        return [(core, core), (2, 3), (0, 2), (3, 0), (4, 4)]
    return [(core, core)] + list(zip(others, others[1:] + others[:1]))


class Total:
    def __init__(self, order, axes, keep, send):
        self.order = order
        self.axes = axes
        self.core = len(axes) - 1
        self.left = stage_bits(axes)
        place = place_of(axes)
        second = ((place >> self.core) & 1) == 1
        sides = [(place >> jnp.where(second, pair[1], pair[0])) & 1 for pair in self.left]
        self.sides = dict(zip(self.left, sides))
        self.back = list(self.left)
        self.terms = (keep, self.exchange(send, self.left.pop(0)))
        self.mine = None

    def exchange(self, value, pair):
        other = lambda source: source ^ (1 << pair[(source >> self.core) & 1])
        self.got = swap(value, self.axes, other)
        return self.got

    def part(self, which, half):
        cut = lambda term: lax.dynamic_slice_in_dim(term, which * half, half, 0).astype(f32)
        return (cut(self.terms[0]) + cut(self.terms[1])).astype(bf16)

    def step(self):
        zero = self.order.zero[0, 0]
        if self.left:
            pair = self.left.pop(0)
            half = self.terms[0].shape[0] // 2
            side = self.sides[pair] + zero
            sent = self.part(1 - side, half)
            sent = self.order.tie(sent)
            self.terms = (self.part(side, half), self.exchange(sent, pair))
            return
        pair = self.back.pop()
        if self.mine is None:
            self.mine = self.part(zero, self.terms[0].shape[0])
        else:
            first = self.last + zero == 0
            low = jnp.where(first, self.mine, self.got)
            high = jnp.where(first, self.got, self.mine)
            self.mine = jnp.concatenate([low, high], axis=0)
        self.mine = self.order.tie(self.mine)
        self.last = self.sides[pair]
        self.exchange(self.mine, pair)


class Doubling:
    def __init__(self, order, value, axis):
        self.order, self.value, self.axis = order, value, axis
        self.bits = list(range(lax.axis_size(axis).bit_length() - 1))
        self.start()

    def start(self):
        bit = self.bits.pop(0)
        self.got = swap(self.value, (self.axis,), lambda source: source ^ (1 << bit))

    def step(self):
        total = self.value + self.got + self.order.zero[0, 0].astype(f32)
        self.value = self.order.tie(total)
        if self.bits:
            self.start()
        return self.value


def on_device(
    hidden_in,
    image_count,
    text_lengths,
    attend_gain,
    attend_shift,
    project_in,
    bias_pair,
    project_out,
    project_bias,
    feed_gain,
    feed_shift,
    expand_weight,
    expand_bias,
    reduce_weight,
    reduce_bias,
    cotangent,
):
    items, _, rows, width = hidden_in.shape
    units = expand_weight.shape[2]
    is_text = lax.axis_index("mod") == 1
    flag = is_text.astype(jnp.int32)[None]
    hidden = hidden_in.reshape(items * rows, width)
    to_text = lambda value: lax.ppermute(value, "mod", [(0, 1)])
    to_image = lambda value: lax.ppermute(value, "mod", [(1, 0)])

    far_rows = [to_text(hidden_in[item, 0, :IMG_PAD]) for item in range(items)]
    far_vecs = to_text(jnp.concatenate([attend_gain, attend_shift], axis=0))
    order = Order()
    normed, projected = project_rows(
        order, hidden, attend_gain, attend_shift, project_in, bias_pair
    )
    scalars = (flag, image_count, text_lengths)
    normed_images, image_pairs, attended, lses = [], [], [], []
    for item in range(items):
        normed_image, image_pair = image_rows(
            order,
            flag,
            item,
            hidden,
            far_rows[item],
            attend_gain,
            attend_shift,
            far_vecs,
            project_in,
            bias_pair,
            rows,
        )
        out, lse = attend_forward(order, scalars, item, projected, image_pair)
        normed_images.append(normed_image)
        image_pairs.append(image_pair)
        attended.append(out)
        lses.append(lse)

    side = (lax.axis_index("dp") & 1)[None]
    (
        hidden_out,
        grad_middle,
        grad_attended,
        project_out_grad,
        vec_grads,
        expand_bias_grad,
        keep0,
        send0,
        keep1,
        send1,
    ) = feed_forward(
        order,
        flag,
        image_count,
        side,
        attended[0],
        attended[1],
        project_out,
        hidden,
        cotangent.reshape(items * rows, width),
        (project_bias[None], feed_gain, feed_shift, reduce_bias),
        expand_weight[0],
        expand_bias,
        reduce_weight[0],
    )
    a = Total(order, ("dp",), keep0, send0)
    c = Total(order, ("dp",), keep1, send1)
    grads = ()

    def backward(item, start, pairs):
        return attend_backward(
            order,
            scalars,
            item,
            start,
            pairs,
            projected,
            image_pairs[item],
            attended[item],
            grad_attended,
            lses[item],
            grads,
        )

    grads = backward(0, 0, 2)
    a.step()
    grads = backward(1, 0, 2)
    c.step()
    grads = backward(0, 2, 2)
    a.step()
    grads = backward(1, 2, 2)
    c.step()
    grads = backward(0, 4, 2)
    a.step()
    grads = backward(1, 4, 2)
    a.step()
    c.step()
    near = image_grads(order, project_in, grads[3], grads[4])
    far = to_image(near)
    images = jnp.concatenate(normed_images, axis=0)
    keep, send, query_sums, value_sums = weight_grads(
        order, side, normed, images, grads, project_out_grad
    )
    p = Total(order, ("dp", "mod"), keep, send)
    c.step()
    a.step()
    p.step()
    grad_in, attend_sums = finish_rows(
        order, flag, hidden, grad_middle, near, far, grads[:3], attend_gain, project_in, rows
    )
    ebias_rows = expand_bias_grad.reshape(-1, width)
    small = [attend_sums, vec_grads[:3], ebias_rows, vec_grads[3:4], query_sums, value_sums]
    small = Doubling(order, jnp.concatenate(small, axis=0), "dp")
    a.step()
    c.step()
    p.step()
    small.step()
    p.step()
    a.step()
    small.step()
    p.step()
    c.step()
    outputs = expert_outputs(order, side, 0, a.mine, width, units, ())
    p.step()
    small.step()
    outputs = expert_outputs(order, 1 - side, 0, a.got, width, units, outputs)
    p.step()
    c.step()
    while small.bits:
        small.step()
    small = small.step()
    shared = Doubling(order, small[-3:], "mod")
    outputs = expert_outputs(order, side, 2, c.mine, width, units, outputs)
    p.step()
    reduce_grad, expand_grad = expert_outputs(order, 1 - side, 2, c.got, width, units, outputs)
    shared = shared.step()
    while p.back:
        p.step()
    projections = projection_outputs(order, side, p.mine, width, ())
    project_in_grad, project_out_grad = projection_outputs(
        order, 1 - side, p.got, width, projections
    )
    return (
        hidden_out.reshape(hidden_in.shape),
        grad_in.reshape(hidden_in.shape),
        small[0:1],
        small[1:2],
        project_in_grad,
        shared[1:3],
        project_out_grad,
        shared[0],
        small[2:3],
        small[3:4],
        expand_grad[None],
        small[5:-3].reshape(1, -1),
        reduce_grad[None],
        small[4:5],
    )


def solution(mesh):
    in_specs = (
        P("dp", "mod", None, None),
        P("dp"),
        P("dp", None),
        P("mod", None),
        P("mod", None),
        P(),
        P(),
        P(),
        P(),
        P("mod", None),
        P("mod", None),
        P("mod", None, None),
        P("mod", None),
        P("mod", None, None),
        P("mod", None),
        P("dp", "mod", None, None),
    )
    out_specs = (
        P("dp", "mod", None, None),
        P("dp", "mod", None, None),
        P("mod", None),
        P("mod", None),
        P(),
        P(),
        P(),
        P(),
        P("mod", None),
        P("mod", None),
        P("mod", None, None),
        P("mod", None),
        P("mod", None, None),
        P("mod", None),
    )
    return jax.shard_map(
        on_device, mesh=mesh, in_specs=in_specs, out_specs=out_specs, check_vma=False
    )
```

```python
import functools

import jax
import jax.numpy as jnp
from jax import lax
from jax.experimental import pallas as pl
from jax.experimental.pallas import tpu as pltpu
from jax.sharding import PartitionSpec as P

HEADS = 12
HEAD = 64
IMG_PAD = 256
PAIR = 2 * HEAD
PAIRS = HEADS // 2
GROUP_PAIRS = 2
GROUPS = PAIRS // GROUP_PAIRS
LANES = GROUP_PAIRS * PAIR
SMALL = 128
FF_BLOCK = 768

masked_value = -1e30
norm_eps = 1e-05

bf16 = jnp.bfloat16
f32 = jnp.float32

NN = (((1,), (0,)), ((), ()))
NT = (((1,), (1,)), ((), ()))
TN = (((0,), (0,)), ((), ()))
VMEM_BYTES = 56 << 20


def dot(left, right, dims=NN):
    return lax.dot_general(left, right, dims, preferred_element_type=f32)


def column_sum(values):
    return jnp.sum(values, axis=0, keepdims=True)


def row_mean(values):
    return jnp.mean(values, axis=1, keepdims=True)


def normalise(values):
    centred = values - row_mean(values)
    scale = lax.rsqrt(row_mean(centred * centred) + norm_eps)
    return centred * scale, scale


def norm_transpose(unit, scale, gain, grad):
    grad_unit = grad * gain
    return scale * (grad_unit - row_mean(grad_unit) - unit * row_mean(grad_unit * unit))


def cost(flops, moved, special=0):
    return pl.CostEstimate(flops=flops, bytes_accessed=moved, transcendentals=special)


class Order:
    def __init__(self):
        self.last = None

    def after(self, *values):
        if self.last is None:
            return values
        *values, _ = lax.optimization_barrier((*values, self.last))
        return values


def call(order, kernel, inputs, out_shape, name, estimate, scalars=(), grid=(), specs=None, outs=None,
         scratch=(), aliases=None):
    inputs = (*order.after(inputs[0]), *inputs[1:])
    vmem = pl.BlockSpec(memory_space=pltpu.VMEM)
    found = pl.pallas_call(
        kernel,
        grid_spec=pltpu.PrefetchScalarGridSpec(
            num_scalar_prefetch=len(scalars),
            grid=grid,
            in_specs=[vmem] * len(inputs) if specs is None else list(specs),
            out_specs=[vmem] * len(out_shape) if outs is None else list(outs),
            scratch_shapes=list(scratch),
        ),
        out_shape=list(out_shape),
        input_output_aliases=aliases or {},
        compiler_params=pltpu.CompilerParams(vmem_limit_bytes=VMEM_BYTES),
        cost_estimate=estimate,
        name=name,
    )(*scalars, *inputs)
    order.last = found[-1]
    return found if len(found) > 1 else found[0]


def shaped(shape, dtype):
    return jax.ShapeDtypeStruct(shape, dtype)


def resident(shape):
    return pl.BlockSpec(shape, lambda *_: (0,) * len(shape), pipeline_mode=pl.Buffered(1))


def project_kernel(hid_ref, gain_ref, shift_ref, weight_ref, bias_ref, normed_ref, out_ref):
    unit, _ = normalise(hid_ref[...].astype(f32))
    normed = (unit * gain_ref[...] + shift_ref[...]).astype(bf16)
    normed_ref[...] = normed
    width = normed.shape[1]
    for part in range(3):
        cols = slice(part * width, (part + 1) * width)
        rows = dot(normed, weight_ref[:, cols])
        if part == 0:
            rows = (rows + bias_ref[0:1]).astype(bf16) * jnp.asarray(HEAD**-0.5, bf16)
        if part == 2:
            rows = rows + bias_ref[1:2]
        out_ref[:, cols] = rows.astype(bf16)


def project_rows(order, hidden, gain, shift, weight, bias):
    rows, width = hidden.shape
    block = 256
    blocked = lambda cols: pl.BlockSpec((block, cols), lambda r: (r, 0))
    inputs = (hidden, gain, shift, weight, bias)
    return call(
        order,
        project_kernel,
        inputs,
        [shaped((rows, width), bf16), shaped((rows, 3 * width), bf16)],
        "project_rows",
        cost(6 * rows * width * width, 10 * rows * width + 6 * width * width),
        grid=(rows // block,),
        specs=[blocked(width)] + [resident(value.shape) for value in inputs[1:]],
        outs=[blocked(width), blocked(3 * width)],
    )


def image_kernel(
    flag_ref,
    own_ref,
    far_ref,
    gain_ref,
    shift_ref,
    vec_ref,
    keys_ref,
    values_ref,
    bias_ref,
    *refs,
):
    normed_ref, out_ref = refs[-2:]
    is_text = flag_ref[0] == 1
    hidden = jnp.where(is_text, far_ref[...].astype(f32), own_ref[...].astype(f32))
    gain = jnp.where(is_text, vec_ref[0:1], gain_ref[...])
    shift = jnp.where(is_text, vec_ref[1:2], shift_ref[...])
    unit, _ = normalise(hidden)
    normed = (unit * gain + shift).astype(bf16)
    normed_ref[...] = normed
    width = normed.shape[1]
    out_ref[:, :width] = dot(normed, keys_ref[...]).astype(bf16)
    out_ref[:, width:] = (dot(normed, values_ref[...]) + bias_ref[1:2]).astype(bf16)


def image_rows(
    order, flag, item, hidden, far, gain, shift, vecs, weight, bias, item_rows, items, earlier
):
    width = hidden.shape[1]
    place = item * (item_rows // IMG_PAD)
    half = lambda base: pl.BlockSpec((width, width), lambda *_: (0, base))
    mine = lambda cols: pl.BlockSpec((IMG_PAD, cols), lambda *_: (item, 0))
    inputs = (hidden, far, gain, shift, vecs, weight, weight, bias, *earlier)
    return call(
        order,
        image_kernel,
        inputs,
        [shaped((items * IMG_PAD, width), bf16), shaped((items * IMG_PAD, 2 * width), bf16)],
        "image_rows",
        cost(4 * IMG_PAD * width * width, 6 << 20),
        scalars=(flag,),
        grid=(1,),
        specs=[
            pl.BlockSpec((IMG_PAD, width), lambda *_: (place, 0)),
            resident(far.shape),
            resident(gain.shape),
            resident(shift.shape),
            resident(vecs.shape),
            half(1),
            half(2),
            resident(bias.shape),
        ]
        + [pl.BlockSpec(memory_space=pl.ANY)] * len(earlier),
        outs=[mine(width), mine(2 * width)],
        aliases={9: 0, 10: 1} if earlier else None,
    )


def segments(shape, axis, lengths_ref, item):
    places = lax.broadcasted_iota(jnp.int32, shape, axis)
    total = jnp.zeros(shape, jnp.int32)
    end = 0
    for which in range(lengths_ref.shape[1]):
        end = end + lengths_ref[item, which]
        total += (places >= end).astype(jnp.int32)
    return total


def own_bias(rows, flag_ref, lengths_ref, item):
    shape = (rows, rows)
    same = segments(shape, 0, lengths_ref, item) == segments(shape, 1, lengths_ref, item)
    return jnp.where(same & (flag_ref[0] == 1), 0.0, masked_value).astype(f32)


def image_bias(shape, axis, count_ref, item):
    places = lax.broadcasted_iota(jnp.int32, shape, axis)
    return jnp.where(places < count_ref[item], 0.0, masked_value).astype(f32)


def forward_kernel(
    item,
    flag_ref,
    count_ref,
    lengths_ref,
    q_ref,
    k_ref,
    v_ref,
    ik_ref,
    iv_ref,
    out_ref,
    lse_ref,
    image_part,
    own_part,
):
    rows = q_ref.shape[0]

    @pl.when(pl.program_id(0) == 0)
    def _():
        image_part[...] = image_bias(image_part.shape, 1, count_ref, item)
        own_part[...] = own_bias(rows, flag_ref, lengths_ref, item)

    first = lax.broadcasted_iota(jnp.int32, (rows, PAIR), 1) < HEAD
    zero = jnp.zeros((), bf16)
    q = q_ref[...]
    image_keys, image_values = ik_ref[...], iv_ref[...]
    keys, values = k_ref[...], v_ref[...]
    outs, tops = [], []
    for head in range(2):
        q_head = jnp.where(first, q, zero) if head == 0 else jnp.where(first, zero, q)
        far = dot(q_head, image_keys, NT) + image_part[...]
        own = dot(q_head, keys, NT) + own_part[...]
        top = jnp.maximum(
            jnp.max(far, axis=1, keepdims=True), jnp.max(own, axis=1, keepdims=True)
        )
        far = jnp.exp(far - top)
        own = jnp.exp(own - top)
        total = jnp.sum(far, axis=1, keepdims=True) + jnp.sum(own, axis=1, keepdims=True)
        summed = dot(far.astype(bf16), image_values) + dot(own.astype(bf16), values)
        outs.append(summed / total)
        tops.append(top + jnp.log(total))
    out_ref[...] = jnp.where(first, outs[0], outs[1]).astype(bf16)
    turned = jnp.transpose(jnp.where(first, tops[0], tops[1]))
    lse_ref[0, 0:1, :] = turned[0:1]
    lse_ref[0, 1:2, :] = turned[HEAD : HEAD + 1]


def attend_forward(order, scalars, item, projected, image):
    rows = projected.shape[0] // 2
    spec = lambda base: pl.BlockSpec((rows, PAIR), lambda h, *_: (item, base + h))
    far = lambda base: pl.BlockSpec((IMG_PAD, PAIR), lambda h, *_: (item, base + h))
    keys = rows + IMG_PAD
    return call(
        order,
        functools.partial(forward_kernel, item),
        (projected, projected, projected, image, image),
        [shaped((rows, HEADS * HEAD), bf16), shaped((PAIRS, 2, rows), f32)],
        "attend_forward",
        cost(16 * HEADS * rows * keys * HEAD, 6 << 20, HEADS * rows * keys),
        scalars=scalars,
        grid=(PAIRS,),
        specs=[spec(0), spec(PAIRS), spec(2 * PAIRS), far(0), far(PAIRS)],
        outs=[
            pl.BlockSpec((rows, PAIR), lambda h, *_: (0, h)),
            pl.BlockSpec((1, 2, rows), lambda h, *_: (h, 0, 0)),
        ],
        scratch=[pltpu.VMEM((rows, IMG_PAD), f32), pltpu.VMEM((rows, rows), f32)],
    )


def backward_kernel(
    item,
    flag_ref,
    count_ref,
    lengths_ref,
    q_ref,
    k_ref,
    v_ref,
    ik_ref,
    iv_ref,
    out_ref,
    grad_ref,
    lse_ref,
    *refs,
):
    gq_ref, gk_ref, gv_ref, gik_ref, giv_ref, image_part, own_part = refs[-7:]
    rows = q_ref.shape[0]

    @pl.when(pl.program_id(0) == 0)
    def _():
        image_part[...] = image_bias(image_part.shape, 0, count_ref, item)
        own_part[...] = own_bias(rows, flag_ref, lengths_ref, item)

    first = lax.broadcasted_iota(jnp.int32, (rows, PAIR), 1) < HEAD
    zero = jnp.zeros((), bf16)
    q, grad = q_ref[...], grad_ref[...]
    products = grad.astype(f32) * out_ref[...].astype(f32)
    head_lanes = lax.broadcasted_iota(jnp.int32, (8, PAIR), 1) // HEAD
    head_rows = lax.broadcasted_iota(jnp.int32, (8, PAIR), 0)
    center = lax.dot_general(
        (head_lanes == head_rows).astype(f32),
        products,
        NT,
        preferred_element_type=f32,
        precision=lax.Precision.HIGHEST,
    )
    q_heads = [jnp.where(first, q, zero), jnp.where(first, zero, q)]
    grad_heads = [jnp.where(first, grad, zero), jnp.where(first, zero, grad)]
    lse = lse_ref[0]
    grad_query = [None, None]
    half = rows // 2
    pieces = (
        (ik_ref, iv_ref, gik_ref, giv_ref, image_part, 0, IMG_PAD),
        (k_ref, v_ref, gk_ref, gv_ref, own_part, 0, half),
        (k_ref, v_ref, gk_ref, gv_ref, own_part, half, half),
    )
    for keys_ref, values_ref, gk_out, gv_out, bias, start, count in pieces:
        piece = slice(start, start + count)
        keys, values = keys_ref[piece, :], values_ref[piece, :]
        low_lanes = lax.broadcasted_iota(jnp.int32, (count, PAIR), 1) < HEAD
        grad_keys, grad_values = [], []
        for head in range(2):
            scores = dot(keys, q_heads[head], NT) + bias[piece, :]
            probs = jnp.exp(scores - lse[head : head + 1])
            grad_probs = dot(values, grad_heads[head], NT)
            grad_scores = (probs * (grad_probs - center[head : head + 1])).astype(bf16)
            grad_values.append(dot(probs.astype(bf16), grad))
            grad_keys.append(dot(grad_scores, q))
            term = dot(grad_scores, keys, TN)
            grad_query[head] = term if grad_query[head] is None else grad_query[head] + term
        gk_out[piece, :] = jnp.where(low_lanes, grad_keys[0], grad_keys[1]).astype(bf16)
        gv_out[piece, :] = jnp.where(low_lanes, grad_values[0], grad_values[1]).astype(bf16)
    gq_ref[...] = (jnp.where(first, grad_query[0], grad_query[1]) * HEAD**-0.5).astype(bf16)


def attend_backward(order, scalars, item, start, pairs, projected, image, attended, grad, lse, earlier):
    rows, width = attended.shape
    spec = lambda base: pl.BlockSpec((rows, PAIR), lambda h, *_: (item, base + start + h))
    far = lambda base: pl.BlockSpec((IMG_PAD, PAIR), lambda h, *_: (item, base + start + h))
    own = pl.BlockSpec((rows, PAIR), lambda h, *_: (0, start + h))
    far_outs = pl.BlockSpec((IMG_PAD, PAIR), lambda h, *_: (item, start + h))
    keys = rows + IMG_PAD
    inputs = (projected, projected, projected, image, image, attended, grad, lse)
    first = len(scalars) + len(inputs)
    return call(
        order,
        functools.partial(backward_kernel, item),
        (*inputs, *earlier),
        [shaped((2 * rows, width), bf16)] * 3 + [shaped((2 * IMG_PAD, width), bf16)] * 2,
        "attend_backward",
        cost(80 * pairs * rows * keys * HEAD, pairs * 2 << 20, 2 * pairs * rows * keys),
        scalars=scalars,
        grid=(pairs,),
        specs=[
            spec(0),
            spec(PAIRS),
            spec(2 * PAIRS),
            far(0),
            far(PAIRS),
            own,
            spec(0),
            pl.BlockSpec((1, 2, rows), lambda h, *_: (start + h, 0, 0)),
        ]
        + [pl.BlockSpec(memory_space=pl.ANY)] * len(earlier),
        outs=[spec(0), spec(0), spec(0), far_outs, far_outs],
        scratch=[pltpu.VMEM((IMG_PAD, rows), f32), pltpu.VMEM((rows, rows), f32)],
        aliases={first + at: at for at in range(len(earlier))},
    )


def gelu_pair(values):
    share = 0.5 * (1.0 + lax.erf(values * 0.7071067811865476))
    slope = share + values * jnp.exp(-0.5 * values * values) * 0.3989422804014327
    return values * share, slope


def feed_step(step, rows, item_rows, feed, top, result, gfeed, expand_ref, ebias_ref, reduce_ref):
    width = feed.shape[1]
    expand, reduce = expand_ref[...], reduce_ref[...]
    active_parts, gup_parts = [], []
    for start in range(0, rows, item_rows):
        here = slice(start, start + item_rows)
        upward = dot(feed[here, :], expand) + ebias_ref[...]
        gactive = dot(top[here, :], reduce, NT)
        active, slope = gelu_pair(upward)
        active = active.astype(bf16)
        gup = (gactive * slope).astype(bf16)
        result[here, :] += dot(active, reduce)
        gfeed[here, :] += dot(gup, expand, NT)
        active_parts.append(active)
        gup_parts.append(gup)
    active = jnp.concatenate(active_parts, axis=0)
    gup = jnp.concatenate(gup_parts, axis=0)
    greduce = dot(active, top[...], TN).astype(bf16)
    gexpand = dot(feed[...], gup, TN).astype(bf16)
    pieces = [greduce[:, at : at + LANES] for at in range(0, width, LANES)]
    pieces += [gexpand[:, at : at + LANES] for at in range(0, FF_BLOCK, LANES)]
    return pieces, column_sum(gup.astype(f32))


def store_pieces(out, pieces):
    at = 0
    for half in range(2):
        for piece in pieces:
            rows = piece.shape[0] // 2
            out[at : at + rows, :] = piece[half * rows : (half + 1) * rows]
            at += rows


def feed_kernel(
    flag_ref,
    count_ref,
    side_ref,
    att0_ref,
    att1_ref,
    project_ref,
    hid_ref,
    cot_ref,
    project_bias_ref,
    gain_ref,
    shift_ref,
    reduce_bias_ref,
    expand_ref,
    ebias_ref,
    reduce_ref,
    out_ref,
    gmid_ref,
    gatt_ref,
    gproject_ref,
    gvec_ref,
    keep0_ref,
    send0_ref,
    keep1_ref,
    send1_ref,
    middle,
    feed,
    top,
    result,
    gfeed,
    low_out,
    gatt,
    grads,
    grad_sems,
    row_sems,
    *,
    item_rows,
):
    step = pl.program_id(0)
    rows, width = hid_ref.shape
    block = 256
    att_refs = (att0_ref, att1_ref)
    half = grads.shape[1] // 2

    steps = grads.shape[0]

    def grad_copies(which):
        found = []
        chunk, place = divmod(which, steps // 2)
        outs = (keep1_ref, send1_ref) if chunk else (keep0_ref, send0_ref)
        for number, out in enumerate(outs):
            side = side_ref[0] if number == 0 else 1 - side_ref[0]
            here = grads.at[which, pl.ds(pl.multiple_of(side * half, half), half)]
            there = out.at[pl.ds(place * half, half)]
            found.append(pltpu.make_async_copy(here, there, grad_sems.at[which, number]))
        return found

    @pl.when(step == 0)
    def _():
        for start in range(0, rows, block):
            here = slice(start, start + block)
            inside = slice(start % item_rows, start % item_rows + block)
            att = att_refs[start // item_rows][inside, :]
            branch = dot(att, project_ref[...]) + project_bias_ref[...]
            x = hid_ref[here, :].astype(f32) + branch
            middle[here, :] = x
            unit, _ = normalise(x)
            feed[here, :] = (unit * gain_ref[...] + shift_ref[...]).astype(bf16)
            at = lax.broadcasted_iota(jnp.int32, (block, width), 0) + start % item_rows
            limit = jnp.where(flag_ref[0] == 1, item_rows, count_ref[start // item_rows])
            top[here, :] = jnp.where(at < limit, cot_ref[here, :].astype(f32), 0.0).astype(bf16)
            result[here, :] = x + reduce_bias_ref[...]
            gfeed[here, :] = jnp.zeros((block, width), f32)

    pieces, gvec_ref[pl.ds(4 + step, 1), :] = feed_step(
        step, rows, item_rows, feed, top, result, gfeed, expand_ref, ebias_ref, reduce_ref
    )
    store_pieces(grads.at[step], pieces)
    for which in range(steps):

        @pl.when(step == which)
        def _(which=which):
            for copy in grad_copies(which):
                copy.start()

    @pl.when(step == pl.num_programs(0) - 1)
    def _():
        copies = []
        sums = [jnp.zeros((1, width), f32)] * 4
        for number, start in enumerate(range(0, rows, block)):
            here = slice(start, start + block)
            low_out[here, :] = result[here, :].astype(bf16)
            unit, scale = normalise(middle[here, :])
            grad = gfeed[here, :]
            grad_top = top[here, :].astype(f32)
            gmid = grad_top + norm_transpose(unit, scale, gain_ref[...], grad)
            terms = (grad * unit, grad, grad_top, gmid)
            sums = [old + column_sum(new) for old, new in zip(sums, terms)]
            middle[here, :] = gmid
            gbranch = gmid.astype(bf16)
            feed[here, :] = gbranch
            gatt[here, :] = dot(gbranch, project_ref[...], NT).astype(bf16)
            for kind, (mine, there) in enumerate(
                ((low_out, out_ref), (middle, gmid_ref), (gatt, gatt_ref))
            ):
                span = pl.ds(start, block)
                copy = pltpu.make_async_copy(
                    mine.at[span, :], there.at[span, :], row_sems.at[kind, number]
                )
                copy.start()
                copies.append(copy)
        total = dot(att0_ref[...], feed[:item_rows, :], TN)
        total += dot(att1_ref[...], feed[item_rows:, :], TN)
        gproject_ref[...] = total.astype(bf16)
        gvec_ref[0:4, :] = jnp.concatenate(sums, axis=0)
        for copy in copies:
            copy.wait()
        for which in range(steps):
            for copy in grad_copies(which):
                copy.wait()


def feed_forward(order, flag, count, side, att0, att1, project, hidden, cotangent, vecs, expand, ebias, reduce):
    rows, width = hidden.shape
    item_rows = att0.shape[0]
    units = reduce.shape[0]
    steps = units // FF_BLOCK
    block_rows = 2 * width * FF_BLOCK // LANES
    fixed = (att0, att1, project, hidden, cotangent, *vecs)
    anywhere = pl.BlockSpec(memory_space=pl.ANY)
    return call(
        order,
        functools.partial(feed_kernel, item_rows=item_rows),
        (*fixed, expand, ebias, reduce),
        [
            shaped((rows, width), bf16),
            shaped((rows, width), f32),
            shaped((rows, width), bf16),
            shaped((width, width), bf16),
            shaped((4 + steps, width), f32),
        ]
        + [shaped((steps // 2 * block_rows // 2, LANES), bf16)] * 4,
        "feed_forward",
        cost(12 * rows * width * units, 40 << 20, 2 * rows * units),
        scalars=(flag, count, side),
        grid=(steps,),
        specs=[resident(value.shape) for value in fixed]
        + [
            pl.BlockSpec((width, FF_BLOCK), lambda j, *_: (0, j)),
            pl.BlockSpec((1, FF_BLOCK), lambda j, *_: (0, j)),
            pl.BlockSpec((FF_BLOCK, width), lambda j, *_: (j, 0)),
        ],
        outs=[
            anywhere,
            anywhere,
            anywhere,
            resident((width, width)),
            resident((4 + steps, width)),
        ]
        + [anywhere] * 4,
        scratch=[
            pltpu.VMEM((rows, width), f32),
            pltpu.VMEM((rows, width), bf16),
            pltpu.VMEM((rows, width), bf16),
            pltpu.VMEM((rows, width), f32),
            pltpu.VMEM((rows, width), f32),
            pltpu.VMEM((rows, width), bf16),
            pltpu.VMEM((rows, width), bf16),
            pltpu.VMEM((steps, block_rows, LANES), bf16),
            pltpu.SemaphoreType.DMA((steps, 2)),
            pltpu.SemaphoreType.DMA((3, rows // 256)),
        ],
    )


def weight_kernel(
    side_ref,
    normed_ref,
    image_ref,
    gq_ref,
    gk_ref,
    gv_ref,
    gik_ref,
    giv_ref,
    extra_ref,
    sums_ref,
    keep_ref,
    send_ref,
    keep,
    send,
    sems,
):
    step = pl.program_id(0)
    width = normed_ref.shape[1]
    half = width // 2
    block = half * width // LANES

    def copies(part):
        rows = block if part < 4 else SMALL
        span = pl.ds(part * block, rows)
        pairs = ((keep, keep_ref), (send, send_ref))
        return [
            pltpu.make_async_copy(here.at[span], there.at[span], sems.at[number, part])
            for number, (here, there) in enumerate(pairs)
        ]

    def store(part, total):
        first = side_ref[0] == 0
        mine = jnp.where(first, total[:half], total[half:]).astype(bf16)
        other = jnp.where(first, total[half:], total[:half]).astype(bf16)
        for number in range(width // LANES):
            rows = slice(part * block + number * half, part * block + (number + 1) * half)
            cols = slice(number * LANES, (number + 1) * LANES)
            keep[rows, :] = mine[:, cols]
            send[rows, :] = other[:, cols]
        for copy in copies(part):
            copy.start()

    @pl.when(step == 0)
    def _():
        store(0, dot(normed_ref[...], gq_ref[...], TN))
        sums_ref[0:1] = column_sum(gq_ref[...].astype(f32))

    @pl.when(step == 1)
    def _():
        total = dot(normed_ref[...], gk_ref[...], TN)
        store(1, total + dot(image_ref[...], gik_ref[...], TN))

    @pl.when(step == 2)
    def _():
        total = dot(normed_ref[...], gv_ref[...], TN)
        store(2, total + dot(image_ref[...], giv_ref[...], TN))
        sums = column_sum(gv_ref[...].astype(f32)) + column_sum(giv_ref[...].astype(f32))
        sums_ref[1:2] = sums

    @pl.when(step == 3)
    def _():
        store(3, extra_ref[...].astype(f32))
        keep[4 * block :, :] = jnp.zeros((SMALL, LANES), bf16)
        send[4 * block :, :] = jnp.zeros((SMALL, LANES), bf16)
        for copy in copies(4):
            copy.start()
        for part in range(5):
            for copy in copies(part):
                copy.wait()


def weight_grads(order, side, normed, image, grads, extra):
    rows, width = normed.shape
    all_rows = 4 * (width * width // 2 // LANES) + SMALL
    inputs = (normed, image, *grads, extra)
    anywhere = pl.BlockSpec(memory_space=pl.ANY)
    return call(
        order,
        weight_kernel,
        inputs,
        [shaped((2, width), f32)] + [shaped((all_rows, LANES), bf16)] * 2,
        "weight_grads",
        cost(8 * rows * width * width, 12 << 20),
        scalars=(side,),
        grid=(4,),
        specs=[resident(value.shape) for value in inputs],
        outs=[resident((2, width)), anywhere, anywhere],
        scratch=[pltpu.VMEM((all_rows, LANES), bf16)] * 2 + [pltpu.SemaphoreType.DMA((2, 5))],
    )


def image_grad_kernel(keys_weight, values_weight, keys_ref, values_ref, out_ref):
    total = dot(keys_ref[...], keys_weight[...], NT) + dot(values_ref[...], values_weight[...], NT)
    out_ref[...] = total.astype(bf16)


def image_grads(order, weight, keys, values):
    rows, width = keys.shape
    part = lambda base: pl.BlockSpec((width, width), lambda *_: (0, base))
    return call(
        order,
        image_grad_kernel,
        (weight, weight, keys, values),
        [shaped((rows, width), bf16)],
        "image_grads",
        cost(4 * rows * width * width, 6 << 20),
        grid=(1,),
        specs=[part(1), part(2), resident(keys.shape), resident(values.shape)],
        outs=[resident((rows, width))],
    )


def finish_kernel(
    flag_ref,
    hid_ref,
    gmid_ref,
    near_ref,
    far_ref,
    gq_ref,
    gk_ref,
    gv_ref,
    gain_ref,
    weight_ref,
    feed_sums_ref,
    bias_sums_ref,
    _,
    out_ref,
    small_ref,
    sums,
):
    item, block = pl.program_id(0), pl.program_id(1)
    joined = jnp.concatenate([gq_ref[...], gk_ref[...], gv_ref[...]], axis=1)
    grad = dot(joined, weight_ref[...], NT)
    unit, scale = normalise(hid_ref[...].astype(f32))
    both = near_ref[...].astype(f32) + far_ref[...].astype(f32)
    grad = grad + jnp.where((flag_ref[0] == 0) & (block == 0), both, 0.0)
    total = gmid_ref[...] + norm_transpose(unit, scale, gain_ref[...], grad)
    out_ref[...] = total.astype(bf16)
    found = jnp.concatenate([column_sum(grad * unit), column_sum(grad)], axis=0)

    @pl.when((item == 0) & (block == 0))
    def _():
        sums[...] = jnp.zeros(sums.shape, f32)

    sums[0:2] += found

    @pl.when((item == pl.num_programs(0) - 1) & (block == pl.num_programs(1) - 1))
    def _():
        width = sums.shape[1]
        pad = lambda count: jnp.zeros((count, width), f32)
        own = [sums[0:2], feed_sums_ref[0:3], feed_sums_ref[4:8], pad(7)]
        own = jnp.concatenate(own, axis=0)
        shared = [pad(9), feed_sums_ref[3:4], bias_sums_ref[...], pad(4)]
        shared = jnp.concatenate(shared, axis=0)
        is_text = flag_ref[0] == 1
        first = jnp.where(is_text, 0.0, own) + shared
        rows = jnp.concatenate([first, jnp.where(is_text, own, 0.0)], axis=0).astype(bf16)
        count = rows.shape[0]
        for number in range(width // LANES):
            cols = slice(number * LANES, (number + 1) * LANES)
            small_ref[number * count : (number + 1) * count, :] = rows[:, cols]
        small_ref[width // LANES * count :, :] = jnp.zeros((SMALL - width // LANES * count, LANES), bf16)


def finish_rows(
    order, flag, hidden, gmid, near, far, grads, gain, weight, feed_sums, bias_sums, keep, item_rows
):
    rows, width = hidden.shape
    blocks = item_rows // IMG_PAD
    mine = pl.BlockSpec((IMG_PAD, width), lambda i, j, *_: (i * blocks + j, 0))
    image = pl.BlockSpec((IMG_PAD, width), lambda i, j, *_: (i, 0))
    fixed = (gain, weight, feed_sums, bias_sums)
    place = keep.shape[0] // SMALL - 1
    return call(
        order,
        finish_kernel,
        (hidden, gmid, near, far, *grads, *fixed, keep),
        [shaped((rows, width), bf16), shaped(keep.shape, bf16)],
        "finish_rows",
        cost(6 * rows * width * width, 16 << 20),
        scalars=(flag,),
        grid=(rows // item_rows, blocks),
        specs=[mine, mine, image, image, mine, mine, mine]
        + [resident(value.shape) for value in fixed]
        + [pl.BlockSpec(memory_space=pl.ANY)],
        outs=[mine, pl.BlockSpec((SMALL, LANES), lambda *_: (place, 0))],
        scratch=[pltpu.VMEM((8, width), f32)],
        aliases={12: 1},
    )


def expert_kernel(half_ref, value_ref, *refs):
    at = 0
    for out in refs[-2:]:
        tall = out.shape[0]
        for part in range(out.shape[1] // LANES):
            piece = value_ref[at : at + tall, :]
            out[:, part * LANES : (part + 1) * LANES] = piece.astype(f32)
            at += tall


def expert_outputs(order, half, first, value, width, units, earlier):
    tall = width // 2
    block_rows = 2 * width // LANES * tall
    return call(
        order,
        expert_kernel,
        (value, *earlier),
        [shaped((units, width), f32), shaped((width, units), f32)],
        "expert_outputs",
        cost(value.size, 6 * value.size),
        scalars=(half,),
        grid=(value.shape[0] // block_rows,),
        specs=[pl.BlockSpec((block_rows, LANES), lambda i, at: (i, 0))]
        + [pl.BlockSpec(memory_space=pl.ANY)] * len(earlier),
        outs=[
            pl.BlockSpec((tall, width), lambda i, at: (2 * (first + i) + at[0], 0)),
            pl.BlockSpec((tall, width), lambda i, at: (at[0], first + i)),
        ],
        aliases={2: 0, 3: 1} if earlier else None,
    )


def store_projection(value_ref, in_ref, out_ref):
    tall, wide = in_ref.shape

    def store(ref):
        for part in range(wide // LANES):
            piece = value_ref[part * tall : (part + 1) * tall, :]
            ref[:, part * LANES : (part + 1) * LANES] = piece.astype(f32)

    @pl.when(pl.program_id(0) < 3)
    def _():
        store(in_ref)

    @pl.when(pl.program_id(0) == 3)
    def _():
        store(out_ref)


def projection_kernel(half_ref, value_ref, in_ref, out_ref):
    store_projection(value_ref, in_ref, out_ref)


def last_kernel(half_ref, flag_ref, value_ref, mine_ref, got_ref, *refs):
    in_ref, out_ref, *vec_refs, expand_ref, pair_ref, project_ref = refs[2:]
    store_projection(value_ref, in_ref, out_ref)

    @pl.when(pl.program_id(0) == 0)
    def _():
        both = mine_ref[...].astype(f32) + got_ref[...].astype(f32)
        width = vec_refs[0].shape[1]
        rows = jnp.concatenate([both[at * 32 : (at + 1) * 32] for at in range(width // LANES)], axis=1)
        own = jnp.where(flag_ref[0] == 1, rows[16:], rows[:16])
        for number, ref in enumerate(vec_refs):
            ref[...] = own[number : number + 1]
        for number in range(expand_ref.shape[1] // width):
            cols = slice(number * width, (number + 1) * width)
            expand_ref[:, cols] = own[5 + number : 6 + number]
        project_ref[...] = rows[9:10]
        pair_ref[...] = rows[10:12]


def projection_specs(width):
    tall = width // 2
    value = pl.BlockSpec((tall * width // LANES, LANES), lambda b, *_: (b, 0))
    outs = [
        pl.BlockSpec((tall, width), lambda b, at, *_: (at[0], jnp.minimum(b, 2))),
        pl.BlockSpec((tall, width), lambda b, at, *_: (at[0], 0)),
    ]
    return value, outs, [shaped((width, 3 * width), f32), shaped((width, width), f32)]


def projection_outputs(order, half, value, width):
    spec, outs, shapes = projection_specs(width)
    return call(
        order,
        projection_kernel,
        (value,),
        shapes,
        "projection_outputs",
        cost(value.size, 6 * value.size),
        scalars=(half,),
        grid=(4,),
        specs=[spec],
        outs=outs,
    )


def last_outputs(order, half, flag, mine, got, width, units, earlier):
    spec, outs, shapes = projection_specs(width)
    place = got.shape[0] // SMALL - 1
    small = pl.BlockSpec((SMALL, LANES), lambda *_: (place, 0))
    vecs = [(1, width)] * 5 + [(1, units), (2, width), (1, width)]
    return call(
        order,
        last_kernel,
        (got, mine, got, *earlier),
        shapes + [shaped(shape, f32) for shape in vecs],
        "last_outputs",
        cost(got.size, 6 * got.size),
        scalars=(half, flag),
        grid=(4,),
        specs=[spec, small, small] + [pl.BlockSpec(memory_space=pl.ANY)] * 2,
        outs=outs + [resident(shape) for shape in vecs],
        aliases={5: 0, 6: 1},
    )


def swap(value, axes, pair_of):
    count = 1
    for axis in axes:
        count *= lax.axis_size(axis)
    return lax.ppermute(value, axes, [(source, pair_of(source)) for source in range(count)])


def place_of(axes):
    place = 0
    for axis in axes:
        place = place * lax.axis_size(axis) + lax.axis_index(axis)
    return place


def stage_bits(axes):
    count = 1
    for axis in axes:
        count *= lax.axis_size(axis)
    bits = count.bit_length() - 1
    core = len(axes) - 1
    others = [bit for bit in range(bits) if bit != core]
    if len(axes) == 1 and len(others) == 3:
        return [(core, core), (1, 2), (3, 1), (2, 3)]
    if len(axes) == 2 and len(others) == 4:
        return [(core, core), (2, 3), (0, 2), (3, 0), (4, 4)]
    return [(core, core)] + list(zip(others, others[1:] + others[:1]))


class Total:
    def __init__(self, order, axes, keep, send):
        self.order = order
        self.axes = axes
        self.core = len(axes) - 1
        self.left = stage_bits(axes)
        place = place_of(axes)
        second = ((place >> self.core) & 1) == 1
        sides = [(place >> jnp.where(second, pair[1], pair[0])) & 1 for pair in self.left]
        self.sides = dict(zip(self.left, sides))
        self.back = list(self.left)
        self.terms = (keep, self.exchange(send, self.left.pop(0)))
        self.mine = None

    def exchange(self, value, pair):
        other = lambda source: source ^ (1 << pair[(source >> self.core) & 1])
        self.got = swap(value, self.axes, other)
        return self.got

    def part(self, which, half):
        cut = lambda term: lax.dynamic_slice_in_dim(term, which * half, half, 0).astype(f32)
        return (cut(self.terms[0]) + cut(self.terms[1])).astype(bf16)

    def step(self):
        if self.left:
            pair = self.left.pop(0)
            self.terms = self.order.after(*self.terms)
            half = self.terms[0].shape[0] // 2
            side = self.sides[pair]
            sent = self.part(1 - side, half)
            self.terms = (self.part(side, half), self.exchange(sent, pair))
            self.order.last = sent
            return
        pair = self.back.pop()
        if self.mine is None:
            self.terms = self.order.after(*self.terms)
            self.mine = (self.terms[0].astype(f32) + self.terms[1].astype(f32)).astype(bf16)
        else:
            mine, got = self.order.after(self.mine, self.got)
            low = jnp.where(self.last == 0, mine, got)
            high = jnp.where(self.last == 0, got, mine)
            self.mine = jnp.concatenate([low, high], axis=0)
        self.order.last = self.mine
        self.last = self.sides[pair]
        self.exchange(self.mine, pair)


def on_device(
    hidden_in,
    image_count,
    text_lengths,
    attend_gain,
    attend_shift,
    project_in,
    bias_pair,
    project_out,
    project_bias,
    feed_gain,
    feed_shift,
    expand_weight,
    expand_bias,
    reduce_weight,
    reduce_bias,
    cotangent,
):
    items, _, rows, width = hidden_in.shape
    units = expand_weight.shape[2]
    is_text = lax.axis_index("mod") == 1
    flag = is_text.astype(jnp.int32)[None]
    hidden = hidden_in.reshape(items * rows, width)
    to_text = lambda value: lax.ppermute(value, "mod", [(0, 1)])
    to_image = lambda value: lax.ppermute(value, "mod", [(1, 0)])

    far_rows = [to_text(hidden_in[item, 0, :IMG_PAD]) for item in range(items)]
    far_vecs = to_text(jnp.concatenate([attend_gain, attend_shift], axis=0))
    order = Order()
    normed, projected = project_rows(
        order, hidden, attend_gain, attend_shift, project_in, bias_pair
    )
    scalars = (flag, image_count, text_lengths)
    images, attended, lses = (), [], []
    for item in range(items):
        images = image_rows(
            order,
            flag,
            item,
            hidden,
            far_rows[item],
            attend_gain,
            attend_shift,
            far_vecs,
            project_in,
            bias_pair,
            rows,
            items,
            images,
        )
        out, lse = attend_forward(order, scalars, item, projected, images[1])
        attended.append(out)
        lses.append(lse)

    side = (lax.axis_index("dp") & 1)[None]
    (
        hidden_out,
        grad_middle,
        grad_attended,
        project_out_grad,
        feed_sums,
        keep0,
        send0,
        keep1,
        send1,
    ) = feed_forward(
        order,
        flag,
        image_count,
        side,
        attended[0],
        attended[1],
        project_out,
        hidden,
        cotangent.reshape(items * rows, width),
        (project_bias[None], feed_gain, feed_shift, reduce_bias),
        expand_weight[0],
        expand_bias,
        reduce_weight[0],
    )
    a = Total(order, ("dp",), keep0, send0)
    c = Total(order, ("dp",), keep1, send1)
    grads = ()

    def backward(item, start, pairs):
        return attend_backward(
            order,
            scalars,
            item,
            start,
            pairs,
            projected,
            images[1],
            attended[item],
            grad_attended,
            lses[item],
            grads,
        )

    grads = backward(0, 0, 2)
    a.step()
    grads = backward(1, 0, 2)
    c.step()
    grads = backward(0, 2, 2)
    a.step()
    grads = backward(1, 2, 2)
    c.step()
    grads = backward(0, 4, 2)
    a.step()
    grads = backward(1, 4, 2)
    a.step()
    c.step()
    near = image_grads(order, project_in, grads[3], grads[4])
    far = to_image(near)
    c.step()
    a.step()
    bias_sums, keep, send = weight_grads(order, side, normed, images[0], grads, project_out_grad)
    p = Total(order, ("dp", "mod"), keep, send)
    (far,) = order.after(far)
    order.last = far
    c.step()
    a.step()
    grad_in, keep = finish_rows(
        order,
        flag,
        hidden,
        grad_middle,
        near,
        far,
        grads[:3],
        attend_gain,
        project_in,
        feed_sums,
        bias_sums,
        keep,
        rows,
    )
    p.terms = (keep, p.got)
    p.step()
    c.step()
    p.step()
    a.step()
    p.step()
    p.step()
    outputs = expert_outputs(order, side, 0, a.mine, width, units, ())
    p.step()
    c.step()
    outputs = expert_outputs(order, 1 - side, 0, a.got, width, units, outputs)
    p.step()
    outputs = expert_outputs(order, side, 2, c.mine, width, units, outputs)
    p.step()
    reduce_grad, expand_grad = expert_outputs(order, 1 - side, 2, c.got, width, units, outputs)
    while p.back:
        p.step()
    projections = projection_outputs(order, side, p.mine, width)
    (
        project_in_grad,
        project_out_grad,
        attend_gain_grad,
        attend_shift_grad,
        feed_gain_grad,
        feed_shift_grad,
        reduce_bias_grad,
        expand_bias_grad,
        bias_pair_grad,
        project_bias_grad,
    ) = last_outputs(order, 1 - side, flag, p.mine, p.got, width, units, projections)
    return (
        hidden_out.reshape(hidden_in.shape),
        grad_in.reshape(hidden_in.shape),
        attend_gain_grad,
        attend_shift_grad,
        project_in_grad,
        bias_pair_grad,
        project_out_grad,
        project_bias_grad[0],
        feed_gain_grad,
        feed_shift_grad,
        expand_grad[None],
        expand_bias_grad,
        reduce_grad[None],
        reduce_bias_grad,
    )


def solution(mesh):
    in_specs = (
        P("dp", "mod", None, None),
        P("dp"),
        P("dp", None),
        P("mod", None),
        P("mod", None),
        P(),
        P(),
        P(),
        P(),
        P("mod", None),
        P("mod", None),
        P("mod", None, None),
        P("mod", None),
        P("mod", None, None),
        P("mod", None),
        P("dp", "mod", None, None),
    )
    out_specs = (
        P("dp", "mod", None, None),
        P("dp", "mod", None, None),
        P("mod", None),
        P("mod", None),
        P(),
        P(),
        P(),
        P(),
        P("mod", None),
        P("mod", None),
        P("mod", None, None),
        P("mod", None),
        P("mod", None, None),
        P("mod", None),
    )
    return jax.shard_map(
        on_device, mesh=mesh, in_specs=in_specs, out_specs=out_specs, check_vma=False
    )
```

```python
import functools

import jax
import jax.numpy as jnp
from jax import lax
from jax.experimental import pallas as pl
from jax.experimental.pallas import tpu as pltpu
from jax.sharding import PartitionSpec as P

HEADS = 12
HEAD = 64
IMG_PAD = 256
PAIR = 2 * HEAD
PAIRS = HEADS // 2
GROUP_PAIRS = 2
GROUPS = PAIRS // GROUP_PAIRS
LANES = GROUP_PAIRS * PAIR
SMALL = 128
FF_BLOCK = 768

masked_value = -1e30
norm_eps = 1e-05

bf16 = jnp.bfloat16
f32 = jnp.float32

NN = (((1,), (0,)), ((), ()))
NT = (((1,), (1,)), ((), ()))
TN = (((0,), (0,)), ((), ()))
VMEM_BYTES = 56 << 20


def dot(left, right, dims=NN):
    return lax.dot_general(left, right, dims, preferred_element_type=f32)


def column_sum(values):
    return jnp.sum(values, axis=0, keepdims=True)


def row_mean(values):
    return jnp.mean(values, axis=1, keepdims=True)


def normalise(values):
    centred = values - row_mean(values)
    scale = lax.rsqrt(row_mean(centred * centred) + norm_eps)
    return centred * scale, scale


def norm_transpose(unit, scale, gain, grad):
    grad_unit = grad * gain
    return scale * (grad_unit - row_mean(grad_unit) - unit * row_mean(grad_unit * unit))


def cost(flops, moved, special=0):
    return pl.CostEstimate(flops=flops, bytes_accessed=moved, transcendentals=special)


class Order:
    def __init__(self):
        self.last = None

    def after(self, *values):
        if self.last is None:
            return values
        *values, _ = lax.optimization_barrier((*values, self.last))
        return values


def call(order, kernel, inputs, out_shape, name, estimate, scalars=(), grid=(), specs=None, outs=None,
         scratch=(), aliases=None):
    inputs = (*order.after(inputs[0]), *inputs[1:])
    vmem = pl.BlockSpec(memory_space=pltpu.VMEM)
    found = pl.pallas_call(
        kernel,
        grid_spec=pltpu.PrefetchScalarGridSpec(
            num_scalar_prefetch=len(scalars),
            grid=grid,
            in_specs=[vmem] * len(inputs) if specs is None else list(specs),
            out_specs=[vmem] * len(out_shape) if outs is None else list(outs),
            scratch_shapes=list(scratch),
        ),
        out_shape=list(out_shape),
        input_output_aliases=aliases or {},
        compiler_params=pltpu.CompilerParams(vmem_limit_bytes=VMEM_BYTES),
        cost_estimate=estimate,
        name=name,
    )(*scalars, *inputs)
    order.last = found[-1]
    return found if len(found) > 1 else found[0]


def shaped(shape, dtype):
    return jax.ShapeDtypeStruct(shape, dtype)


def resident(shape):
    return pl.BlockSpec(shape, lambda *_: (0,) * len(shape), pipeline_mode=pl.Buffered(1))


def project_kernel(hid_ref, gain_ref, shift_ref, weight_ref, bias_ref, normed_ref, out_ref):
    unit, _ = normalise(hid_ref[...].astype(f32))
    normed = (unit * gain_ref[...] + shift_ref[...]).astype(bf16)
    normed_ref[...] = normed
    width = normed.shape[1]
    for part in range(3):
        cols = slice(part * width, (part + 1) * width)
        rows = dot(normed, weight_ref[:, cols])
        if part == 0:
            rows = (rows + bias_ref[0:1]).astype(bf16) * jnp.asarray(HEAD**-0.5, bf16)
        if part == 2:
            rows = rows + bias_ref[1:2]
        out_ref[:, cols] = rows.astype(bf16)


def project_rows(order, hidden, gain, shift, weight, bias):
    rows, width = hidden.shape
    block = 256
    blocked = lambda cols: pl.BlockSpec((block, cols), lambda r: (r, 0))
    inputs = (hidden, gain, shift, weight, bias)
    return call(
        order,
        project_kernel,
        inputs,
        [shaped((rows, width), bf16), shaped((rows, 3 * width), bf16)],
        "project_rows",
        cost(6 * rows * width * width, 10 * rows * width + 6 * width * width),
        grid=(rows // block,),
        specs=[blocked(width)] + [resident(value.shape) for value in inputs[1:]],
        outs=[blocked(width), blocked(3 * width)],
    )


def image_kernel(
    flag_ref,
    own_ref,
    far_ref,
    gain_ref,
    shift_ref,
    vec_ref,
    keys_ref,
    values_ref,
    bias_ref,
    *refs,
):
    normed_ref, out_ref = refs[-2:]
    is_text = flag_ref[0] == 1
    hidden = jnp.where(is_text, far_ref[...].astype(f32), own_ref[...].astype(f32))
    gain = jnp.where(is_text, vec_ref[0:1], gain_ref[...])
    shift = jnp.where(is_text, vec_ref[1:2], shift_ref[...])
    unit, _ = normalise(hidden)
    normed = (unit * gain + shift).astype(bf16)
    normed_ref[...] = normed
    width = normed.shape[1]
    out_ref[:, :width] = dot(normed, keys_ref[...]).astype(bf16)
    out_ref[:, width:] = (dot(normed, values_ref[...]) + bias_ref[1:2]).astype(bf16)


def image_rows(
    order, flag, item, hidden, far, gain, shift, vecs, weight, bias, item_rows, items, earlier
):
    width = hidden.shape[1]
    place = item * (item_rows // IMG_PAD)
    half = lambda base: pl.BlockSpec((width, width), lambda *_: (0, base))
    mine = lambda cols: pl.BlockSpec((IMG_PAD, cols), lambda *_: (item, 0))
    inputs = (hidden, far, gain, shift, vecs, weight, weight, bias, *earlier)
    return call(
        order,
        image_kernel,
        inputs,
        [shaped((items * IMG_PAD, width), bf16), shaped((items * IMG_PAD, 2 * width), bf16)],
        "image_rows",
        cost(4 * IMG_PAD * width * width, 6 << 20),
        scalars=(flag,),
        grid=(1,),
        specs=[
            pl.BlockSpec((IMG_PAD, width), lambda *_: (place, 0)),
            resident(far.shape),
            resident(gain.shape),
            resident(shift.shape),
            resident(vecs.shape),
            half(1),
            half(2),
            resident(bias.shape),
        ]
        + [pl.BlockSpec(memory_space=pl.ANY)] * len(earlier),
        outs=[mine(width), mine(2 * width)],
        aliases={9: 0, 10: 1} if earlier else None,
    )


def segments(shape, axis, lengths_ref, item):
    places = lax.broadcasted_iota(jnp.int32, shape, axis)
    total = jnp.zeros(shape, jnp.int32)
    end = 0
    for which in range(lengths_ref.shape[1]):
        end = end + lengths_ref[item, which]
        total += (places >= end).astype(jnp.int32)
    return total


def own_bias(rows, flag_ref, lengths_ref, item):
    shape = (rows, rows)
    same = segments(shape, 0, lengths_ref, item) == segments(shape, 1, lengths_ref, item)
    return jnp.where(same & (flag_ref[0] == 1), 0.0, masked_value).astype(f32)


def image_bias(shape, axis, count_ref, item):
    places = lax.broadcasted_iota(jnp.int32, shape, axis)
    return jnp.where(places < count_ref[item], 0.0, masked_value).astype(f32)


def forward_kernel(
    item,
    flag_ref,
    count_ref,
    lengths_ref,
    q_ref,
    k_ref,
    v_ref,
    ik_ref,
    iv_ref,
    out_ref,
    lse_ref,
    image_part,
    own_part,
):
    rows = q_ref.shape[0]

    @pl.when(pl.program_id(0) == 0)
    def _():
        image_part[...] = image_bias(image_part.shape, 1, count_ref, item)
        own_part[...] = own_bias(rows, flag_ref, lengths_ref, item)

    first = lax.broadcasted_iota(jnp.int32, (rows, PAIR), 1) < HEAD
    zero = jnp.zeros((), bf16)
    q = q_ref[...]
    image_keys, image_values = ik_ref[...], iv_ref[...]
    keys, values = k_ref[...], v_ref[...]
    outs, tops = [], []
    for head in range(2):
        q_head = jnp.where(first, q, zero) if head == 0 else jnp.where(first, zero, q)
        far = dot(q_head, image_keys, NT) + image_part[...]
        own = dot(q_head, keys, NT) + own_part[...]
        top = jnp.maximum(
            jnp.max(far, axis=1, keepdims=True), jnp.max(own, axis=1, keepdims=True)
        )
        far = jnp.exp(far - top)
        own = jnp.exp(own - top)
        total = jnp.sum(far, axis=1, keepdims=True) + jnp.sum(own, axis=1, keepdims=True)
        summed = dot(far.astype(bf16), image_values) + dot(own.astype(bf16), values)
        outs.append(summed / total)
        tops.append(top + jnp.log(total))
    out_ref[...] = jnp.where(first, outs[0], outs[1]).astype(bf16)
    turned = jnp.transpose(jnp.where(first, tops[0], tops[1]))
    lse_ref[0, 0:1, :] = turned[0:1]
    lse_ref[0, 1:2, :] = turned[HEAD : HEAD + 1]


def attend_forward(order, scalars, item, projected, image):
    rows = projected.shape[0] // 2
    spec = lambda base: pl.BlockSpec((rows, PAIR), lambda h, *_: (item, base + h))
    far = lambda base: pl.BlockSpec((IMG_PAD, PAIR), lambda h, *_: (item, base + h))
    keys = rows + IMG_PAD
    return call(
        order,
        functools.partial(forward_kernel, item),
        (projected, projected, projected, image, image),
        [shaped((rows, HEADS * HEAD), bf16), shaped((PAIRS, 2, rows), f32)],
        "attend_forward",
        cost(16 * HEADS * rows * keys * HEAD, 6 << 20, HEADS * rows * keys),
        scalars=scalars,
        grid=(PAIRS,),
        specs=[spec(0), spec(PAIRS), spec(2 * PAIRS), far(0), far(PAIRS)],
        outs=[
            pl.BlockSpec((rows, PAIR), lambda h, *_: (0, h)),
            pl.BlockSpec((1, 2, rows), lambda h, *_: (h, 0, 0)),
        ],
        scratch=[pltpu.VMEM((rows, IMG_PAD), f32), pltpu.VMEM((rows, rows), f32)],
    )


def backward_kernel(
    item,
    flag_ref,
    count_ref,
    lengths_ref,
    q_ref,
    k_ref,
    v_ref,
    ik_ref,
    iv_ref,
    out_ref,
    grad_ref,
    lse_ref,
    *refs,
):
    gq_ref, gk_ref, gv_ref, gik_ref, giv_ref, image_part, own_part = refs[-7:]
    rows = q_ref.shape[0]

    @pl.when(pl.program_id(0) == 0)
    def _():
        image_part[...] = image_bias(image_part.shape, 0, count_ref, item)
        own_part[...] = own_bias(rows, flag_ref, lengths_ref, item)

    first = lax.broadcasted_iota(jnp.int32, (rows, PAIR), 1) < HEAD
    zero = jnp.zeros((), bf16)
    q, grad = q_ref[...], grad_ref[...]
    products = grad.astype(f32) * out_ref[...].astype(f32)
    head_lanes = lax.broadcasted_iota(jnp.int32, (8, PAIR), 1) // HEAD
    head_rows = lax.broadcasted_iota(jnp.int32, (8, PAIR), 0)
    center = lax.dot_general(
        (head_lanes == head_rows).astype(f32),
        products,
        NT,
        preferred_element_type=f32,
        precision=lax.Precision.HIGHEST,
    )
    q_heads = [jnp.where(first, q, zero), jnp.where(first, zero, q)]
    grad_heads = [jnp.where(first, grad, zero), jnp.where(first, zero, grad)]
    lse = lse_ref[0]
    grad_query = [None, None]
    half = rows // 2
    pieces = (
        (ik_ref, iv_ref, gik_ref, giv_ref, image_part, 0, IMG_PAD),
        (k_ref, v_ref, gk_ref, gv_ref, own_part, 0, half),
        (k_ref, v_ref, gk_ref, gv_ref, own_part, half, half),
    )
    for keys_ref, values_ref, gk_out, gv_out, bias, start, count in pieces:
        piece = slice(start, start + count)
        keys, values = keys_ref[piece, :], values_ref[piece, :]
        low_lanes = lax.broadcasted_iota(jnp.int32, (count, PAIR), 1) < HEAD
        grad_keys, grad_values = [], []
        for head in range(2):
            scores = dot(keys, q_heads[head], NT) + bias[piece, :]
            probs = jnp.exp(scores - lse[head : head + 1])
            grad_probs = dot(values, grad_heads[head], NT)
            grad_scores = (probs * (grad_probs - center[head : head + 1])).astype(bf16)
            grad_values.append(dot(probs.astype(bf16), grad))
            grad_keys.append(dot(grad_scores, q))
            term = dot(grad_scores, keys, TN)
            grad_query[head] = term if grad_query[head] is None else grad_query[head] + term
        gk_out[piece, :] = jnp.where(low_lanes, grad_keys[0], grad_keys[1]).astype(bf16)
        gv_out[piece, :] = jnp.where(low_lanes, grad_values[0], grad_values[1]).astype(bf16)
    gq_ref[...] = (jnp.where(first, grad_query[0], grad_query[1]) * HEAD**-0.5).astype(bf16)


def attend_backward(order, scalars, item, start, pairs, projected, image, attended, grad, lse, earlier):
    rows, width = attended.shape
    spec = lambda base: pl.BlockSpec((rows, PAIR), lambda h, *_: (item, base + start + h))
    far = lambda base: pl.BlockSpec((IMG_PAD, PAIR), lambda h, *_: (item, base + start + h))
    own = pl.BlockSpec((rows, PAIR), lambda h, *_: (0, start + h))
    far_outs = pl.BlockSpec((IMG_PAD, PAIR), lambda h, *_: (item, start + h))
    keys = rows + IMG_PAD
    inputs = (projected, projected, projected, image, image, attended, grad, lse)
    first = len(scalars) + len(inputs)
    return call(
        order,
        functools.partial(backward_kernel, item),
        (*inputs, *earlier),
        [shaped((2 * rows, width), bf16)] * 3 + [shaped((2 * IMG_PAD, width), bf16)] * 2,
        "attend_backward",
        cost(80 * pairs * rows * keys * HEAD, pairs * 2 << 20, 2 * pairs * rows * keys),
        scalars=scalars,
        grid=(pairs,),
        specs=[
            spec(0),
            spec(PAIRS),
            spec(2 * PAIRS),
            far(0),
            far(PAIRS),
            own,
            spec(0),
            pl.BlockSpec((1, 2, rows), lambda h, *_: (start + h, 0, 0)),
        ]
        + [pl.BlockSpec(memory_space=pl.ANY)] * len(earlier),
        outs=[spec(0), spec(0), spec(0), far_outs, far_outs],
        scratch=[pltpu.VMEM((IMG_PAD, rows), f32), pltpu.VMEM((rows, rows), f32)],
        aliases={first + at: at for at in range(len(earlier))},
    )


def gelu_pair(values):
    share = 0.5 * (1.0 + lax.erf(values * 0.7071067811865476))
    slope = share + values * jnp.exp(-0.5 * values * values) * 0.3989422804014327
    return values * share, slope


def feed_step(step, rows, item_rows, feed, top, result, gfeed, expand_ref, ebias_ref, reduce_ref):
    width = feed.shape[1]
    expand, reduce = expand_ref[...], reduce_ref[...]
    active_parts, gup_parts = [], []
    for start in range(0, rows, item_rows):
        here = slice(start, start + item_rows)
        upward = dot(feed[here, :], expand) + ebias_ref[...]
        gactive = dot(top[here, :], reduce, NT)
        active, slope = gelu_pair(upward)
        active = active.astype(bf16)
        gup = (gactive * slope).astype(bf16)
        result[here, :] += dot(active, reduce)
        gfeed[here, :] += dot(gup, expand, NT)
        active_parts.append(active)
        gup_parts.append(gup)
    active = jnp.concatenate(active_parts, axis=0)
    gup = jnp.concatenate(gup_parts, axis=0)
    greduce = dot(active, top[...], TN).astype(bf16)
    gexpand = dot(feed[...], gup, TN).astype(bf16)
    pieces = [greduce[:, at : at + LANES] for at in range(0, width, LANES)]
    pieces += [gexpand[:, at : at + LANES] for at in range(0, FF_BLOCK, LANES)]
    return pieces, column_sum(gup.astype(f32))


def store_pieces(out, pieces):
    at = 0
    for half in range(2):
        for piece in pieces:
            rows = piece.shape[0] // 2
            out[at : at + rows, :] = piece[half * rows : (half + 1) * rows]
            at += rows


def feed_kernel(
    flag_ref,
    count_ref,
    side_ref,
    att0_ref,
    att1_ref,
    project_ref,
    hid_ref,
    cot_ref,
    project_bias_ref,
    gain_ref,
    shift_ref,
    reduce_bias_ref,
    expand_ref,
    ebias_ref,
    reduce_ref,
    out_ref,
    gmid_ref,
    gatt_ref,
    gproject_ref,
    gvec_ref,
    keep0_ref,
    send0_ref,
    keep1_ref,
    send1_ref,
    middle,
    feed,
    top,
    result,
    gfeed,
    low_out,
    gatt,
    grads,
    grad_sems,
    row_sems,
    *,
    item_rows,
):
    step = pl.program_id(0)
    rows, width = hid_ref.shape
    block = 256
    att_refs = (att0_ref, att1_ref)
    half = grads.shape[1] // 2

    steps = grads.shape[0]

    def grad_copies(which):
        found = []
        chunk, place = divmod(which, steps // 2)
        outs = (keep1_ref, send1_ref) if chunk else (keep0_ref, send0_ref)
        for number, out in enumerate(outs):
            side = side_ref[0] if number == 0 else 1 - side_ref[0]
            here = grads.at[which, pl.ds(pl.multiple_of(side * half, half), half)]
            there = out.at[pl.ds(place * half, half)]
            found.append(pltpu.make_async_copy(here, there, grad_sems.at[which, number]))
        return found

    @pl.when(step == 0)
    def _():
        for start in range(0, rows, block):
            here = slice(start, start + block)
            inside = slice(start % item_rows, start % item_rows + block)
            att = att_refs[start // item_rows][inside, :]
            branch = dot(att, project_ref[...]) + project_bias_ref[...]
            x = hid_ref[here, :].astype(f32) + branch
            middle[here, :] = x
            unit, _ = normalise(x)
            feed[here, :] = (unit * gain_ref[...] + shift_ref[...]).astype(bf16)
            at = lax.broadcasted_iota(jnp.int32, (block, width), 0) + start % item_rows
            limit = jnp.where(flag_ref[0] == 1, item_rows, count_ref[start // item_rows])
            top[here, :] = jnp.where(at < limit, cot_ref[here, :].astype(f32), 0.0).astype(bf16)
            result[here, :] = x + reduce_bias_ref[...]
            gfeed[here, :] = jnp.zeros((block, width), f32)

    pieces, gvec_ref[pl.ds(4 + step, 1), :] = feed_step(
        step, rows, item_rows, feed, top, result, gfeed, expand_ref, ebias_ref, reduce_ref
    )
    store_pieces(grads.at[step], pieces)
    for which in range(steps):

        @pl.when(step == which)
        def _(which=which):
            for copy in grad_copies(which):
                copy.start()

    @pl.when(step == pl.num_programs(0) - 1)
    def _():
        copies = []
        sums = [jnp.zeros((1, width), f32)] * 4
        for number, start in enumerate(range(0, rows, block)):
            here = slice(start, start + block)
            low_out[here, :] = result[here, :].astype(bf16)
            unit, scale = normalise(middle[here, :])
            grad = gfeed[here, :]
            grad_top = top[here, :].astype(f32)
            gmid = grad_top + norm_transpose(unit, scale, gain_ref[...], grad)
            terms = (grad * unit, grad, grad_top, gmid)
            sums = [old + column_sum(new) for old, new in zip(sums, terms)]
            middle[here, :] = gmid
            gbranch = gmid.astype(bf16)
            feed[here, :] = gbranch
            gatt[here, :] = dot(gbranch, project_ref[...], NT).astype(bf16)
            for kind, (mine, there) in enumerate(
                ((low_out, out_ref), (middle, gmid_ref), (gatt, gatt_ref))
            ):
                span = pl.ds(start, block)
                copy = pltpu.make_async_copy(
                    mine.at[span, :], there.at[span, :], row_sems.at[kind, number]
                )
                copy.start()
                copies.append(copy)
        total = dot(att0_ref[...], feed[:item_rows, :], TN)
        total += dot(att1_ref[...], feed[item_rows:, :], TN)
        gproject_ref[...] = total.astype(bf16)
        gvec_ref[0:4, :] = jnp.concatenate(sums, axis=0)
        for copy in copies:
            copy.wait()
        for which in range(steps):
            for copy in grad_copies(which):
                copy.wait()


def feed_forward(order, flag, count, side, att0, att1, project, hidden, cotangent, vecs, expand, ebias, reduce):
    rows, width = hidden.shape
    item_rows = att0.shape[0]
    units = reduce.shape[0]
    steps = units // FF_BLOCK
    block_rows = 2 * width * FF_BLOCK // LANES
    fixed = (att0, att1, project, hidden, cotangent, *vecs)
    anywhere = pl.BlockSpec(memory_space=pl.ANY)
    return call(
        order,
        functools.partial(feed_kernel, item_rows=item_rows),
        (*fixed, expand, ebias, reduce),
        [
            shaped((rows, width), bf16),
            shaped((rows, width), f32),
            shaped((rows, width), bf16),
            shaped((width, width), bf16),
            shaped((4 + steps, width), f32),
        ]
        + [shaped((steps // 2 * block_rows // 2, LANES), bf16)] * 4,
        "feed_forward",
        cost(12 * rows * width * units, 40 << 20, 2 * rows * units),
        scalars=(flag, count, side),
        grid=(steps,),
        specs=[resident(value.shape) for value in fixed]
        + [
            pl.BlockSpec((width, FF_BLOCK), lambda j, *_: (0, j)),
            pl.BlockSpec((1, FF_BLOCK), lambda j, *_: (0, j)),
            pl.BlockSpec((FF_BLOCK, width), lambda j, *_: (j, 0)),
        ],
        outs=[
            anywhere,
            anywhere,
            anywhere,
            resident((width, width)),
            resident((4 + steps, width)),
        ]
        + [anywhere] * 4,
        scratch=[
            pltpu.VMEM((rows, width), f32),
            pltpu.VMEM((rows, width), bf16),
            pltpu.VMEM((rows, width), bf16),
            pltpu.VMEM((rows, width), f32),
            pltpu.VMEM((rows, width), f32),
            pltpu.VMEM((rows, width), bf16),
            pltpu.VMEM((rows, width), bf16),
            pltpu.VMEM((steps, block_rows, LANES), bf16),
            pltpu.SemaphoreType.DMA((steps, 2)),
            pltpu.SemaphoreType.DMA((3, rows // 256)),
        ],
    )


def weight_kernel(
    side_ref,
    normed_ref,
    image_ref,
    gq_ref,
    gk_ref,
    gv_ref,
    gik_ref,
    giv_ref,
    extra_ref,
    sums_ref,
    keep_ref,
    send_ref,
    keep,
    send,
    sems,
):
    step = pl.program_id(0)
    width = normed_ref.shape[1]
    half = width // 2
    block = half * width // LANES

    def copies(part):
        rows = block if part < 4 else SMALL
        span = pl.ds(part * block, rows)
        pairs = ((keep, keep_ref), (send, send_ref))
        return [
            pltpu.make_async_copy(here.at[span], there.at[span], sems.at[number, part])
            for number, (here, there) in enumerate(pairs)
        ]

    def store(part, total):
        first = side_ref[0] == 0
        mine = jnp.where(first, total[:half], total[half:]).astype(bf16)
        other = jnp.where(first, total[half:], total[:half]).astype(bf16)
        for number in range(width // LANES):
            rows = slice(part * block + number * half, part * block + (number + 1) * half)
            cols = slice(number * LANES, (number + 1) * LANES)
            keep[rows, :] = mine[:, cols]
            send[rows, :] = other[:, cols]
        for copy in copies(part):
            copy.start()

    @pl.when(step == 0)
    def _():
        store(0, dot(normed_ref[...], gq_ref[...], TN))
        sums_ref[0:1] = column_sum(gq_ref[...].astype(f32))

    @pl.when(step == 1)
    def _():
        total = dot(normed_ref[...], gk_ref[...], TN)
        store(1, total + dot(image_ref[...], gik_ref[...], TN))

    @pl.when(step == 2)
    def _():
        total = dot(normed_ref[...], gv_ref[...], TN)
        store(2, total + dot(image_ref[...], giv_ref[...], TN))
        sums = column_sum(gv_ref[...].astype(f32)) + column_sum(giv_ref[...].astype(f32))
        sums_ref[1:2] = sums

    @pl.when(step == 3)
    def _():
        store(3, extra_ref[...].astype(f32))
        keep[4 * block :, :] = jnp.zeros((SMALL, LANES), bf16)
        send[4 * block :, :] = jnp.zeros((SMALL, LANES), bf16)
        for copy in copies(4):
            copy.start()
        for part in range(5):
            for copy in copies(part):
                copy.wait()


def weight_grads(order, side, normed, image, grads, extra):
    rows, width = normed.shape
    all_rows = 4 * (width * width // 2 // LANES) + SMALL
    inputs = (normed, image, *grads, extra)
    anywhere = pl.BlockSpec(memory_space=pl.ANY)
    return call(
        order,
        weight_kernel,
        inputs,
        [shaped((2, width), f32)] + [shaped((all_rows, LANES), bf16)] * 2,
        "weight_grads",
        cost(8 * rows * width * width, 12 << 20),
        scalars=(side,),
        grid=(4,),
        specs=[resident(value.shape) for value in inputs],
        outs=[resident((2, width)), anywhere, anywhere],
        scratch=[pltpu.VMEM((all_rows, LANES), bf16)] * 2 + [pltpu.SemaphoreType.DMA((2, 5))],
    )


def image_grad_kernel(keys_weight, values_weight, keys_ref, values_ref, out_ref):
    total = dot(keys_ref[...], keys_weight[...], NT) + dot(values_ref[...], values_weight[...], NT)
    out_ref[...] = total.astype(bf16)


def image_grads(order, weight, keys, values):
    rows, width = keys.shape
    part = lambda base: pl.BlockSpec((width, width), lambda *_: (0, base))
    return call(
        order,
        image_grad_kernel,
        (weight, weight, keys, values),
        [shaped((rows, width), bf16)],
        "image_grads",
        cost(4 * rows * width * width, 6 << 20),
        grid=(1,),
        specs=[part(1), part(2), resident(keys.shape), resident(values.shape)],
        outs=[resident((rows, width))],
    )


def finish_kernel(
    flag_ref,
    hid_ref,
    gmid_ref,
    near_ref,
    far_ref,
    gq_ref,
    gk_ref,
    gv_ref,
    gain_ref,
    weight_ref,
    feed_sums_ref,
    bias_sums_ref,
    _,
    out_ref,
    small_ref,
    sums,
):
    item, block = pl.program_id(0), pl.program_id(1)
    joined = jnp.concatenate([gq_ref[...], gk_ref[...], gv_ref[...]], axis=1)
    grad = dot(joined, weight_ref[...], NT)
    unit, scale = normalise(hid_ref[...].astype(f32))
    both = near_ref[...].astype(f32) + far_ref[...].astype(f32)
    grad = grad + jnp.where((flag_ref[0] == 0) & (block == 0), both, 0.0)
    total = gmid_ref[...] + norm_transpose(unit, scale, gain_ref[...], grad)
    out_ref[...] = total.astype(bf16)
    found = jnp.concatenate([column_sum(grad * unit), column_sum(grad)], axis=0)

    @pl.when((item == 0) & (block == 0))
    def _():
        sums[...] = jnp.zeros(sums.shape, f32)

    sums[0:2] += found

    @pl.when((item == pl.num_programs(0) - 1) & (block == pl.num_programs(1) - 1))
    def _():
        width = sums.shape[1]
        pad = lambda count: jnp.zeros((count, width), f32)
        own = [sums[0:2], feed_sums_ref[0:3], feed_sums_ref[4:8], pad(7)]
        own = jnp.concatenate(own, axis=0)
        shared = [pad(9), feed_sums_ref[3:4], bias_sums_ref[...], pad(4)]
        shared = jnp.concatenate(shared, axis=0)
        is_text = flag_ref[0] == 1
        first = jnp.where(is_text, 0.0, own) + shared
        rows = jnp.concatenate([first, jnp.where(is_text, own, 0.0)], axis=0).astype(bf16)
        count = rows.shape[0]
        for number in range(width // LANES):
            cols = slice(number * LANES, (number + 1) * LANES)
            small_ref[number * count : (number + 1) * count, :] = rows[:, cols]
        small_ref[width // LANES * count :, :] = jnp.zeros((SMALL - width // LANES * count, LANES), bf16)


def finish_rows(
    order, flag, hidden, gmid, near, far, grads, gain, weight, feed_sums, bias_sums, keep, item_rows
):
    rows, width = hidden.shape
    blocks = item_rows // IMG_PAD
    mine = pl.BlockSpec((IMG_PAD, width), lambda i, j, *_: (i * blocks + j, 0))
    image = pl.BlockSpec((IMG_PAD, width), lambda i, j, *_: (i, 0))
    fixed = (gain, weight, feed_sums, bias_sums)
    place = keep.shape[0] // SMALL - 1
    return call(
        order,
        finish_kernel,
        (hidden, gmid, near, far, *grads, *fixed, keep),
        [shaped((rows, width), bf16), shaped(keep.shape, bf16)],
        "finish_rows",
        cost(60 * rows * width * width, 160 << 20),
        scalars=(flag,),
        grid=(rows // item_rows, blocks),
        specs=[mine, mine, image, image, mine, mine, mine]
        + [resident(value.shape) for value in fixed]
        + [pl.BlockSpec(memory_space=pl.ANY)],
        outs=[mine, pl.BlockSpec((SMALL, LANES), lambda *_: (place, 0))],
        scratch=[pltpu.VMEM((8, width), f32)],
        aliases={12: 1},
    )


def expert_kernel(half_ref, value_ref, *refs):
    at = 0
    for out in refs[-2:]:
        tall = out.shape[0]
        for part in range(out.shape[1] // LANES):
            piece = value_ref[at : at + tall, :]
            out[:, part * LANES : (part + 1) * LANES] = piece.astype(f32)
            at += tall


def expert_outputs(order, half, first, value, width, units, earlier):
    tall = width // 2
    block_rows = 2 * width // LANES * tall
    return call(
        order,
        expert_kernel,
        (value, *earlier),
        [shaped((units, width), f32), shaped((width, units), f32)],
        "expert_outputs",
        cost(value.size, 6 * value.size),
        scalars=(half,),
        grid=(value.shape[0] // block_rows,),
        specs=[pl.BlockSpec((block_rows, LANES), lambda i, at: (i, 0))]
        + [pl.BlockSpec(memory_space=pl.ANY)] * len(earlier),
        outs=[
            pl.BlockSpec((tall, width), lambda i, at: (2 * (first + i) + at[0], 0)),
            pl.BlockSpec((tall, width), lambda i, at: (at[0], first + i)),
        ],
        aliases={2: 0, 3: 1} if earlier else None,
    )


def store_projection(value_ref, in_ref, out_ref):
    tall, wide = in_ref.shape

    def store(ref):
        for part in range(wide // LANES):
            piece = value_ref[part * tall : (part + 1) * tall, :]
            ref[:, part * LANES : (part + 1) * LANES] = piece.astype(f32)

    @pl.when(pl.program_id(0) < 3)
    def _():
        store(in_ref)

    @pl.when(pl.program_id(0) == 3)
    def _():
        store(out_ref)


def projection_kernel(half_ref, value_ref, in_ref, out_ref):
    store_projection(value_ref, in_ref, out_ref)


def last_kernel(half_ref, flag_ref, value_ref, mine_ref, got_ref, *refs):
    in_ref, out_ref, *vec_refs, expand_ref, pair_ref, project_ref = refs[2:]
    store_projection(value_ref, in_ref, out_ref)

    @pl.when(pl.program_id(0) == 0)
    def _():
        both = mine_ref[...].astype(f32) + got_ref[...].astype(f32)
        width = vec_refs[0].shape[1]
        rows = jnp.concatenate([both[at * 32 : (at + 1) * 32] for at in range(width // LANES)], axis=1)
        own = jnp.where(flag_ref[0] == 1, rows[16:], rows[:16])
        for number, ref in enumerate(vec_refs):
            ref[...] = own[number : number + 1]
        for number in range(expand_ref.shape[1] // width):
            cols = slice(number * width, (number + 1) * width)
            expand_ref[:, cols] = own[5 + number : 6 + number]
        project_ref[...] = rows[9:10]
        pair_ref[...] = rows[10:12]


def projection_specs(width):
    tall = width // 2
    value = pl.BlockSpec((tall * width // LANES, LANES), lambda b, *_: (b, 0))
    outs = [
        pl.BlockSpec((tall, width), lambda b, at, *_: (at[0], jnp.minimum(b, 2))),
        pl.BlockSpec((tall, width), lambda b, at, *_: (at[0], 0)),
    ]
    return value, outs, [shaped((width, 3 * width), f32), shaped((width, width), f32)]


def projection_outputs(order, half, value, width):
    spec, outs, shapes = projection_specs(width)
    return call(
        order,
        projection_kernel,
        (value,),
        shapes,
        "projection_outputs",
        cost(value.size, 6 * value.size),
        scalars=(half,),
        grid=(4,),
        specs=[spec],
        outs=outs,
    )


def last_outputs(order, half, flag, mine, got, width, units, earlier):
    spec, outs, shapes = projection_specs(width)
    place = got.shape[0] // SMALL - 1
    small = pl.BlockSpec((SMALL, LANES), lambda *_: (place, 0))
    vecs = [(1, width)] * 5 + [(1, units), (2, width), (1, width)]
    return call(
        order,
        last_kernel,
        (got, mine, got, *earlier),
        shapes + [shaped(shape, f32) for shape in vecs],
        "last_outputs",
        cost(got.size, 6 * got.size),
        scalars=(half, flag),
        grid=(4,),
        specs=[spec, small, small] + [pl.BlockSpec(memory_space=pl.ANY)] * 2,
        outs=outs + [resident(shape) for shape in vecs],
        aliases={5: 0, 6: 1},
    )


def swap(value, axes, pair_of):
    count = 1
    for axis in axes:
        count *= lax.axis_size(axis)
    return lax.ppermute(value, axes, [(source, pair_of(source)) for source in range(count)])


def place_of(axes):
    place = 0
    for axis in axes:
        place = place * lax.axis_size(axis) + lax.axis_index(axis)
    return place


def stage_bits(axes):
    count = 1
    for axis in axes:
        count *= lax.axis_size(axis)
    bits = count.bit_length() - 1
    core = len(axes) - 1
    others = [bit for bit in range(bits) if bit != core]
    if len(axes) == 1 and len(others) == 3:
        return [(core, core), (1, 2), (3, 1), (2, 3)]
    if len(axes) == 2 and len(others) == 4:
        return [(core, core), (0, 2), (2, 0), (3, 3), (4, 4)]
    return [(core, core)] + list(zip(others, others[1:] + others[:1]))


class Total:
    def __init__(self, order, axes, keep, send):
        self.order = order
        self.axes = axes
        self.core = len(axes) - 1
        self.left = stage_bits(axes)
        place = place_of(axes)
        second = ((place >> self.core) & 1) == 1
        sides = [(place >> jnp.where(second, pair[1], pair[0])) & 1 for pair in self.left]
        self.sides = dict(zip(self.left, sides))
        self.back = list(self.left)
        self.terms = (keep, self.exchange(send, self.left.pop(0)))
        self.mine = None

    def exchange(self, value, pair):
        other = lambda source: source ^ (1 << pair[(source >> self.core) & 1])
        self.got = swap(value, self.axes, other)
        return self.got

    def part(self, which, half):
        cut = lambda term: lax.dynamic_slice_in_dim(term, which * half, half, 0).astype(f32)
        return (cut(self.terms[0]) + cut(self.terms[1])).astype(bf16)

    def step(self):
        if self.left:
            pair = self.left.pop(0)
            self.terms = self.order.after(*self.terms)
            half = self.terms[0].shape[0] // 2
            side = self.sides[pair]
            sent = self.part(1 - side, half)
            self.terms = (self.part(side, half), self.exchange(sent, pair))
            self.order.last = sent
            return
        pair = self.back.pop()
        if self.mine is None:
            self.terms = self.order.after(*self.terms)
            self.mine = (self.terms[0].astype(f32) + self.terms[1].astype(f32)).astype(bf16)
        else:
            mine, got = self.order.after(self.mine, self.got)
            low = jnp.where(self.last == 0, mine, got)
            high = jnp.where(self.last == 0, got, mine)
            self.mine = jnp.concatenate([low, high], axis=0)
        self.order.last = self.mine
        self.last = self.sides[pair]
        self.exchange(self.mine, pair)


def on_device(
    hidden_in,
    image_count,
    text_lengths,
    attend_gain,
    attend_shift,
    project_in,
    bias_pair,
    project_out,
    project_bias,
    feed_gain,
    feed_shift,
    expand_weight,
    expand_bias,
    reduce_weight,
    reduce_bias,
    cotangent,
):
    items, _, rows, width = hidden_in.shape
    units = expand_weight.shape[2]
    is_text = lax.axis_index("mod") == 1
    flag = is_text.astype(jnp.int32)[None]
    hidden = hidden_in.reshape(items * rows, width)
    to_text = lambda value: lax.ppermute(value, "mod", [(0, 1)])
    to_image = lambda value: lax.ppermute(value, "mod", [(1, 0)])

    far_rows = [to_text(hidden_in[item, 0, :IMG_PAD]) for item in range(items)]
    far_vecs = to_text(jnp.concatenate([attend_gain, attend_shift], axis=0))
    order = Order()
    normed, projected = project_rows(
        order, hidden, attend_gain, attend_shift, project_in, bias_pair
    )
    scalars = (flag, image_count, text_lengths)
    images, attended, lses = (), [], []
    for item in range(items):
        images = image_rows(
            order,
            flag,
            item,
            hidden,
            far_rows[item],
            attend_gain,
            attend_shift,
            far_vecs,
            project_in,
            bias_pair,
            rows,
            items,
            images,
        )
        out, lse = attend_forward(order, scalars, item, projected, images[1])
        attended.append(out)
        lses.append(lse)

    side = (lax.axis_index("dp") & 1)[None]
    (
        hidden_out,
        grad_middle,
        grad_attended,
        project_out_grad,
        feed_sums,
        keep0,
        send0,
        keep1,
        send1,
    ) = feed_forward(
        order,
        flag,
        image_count,
        side,
        attended[0],
        attended[1],
        project_out,
        hidden,
        cotangent.reshape(items * rows, width),
        (project_bias[None], feed_gain, feed_shift, reduce_bias),
        expand_weight[0],
        expand_bias,
        reduce_weight[0],
    )
    a = Total(order, ("dp",), keep0, send0)
    c = Total(order, ("dp",), keep1, send1)
    grads = ()

    def backward(item, start, pairs):
        return attend_backward(
            order,
            scalars,
            item,
            start,
            pairs,
            projected,
            images[1],
            attended[item],
            grad_attended,
            lses[item],
            grads,
        )

    grads = backward(0, 0, 2)
    a.step()
    grads = backward(1, 0, 2)
    c.step()
    grads = backward(0, 2, 2)
    a.step()
    grads = backward(1, 2, 2)
    c.step()
    grads = backward(0, 4, 2)
    a.step()
    grads = backward(1, 4, 2)
    a.step()
    c.step()
    near = image_grads(order, project_in, grads[3], grads[4])
    far = to_image(near)
    c.step()
    a.step()
    bias_sums, keep, send = weight_grads(order, side, normed, images[0], grads, project_out_grad)
    p = Total(order, ("dp", "mod"), keep, send)
    c.step()
    a.step()
    (far,) = order.after(far)
    order.last = far
    grad_in, keep = finish_rows(
        order,
        flag,
        hidden,
        grad_middle,
        near,
        far,
        grads[:3],
        attend_gain,
        project_in,
        feed_sums,
        bias_sums,
        keep,
        rows,
    )
    p.terms = (keep, p.got)
    p.step()
    a.step()
    c.step()
    p.step()
    outputs = expert_outputs(order, side, 0, a.mine, width, units, ())
    p.step()
    outputs = expert_outputs(order, 1 - side, 0, a.got, width, units, outputs)
    c.step()
    p.step()
    p.step()
    outputs = expert_outputs(order, side, 2, c.mine, width, units, outputs)
    p.step()
    reduce_grad, expand_grad = expert_outputs(order, 1 - side, 2, c.got, width, units, outputs)
    while p.back:
        p.step()
    projections = projection_outputs(order, side, p.mine, width)
    (
        project_in_grad,
        project_out_grad,
        attend_gain_grad,
        attend_shift_grad,
        feed_gain_grad,
        feed_shift_grad,
        reduce_bias_grad,
        expand_bias_grad,
        bias_pair_grad,
        project_bias_grad,
    ) = last_outputs(order, 1 - side, flag, p.mine, p.got, width, units, projections)
    return (
        hidden_out.reshape(hidden_in.shape),
        grad_in.reshape(hidden_in.shape),
        attend_gain_grad,
        attend_shift_grad,
        project_in_grad,
        bias_pair_grad,
        project_out_grad,
        project_bias_grad[0],
        feed_gain_grad,
        feed_shift_grad,
        expand_grad[None],
        expand_bias_grad,
        reduce_grad[None],
        reduce_bias_grad,
    )


def solution(mesh):
    in_specs = (
        P("dp", "mod", None, None),
        P("dp"),
        P("dp", None),
        P("mod", None),
        P("mod", None),
        P(),
        P(),
        P(),
        P(),
        P("mod", None),
        P("mod", None),
        P("mod", None, None),
        P("mod", None),
        P("mod", None, None),
        P("mod", None),
        P("dp", "mod", None, None),
    )
    out_specs = (
        P("dp", "mod", None, None),
        P("dp", "mod", None, None),
        P("mod", None),
        P("mod", None),
        P(),
        P(),
        P(),
        P(),
        P("mod", None),
        P("mod", None),
        P("mod", None, None),
        P("mod", None),
        P("mod", None, None),
        P("mod", None),
    )
    return jax.shard_map(
        on_device, mesh=mesh, in_specs=in_specs, out_specs=out_specs, check_vma=False
    )
```

```python
import functools

import jax
import jax.numpy as jnp
from jax import lax
from jax.experimental import pallas as pl
from jax.experimental.pallas import tpu as pltpu
from jax.sharding import PartitionSpec as P

HEADS = 12
HEAD = 64
IMG_PAD = 256
PAIR = 2 * HEAD
PAIRS = HEADS // 2
GROUP_PAIRS = 2
GROUPS = PAIRS // GROUP_PAIRS
LANES = GROUP_PAIRS * PAIR
SMALL = 128
FF_BLOCK = 768

masked_value = -1e30
norm_eps = 1e-05

bf16 = jnp.bfloat16
f32 = jnp.float32

NN = (((1,), (0,)), ((), ()))
NT = (((1,), (1,)), ((), ()))
TN = (((0,), (0,)), ((), ()))
VMEM_BYTES = 56 << 20


def dot(left, right, dims=NN):
    return lax.dot_general(left, right, dims, preferred_element_type=f32)


def column_sum(values):
    return jnp.sum(values, axis=0, keepdims=True)


def row_mean(values):
    return jnp.mean(values, axis=1, keepdims=True)


def normalise(values):
    centred = values - row_mean(values)
    scale = lax.rsqrt(row_mean(centred * centred) + norm_eps)
    return centred * scale, scale


def norm_transpose(unit, scale, gain, grad):
    grad_unit = grad * gain
    return scale * (grad_unit - row_mean(grad_unit) - unit * row_mean(grad_unit * unit))


def cost(flops, moved, special=0):
    return pl.CostEstimate(flops=flops, bytes_accessed=moved, transcendentals=special)


class Order:
    def __init__(self):
        self.last = None

    def after(self, *values):
        if self.last is None:
            return values
        *values, _ = lax.optimization_barrier((*values, self.last))
        return values


def call(order, kernel, inputs, out_shape, name, estimate, scalars=(), grid=(), specs=None, outs=None,
         scratch=(), aliases=None):
    inputs = (*order.after(inputs[0]), *inputs[1:])
    vmem = pl.BlockSpec(memory_space=pltpu.VMEM)
    found = pl.pallas_call(
        kernel,
        grid_spec=pltpu.PrefetchScalarGridSpec(
            num_scalar_prefetch=len(scalars),
            grid=grid,
            in_specs=[vmem] * len(inputs) if specs is None else list(specs),
            out_specs=[vmem] * len(out_shape) if outs is None else list(outs),
            scratch_shapes=list(scratch),
        ),
        out_shape=list(out_shape),
        input_output_aliases=aliases or {},
        compiler_params=pltpu.CompilerParams(vmem_limit_bytes=VMEM_BYTES),
        cost_estimate=estimate,
        name=name,
    )(*scalars, *inputs)
    order.last = found[-1]
    return found if len(found) > 1 else found[0]


def shaped(shape, dtype):
    return jax.ShapeDtypeStruct(shape, dtype)


def resident(shape):
    return pl.BlockSpec(shape, lambda *_: (0,) * len(shape), pipeline_mode=pl.Buffered(1))


def project_kernel(hid_ref, gain_ref, shift_ref, weight_ref, bias_ref, normed_ref, out_ref):
    unit, _ = normalise(hid_ref[...].astype(f32))
    normed = (unit * gain_ref[...] + shift_ref[...]).astype(bf16)
    normed_ref[...] = normed
    width = normed.shape[1]
    for part in range(3):
        cols = slice(part * width, (part + 1) * width)
        rows = dot(normed, weight_ref[:, cols])
        if part == 0:
            rows = (rows + bias_ref[0:1]).astype(bf16) * jnp.asarray(HEAD**-0.5, bf16)
        if part == 2:
            rows = rows + bias_ref[1:2]
        out_ref[:, cols] = rows.astype(bf16)


def project_rows(order, hidden, gain, shift, weight, bias):
    rows, width = hidden.shape
    block = 256
    blocked = lambda cols: pl.BlockSpec((block, cols), lambda r: (r, 0))
    inputs = (hidden, gain, shift, weight, bias)
    return call(
        order,
        project_kernel,
        inputs,
        [shaped((rows, width), bf16), shaped((rows, 3 * width), bf16)],
        "project_rows",
        cost(6 * rows * width * width, 10 * rows * width + 6 * width * width),
        grid=(rows // block,),
        specs=[blocked(width)] + [resident(value.shape) for value in inputs[1:]],
        outs=[blocked(width), blocked(3 * width)],
    )


def image_kernel(
    flag_ref,
    own_ref,
    far_ref,
    gain_ref,
    shift_ref,
    vec_ref,
    keys_ref,
    values_ref,
    bias_ref,
    *refs,
):
    normed_ref, out_ref = refs[-2:]
    is_text = flag_ref[0] == 1
    hidden = jnp.where(is_text, far_ref[...].astype(f32), own_ref[...].astype(f32))
    gain = jnp.where(is_text, vec_ref[0:1], gain_ref[...])
    shift = jnp.where(is_text, vec_ref[1:2], shift_ref[...])
    unit, _ = normalise(hidden)
    normed = (unit * gain + shift).astype(bf16)
    normed_ref[...] = normed
    width = normed.shape[1]
    out_ref[:, :width] = dot(normed, keys_ref[...]).astype(bf16)
    out_ref[:, width:] = (dot(normed, values_ref[...]) + bias_ref[1:2]).astype(bf16)


def image_rows(
    order, flag, item, hidden, far, gain, shift, vecs, weight, bias, item_rows, items, earlier
):
    width = hidden.shape[1]
    place = item * (item_rows // IMG_PAD)
    half = lambda base: pl.BlockSpec((width, width), lambda *_: (0, base))
    mine = lambda cols: pl.BlockSpec((IMG_PAD, cols), lambda *_: (item, 0))
    inputs = (hidden, far, gain, shift, vecs, weight, weight, bias, *earlier)
    return call(
        order,
        image_kernel,
        inputs,
        [shaped((items * IMG_PAD, width), bf16), shaped((items * IMG_PAD, 2 * width), bf16)],
        "image_rows",
        cost(4 * IMG_PAD * width * width, 6 << 20),
        scalars=(flag,),
        grid=(1,),
        specs=[
            pl.BlockSpec((IMG_PAD, width), lambda *_: (place, 0)),
            resident(far.shape),
            resident(gain.shape),
            resident(shift.shape),
            resident(vecs.shape),
            half(1),
            half(2),
            resident(bias.shape),
        ]
        + [pl.BlockSpec(memory_space=pl.ANY)] * len(earlier),
        outs=[mine(width), mine(2 * width)],
        aliases={9: 0, 10: 1} if earlier else None,
    )


def segments(shape, axis, lengths_ref, item):
    places = lax.broadcasted_iota(jnp.int32, shape, axis)
    total = jnp.zeros(shape, jnp.int32)
    end = 0
    for which in range(lengths_ref.shape[1]):
        end = end + lengths_ref[item, which]
        total += (places >= end).astype(jnp.int32)
    return total


def own_bias(rows, flag_ref, lengths_ref, item):
    shape = (rows, rows)
    same = segments(shape, 0, lengths_ref, item) == segments(shape, 1, lengths_ref, item)
    return jnp.where(same & (flag_ref[0] == 1), 0.0, masked_value).astype(f32)


def image_bias(shape, axis, count_ref, item):
    places = lax.broadcasted_iota(jnp.int32, shape, axis)
    return jnp.where(places < count_ref[item], 0.0, masked_value).astype(f32)


def forward_kernel(
    item,
    flag_ref,
    count_ref,
    lengths_ref,
    q_ref,
    k_ref,
    v_ref,
    ik_ref,
    iv_ref,
    out_ref,
    lse_ref,
    image_part,
    own_part,
):
    rows = q_ref.shape[0]

    @pl.when(pl.program_id(0) == 0)
    def _():
        image_part[...] = image_bias(image_part.shape, 1, count_ref, item)
        own_part[...] = own_bias(rows, flag_ref, lengths_ref, item)

    first = lax.broadcasted_iota(jnp.int32, (rows, PAIR), 1) < HEAD
    zero = jnp.zeros((), bf16)
    q = q_ref[...]
    image_keys, image_values = ik_ref[...], iv_ref[...]
    keys, values = k_ref[...], v_ref[...]
    outs, tops = [], []
    for head in range(2):
        q_head = jnp.where(first, q, zero) if head == 0 else jnp.where(first, zero, q)
        far = dot(q_head, image_keys, NT) + image_part[...]
        own = dot(q_head, keys, NT) + own_part[...]
        top = jnp.maximum(
            jnp.max(far, axis=1, keepdims=True), jnp.max(own, axis=1, keepdims=True)
        )
        far = jnp.exp(far - top)
        own = jnp.exp(own - top)
        total = jnp.sum(far, axis=1, keepdims=True) + jnp.sum(own, axis=1, keepdims=True)
        summed = dot(far.astype(bf16), image_values) + dot(own.astype(bf16), values)
        outs.append(summed / total)
        tops.append(top + jnp.log(total))
    out_ref[...] = jnp.where(first, outs[0], outs[1]).astype(bf16)
    turned = jnp.transpose(jnp.where(first, tops[0], tops[1]))
    lse_ref[0, 0:1, :] = turned[0:1]
    lse_ref[0, 1:2, :] = turned[HEAD : HEAD + 1]


def attend_forward(order, scalars, item, projected, image):
    rows = projected.shape[0] // 2
    spec = lambda base: pl.BlockSpec((rows, PAIR), lambda h, *_: (item, base + h))
    far = lambda base: pl.BlockSpec((IMG_PAD, PAIR), lambda h, *_: (item, base + h))
    keys = rows + IMG_PAD
    return call(
        order,
        functools.partial(forward_kernel, item),
        (projected, projected, projected, image, image),
        [shaped((rows, HEADS * HEAD), bf16), shaped((PAIRS, 2, rows), f32)],
        "attend_forward",
        cost(16 * HEADS * rows * keys * HEAD, 6 << 20, HEADS * rows * keys),
        scalars=scalars,
        grid=(PAIRS,),
        specs=[spec(0), spec(PAIRS), spec(2 * PAIRS), far(0), far(PAIRS)],
        outs=[
            pl.BlockSpec((rows, PAIR), lambda h, *_: (0, h)),
            pl.BlockSpec((1, 2, rows), lambda h, *_: (h, 0, 0)),
        ],
        scratch=[pltpu.VMEM((rows, IMG_PAD), f32), pltpu.VMEM((rows, rows), f32)],
    )


def backward_kernel(
    item,
    flag_ref,
    count_ref,
    lengths_ref,
    q_ref,
    k_ref,
    v_ref,
    ik_ref,
    iv_ref,
    out_ref,
    grad_ref,
    lse_ref,
    *refs,
):
    gq_ref, gk_ref, gv_ref, gik_ref, giv_ref, image_part, own_part = refs[-7:]
    rows = q_ref.shape[0]

    @pl.when(pl.program_id(0) == 0)
    def _():
        image_part[...] = image_bias(image_part.shape, 0, count_ref, item)
        own_part[...] = own_bias(rows, flag_ref, lengths_ref, item)

    first = lax.broadcasted_iota(jnp.int32, (rows, PAIR), 1) < HEAD
    zero = jnp.zeros((), bf16)
    q, grad = q_ref[...], grad_ref[...]
    products = grad.astype(f32) * out_ref[...].astype(f32)
    head_lanes = lax.broadcasted_iota(jnp.int32, (8, PAIR), 1) // HEAD
    head_rows = lax.broadcasted_iota(jnp.int32, (8, PAIR), 0)
    center = lax.dot_general(
        (head_lanes == head_rows).astype(f32),
        products,
        NT,
        preferred_element_type=f32,
        precision=lax.Precision.HIGHEST,
    )
    q_heads = [jnp.where(first, q, zero), jnp.where(first, zero, q)]
    grad_heads = [jnp.where(first, grad, zero), jnp.where(first, zero, grad)]
    lse = lse_ref[0]
    grad_query = [None, None]
    half = rows // 2
    pieces = (
        (ik_ref, iv_ref, gik_ref, giv_ref, image_part, 0, IMG_PAD),
        (k_ref, v_ref, gk_ref, gv_ref, own_part, 0, half),
        (k_ref, v_ref, gk_ref, gv_ref, own_part, half, half),
    )
    for keys_ref, values_ref, gk_out, gv_out, bias, start, count in pieces:
        piece = slice(start, start + count)
        keys, values = keys_ref[piece, :], values_ref[piece, :]
        low_lanes = lax.broadcasted_iota(jnp.int32, (count, PAIR), 1) < HEAD
        grad_keys, grad_values = [], []
        for head in range(2):
            scores = dot(keys, q_heads[head], NT) + bias[piece, :]
            probs = jnp.exp(scores - lse[head : head + 1])
            grad_probs = dot(values, grad_heads[head], NT)
            grad_scores = (probs * (grad_probs - center[head : head + 1])).astype(bf16)
            grad_values.append(dot(probs.astype(bf16), grad))
            grad_keys.append(dot(grad_scores, q))
            term = dot(grad_scores, keys, TN)
            grad_query[head] = term if grad_query[head] is None else grad_query[head] + term
        gk_out[piece, :] = jnp.where(low_lanes, grad_keys[0], grad_keys[1]).astype(bf16)
        gv_out[piece, :] = jnp.where(low_lanes, grad_values[0], grad_values[1]).astype(bf16)
    gq_ref[...] = (jnp.where(first, grad_query[0], grad_query[1]) * HEAD**-0.5).astype(bf16)


def attend_backward(order, scalars, item, start, pairs, projected, image, attended, grad, lse, earlier):
    rows, width = attended.shape
    spec = lambda base: pl.BlockSpec((rows, PAIR), lambda h, *_: (item, base + start + h))
    far = lambda base: pl.BlockSpec((IMG_PAD, PAIR), lambda h, *_: (item, base + start + h))
    own = pl.BlockSpec((rows, PAIR), lambda h, *_: (0, start + h))
    far_outs = pl.BlockSpec((IMG_PAD, PAIR), lambda h, *_: (item, start + h))
    keys = rows + IMG_PAD
    inputs = (projected, projected, projected, image, image, attended, grad, lse)
    first = len(scalars) + len(inputs)
    return call(
        order,
        functools.partial(backward_kernel, item),
        (*inputs, *earlier),
        [shaped((2 * rows, width), bf16)] * 3 + [shaped((2 * IMG_PAD, width), bf16)] * 2,
        "attend_backward",
        cost(80 * pairs * rows * keys * HEAD, pairs * 2 << 20, 2 * pairs * rows * keys),
        scalars=scalars,
        grid=(pairs,),
        specs=[
            spec(0),
            spec(PAIRS),
            spec(2 * PAIRS),
            far(0),
            far(PAIRS),
            own,
            spec(0),
            pl.BlockSpec((1, 2, rows), lambda h, *_: (start + h, 0, 0)),
        ]
        + [pl.BlockSpec(memory_space=pl.ANY)] * len(earlier),
        outs=[spec(0), spec(0), spec(0), far_outs, far_outs],
        scratch=[pltpu.VMEM((IMG_PAD, rows), f32), pltpu.VMEM((rows, rows), f32)],
        aliases={first + at: at for at in range(len(earlier))},
    )


def gelu_pair(values):
    share = 0.5 * (1.0 + lax.erf(values * 0.7071067811865476))
    slope = share + values * jnp.exp(-0.5 * values * values) * 0.3989422804014327
    return values * share, slope


def feed_step(step, rows, item_rows, feed, top, result, gfeed, expand_ref, ebias_ref, reduce_ref):
    width = feed.shape[1]
    expand, reduce = expand_ref[...], reduce_ref[...]
    active_parts, gup_parts = [], []
    for start in range(0, rows, item_rows):
        here = slice(start, start + item_rows)
        upward = dot(feed[here, :], expand) + ebias_ref[...]
        gactive = dot(top[here, :], reduce, NT)
        active, slope = gelu_pair(upward)
        active = active.astype(bf16)
        gup = (gactive * slope).astype(bf16)
        result[here, :] += dot(active, reduce)
        gfeed[here, :] += dot(gup, expand, NT)
        active_parts.append(active)
        gup_parts.append(gup)
    active = jnp.concatenate(active_parts, axis=0)
    gup = jnp.concatenate(gup_parts, axis=0)
    greduce = dot(active, top[...], TN).astype(bf16)
    gexpand = dot(feed[...], gup, TN).astype(bf16)
    pieces = [greduce[:, at : at + LANES] for at in range(0, width, LANES)]
    pieces += [gexpand[:, at : at + LANES] for at in range(0, FF_BLOCK, LANES)]
    return pieces, column_sum(gup.astype(f32))


def store_pieces(out, pieces):
    at = 0
    for half in range(2):
        for piece in pieces:
            rows = piece.shape[0] // 2
            out[at : at + rows, :] = piece[half * rows : (half + 1) * rows]
            at += rows


def feed_kernel(
    flag_ref,
    count_ref,
    side_ref,
    att0_ref,
    att1_ref,
    project_ref,
    hid_ref,
    cot_ref,
    project_bias_ref,
    gain_ref,
    shift_ref,
    reduce_bias_ref,
    expand_ref,
    ebias_ref,
    reduce_ref,
    out_ref,
    gmid_ref,
    gatt_ref,
    gproject_ref,
    gvec_ref,
    keep0_ref,
    send0_ref,
    keep1_ref,
    send1_ref,
    middle,
    feed,
    top,
    result,
    gfeed,
    low_out,
    gatt,
    grads,
    grad_sems,
    row_sems,
    *,
    item_rows,
):
    step = pl.program_id(0)
    rows, width = hid_ref.shape
    block = 256
    att_refs = (att0_ref, att1_ref)
    half = grads.shape[1] // 2

    steps = grads.shape[0]

    def grad_copies(which):
        found = []
        chunk, place = divmod(which, steps // 2)
        outs = (keep1_ref, send1_ref) if chunk else (keep0_ref, send0_ref)
        for number, out in enumerate(outs):
            side = side_ref[0] if number == 0 else 1 - side_ref[0]
            here = grads.at[which, pl.ds(pl.multiple_of(side * half, half), half)]
            there = out.at[pl.ds(place * half, half)]
            found.append(pltpu.make_async_copy(here, there, grad_sems.at[which, number]))
        return found

    @pl.when(step == 0)
    def _():
        for start in range(0, rows, block):
            here = slice(start, start + block)
            inside = slice(start % item_rows, start % item_rows + block)
            att = att_refs[start // item_rows][inside, :]
            branch = dot(att, project_ref[...]) + project_bias_ref[...]
            x = hid_ref[here, :].astype(f32) + branch
            middle[here, :] = x
            unit, _ = normalise(x)
            feed[here, :] = (unit * gain_ref[...] + shift_ref[...]).astype(bf16)
            at = lax.broadcasted_iota(jnp.int32, (block, width), 0) + start % item_rows
            limit = jnp.where(flag_ref[0] == 1, item_rows, count_ref[start // item_rows])
            top[here, :] = jnp.where(at < limit, cot_ref[here, :].astype(f32), 0.0).astype(bf16)
            result[here, :] = x + reduce_bias_ref[...]
            gfeed[here, :] = jnp.zeros((block, width), f32)

    pieces, gvec_ref[pl.ds(4 + step, 1), :] = feed_step(
        step, rows, item_rows, feed, top, result, gfeed, expand_ref, ebias_ref, reduce_ref
    )
    store_pieces(grads.at[step], pieces)
    for which in range(steps):

        @pl.when(step == which)
        def _(which=which):
            for copy in grad_copies(which):
                copy.start()

    @pl.when(step == pl.num_programs(0) - 1)
    def _():
        copies = []
        sums = [jnp.zeros((1, width), f32)] * 4
        for number, start in enumerate(range(0, rows, block)):
            here = slice(start, start + block)
            low_out[here, :] = result[here, :].astype(bf16)
            unit, scale = normalise(middle[here, :])
            grad = gfeed[here, :]
            grad_top = top[here, :].astype(f32)
            gmid = grad_top + norm_transpose(unit, scale, gain_ref[...], grad)
            terms = (grad * unit, grad, grad_top, gmid)
            sums = [old + column_sum(new) for old, new in zip(sums, terms)]
            middle[here, :] = gmid
            gbranch = gmid.astype(bf16)
            feed[here, :] = gbranch
            gatt[here, :] = dot(gbranch, project_ref[...], NT).astype(bf16)
            for kind, (mine, there) in enumerate(
                ((low_out, out_ref), (middle, gmid_ref), (gatt, gatt_ref))
            ):
                span = pl.ds(start, block)
                copy = pltpu.make_async_copy(
                    mine.at[span, :], there.at[span, :], row_sems.at[kind, number]
                )
                copy.start()
                copies.append(copy)
        total = dot(att0_ref[...], feed[:item_rows, :], TN)
        total += dot(att1_ref[...], feed[item_rows:, :], TN)
        gproject_ref[...] = total.astype(bf16)
        gvec_ref[0:4, :] = jnp.concatenate(sums, axis=0)
        for copy in copies:
            copy.wait()
        for which in range(steps):
            for copy in grad_copies(which):
                copy.wait()


def feed_forward(order, flag, count, side, att0, att1, project, hidden, cotangent, vecs, expand, ebias, reduce):
    rows, width = hidden.shape
    item_rows = att0.shape[0]
    units = reduce.shape[0]
    steps = units // FF_BLOCK
    block_rows = 2 * width * FF_BLOCK // LANES
    fixed = (att0, att1, project, hidden, cotangent, *vecs)
    anywhere = pl.BlockSpec(memory_space=pl.ANY)
    return call(
        order,
        functools.partial(feed_kernel, item_rows=item_rows),
        (*fixed, expand, ebias, reduce),
        [
            shaped((rows, width), bf16),
            shaped((rows, width), f32),
            shaped((rows, width), bf16),
            shaped((width, width), bf16),
            shaped((4 + steps, width), f32),
        ]
        + [shaped((steps // 2 * block_rows // 2, LANES), bf16)] * 4,
        "feed_forward",
        cost(12 * rows * width * units, 40 << 20, 2 * rows * units),
        scalars=(flag, count, side),
        grid=(steps,),
        specs=[resident(value.shape) for value in fixed]
        + [
            pl.BlockSpec((width, FF_BLOCK), lambda j, *_: (0, j)),
            pl.BlockSpec((1, FF_BLOCK), lambda j, *_: (0, j)),
            pl.BlockSpec((FF_BLOCK, width), lambda j, *_: (j, 0)),
        ],
        outs=[
            anywhere,
            anywhere,
            anywhere,
            resident((width, width)),
            resident((4 + steps, width)),
        ]
        + [anywhere] * 4,
        scratch=[
            pltpu.VMEM((rows, width), f32),
            pltpu.VMEM((rows, width), bf16),
            pltpu.VMEM((rows, width), bf16),
            pltpu.VMEM((rows, width), f32),
            pltpu.VMEM((rows, width), f32),
            pltpu.VMEM((rows, width), bf16),
            pltpu.VMEM((rows, width), bf16),
            pltpu.VMEM((steps, block_rows, LANES), bf16),
            pltpu.SemaphoreType.DMA((steps, 2)),
            pltpu.SemaphoreType.DMA((3, rows // 256)),
        ],
    )


def weight_kernel(
    spare,
    side_ref,
    normed_ref,
    image_ref,
    gq_ref,
    gk_ref,
    gv_ref,
    gik_ref,
    giv_ref,
    *refs,
):
    extra_ref = None if spare else refs[0]
    sums_ref, keep_ref, send_ref, keep, send, sems = refs[-6:]
    step = pl.program_id(0)
    width = normed_ref.shape[1]
    half = width // 2
    columns = gq_ref.shape[1] // LANES
    block = half * (columns if spare else columns + 1)

    def copies(part):
        span = pl.ds(part * block, block if part < 3 else spare)
        pairs = ((keep, keep_ref), (send, send_ref))
        return [
            pltpu.make_async_copy(here.at[span], there.at[span], sems.at[number, part])
            for number, (here, there) in enumerate(pairs)
        ]

    def store(part, total):
        if extra_ref is not None:
            more = extra_ref[:, part * LANES : (part + 1) * LANES].astype(f32)
            total = jnp.concatenate([total, more], axis=1)
        first = side_ref[0] == 0
        mine = jnp.where(first, total[:half], total[half:]).astype(bf16)
        other = jnp.where(first, total[half:], total[:half]).astype(bf16)
        for number in range(block // half):
            rows = slice(part * block + number * half, part * block + (number + 1) * half)
            cols = slice(number * LANES, (number + 1) * LANES)
            keep[rows, :] = mine[:, cols]
            send[rows, :] = other[:, cols]
        for copy in copies(part):
            copy.start()

    @pl.when(step == 0)
    def _():
        store(0, dot(normed_ref[...], gq_ref[...], TN))
        sums_ref[0:1] = column_sum(gq_ref[...].astype(f32))

    @pl.when(step == 1)
    def _():
        total = dot(normed_ref[...], gk_ref[...], TN)
        store(1, total + dot(image_ref[...], gik_ref[...], TN))

    @pl.when(step == 2)
    def _():
        total = dot(normed_ref[...], gv_ref[...], TN)
        store(2, total + dot(image_ref[...], giv_ref[...], TN))
        sums = column_sum(gv_ref[...].astype(f32)) + column_sum(giv_ref[...].astype(f32))
        sums_ref[1:2] = sums
        if spare:
            keep[3 * block :, :] = jnp.zeros((spare, LANES), bf16)
            send[3 * block :, :] = jnp.zeros((spare, LANES), bf16)
            for copy in copies(3):
                copy.start()
        for part in range(4 if spare else 3):
            for copy in copies(part):
                copy.wait()


def weight_grads(order, side, normed, image, grads, lanes, place, spare, extra):
    rows, width = normed.shape
    half_rows = 3 * (lanes // LANES + len(extra)) * width // 2 + spare
    column = lambda height: pl.BlockSpec((height, lanes), lambda *_: (0, place))
    anywhere = pl.BlockSpec(memory_space=pl.ANY)
    return call(
        order,
        functools.partial(weight_kernel, spare),
        (normed, image, *grads, *extra),
        [shaped((2, lanes), f32)] + [shaped((half_rows, LANES), bf16)] * 2,
        "weight_grads",
        cost(8 * rows * width * lanes, 12 << 20),
        scalars=(side,),
        grid=(3,),
        specs=[resident(normed.shape), resident(image.shape)]
        + [column(value.shape[0]) for value in grads]
        + [resident(value.shape) for value in extra],
        outs=[resident((2, lanes)), anywhere, anywhere],
        scratch=[pltpu.VMEM((half_rows, LANES), bf16)] * 2 + [pltpu.SemaphoreType.DMA((2, 4))],
    )


def image_grad_kernel(keys_weight, values_weight, keys_ref, values_ref, out_ref):
    total = dot(keys_ref[...], keys_weight[...], NT) + dot(values_ref[...], values_weight[...], NT)
    out_ref[...] = total.astype(bf16)


def image_grads(order, weight, keys, values):
    rows, width = keys.shape
    part = lambda base: pl.BlockSpec((width, width), lambda *_: (0, base))
    return call(
        order,
        image_grad_kernel,
        (weight, weight, keys, values),
        [shaped((rows, width), bf16)],
        "image_grads",
        cost(4 * rows * width * width, 6 << 20),
        grid=(1,),
        specs=[part(1), part(2), resident(keys.shape), resident(values.shape)],
        outs=[resident((rows, width))],
    )


def finish_kernel(
    flag_ref,
    hid_ref,
    gmid_ref,
    near_ref,
    far_ref,
    gq_ref,
    gk_ref,
    gv_ref,
    gain_ref,
    weight_ref,
    feed_sums_ref,
    first_sums_ref,
    last_sums_ref,
    _,
    out_ref,
    small_ref,
    sums,
):
    item, block = pl.program_id(0), pl.program_id(1)
    joined = jnp.concatenate([gq_ref[...], gk_ref[...], gv_ref[...]], axis=1)
    grad = dot(joined, weight_ref[...], NT)
    unit, scale = normalise(hid_ref[...].astype(f32))
    both = near_ref[...].astype(f32) + far_ref[...].astype(f32)
    grad = grad + jnp.where((flag_ref[0] == 0) & (block == 0), both, 0.0)
    total = gmid_ref[...] + norm_transpose(unit, scale, gain_ref[...], grad)
    out_ref[...] = total.astype(bf16)
    found = jnp.concatenate([column_sum(grad * unit), column_sum(grad)], axis=0)

    @pl.when((item == 0) & (block == 0))
    def _():
        sums[...] = jnp.zeros(sums.shape, f32)

    sums[0:2] += found

    @pl.when((item == pl.num_programs(0) - 1) & (block == pl.num_programs(1) - 1))
    def _():
        width = sums.shape[1]
        pad = lambda count: jnp.zeros((count, width), f32)
        own = [sums[0:2], feed_sums_ref[0:3], feed_sums_ref[4:8], pad(7)]
        own = jnp.concatenate(own, axis=0)
        bias_sums = jnp.concatenate([first_sums_ref[...], last_sums_ref[...]], axis=1)
        shared = [pad(9), feed_sums_ref[3:4], bias_sums, pad(4)]
        shared = jnp.concatenate(shared, axis=0)
        is_text = flag_ref[0] == 1
        first = jnp.where(is_text, 0.0, own) + shared
        rows = jnp.concatenate([first, jnp.where(is_text, own, 0.0)], axis=0).astype(bf16)
        count = rows.shape[0]
        for number in range(width // LANES):
            cols = slice(number * LANES, (number + 1) * LANES)
            small_ref[number * count : (number + 1) * count, :] = rows[:, cols]
        small_ref[width // LANES * count :, :] = jnp.zeros((SMALL - width // LANES * count, LANES), bf16)


def finish_rows(
    order, flag, hidden, gmid, near, far, grads, gain, weight, feed_sums, bias_sums, keep, item_rows
):
    rows, width = hidden.shape
    blocks = item_rows // IMG_PAD
    mine = pl.BlockSpec((IMG_PAD, width), lambda i, j, *_: (i * blocks + j, 0))
    image = pl.BlockSpec((IMG_PAD, width), lambda i, j, *_: (i, 0))
    fixed = (gain, weight, feed_sums, *bias_sums)
    place = keep.shape[0] // SMALL - 1
    return call(
        order,
        finish_kernel,
        (hidden, gmid, near, far, *grads, *fixed, keep),
        [shaped((rows, width), bf16), shaped(keep.shape, bf16)],
        "finish_rows",
        cost(60 * rows * width * width, 160 << 20),
        scalars=(flag,),
        grid=(rows // item_rows, blocks),
        specs=[mine, mine, image, image, mine, mine, mine]
        + [resident(value.shape) for value in fixed]
        + [pl.BlockSpec(memory_space=pl.ANY)],
        outs=[mine, pl.BlockSpec((SMALL, LANES), lambda *_: (place, 0))],
        scratch=[pltpu.VMEM((8, width), f32)],
        aliases={13: 1},
    )


def expert_kernel(half_ref, value_ref, *refs):
    at = 0
    for out in refs[-2:]:
        tall = out.shape[0]
        for part in range(out.shape[1] // LANES):
            piece = value_ref[at : at + tall, :]
            out[:, part * LANES : (part + 1) * LANES] = piece.astype(f32)
            at += tall


def expert_outputs(order, half, first, value, width, units, earlier):
    tall = width // 2
    block_rows = 2 * width // LANES * tall
    return call(
        order,
        expert_kernel,
        (value, *earlier),
        [shaped((units, width), f32), shaped((width, units), f32)],
        "expert_outputs",
        cost(value.size, 6 * value.size),
        scalars=(half,),
        grid=(value.shape[0] // block_rows,),
        specs=[pl.BlockSpec((block_rows, LANES), lambda i, at: (i, 0))]
        + [pl.BlockSpec(memory_space=pl.ANY)] * len(earlier),
        outs=[
            pl.BlockSpec((tall, width), lambda i, at: (2 * (first + i) + at[0], 0)),
            pl.BlockSpec((tall, width), lambda i, at: (at[0], first + i)),
        ],
        aliases={2: 0, 3: 1} if earlier else None,
    )


def store_projection(first_ref, last_ref, in_ref, out_ref):
    tall = in_ref.shape[0]
    count = first_ref.shape[0] // tall
    for part in range(count - 1):
        piece = first_ref[part * tall : (part + 1) * tall, :]
        in_ref[:, part * LANES : (part + 1) * LANES] = piece.astype(f32)
    in_ref[:, (count - 1) * LANES :] = last_ref[...].astype(f32)
    out_ref[...] = first_ref[(count - 1) * tall :, :].astype(f32)


def projection_kernel(half_ref, first_ref, last_ref, in_ref, out_ref):
    store_projection(first_ref, last_ref, in_ref, out_ref)


def last_kernel(half_ref, flag_ref, first_ref, last_ref, mine_ref, got_ref, *refs):
    in_ref, out_ref, *vec_refs, expand_ref, pair_ref, project_ref = refs[2:]
    store_projection(first_ref, last_ref, in_ref, out_ref)

    @pl.when(pl.program_id(0) == 0)
    def _():
        both = mine_ref[...].astype(f32) + got_ref[...].astype(f32)
        width = vec_refs[0].shape[1]
        rows = jnp.concatenate([both[at * 32 : (at + 1) * 32] for at in range(width // LANES)], axis=1)
        own = jnp.where(flag_ref[0] == 1, rows[16:], rows[:16])
        for number, ref in enumerate(vec_refs):
            ref[...] = own[number : number + 1]
        for number in range(expand_ref.shape[1] // width):
            cols = slice(number * width, (number + 1) * width)
            expand_ref[:, cols] = own[5 + number : 6 + number]
        project_ref[...] = rows[9:10]
        pair_ref[...] = rows[10:12]


def projection_specs(width):
    tall = width // 2
    ins = [
        pl.BlockSpec((tall * width // LANES, LANES), lambda b, *_: (b, 0)),
        pl.BlockSpec((tall, LANES), lambda b, *_: (b, 0)),
    ]
    outs = [
        pl.BlockSpec((tall, width), lambda b, at, *_: (at[0], b)),
        pl.BlockSpec((tall, LANES), lambda b, at, *_: (at[0], b)),
    ]
    return ins, outs, [shaped((width, 3 * width), f32), shaped((width, width), f32)]


def projection_outputs(order, half, first, last, width):
    ins, outs, shapes = projection_specs(width)
    return call(
        order,
        projection_kernel,
        (first, last),
        shapes,
        "projection_outputs",
        cost(first.size, 6 * first.size),
        scalars=(half,),
        grid=(3,),
        specs=ins,
        outs=outs,
    )


def last_outputs(order, half, flag, first, mine, got, width, units, earlier):
    ins, outs, shapes = projection_specs(width)
    place = got.shape[0] // SMALL - 1
    small = pl.BlockSpec((SMALL, LANES), lambda *_: (place, 0))
    vecs = [(1, width)] * 5 + [(1, units), (2, width), (1, width)]
    return call(
        order,
        last_kernel,
        (first, got, mine, got, *earlier),
        shapes + [shaped(shape, f32) for shape in vecs],
        "last_outputs",
        cost(got.size, 6 * got.size),
        scalars=(half, flag),
        grid=(3,),
        specs=ins + [small, small] + [pl.BlockSpec(memory_space=pl.ANY)] * 2,
        outs=outs + [resident(shape) for shape in vecs],
        aliases={6: 0, 7: 1},
    )


def swap(value, axes, pair_of):
    count = 1
    for axis in axes:
        count *= lax.axis_size(axis)
    return lax.ppermute(value, axes, [(source, pair_of(source)) for source in range(count)])


def place_of(axes):
    place = 0
    for axis in axes:
        place = place * lax.axis_size(axis) + lax.axis_index(axis)
    return place


def stage_bits(axes):
    count = 1
    for axis in axes:
        count *= lax.axis_size(axis)
    bits = count.bit_length() - 1
    core = len(axes) - 1
    others = [bit for bit in range(bits) if bit != core]
    if len(axes) == 1 and len(others) == 3:
        return [(core, core), (1, 2), (3, 1), (2, 3)]
    if len(axes) == 2 and len(others) == 4:
        return [(core, core), (0, 2), (2, 0), (3, 3), (4, 4)]
    return [(core, core)] + list(zip(others, others[1:] + others[:1]))


class Total:
    def __init__(self, order, axes, keep, send):
        self.order = order
        self.axes = axes
        self.core = len(axes) - 1
        self.left = stage_bits(axes)
        place = place_of(axes)
        second = ((place >> self.core) & 1) == 1
        sides = [(place >> jnp.where(second, pair[1], pair[0])) & 1 for pair in self.left]
        self.sides = dict(zip(self.left, sides))
        self.back = list(self.left)
        self.terms = (keep, self.exchange(send, self.left.pop(0)))
        self.mine = None

    def exchange(self, value, pair):
        other = lambda source: source ^ (1 << pair[(source >> self.core) & 1])
        self.got = swap(value, self.axes, other)
        return self.got

    def part(self, which, half):
        cut = lambda term: lax.dynamic_slice_in_dim(term, which * half, half, 0).astype(f32)
        return (cut(self.terms[0]) + cut(self.terms[1])).astype(bf16)

    def step(self):
        if self.left:
            pair = self.left.pop(0)
            self.terms = self.order.after(*self.terms)
            half = self.terms[0].shape[0] // 2
            side = self.sides[pair]
            sent = self.part(1 - side, half)
            self.terms = (self.part(side, half), self.exchange(sent, pair))
            self.order.last = sent
            return
        pair = self.back.pop()
        if self.mine is None:
            self.terms = self.order.after(*self.terms)
            self.mine = (self.terms[0].astype(f32) + self.terms[1].astype(f32)).astype(bf16)
        else:
            mine, got = self.order.after(self.mine, self.got)
            low = jnp.where(self.last == 0, mine, got)
            high = jnp.where(self.last == 0, got, mine)
            self.mine = jnp.concatenate([low, high], axis=0)
        self.order.last = self.mine
        self.last = self.sides[pair]
        self.exchange(self.mine, pair)


def on_device(
    hidden_in,
    image_count,
    text_lengths,
    attend_gain,
    attend_shift,
    project_in,
    bias_pair,
    project_out,
    project_bias,
    feed_gain,
    feed_shift,
    expand_weight,
    expand_bias,
    reduce_weight,
    reduce_bias,
    cotangent,
):
    items, _, rows, width = hidden_in.shape
    units = expand_weight.shape[2]
    is_text = lax.axis_index("mod") == 1
    flag = is_text.astype(jnp.int32)[None]
    hidden = hidden_in.reshape(items * rows, width)
    to_text = lambda value: lax.ppermute(value, "mod", [(0, 1)])
    to_image = lambda value: lax.ppermute(value, "mod", [(1, 0)])

    far_rows = [to_text(hidden_in[item, 0, :IMG_PAD]) for item in range(items)]
    far_vecs = to_text(jnp.concatenate([attend_gain, attend_shift], axis=0))
    order = Order()
    normed, projected = project_rows(
        order, hidden, attend_gain, attend_shift, project_in, bias_pair
    )
    scalars = (flag, image_count, text_lengths)
    images, attended, lses = (), [], []
    for item in range(items):
        images = image_rows(
            order,
            flag,
            item,
            hidden,
            far_rows[item],
            attend_gain,
            attend_shift,
            far_vecs,
            project_in,
            bias_pair,
            rows,
            items,
            images,
        )
        out, lse = attend_forward(order, scalars, item, projected, images[1])
        attended.append(out)
        lses.append(lse)

    side = (lax.axis_index("dp") & 1)[None]
    (
        hidden_out,
        grad_middle,
        grad_attended,
        project_out_grad,
        feed_sums,
        keep0,
        send0,
        keep1,
        send1,
    ) = feed_forward(
        order,
        flag,
        image_count,
        side,
        attended[0],
        attended[1],
        project_out,
        hidden,
        cotangent.reshape(items * rows, width),
        (project_bias[None], feed_gain, feed_shift, reduce_bias),
        expand_weight[0],
        expand_bias,
        reduce_weight[0],
    )
    a = Total(order, ("dp",), keep0, send0)
    c = Total(order, ("dp",), keep1, send1)
    grads = ()

    def backward(item, start, pairs):
        return attend_backward(
            order,
            scalars,
            item,
            start,
            pairs,
            projected,
            images[1],
            attended[item],
            grad_attended,
            lses[item],
            grads,
        )

    def weights(lanes, place, spare, *extra):
        return weight_grads(
            order, side, normed, images[0], grads, lanes, place, spare, extra
        )

    def unpack(half, first, value, earlier=()):
        return expert_outputs(order, half, first, value, width, units, earlier)

    grads = backward(0, 0, 2)
    a.step()
    grads = backward(1, 0, 2)
    c.step()
    grads = backward(0, 2, 2)
    a.step()
    grads = backward(1, 2, 2)
    c.step()
    first_sums, keep, send = weights(2 * LANES, 0, 0, project_out_grad)
    s = Total(order, ("dp", "mod"), keep, send)
    a.step()
    grads = backward(0, 4, 2)
    s.step()
    a.step()
    grads = backward(1, 4, 2)
    c.step()
    s.step()
    near = image_grads(order, project_in, grads[3], grads[4])
    far = to_image(near)
    c.step()
    a.step()
    last_sums, keep, send = weights(LANES, 2, SMALL)
    p = Total(order, ("dp", "mod"), keep, send)
    s.step()
    c.step()
    a.step()
    (far,) = order.after(far)
    order.last = far
    grad_in, keep = finish_rows(
        order,
        flag,
        hidden,
        grad_middle,
        near,
        far,
        grads[:3],
        attend_gain,
        project_in,
        feed_sums,
        (first_sums, last_sums),
        keep,
        rows,
    )
    p.terms = (keep, p.got)
    p.step()
    s.step()
    a.step()
    p.step()
    c.step()
    p.step()
    s.step()
    outputs = unpack(side, 0, a.mine)
    p.step()
    s.step()
    p.step()
    outputs = unpack(1 - side, 0, a.got, outputs)
    p.step()
    s.step()
    c.step()
    p.step()
    s.step()
    outputs = unpack(side, 2, c.mine, outputs)
    p.step()
    s.step()
    reduce_grad, expand_grad = unpack(1 - side, 2, c.got, outputs)
    while p.back:
        p.step()
    projections = projection_outputs(order, side, s.mine, p.mine, width)
    (
        project_in_grad,
        project_out_grad,
        attend_gain_grad,
        attend_shift_grad,
        feed_gain_grad,
        feed_shift_grad,
        reduce_bias_grad,
        expand_bias_grad,
        bias_pair_grad,
        project_bias_grad,
    ) = last_outputs(order, 1 - side, flag, s.got, p.mine, p.got, width, units, projections)
    return (
        hidden_out.reshape(hidden_in.shape),
        grad_in.reshape(hidden_in.shape),
        attend_gain_grad,
        attend_shift_grad,
        project_in_grad,
        bias_pair_grad,
        project_out_grad,
        project_bias_grad[0],
        feed_gain_grad,
        feed_shift_grad,
        expand_grad[None],
        expand_bias_grad,
        reduce_grad[None],
        reduce_bias_grad,
    )


def solution(mesh):
    in_specs = (
        P("dp", "mod", None, None),
        P("dp"),
        P("dp", None),
        P("mod", None),
        P("mod", None),
        P(),
        P(),
        P(),
        P(),
        P("mod", None),
        P("mod", None),
        P("mod", None, None),
        P("mod", None),
        P("mod", None, None),
        P("mod", None),
        P("dp", "mod", None, None),
    )
    out_specs = (
        P("dp", "mod", None, None),
        P("dp", "mod", None, None),
        P("mod", None),
        P("mod", None),
        P(),
        P(),
        P(),
        P(),
        P("mod", None),
        P("mod", None),
        P("mod", None, None),
        P("mod", None),
        P("mod", None, None),
        P("mod", None),
    )
    return jax.shard_map(
        on_device, mesh=mesh, in_specs=in_specs, out_specs=out_specs, check_vma=False
    )
```

```python
import functools

import jax
import jax.numpy as jnp
from jax import lax
from jax.experimental import pallas as pl
from jax.experimental.pallas import tpu as pltpu
from jax.sharding import PartitionSpec as P

HEADS = 12
HEAD = 64
IMG_PAD = 256
PAIR = 2 * HEAD
PAIRS = HEADS // 2
GROUP_PAIRS = 2
GROUPS = PAIRS // GROUP_PAIRS
LANES = GROUP_PAIRS * PAIR
SMALL = 128
FF_BLOCK = 768

masked_value = -1e30
norm_eps = 1e-05

bf16 = jnp.bfloat16
f32 = jnp.float32

NN = (((1,), (0,)), ((), ()))
NT = (((1,), (1,)), ((), ()))
TN = (((0,), (0,)), ((), ()))
VMEM_BYTES = 56 << 20


def dot(left, right, dims=NN):
    return lax.dot_general(left, right, dims, preferred_element_type=f32)


def column_sum(values):
    return jnp.sum(values, axis=0, keepdims=True)


def row_mean(values):
    return jnp.mean(values, axis=1, keepdims=True)


def normalise(values):
    centred = values - row_mean(values)
    scale = lax.rsqrt(row_mean(centred * centred) + norm_eps)
    return centred * scale, scale


def norm_transpose(unit, scale, gain, grad):
    grad_unit = grad * gain
    return scale * (grad_unit - row_mean(grad_unit) - unit * row_mean(grad_unit * unit))


def cost(flops, moved, special=0):
    return pl.CostEstimate(flops=flops, bytes_accessed=moved, transcendentals=special)


def weighed(estimate):
    return pl.CostEstimate(
        flops=10 * estimate.flops,
        bytes_accessed=10 * estimate.bytes_accessed,
        transcendentals=10 * estimate.transcendentals,
    )


class Order:
    def __init__(self):
        self.last = None

    def after(self, *values):
        if self.last is None:
            return values
        *values, _ = lax.optimization_barrier((*values, self.last))
        return values


def call(order, kernel, inputs, out_shape, name, estimate, scalars=(), grid=(), specs=None, outs=None,
         scratch=(), aliases=None):
    inputs = (*order.after(inputs[0]), *inputs[1:])
    vmem = pl.BlockSpec(memory_space=pltpu.VMEM)
    found = pl.pallas_call(
        kernel,
        grid_spec=pltpu.PrefetchScalarGridSpec(
            num_scalar_prefetch=len(scalars),
            grid=grid,
            in_specs=[vmem] * len(inputs) if specs is None else list(specs),
            out_specs=[vmem] * len(out_shape) if outs is None else list(outs),
            scratch_shapes=list(scratch),
        ),
        out_shape=list(out_shape),
        input_output_aliases=aliases or {},
        compiler_params=pltpu.CompilerParams(vmem_limit_bytes=VMEM_BYTES),
        cost_estimate=estimate,
        name=name,
    )(*scalars, *inputs)
    order.last = found[-1]
    return found if len(found) > 1 else found[0]


def shaped(shape, dtype):
    return jax.ShapeDtypeStruct(shape, dtype)


def resident(shape):
    return pl.BlockSpec(shape, lambda *_: (0,) * len(shape), pipeline_mode=pl.Buffered(1))


def project_kernel(hid_ref, gain_ref, shift_ref, weight_ref, bias_ref, normed_ref, out_ref):
    unit, _ = normalise(hid_ref[...].astype(f32))
    normed = (unit * gain_ref[...] + shift_ref[...]).astype(bf16)
    normed_ref[...] = normed
    width = normed.shape[1]
    for part in range(3):
        cols = slice(part * width, (part + 1) * width)
        rows = dot(normed, weight_ref[:, cols])
        if part == 0:
            rows = (rows + bias_ref[0:1]).astype(bf16) * jnp.asarray(HEAD**-0.5, bf16)
        if part == 2:
            rows = rows + bias_ref[1:2]
        out_ref[:, cols] = rows.astype(bf16)


def project_rows(order, hidden, gain, shift, weight, bias):
    rows, width = hidden.shape
    block = 256
    blocked = lambda cols: pl.BlockSpec((block, cols), lambda r: (r, 0))
    inputs = (hidden, gain, shift, weight, bias)
    return call(
        order,
        project_kernel,
        inputs,
        [shaped((rows, width), bf16), shaped((rows, 3 * width), bf16)],
        "project_rows",
        cost(6 * rows * width * width, 10 * rows * width + 6 * width * width),
        grid=(rows // block,),
        specs=[blocked(width)] + [resident(value.shape) for value in inputs[1:]],
        outs=[blocked(width), blocked(3 * width)],
    )


def image_kernel(
    flag_ref,
    own_ref,
    far_ref,
    gain_ref,
    shift_ref,
    vec_ref,
    keys_ref,
    values_ref,
    bias_ref,
    *refs,
):
    normed_ref, out_ref = refs[-2:]
    is_text = flag_ref[0] == 1
    hidden = jnp.where(is_text, far_ref[...].astype(f32), own_ref[...].astype(f32))
    gain = jnp.where(is_text, vec_ref[0:1], gain_ref[...])
    shift = jnp.where(is_text, vec_ref[1:2], shift_ref[...])
    unit, _ = normalise(hidden)
    normed = (unit * gain + shift).astype(bf16)
    normed_ref[...] = normed
    width = normed.shape[1]
    out_ref[:, :width] = dot(normed, keys_ref[...]).astype(bf16)
    out_ref[:, width:] = (dot(normed, values_ref[...]) + bias_ref[1:2]).astype(bf16)


def image_rows(
    order, flag, item, hidden, far, gain, shift, vecs, weight, bias, item_rows, items, earlier
):
    width = hidden.shape[1]
    place = item * (item_rows // IMG_PAD)
    half = lambda base: pl.BlockSpec((width, width), lambda *_: (0, base))
    mine = lambda cols: pl.BlockSpec((IMG_PAD, cols), lambda *_: (item, 0))
    inputs = (hidden, far, gain, shift, vecs, weight, weight, bias, *earlier)
    return call(
        order,
        image_kernel,
        inputs,
        [shaped((items * IMG_PAD, width), bf16), shaped((items * IMG_PAD, 2 * width), bf16)],
        "image_rows",
        cost(4 * IMG_PAD * width * width, 6 << 20),
        scalars=(flag,),
        grid=(1,),
        specs=[
            pl.BlockSpec((IMG_PAD, width), lambda *_: (place, 0)),
            resident(far.shape),
            resident(gain.shape),
            resident(shift.shape),
            resident(vecs.shape),
            half(1),
            half(2),
            resident(bias.shape),
        ]
        + [pl.BlockSpec(memory_space=pl.ANY)] * len(earlier),
        outs=[mine(width), mine(2 * width)],
        aliases={9: 0, 10: 1} if earlier else None,
    )


def segments(shape, axis, lengths_ref, item):
    places = lax.broadcasted_iota(jnp.int32, shape, axis)
    total = jnp.zeros(shape, jnp.int32)
    end = 0
    for which in range(lengths_ref.shape[1]):
        end = end + lengths_ref[item, which]
        total += (places >= end).astype(jnp.int32)
    return total


def own_bias(rows, flag_ref, lengths_ref, item):
    shape = (rows, rows)
    same = segments(shape, 0, lengths_ref, item) == segments(shape, 1, lengths_ref, item)
    return jnp.where(same & (flag_ref[0] == 1), 0.0, masked_value).astype(f32)


def image_bias(shape, axis, count_ref, item):
    places = lax.broadcasted_iota(jnp.int32, shape, axis)
    return jnp.where(places < count_ref[item], 0.0, masked_value).astype(f32)


def forward_kernel(
    item,
    flag_ref,
    count_ref,
    lengths_ref,
    q_ref,
    k_ref,
    v_ref,
    ik_ref,
    iv_ref,
    out_ref,
    lse_ref,
    image_part,
    own_part,
):
    rows = q_ref.shape[0]

    @pl.when(pl.program_id(0) == 0)
    def _():
        image_part[...] = image_bias(image_part.shape, 1, count_ref, item)
        own_part[...] = own_bias(rows, flag_ref, lengths_ref, item)

    first = lax.broadcasted_iota(jnp.int32, (rows, PAIR), 1) < HEAD
    zero = jnp.zeros((), bf16)
    q = q_ref[...]
    image_keys, image_values = ik_ref[...], iv_ref[...]
    keys, values = k_ref[...], v_ref[...]
    outs, tops = [], []
    for head in range(2):
        q_head = jnp.where(first, q, zero) if head == 0 else jnp.where(first, zero, q)
        far = dot(q_head, image_keys, NT) + image_part[...]
        own = dot(q_head, keys, NT) + own_part[...]
        top = jnp.maximum(
            jnp.max(far, axis=1, keepdims=True), jnp.max(own, axis=1, keepdims=True)
        )
        far = jnp.exp(far - top)
        own = jnp.exp(own - top)
        total = jnp.sum(far, axis=1, keepdims=True) + jnp.sum(own, axis=1, keepdims=True)
        summed = dot(far.astype(bf16), image_values) + dot(own.astype(bf16), values)
        outs.append(summed / total)
        tops.append(top + jnp.log(total))
    out_ref[...] = jnp.where(first, outs[0], outs[1]).astype(bf16)
    turned = jnp.transpose(jnp.where(first, tops[0], tops[1]))
    lse_ref[0, 0:1, :] = turned[0:1]
    lse_ref[0, 1:2, :] = turned[HEAD : HEAD + 1]


def attend_forward(order, scalars, item, projected, image):
    rows = projected.shape[0] // 2
    spec = lambda base: pl.BlockSpec((rows, PAIR), lambda h, *_: (item, base + h))
    far = lambda base: pl.BlockSpec((IMG_PAD, PAIR), lambda h, *_: (item, base + h))
    keys = rows + IMG_PAD
    return call(
        order,
        functools.partial(forward_kernel, item),
        (projected, projected, projected, image, image),
        [shaped((rows, HEADS * HEAD), bf16), shaped((PAIRS, 2, rows), f32)],
        "attend_forward",
        cost(16 * HEADS * rows * keys * HEAD, 6 << 20, HEADS * rows * keys),
        scalars=scalars,
        grid=(PAIRS,),
        specs=[spec(0), spec(PAIRS), spec(2 * PAIRS), far(0), far(PAIRS)],
        outs=[
            pl.BlockSpec((rows, PAIR), lambda h, *_: (0, h)),
            pl.BlockSpec((1, 2, rows), lambda h, *_: (h, 0, 0)),
        ],
        scratch=[pltpu.VMEM((rows, IMG_PAD), f32), pltpu.VMEM((rows, rows), f32)],
    )


def backward_kernel(
    item,
    flag_ref,
    count_ref,
    lengths_ref,
    q_ref,
    k_ref,
    v_ref,
    ik_ref,
    iv_ref,
    out_ref,
    grad_ref,
    lse_ref,
    *refs,
):
    gq_ref, gk_ref, gv_ref, gik_ref, giv_ref, image_part, own_part = refs[-7:]
    rows = q_ref.shape[0]

    @pl.when(pl.program_id(0) == 0)
    def _():
        image_part[...] = image_bias(image_part.shape, 0, count_ref, item)
        own_part[...] = own_bias(rows, flag_ref, lengths_ref, item)

    first = lax.broadcasted_iota(jnp.int32, (rows, PAIR), 1) < HEAD
    zero = jnp.zeros((), bf16)
    q, grad = q_ref[...], grad_ref[...]
    products = grad.astype(f32) * out_ref[...].astype(f32)
    head_lanes = lax.broadcasted_iota(jnp.int32, (8, PAIR), 1) // HEAD
    head_rows = lax.broadcasted_iota(jnp.int32, (8, PAIR), 0)
    center = lax.dot_general(
        (head_lanes == head_rows).astype(f32),
        products,
        NT,
        preferred_element_type=f32,
        precision=lax.Precision.HIGHEST,
    )
    q_heads = [jnp.where(first, q, zero), jnp.where(first, zero, q)]
    grad_heads = [jnp.where(first, grad, zero), jnp.where(first, zero, grad)]
    lse = lse_ref[0]
    grad_query = [None, None]
    half = rows // 2
    pieces = (
        (ik_ref, iv_ref, gik_ref, giv_ref, image_part, 0, IMG_PAD),
        (k_ref, v_ref, gk_ref, gv_ref, own_part, 0, half),
        (k_ref, v_ref, gk_ref, gv_ref, own_part, half, half),
    )
    for keys_ref, values_ref, gk_out, gv_out, bias, start, count in pieces:
        piece = slice(start, start + count)
        keys, values = keys_ref[piece, :], values_ref[piece, :]
        low_lanes = lax.broadcasted_iota(jnp.int32, (count, PAIR), 1) < HEAD
        grad_keys, grad_values = [], []
        for head in range(2):
            scores = dot(keys, q_heads[head], NT) + bias[piece, :]
            probs = jnp.exp(scores - lse[head : head + 1])
            grad_probs = dot(values, grad_heads[head], NT)
            grad_scores = (probs * (grad_probs - center[head : head + 1])).astype(bf16)
            grad_values.append(dot(probs.astype(bf16), grad))
            grad_keys.append(dot(grad_scores, q))
            term = dot(grad_scores, keys, TN)
            grad_query[head] = term if grad_query[head] is None else grad_query[head] + term
        gk_out[piece, :] = jnp.where(low_lanes, grad_keys[0], grad_keys[1]).astype(bf16)
        gv_out[piece, :] = jnp.where(low_lanes, grad_values[0], grad_values[1]).astype(bf16)
    gq_ref[...] = (jnp.where(first, grad_query[0], grad_query[1]) * HEAD**-0.5).astype(bf16)


def attend_backward(order, scalars, item, start, pairs, projected, image, attended, grad, lse, earlier):
    rows, width = attended.shape
    spec = lambda base: pl.BlockSpec((rows, PAIR), lambda h, *_: (item, base + start + h))
    far = lambda base: pl.BlockSpec((IMG_PAD, PAIR), lambda h, *_: (item, base + start + h))
    own = pl.BlockSpec((rows, PAIR), lambda h, *_: (0, start + h))
    far_outs = pl.BlockSpec((IMG_PAD, PAIR), lambda h, *_: (item, start + h))
    keys = rows + IMG_PAD
    inputs = (projected, projected, projected, image, image, attended, grad, lse)
    first = len(scalars) + len(inputs)
    return call(
        order,
        functools.partial(backward_kernel, item),
        (*inputs, *earlier),
        [shaped((2 * rows, width), bf16)] * 3 + [shaped((2 * IMG_PAD, width), bf16)] * 2,
        "attend_backward",
        weighed(cost(80 * pairs * rows * keys * HEAD, pairs * 2 << 20, 2 * pairs * rows * keys)),
        scalars=scalars,
        grid=(pairs,),
        specs=[
            spec(0),
            spec(PAIRS),
            spec(2 * PAIRS),
            far(0),
            far(PAIRS),
            own,
            spec(0),
            pl.BlockSpec((1, 2, rows), lambda h, *_: (start + h, 0, 0)),
        ]
        + [pl.BlockSpec(memory_space=pl.ANY)] * len(earlier),
        outs=[spec(0), spec(0), spec(0), far_outs, far_outs],
        scratch=[pltpu.VMEM((IMG_PAD, rows), f32), pltpu.VMEM((rows, rows), f32)],
        aliases={first + at: at for at in range(len(earlier))},
    )


def gelu_pair(values):
    share = 0.5 * (1.0 + lax.erf(values * 0.7071067811865476))
    slope = share + values * jnp.exp(-0.5 * values * values) * 0.3989422804014327
    return values * share, slope


def feed_step(step, rows, item_rows, feed, top, result, gfeed, expand_ref, ebias_ref, reduce_ref):
    width = feed.shape[1]
    expand, reduce = expand_ref[...], reduce_ref[...]
    active_parts, gup_parts = [], []
    for start in range(0, rows, item_rows):
        here = slice(start, start + item_rows)
        upward = dot(feed[here, :], expand) + ebias_ref[...]
        gactive = dot(top[here, :], reduce, NT)
        active, slope = gelu_pair(upward)
        active = active.astype(bf16)
        gup = (gactive * slope).astype(bf16)
        result[here, :] += dot(active, reduce)
        gfeed[here, :] += dot(gup, expand, NT)
        active_parts.append(active)
        gup_parts.append(gup)
    active = jnp.concatenate(active_parts, axis=0)
    gup = jnp.concatenate(gup_parts, axis=0)
    greduce = dot(active, top[...], TN).astype(bf16)
    gexpand = dot(feed[...], gup, TN).astype(bf16)
    pieces = [greduce[:, at : at + LANES] for at in range(0, width, LANES)]
    pieces += [gexpand[:, at : at + LANES] for at in range(0, FF_BLOCK, LANES)]
    return pieces, column_sum(gup.astype(f32))


def store_pieces(out, pieces):
    at = 0
    for half in range(2):
        for piece in pieces:
            rows = piece.shape[0] // 2
            out[at : at + rows, :] = piece[half * rows : (half + 1) * rows]
            at += rows


def feed_kernel(
    flag_ref,
    count_ref,
    side_ref,
    att0_ref,
    att1_ref,
    project_ref,
    hid_ref,
    cot_ref,
    project_bias_ref,
    gain_ref,
    shift_ref,
    reduce_bias_ref,
    expand_ref,
    ebias_ref,
    reduce_ref,
    out_ref,
    gmid_ref,
    gatt_ref,
    gproject_ref,
    gvec_ref,
    keep0_ref,
    send0_ref,
    keep1_ref,
    send1_ref,
    middle,
    feed,
    top,
    result,
    gfeed,
    low_out,
    gatt,
    grads,
    grad_sems,
    row_sems,
    *,
    item_rows,
):
    step = pl.program_id(0)
    rows, width = hid_ref.shape
    block = 256
    att_refs = (att0_ref, att1_ref)
    half = grads.shape[1] // 2

    steps = grads.shape[0]

    def grad_copies(which):
        found = []
        chunk, place = divmod(which, steps // 2)
        outs = (keep1_ref, send1_ref) if chunk else (keep0_ref, send0_ref)
        for number, out in enumerate(outs):
            side = side_ref[0] if number == 0 else 1 - side_ref[0]
            here = grads.at[which, pl.ds(pl.multiple_of(side * half, half), half)]
            there = out.at[pl.ds(place * half, half)]
            found.append(pltpu.make_async_copy(here, there, grad_sems.at[which, number]))
        return found

    @pl.when(step == 0)
    def _():
        for start in range(0, rows, block):
            here = slice(start, start + block)
            inside = slice(start % item_rows, start % item_rows + block)
            att = att_refs[start // item_rows][inside, :]
            branch = dot(att, project_ref[...]) + project_bias_ref[...]
            x = hid_ref[here, :].astype(f32) + branch
            middle[here, :] = x
            unit, _ = normalise(x)
            feed[here, :] = (unit * gain_ref[...] + shift_ref[...]).astype(bf16)
            at = lax.broadcasted_iota(jnp.int32, (block, width), 0) + start % item_rows
            limit = jnp.where(flag_ref[0] == 1, item_rows, count_ref[start // item_rows])
            top[here, :] = jnp.where(at < limit, cot_ref[here, :].astype(f32), 0.0).astype(bf16)
            result[here, :] = x + reduce_bias_ref[...]
            gfeed[here, :] = jnp.zeros((block, width), f32)

    pieces, gvec_ref[pl.ds(4 + step, 1), :] = feed_step(
        step, rows, item_rows, feed, top, result, gfeed, expand_ref, ebias_ref, reduce_ref
    )
    store_pieces(grads.at[step], pieces)
    for which in range(steps):

        @pl.when(step == which)
        def _(which=which):
            for copy in grad_copies(which):
                copy.start()

    @pl.when(step == pl.num_programs(0) - 1)
    def _():
        copies = []
        sums = [jnp.zeros((1, width), f32)] * 4
        for number, start in enumerate(range(0, rows, block)):
            here = slice(start, start + block)
            low_out[here, :] = result[here, :].astype(bf16)
            unit, scale = normalise(middle[here, :])
            grad = gfeed[here, :]
            grad_top = top[here, :].astype(f32)
            gmid = grad_top + norm_transpose(unit, scale, gain_ref[...], grad)
            terms = (grad * unit, grad, grad_top, gmid)
            sums = [old + column_sum(new) for old, new in zip(sums, terms)]
            middle[here, :] = gmid
            gbranch = gmid.astype(bf16)
            feed[here, :] = gbranch
            gatt[here, :] = dot(gbranch, project_ref[...], NT).astype(bf16)
            for kind, (mine, there) in enumerate(
                ((low_out, out_ref), (middle, gmid_ref), (gatt, gatt_ref))
            ):
                span = pl.ds(start, block)
                copy = pltpu.make_async_copy(
                    mine.at[span, :], there.at[span, :], row_sems.at[kind, number]
                )
                copy.start()
                copies.append(copy)
        total = dot(att0_ref[...], feed[:item_rows, :], TN)
        total += dot(att1_ref[...], feed[item_rows:, :], TN)
        gproject_ref[...] = total.astype(bf16)
        gvec_ref[0:4, :] = jnp.concatenate(sums, axis=0)
        for copy in copies:
            copy.wait()
        for which in range(steps):
            for copy in grad_copies(which):
                copy.wait()


def feed_forward(order, flag, count, side, att0, att1, project, hidden, cotangent, vecs, expand, ebias, reduce):
    rows, width = hidden.shape
    item_rows = att0.shape[0]
    units = reduce.shape[0]
    steps = units // FF_BLOCK
    block_rows = 2 * width * FF_BLOCK // LANES
    fixed = (att0, att1, project, hidden, cotangent, *vecs)
    anywhere = pl.BlockSpec(memory_space=pl.ANY)
    return call(
        order,
        functools.partial(feed_kernel, item_rows=item_rows),
        (*fixed, expand, ebias, reduce),
        [
            shaped((rows, width), bf16),
            shaped((rows, width), f32),
            shaped((rows, width), bf16),
            shaped((width, width), bf16),
            shaped((4 + steps, width), f32),
        ]
        + [shaped((steps // 2 * block_rows // 2, LANES), bf16)] * 4,
        "feed_forward",
        cost(12 * rows * width * units, 40 << 20, 2 * rows * units),
        scalars=(flag, count, side),
        grid=(steps,),
        specs=[resident(value.shape) for value in fixed]
        + [
            pl.BlockSpec((width, FF_BLOCK), lambda j, *_: (0, j)),
            pl.BlockSpec((1, FF_BLOCK), lambda j, *_: (0, j)),
            pl.BlockSpec((FF_BLOCK, width), lambda j, *_: (j, 0)),
        ],
        outs=[
            anywhere,
            anywhere,
            anywhere,
            resident((width, width)),
            resident((4 + steps, width)),
        ]
        + [anywhere] * 4,
        scratch=[
            pltpu.VMEM((rows, width), f32),
            pltpu.VMEM((rows, width), bf16),
            pltpu.VMEM((rows, width), bf16),
            pltpu.VMEM((rows, width), f32),
            pltpu.VMEM((rows, width), f32),
            pltpu.VMEM((rows, width), bf16),
            pltpu.VMEM((rows, width), bf16),
            pltpu.VMEM((steps, block_rows, LANES), bf16),
            pltpu.SemaphoreType.DMA((steps, 2)),
            pltpu.SemaphoreType.DMA((3, rows // 256)),
        ],
    )


def weight_kernel(
    spare,
    side_ref,
    normed_ref,
    image_ref,
    gq_ref,
    gk_ref,
    gv_ref,
    gik_ref,
    giv_ref,
    *refs,
):
    extra_ref = None if spare else refs[0]
    sums_ref, keep_ref, send_ref, keep, send, sems = refs[-6:]
    step = pl.program_id(0)
    width = normed_ref.shape[1]
    half = width // 2
    columns = gq_ref.shape[1] // LANES
    block = half * (columns if spare else columns + 1)

    def copies(part):
        span = pl.ds(part * block, block if part < 3 else spare)
        pairs = ((keep, keep_ref), (send, send_ref))
        return [
            pltpu.make_async_copy(here.at[span], there.at[span], sems.at[number, part])
            for number, (here, there) in enumerate(pairs)
        ]

    def store(part, total):
        if extra_ref is not None:
            more = extra_ref[:, part * LANES : (part + 1) * LANES].astype(f32)
            total = jnp.concatenate([total, more], axis=1)
        first = side_ref[0] == 0
        mine = jnp.where(first, total[:half], total[half:]).astype(bf16)
        other = jnp.where(first, total[half:], total[:half]).astype(bf16)
        for number in range(block // half):
            rows = slice(part * block + number * half, part * block + (number + 1) * half)
            cols = slice(number * LANES, (number + 1) * LANES)
            keep[rows, :] = mine[:, cols]
            send[rows, :] = other[:, cols]
        for copy in copies(part):
            copy.start()

    @pl.when(step == 0)
    def _():
        store(0, dot(normed_ref[...], gq_ref[...], TN))
        sums_ref[0:1] = column_sum(gq_ref[...].astype(f32))

    @pl.when(step == 1)
    def _():
        total = dot(normed_ref[...], gk_ref[...], TN)
        store(1, total + dot(image_ref[...], gik_ref[...], TN))

    @pl.when(step == 2)
    def _():
        total = dot(normed_ref[...], gv_ref[...], TN)
        store(2, total + dot(image_ref[...], giv_ref[...], TN))
        sums = column_sum(gv_ref[...].astype(f32)) + column_sum(giv_ref[...].astype(f32))
        sums_ref[1:2] = sums
        if spare:
            keep[3 * block :, :] = jnp.zeros((spare, LANES), bf16)
            send[3 * block :, :] = jnp.zeros((spare, LANES), bf16)
            for copy in copies(3):
                copy.start()
        for part in range(4 if spare else 3):
            for copy in copies(part):
                copy.wait()


def weight_grads(order, side, normed, image, grads, lanes, place, spare, extra):
    rows, width = normed.shape
    half_rows = 3 * (lanes // LANES + len(extra)) * width // 2 + spare
    column = lambda height: pl.BlockSpec((height, lanes), lambda *_: (0, place))
    anywhere = pl.BlockSpec(memory_space=pl.ANY)
    return call(
        order,
        functools.partial(weight_kernel, spare),
        (normed, image, *grads, *extra),
        [shaped((2, lanes), f32)] + [shaped((half_rows, LANES), bf16)] * 2,
        "weight_grads",
        weighed(cost(8 * rows * width * lanes, 12 << 20)),
        scalars=(side,),
        grid=(3,),
        specs=[resident(normed.shape), resident(image.shape)]
        + [column(value.shape[0]) for value in grads]
        + [resident(value.shape) for value in extra],
        outs=[resident((2, lanes)), anywhere, anywhere],
        scratch=[pltpu.VMEM((half_rows, LANES), bf16)] * 2 + [pltpu.SemaphoreType.DMA((2, 4))],
    )


def image_grad_kernel(keys_weight, values_weight, keys_ref, values_ref, out_ref):
    total = dot(keys_ref[...], keys_weight[...], NT) + dot(values_ref[...], values_weight[...], NT)
    out_ref[...] = total.astype(bf16)


def image_grads(order, weight, keys, values):
    rows, width = keys.shape
    part = lambda base: pl.BlockSpec((width, width), lambda *_: (0, base))
    return call(
        order,
        image_grad_kernel,
        (weight, weight, keys, values),
        [shaped((rows, width), bf16)],
        "image_grads",
        weighed(cost(4 * rows * width * width, 6 << 20)),
        grid=(1,),
        specs=[part(1), part(2), resident(keys.shape), resident(values.shape)],
        outs=[resident((rows, width))],
    )


def finish_kernel(
    flag_ref,
    hid_ref,
    gmid_ref,
    near_ref,
    far_ref,
    gq_ref,
    gk_ref,
    gv_ref,
    gain_ref,
    weight_ref,
    feed_sums_ref,
    first_sums_ref,
    last_sums_ref,
    _,
    out_ref,
    small_ref,
    sums,
):
    item, block = pl.program_id(0), pl.program_id(1)
    joined = jnp.concatenate([gq_ref[...], gk_ref[...], gv_ref[...]], axis=1)
    grad = dot(joined, weight_ref[...], NT)
    unit, scale = normalise(hid_ref[...].astype(f32))
    both = near_ref[...].astype(f32) + far_ref[...].astype(f32)
    grad = grad + jnp.where((flag_ref[0] == 0) & (block == 0), both, 0.0)
    total = gmid_ref[...] + norm_transpose(unit, scale, gain_ref[...], grad)
    out_ref[...] = total.astype(bf16)
    found = jnp.concatenate([column_sum(grad * unit), column_sum(grad)], axis=0)

    @pl.when((item == 0) & (block == 0))
    def _():
        sums[...] = jnp.zeros(sums.shape, f32)

    sums[0:2] += found

    @pl.when((item == pl.num_programs(0) - 1) & (block == pl.num_programs(1) - 1))
    def _():
        width = sums.shape[1]
        pad = lambda count: jnp.zeros((count, width), f32)
        own = [sums[0:2], feed_sums_ref[0:3], feed_sums_ref[4:8], pad(7)]
        own = jnp.concatenate(own, axis=0)
        bias_sums = jnp.concatenate([first_sums_ref[...], last_sums_ref[...]], axis=1)
        shared = [pad(9), feed_sums_ref[3:4], bias_sums, pad(4)]
        shared = jnp.concatenate(shared, axis=0)
        is_text = flag_ref[0] == 1
        first = jnp.where(is_text, 0.0, own) + shared
        rows = jnp.concatenate([first, jnp.where(is_text, own, 0.0)], axis=0).astype(bf16)
        count = rows.shape[0]
        for number in range(width // LANES):
            cols = slice(number * LANES, (number + 1) * LANES)
            small_ref[number * count : (number + 1) * count, :] = rows[:, cols]
        small_ref[width // LANES * count :, :] = jnp.zeros((SMALL - width // LANES * count, LANES), bf16)


def finish_rows(
    order, flag, hidden, gmid, near, far, grads, gain, weight, feed_sums, bias_sums, keep, item_rows
):
    rows, width = hidden.shape
    blocks = item_rows // IMG_PAD
    mine = pl.BlockSpec((IMG_PAD, width), lambda i, j, *_: (i * blocks + j, 0))
    image = pl.BlockSpec((IMG_PAD, width), lambda i, j, *_: (i, 0))
    fixed = (gain, weight, feed_sums, *bias_sums)
    place = keep.shape[0] // SMALL - 1
    return call(
        order,
        finish_kernel,
        (hidden, gmid, near, far, *grads, *fixed, keep),
        [shaped((rows, width), bf16), shaped(keep.shape, bf16)],
        "finish_rows",
        weighed(cost(6 * rows * width * width, 16 << 20)),
        scalars=(flag,),
        grid=(rows // item_rows, blocks),
        specs=[mine, mine, image, image, mine, mine, mine]
        + [resident(value.shape) for value in fixed]
        + [pl.BlockSpec(memory_space=pl.ANY)],
        outs=[mine, pl.BlockSpec((SMALL, LANES), lambda *_: (place, 0))],
        scratch=[pltpu.VMEM((8, width), f32)],
        aliases={13: 1},
    )


def expert_kernel(half_ref, value_ref, *refs):
    at = 0
    for out in refs[-2:]:
        tall = out.shape[0]
        for part in range(out.shape[1] // LANES):
            piece = value_ref[at : at + tall, :]
            out[:, part * LANES : (part + 1) * LANES] = piece.astype(f32)
            at += tall


def expert_outputs(order, half, first, value, width, units, earlier):
    tall = width // 2
    block_rows = 2 * width // LANES * tall
    return call(
        order,
        expert_kernel,
        (value, *earlier),
        [shaped((units, width), f32), shaped((width, units), f32)],
        "expert_outputs",
        cost(value.size, 6 * value.size),
        scalars=(half,),
        grid=(value.shape[0] // block_rows,),
        specs=[pl.BlockSpec((block_rows, LANES), lambda i, at: (i, 0))]
        + [pl.BlockSpec(memory_space=pl.ANY)] * len(earlier),
        outs=[
            pl.BlockSpec((tall, width), lambda i, at: (2 * (first + i) + at[0], 0)),
            pl.BlockSpec((tall, width), lambda i, at: (at[0], first + i)),
        ],
        aliases={2: 0, 3: 1} if earlier else None,
    )


def store_projection(first_ref, last_ref, in_ref, out_ref):
    tall = in_ref.shape[0]
    count = first_ref.shape[0] // tall
    for part in range(count - 1):
        piece = first_ref[part * tall : (part + 1) * tall, :]
        in_ref[:, part * LANES : (part + 1) * LANES] = piece.astype(f32)
    in_ref[:, (count - 1) * LANES :] = last_ref[...].astype(f32)
    out_ref[...] = first_ref[(count - 1) * tall :, :].astype(f32)


def projection_kernel(half_ref, first_ref, last_ref, in_ref, out_ref):
    store_projection(first_ref, last_ref, in_ref, out_ref)


def last_kernel(half_ref, flag_ref, first_ref, last_ref, mine_ref, got_ref, *refs):
    in_ref, out_ref, *vec_refs, expand_ref, pair_ref, project_ref = refs[2:]
    store_projection(first_ref, last_ref, in_ref, out_ref)

    @pl.when(pl.program_id(0) == 0)
    def _():
        both = mine_ref[...].astype(f32) + got_ref[...].astype(f32)
        width = vec_refs[0].shape[1]
        rows = jnp.concatenate([both[at * 32 : (at + 1) * 32] for at in range(width // LANES)], axis=1)
        own = jnp.where(flag_ref[0] == 1, rows[16:], rows[:16])
        for number, ref in enumerate(vec_refs):
            ref[...] = own[number : number + 1]
        for number in range(expand_ref.shape[1] // width):
            cols = slice(number * width, (number + 1) * width)
            expand_ref[:, cols] = own[5 + number : 6 + number]
        project_ref[...] = rows[9:10]
        pair_ref[...] = rows[10:12]


def projection_specs(width):
    tall = width // 2
    ins = [
        pl.BlockSpec((tall * width // LANES, LANES), lambda b, *_: (b, 0)),
        pl.BlockSpec((tall, LANES), lambda b, *_: (b, 0)),
    ]
    outs = [
        pl.BlockSpec((tall, width), lambda b, at, *_: (at[0], b)),
        pl.BlockSpec((tall, LANES), lambda b, at, *_: (at[0], b)),
    ]
    return ins, outs, [shaped((width, 3 * width), f32), shaped((width, width), f32)]


def projection_outputs(order, half, first, last, width):
    ins, outs, shapes = projection_specs(width)
    return call(
        order,
        projection_kernel,
        (first, last),
        shapes,
        "projection_outputs",
        cost(first.size, 6 * first.size),
        scalars=(half,),
        grid=(3,),
        specs=ins,
        outs=outs,
    )


def last_outputs(order, half, flag, first, mine, got, width, units, earlier):
    ins, outs, shapes = projection_specs(width)
    place = got.shape[0] // SMALL - 1
    small = pl.BlockSpec((SMALL, LANES), lambda *_: (place, 0))
    vecs = [(1, width)] * 5 + [(1, units), (2, width), (1, width)]
    return call(
        order,
        last_kernel,
        (first, got, mine, got, *earlier),
        shapes + [shaped(shape, f32) for shape in vecs],
        "last_outputs",
        cost(got.size, 6 * got.size),
        scalars=(half, flag),
        grid=(3,),
        specs=ins + [small, small] + [pl.BlockSpec(memory_space=pl.ANY)] * 2,
        outs=outs + [resident(shape) for shape in vecs],
        aliases={6: 0, 7: 1},
    )


def swap(value, axes, pair_of):
    count = 1
    for axis in axes:
        count *= lax.axis_size(axis)
    return lax.ppermute(value, axes, [(source, pair_of(source)) for source in range(count)])


def place_of(axes):
    place = 0
    for axis in axes:
        place = place * lax.axis_size(axis) + lax.axis_index(axis)
    return place


def stage_bits(axes):
    count = 1
    for axis in axes:
        count *= lax.axis_size(axis)
    bits = count.bit_length() - 1
    core = len(axes) - 1
    others = [bit for bit in range(bits) if bit != core]
    if len(axes) == 1 and len(others) == 3:
        return [(core, core), (1, 2), (3, 1), (2, 3)]
    if len(axes) == 2 and len(others) == 4:
        return [(core, core), (0, 2), (2, 0), (3, 3), (4, 4)]
    return [(core, core)] + list(zip(others, others[1:] + others[:1]))


class Total:
    def __init__(self, order, axes, keep, send):
        self.order = order
        self.axes = axes
        self.core = len(axes) - 1
        self.left = stage_bits(axes)
        place = place_of(axes)
        second = ((place >> self.core) & 1) == 1
        sides = [(place >> jnp.where(second, pair[1], pair[0])) & 1 for pair in self.left]
        self.sides = dict(zip(self.left, sides))
        self.back = list(self.left)
        self.terms = (keep, self.exchange(send, self.left.pop(0)))
        self.mine = None

    def exchange(self, value, pair):
        other = lambda source: source ^ (1 << pair[(source >> self.core) & 1])
        self.got = swap(value, self.axes, other)
        return self.got

    def part(self, which, half):
        cut = lambda term: lax.dynamic_slice_in_dim(term, which * half, half, 0).astype(f32)
        return (cut(self.terms[0]) + cut(self.terms[1])).astype(bf16)

    def step(self):
        if self.left:
            pair = self.left.pop(0)
            self.terms = self.order.after(*self.terms)
            half = self.terms[0].shape[0] // 2
            side = self.sides[pair]
            sent = self.part(1 - side, half)
            self.terms = (self.part(side, half), self.exchange(sent, pair))
            self.order.last = sent
            return
        pair = self.back.pop()
        if self.mine is None:
            self.terms = self.order.after(*self.terms)
            self.mine = (self.terms[0].astype(f32) + self.terms[1].astype(f32)).astype(bf16)
        else:
            mine, got = self.order.after(self.mine, self.got)
            low = jnp.where(self.last == 0, mine, got)
            high = jnp.where(self.last == 0, got, mine)
            self.mine = jnp.concatenate([low, high], axis=0)
        self.order.last = self.mine
        self.last = self.sides[pair]
        self.exchange(self.mine, pair)


def on_device(
    hidden_in,
    image_count,
    text_lengths,
    attend_gain,
    attend_shift,
    project_in,
    bias_pair,
    project_out,
    project_bias,
    feed_gain,
    feed_shift,
    expand_weight,
    expand_bias,
    reduce_weight,
    reduce_bias,
    cotangent,
):
    items, _, rows, width = hidden_in.shape
    units = expand_weight.shape[2]
    is_text = lax.axis_index("mod") == 1
    flag = is_text.astype(jnp.int32)[None]
    hidden = hidden_in.reshape(items * rows, width)
    to_text = lambda value: lax.ppermute(value, "mod", [(0, 1)])
    to_image = lambda value: lax.ppermute(value, "mod", [(1, 0)])

    far_rows = [to_text(hidden_in[item, 0, :IMG_PAD]) for item in range(items)]
    far_vecs = to_text(jnp.concatenate([attend_gain, attend_shift], axis=0))
    order = Order()
    normed, projected = project_rows(
        order, hidden, attend_gain, attend_shift, project_in, bias_pair
    )
    scalars = (flag, image_count, text_lengths)
    images, attended, lses = (), [], []
    for item in range(items):
        images = image_rows(
            order,
            flag,
            item,
            hidden,
            far_rows[item],
            attend_gain,
            attend_shift,
            far_vecs,
            project_in,
            bias_pair,
            rows,
            items,
            images,
        )
        out, lse = attend_forward(order, scalars, item, projected, images[1])
        attended.append(out)
        lses.append(lse)

    side = (lax.axis_index("dp") & 1)[None]
    (
        hidden_out,
        grad_middle,
        grad_attended,
        project_out_grad,
        feed_sums,
        keep0,
        send0,
        keep1,
        send1,
    ) = feed_forward(
        order,
        flag,
        image_count,
        side,
        attended[0],
        attended[1],
        project_out,
        hidden,
        cotangent.reshape(items * rows, width),
        (project_bias[None], feed_gain, feed_shift, reduce_bias),
        expand_weight[0],
        expand_bias,
        reduce_weight[0],
    )
    a = Total(order, ("dp",), keep0, send0)
    c = Total(order, ("dp",), keep1, send1)
    grads = ()

    def backward(item, start, pairs):
        return attend_backward(
            order,
            scalars,
            item,
            start,
            pairs,
            projected,
            images[1],
            attended[item],
            grad_attended,
            lses[item],
            grads,
        )

    def weights(lanes, place, spare, *extra):
        return weight_grads(
            order, side, normed, images[0], grads, lanes, place, spare, extra
        )

    def unpack(half, first, value, earlier=()):
        return expert_outputs(order, half, first, value, width, units, earlier)

    grads = backward(0, 0, 2)
    a.step()
    grads = backward(1, 0, 2)
    c.step()
    grads = backward(0, 2, 2)
    a.step()
    grads = backward(1, 2, 2)
    c.step()
    first_sums, keep, send = weights(2 * LANES, 0, 0, project_out_grad)
    s = Total(order, ("dp", "mod"), keep, send)
    a.step()
    grads = backward(0, 4, 2)
    s.step()
    a.step()
    grads = backward(1, 4, 2)
    c.step()
    s.step()
    near = image_grads(order, project_in, grads[3], grads[4])
    far = to_image(near)
    c.step()
    a.step()
    last_sums, keep, send = weights(LANES, 2, SMALL)
    p = Total(order, ("dp", "mod"), keep, send)
    s.step()
    c.step()
    a.step()
    (far,) = order.after(far)
    order.last = far
    grad_in, keep = finish_rows(
        order,
        flag,
        hidden,
        grad_middle,
        near,
        far,
        grads[:3],
        attend_gain,
        project_in,
        feed_sums,
        (first_sums, last_sums),
        keep,
        rows,
    )
    p.terms = (keep, p.got)
    p.step()
    s.step()
    a.step()
    p.step()
    c.step()
    p.step()
    s.step()
    outputs = unpack(side, 0, a.mine)
    p.step()
    s.step()
    p.step()
    outputs = unpack(1 - side, 0, a.got, outputs)
    p.step()
    s.step()
    c.step()
    p.step()
    s.step()
    outputs = unpack(side, 2, c.mine, outputs)
    p.step()
    s.step()
    reduce_grad, expand_grad = unpack(1 - side, 2, c.got, outputs)
    while p.back:
        p.step()
    projections = projection_outputs(order, side, s.mine, p.mine, width)
    (
        project_in_grad,
        project_out_grad,
        attend_gain_grad,
        attend_shift_grad,
        feed_gain_grad,
        feed_shift_grad,
        reduce_bias_grad,
        expand_bias_grad,
        bias_pair_grad,
        project_bias_grad,
    ) = last_outputs(order, 1 - side, flag, s.got, p.mine, p.got, width, units, projections)
    return (
        hidden_out.reshape(hidden_in.shape),
        grad_in.reshape(hidden_in.shape),
        attend_gain_grad,
        attend_shift_grad,
        project_in_grad,
        bias_pair_grad,
        project_out_grad,
        project_bias_grad[0],
        feed_gain_grad,
        feed_shift_grad,
        expand_grad[None],
        expand_bias_grad,
        reduce_grad[None],
        reduce_bias_grad,
    )


def solution(mesh):
    in_specs = (
        P("dp", "mod", None, None),
        P("dp"),
        P("dp", None),
        P("mod", None),
        P("mod", None),
        P(),
        P(),
        P(),
        P(),
        P("mod", None),
        P("mod", None),
        P("mod", None, None),
        P("mod", None),
        P("mod", None, None),
        P("mod", None),
        P("dp", "mod", None, None),
    )
    out_specs = (
        P("dp", "mod", None, None),
        P("dp", "mod", None, None),
        P("mod", None),
        P("mod", None),
        P(),
        P(),
        P(),
        P(),
        P("mod", None),
        P("mod", None),
        P("mod", None, None),
        P("mod", None),
        P("mod", None, None),
        P("mod", None),
    )
    return jax.shard_map(
        on_device, mesh=mesh, in_specs=in_specs, out_specs=out_specs, check_vma=False
    )
```

```python
import functools

import jax
import jax.numpy as jnp
from jax import lax
from jax.experimental import pallas as pl
from jax.experimental.pallas import tpu as pltpu
from jax.sharding import PartitionSpec as P

HEADS = 12
HEAD = 64
IMG_PAD = 256
PAIR = 2 * HEAD
PAIRS = HEADS // 2
GROUP_PAIRS = 2
GROUPS = PAIRS // GROUP_PAIRS
LANES = GROUP_PAIRS * PAIR
SMALL = 128
FF_BLOCK = 768

masked_value = -1e30
norm_eps = 1e-05

bf16 = jnp.bfloat16
f32 = jnp.float32

NN = (((1,), (0,)), ((), ()))
NT = (((1,), (1,)), ((), ()))
TN = (((0,), (0,)), ((), ()))
VMEM_BYTES = 56 << 20


def dot(left, right, dims=NN):
    return lax.dot_general(left, right, dims, preferred_element_type=f32)


def column_sum(values):
    return jnp.sum(values, axis=0, keepdims=True)


def row_mean(values):
    return jnp.mean(values, axis=1, keepdims=True)


def normalise(values):
    centred = values - row_mean(values)
    scale = lax.rsqrt(row_mean(centred * centred) + norm_eps)
    return centred * scale, scale


def norm_transpose(unit, scale, gain, grad):
    grad_unit = grad * gain
    return scale * (grad_unit - row_mean(grad_unit) - unit * row_mean(grad_unit * unit))


def cost(flops, moved, special=0):
    return pl.CostEstimate(flops=flops, bytes_accessed=moved, transcendentals=special)


def weighed(estimate):
    return pl.CostEstimate(
        flops=10 * estimate.flops,
        bytes_accessed=10 * estimate.bytes_accessed,
        transcendentals=10 * estimate.transcendentals,
    )


class Order:
    def __init__(self):
        self.last = None

    def after(self, *values):
        if self.last is None:
            return values
        *values, _ = lax.optimization_barrier((*values, self.last))
        return values


def call(order, kernel, inputs, out_shape, name, estimate, scalars=(), grid=(), specs=None, outs=None,
         scratch=(), aliases=None):
    inputs = (*order.after(inputs[0]), *inputs[1:])
    vmem = pl.BlockSpec(memory_space=pltpu.VMEM)
    found = pl.pallas_call(
        kernel,
        grid_spec=pltpu.PrefetchScalarGridSpec(
            num_scalar_prefetch=len(scalars),
            grid=grid,
            in_specs=[vmem] * len(inputs) if specs is None else list(specs),
            out_specs=[vmem] * len(out_shape) if outs is None else list(outs),
            scratch_shapes=list(scratch),
        ),
        out_shape=list(out_shape),
        input_output_aliases=aliases or {},
        compiler_params=pltpu.CompilerParams(vmem_limit_bytes=VMEM_BYTES),
        cost_estimate=estimate,
        name=name,
    )(*scalars, *inputs)
    order.last = found[-1]
    return found if len(found) > 1 else found[0]


def shaped(shape, dtype):
    return jax.ShapeDtypeStruct(shape, dtype)


def resident(shape):
    return pl.BlockSpec(shape, lambda *_: (0,) * len(shape), pipeline_mode=pl.Buffered(1))


def project_kernel(hid_ref, gain_ref, shift_ref, weight_ref, bias_ref, normed_ref, out_ref):
    unit, _ = normalise(hid_ref[...].astype(f32))
    normed = (unit * gain_ref[...] + shift_ref[...]).astype(bf16)
    normed_ref[...] = normed
    width = normed.shape[1]
    for part in range(3):
        cols = slice(part * width, (part + 1) * width)
        rows = dot(normed, weight_ref[:, cols])
        if part == 0:
            rows = (rows + bias_ref[0:1]).astype(bf16) * jnp.asarray(HEAD**-0.5, bf16)
        if part == 2:
            rows = rows + bias_ref[1:2]
        out_ref[:, cols] = rows.astype(bf16)


def project_rows(order, hidden, gain, shift, weight, bias):
    rows, width = hidden.shape
    block = 256
    blocked = lambda cols: pl.BlockSpec((block, cols), lambda r: (r, 0))
    inputs = (hidden, gain, shift, weight, bias)
    return call(
        order,
        project_kernel,
        inputs,
        [shaped((rows, width), bf16), shaped((rows, 3 * width), bf16)],
        "project_rows",
        cost(6 * rows * width * width, 10 * rows * width + 6 * width * width),
        grid=(rows // block,),
        specs=[blocked(width)] + [resident(value.shape) for value in inputs[1:]],
        outs=[blocked(width), blocked(3 * width)],
    )


def image_kernel(
    flag_ref,
    own_ref,
    far_ref,
    gain_ref,
    shift_ref,
    vec_ref,
    keys_ref,
    values_ref,
    bias_ref,
    *refs,
):
    normed_ref, out_ref = refs[-2:]
    is_text = flag_ref[0] == 1
    hidden = jnp.where(is_text, far_ref[...].astype(f32), own_ref[...].astype(f32))
    gain = jnp.where(is_text, vec_ref[0:1], gain_ref[...])
    shift = jnp.where(is_text, vec_ref[1:2], shift_ref[...])
    unit, _ = normalise(hidden)
    normed = (unit * gain + shift).astype(bf16)
    normed_ref[...] = normed
    width = normed.shape[1]
    out_ref[:, :width] = dot(normed, keys_ref[...]).astype(bf16)
    out_ref[:, width:] = (dot(normed, values_ref[...]) + bias_ref[1:2]).astype(bf16)


def image_rows(
    order, flag, item, hidden, far, gain, shift, vecs, weight, bias, item_rows, items, earlier
):
    width = hidden.shape[1]
    place = item * (item_rows // IMG_PAD)
    half = lambda base: pl.BlockSpec((width, width), lambda *_: (0, base))
    mine = lambda cols: pl.BlockSpec((IMG_PAD, cols), lambda *_: (item, 0))
    inputs = (hidden, far, gain, shift, vecs, weight, weight, bias, *earlier)
    return call(
        order,
        image_kernel,
        inputs,
        [shaped((items * IMG_PAD, width), bf16), shaped((items * IMG_PAD, 2 * width), bf16)],
        "image_rows",
        cost(4 * IMG_PAD * width * width, 6 << 20),
        scalars=(flag,),
        grid=(1,),
        specs=[
            pl.BlockSpec((IMG_PAD, width), lambda *_: (place, 0)),
            resident(far.shape),
            resident(gain.shape),
            resident(shift.shape),
            resident(vecs.shape),
            half(1),
            half(2),
            resident(bias.shape),
        ]
        + [pl.BlockSpec(memory_space=pl.ANY)] * len(earlier),
        outs=[mine(width), mine(2 * width)],
        aliases={9: 0, 10: 1} if earlier else None,
    )


def segments(shape, axis, lengths_ref, item):
    places = lax.broadcasted_iota(jnp.int32, shape, axis)
    total = jnp.zeros(shape, jnp.int32)
    end = 0
    for which in range(lengths_ref.shape[1]):
        end = end + lengths_ref[item, which]
        total += (places >= end).astype(jnp.int32)
    return total


def own_bias(rows, flag_ref, lengths_ref, item):
    shape = (rows, rows)
    same = segments(shape, 0, lengths_ref, item) == segments(shape, 1, lengths_ref, item)
    return jnp.where(same & (flag_ref[0] == 1), 0.0, masked_value).astype(f32)


def image_bias(shape, axis, count_ref, item):
    places = lax.broadcasted_iota(jnp.int32, shape, axis)
    return jnp.where(places < count_ref[item], 0.0, masked_value).astype(f32)


def forward_kernel(
    item,
    flag_ref,
    count_ref,
    lengths_ref,
    q_ref,
    k_ref,
    v_ref,
    ik_ref,
    iv_ref,
    out_ref,
    lse_ref,
    image_part,
    own_part,
):
    rows = q_ref.shape[0]

    @pl.when(pl.program_id(0) == 0)
    def _():
        image_part[...] = image_bias(image_part.shape, 1, count_ref, item)
        own_part[...] = own_bias(rows, flag_ref, lengths_ref, item)

    first = lax.broadcasted_iota(jnp.int32, (rows, PAIR), 1) < HEAD
    zero = jnp.zeros((), bf16)
    q = q_ref[...]
    image_keys, image_values = ik_ref[...], iv_ref[...]
    keys, values = k_ref[...], v_ref[...]
    outs, tops = [], []
    for head in range(2):
        q_head = jnp.where(first, q, zero) if head == 0 else jnp.where(first, zero, q)
        far = dot(q_head, image_keys, NT) + image_part[...]
        own = dot(q_head, keys, NT) + own_part[...]
        top = jnp.maximum(
            jnp.max(far, axis=1, keepdims=True), jnp.max(own, axis=1, keepdims=True)
        )
        far = jnp.exp(far - top)
        own = jnp.exp(own - top)
        total = jnp.sum(far, axis=1, keepdims=True) + jnp.sum(own, axis=1, keepdims=True)
        summed = dot(far.astype(bf16), image_values) + dot(own.astype(bf16), values)
        outs.append(summed / total)
        tops.append(top + jnp.log(total))
    out_ref[...] = jnp.where(first, outs[0], outs[1]).astype(bf16)
    turned = jnp.transpose(jnp.where(first, tops[0], tops[1]))
    lse_ref[0, 0:1, :] = turned[0:1]
    lse_ref[0, 1:2, :] = turned[HEAD : HEAD + 1]


def attend_forward(order, scalars, item, projected, image):
    rows = projected.shape[0] // 2
    spec = lambda base: pl.BlockSpec((rows, PAIR), lambda h, *_: (item, base + h))
    far = lambda base: pl.BlockSpec((IMG_PAD, PAIR), lambda h, *_: (item, base + h))
    keys = rows + IMG_PAD
    return call(
        order,
        functools.partial(forward_kernel, item),
        (projected, projected, projected, image, image),
        [shaped((rows, HEADS * HEAD), bf16), shaped((PAIRS, 2, rows), f32)],
        "attend_forward",
        cost(16 * HEADS * rows * keys * HEAD, 6 << 20, HEADS * rows * keys),
        scalars=scalars,
        grid=(PAIRS,),
        specs=[spec(0), spec(PAIRS), spec(2 * PAIRS), far(0), far(PAIRS)],
        outs=[
            pl.BlockSpec((rows, PAIR), lambda h, *_: (0, h)),
            pl.BlockSpec((1, 2, rows), lambda h, *_: (h, 0, 0)),
        ],
        scratch=[pltpu.VMEM((rows, IMG_PAD), f32), pltpu.VMEM((rows, rows), f32)],
    )


def backward_kernel(
    item,
    flag_ref,
    count_ref,
    lengths_ref,
    q_ref,
    k_ref,
    v_ref,
    ik_ref,
    iv_ref,
    out_ref,
    grad_ref,
    lse_ref,
    *refs,
):
    gq_ref, gk_ref, gv_ref, gik_ref, giv_ref, image_part, own_part = refs[-7:]
    rows = q_ref.shape[0]

    @pl.when(pl.program_id(0) == 0)
    def _():
        image_part[...] = image_bias(image_part.shape, 0, count_ref, item)
        own_part[...] = own_bias(rows, flag_ref, lengths_ref, item)

    first = lax.broadcasted_iota(jnp.int32, (rows, PAIR), 1) < HEAD
    zero = jnp.zeros((), bf16)
    q, grad = q_ref[...], grad_ref[...]
    products = grad.astype(f32) * out_ref[...].astype(f32)
    head_lanes = lax.broadcasted_iota(jnp.int32, (8, PAIR), 1) // HEAD
    head_rows = lax.broadcasted_iota(jnp.int32, (8, PAIR), 0)
    center = lax.dot_general(
        (head_lanes == head_rows).astype(f32),
        products,
        NT,
        preferred_element_type=f32,
        precision=lax.Precision.HIGHEST,
    )
    q_heads = [jnp.where(first, q, zero), jnp.where(first, zero, q)]
    grad_heads = [jnp.where(first, grad, zero), jnp.where(first, zero, grad)]
    lse = lse_ref[0]
    grad_query = [None, None]
    half = rows // 2
    pieces = (
        (ik_ref, iv_ref, gik_ref, giv_ref, image_part, 0, IMG_PAD),
        (k_ref, v_ref, gk_ref, gv_ref, own_part, 0, half),
        (k_ref, v_ref, gk_ref, gv_ref, own_part, half, half),
    )
    for keys_ref, values_ref, gk_out, gv_out, bias, start, count in pieces:
        piece = slice(start, start + count)
        keys, values = keys_ref[piece, :], values_ref[piece, :]
        low_lanes = lax.broadcasted_iota(jnp.int32, (count, PAIR), 1) < HEAD
        grad_keys, grad_values = [], []
        for head in range(2):
            scores = dot(keys, q_heads[head], NT) + bias[piece, :]
            probs = jnp.exp(scores - lse[head : head + 1])
            grad_probs = dot(values, grad_heads[head], NT)
            grad_scores = (probs * (grad_probs - center[head : head + 1])).astype(bf16)
            grad_values.append(dot(probs.astype(bf16), grad))
            grad_keys.append(dot(grad_scores, q))
            term = dot(grad_scores, keys, TN)
            grad_query[head] = term if grad_query[head] is None else grad_query[head] + term
        gk_out[piece, :] = jnp.where(low_lanes, grad_keys[0], grad_keys[1]).astype(bf16)
        gv_out[piece, :] = jnp.where(low_lanes, grad_values[0], grad_values[1]).astype(bf16)
    gq_ref[...] = (jnp.where(first, grad_query[0], grad_query[1]) * HEAD**-0.5).astype(bf16)


def attend_backward(order, scalars, item, start, pairs, projected, image, attended, grad, lse, earlier):
    rows, width = attended.shape
    spec = lambda base: pl.BlockSpec((rows, PAIR), lambda h, *_: (item, base + start + h))
    far = lambda base: pl.BlockSpec((IMG_PAD, PAIR), lambda h, *_: (item, base + start + h))
    own = pl.BlockSpec((rows, PAIR), lambda h, *_: (0, start + h))
    far_outs = pl.BlockSpec((IMG_PAD, PAIR), lambda h, *_: (item, start + h))
    keys = rows + IMG_PAD
    inputs = (projected, projected, projected, image, image, attended, grad, lse)
    first = len(scalars) + len(inputs)
    return call(
        order,
        functools.partial(backward_kernel, item),
        (*inputs, *earlier),
        [shaped((2 * rows, width), bf16)] * 3 + [shaped((2 * IMG_PAD, width), bf16)] * 2,
        "attend_backward",
        weighed(cost(80 * pairs * rows * keys * HEAD, pairs * 2 << 20, 2 * pairs * rows * keys)),
        scalars=scalars,
        grid=(pairs,),
        specs=[
            spec(0),
            spec(PAIRS),
            spec(2 * PAIRS),
            far(0),
            far(PAIRS),
            own,
            spec(0),
            pl.BlockSpec((1, 2, rows), lambda h, *_: (start + h, 0, 0)),
        ]
        + [pl.BlockSpec(memory_space=pl.ANY)] * len(earlier),
        outs=[spec(0), spec(0), spec(0), far_outs, far_outs],
        scratch=[pltpu.VMEM((IMG_PAD, rows), f32), pltpu.VMEM((rows, rows), f32)],
        aliases={first + at: at for at in range(len(earlier))},
    )


def gelu_pair(values):
    share = 0.5 * (1.0 + lax.erf(values * 0.7071067811865476))
    slope = share + values * jnp.exp(-0.5 * values * values) * 0.3989422804014327
    return values * share, slope


def feed_step(step, rows, item_rows, feed, top, result, gfeed, expand_ref, ebias_ref, reduce_ref):
    width = feed.shape[1]
    expand, reduce = expand_ref[...], reduce_ref[...]
    active_parts, gup_parts = [], []
    for start in range(0, rows, item_rows):
        here = slice(start, start + item_rows)
        upward = dot(feed[here, :], expand) + ebias_ref[...]
        gactive = dot(top[here, :], reduce, NT)
        active, slope = gelu_pair(upward)
        active = active.astype(bf16)
        gup = (gactive * slope).astype(bf16)
        result[here, :] += dot(active, reduce)
        gfeed[here, :] += dot(gup, expand, NT)
        active_parts.append(active)
        gup_parts.append(gup)
    active = jnp.concatenate(active_parts, axis=0)
    gup = jnp.concatenate(gup_parts, axis=0)
    greduce = dot(active, top[...], TN).astype(bf16)
    gexpand = dot(feed[...], gup, TN).astype(bf16)
    pieces = [greduce[:, at : at + LANES] for at in range(0, width, LANES)]
    pieces += [gexpand[:, at : at + LANES] for at in range(0, FF_BLOCK, LANES)]
    return pieces, column_sum(gup.astype(f32))


def store_pieces(out, pieces):
    at = 0
    for half in range(2):
        for piece in pieces:
            rows = piece.shape[0] // 2
            out[at : at + rows, :] = piece[half * rows : (half + 1) * rows]
            at += rows


def feed_kernel(
    flag_ref,
    count_ref,
    side_ref,
    att0_ref,
    att1_ref,
    project_ref,
    hid_ref,
    cot_ref,
    project_bias_ref,
    gain_ref,
    shift_ref,
    reduce_bias_ref,
    expand_ref,
    ebias_ref,
    reduce_ref,
    out_ref,
    gmid_ref,
    gatt_ref,
    gproject_ref,
    gvec_ref,
    keep0_ref,
    send0_ref,
    keep1_ref,
    send1_ref,
    middle,
    feed,
    top,
    result,
    gfeed,
    low_out,
    gatt,
    grads,
    grad_sems,
    row_sems,
    *,
    item_rows,
):
    step = pl.program_id(0)
    rows, width = hid_ref.shape
    block = 256
    att_refs = (att0_ref, att1_ref)
    half = grads.shape[1] // 2

    steps = grads.shape[0]

    def grad_copies(which):
        found = []
        chunk, place = divmod(which, steps // 2)
        outs = (keep1_ref, send1_ref) if chunk else (keep0_ref, send0_ref)
        for number, out in enumerate(outs):
            side = side_ref[0] if number == 0 else 1 - side_ref[0]
            here = grads.at[which, pl.ds(pl.multiple_of(side * half, half), half)]
            there = out.at[pl.ds(place * half, half)]
            found.append(pltpu.make_async_copy(here, there, grad_sems.at[which, number]))
        return found

    @pl.when(step == 0)
    def _():
        for start in range(0, rows, block):
            here = slice(start, start + block)
            inside = slice(start % item_rows, start % item_rows + block)
            att = att_refs[start // item_rows][inside, :]
            branch = dot(att, project_ref[...]) + project_bias_ref[...]
            x = hid_ref[here, :].astype(f32) + branch
            middle[here, :] = x
            unit, _ = normalise(x)
            feed[here, :] = (unit * gain_ref[...] + shift_ref[...]).astype(bf16)
            at = lax.broadcasted_iota(jnp.int32, (block, width), 0) + start % item_rows
            limit = jnp.where(flag_ref[0] == 1, item_rows, count_ref[start // item_rows])
            top[here, :] = jnp.where(at < limit, cot_ref[here, :].astype(f32), 0.0).astype(bf16)
            result[here, :] = x + reduce_bias_ref[...]
            gfeed[here, :] = jnp.zeros((block, width), f32)

    pieces, gvec_ref[pl.ds(4 + step, 1), :] = feed_step(
        step, rows, item_rows, feed, top, result, gfeed, expand_ref, ebias_ref, reduce_ref
    )
    store_pieces(grads.at[step], pieces)
    for which in range(steps):

        @pl.when(step == which)
        def _(which=which):
            for copy in grad_copies(which):
                copy.start()

    @pl.when(step == pl.num_programs(0) - 1)
    def _():
        copies = []
        sums = [jnp.zeros((1, width), f32)] * 4
        for number, start in enumerate(range(0, rows, block)):
            here = slice(start, start + block)
            low_out[here, :] = result[here, :].astype(bf16)
            unit, scale = normalise(middle[here, :])
            grad = gfeed[here, :]
            grad_top = top[here, :].astype(f32)
            gmid = grad_top + norm_transpose(unit, scale, gain_ref[...], grad)
            terms = (grad * unit, grad, grad_top, gmid)
            sums = [old + column_sum(new) for old, new in zip(sums, terms)]
            middle[here, :] = gmid
            gbranch = gmid.astype(bf16)
            feed[here, :] = gbranch
            gatt[here, :] = dot(gbranch, project_ref[...], NT).astype(bf16)
            for kind, (mine, there) in enumerate(
                ((low_out, out_ref), (middle, gmid_ref), (gatt, gatt_ref))
            ):
                span = pl.ds(start, block)
                copy = pltpu.make_async_copy(
                    mine.at[span, :], there.at[span, :], row_sems.at[kind, number]
                )
                copy.start()
                copies.append(copy)
        total = dot(att0_ref[...], feed[:item_rows, :], TN)
        total += dot(att1_ref[...], feed[item_rows:, :], TN)
        gproject_ref[...] = total.astype(bf16)
        gvec_ref[0:4, :] = jnp.concatenate(sums, axis=0)
        for copy in copies:
            copy.wait()
        for which in range(steps):
            for copy in grad_copies(which):
                copy.wait()


def feed_forward(order, flag, count, side, att0, att1, project, hidden, cotangent, vecs, expand, ebias, reduce):
    rows, width = hidden.shape
    item_rows = att0.shape[0]
    units = reduce.shape[0]
    steps = units // FF_BLOCK
    block_rows = 2 * width * FF_BLOCK // LANES
    fixed = (att0, att1, project, hidden, cotangent, *vecs)
    anywhere = pl.BlockSpec(memory_space=pl.ANY)
    return call(
        order,
        functools.partial(feed_kernel, item_rows=item_rows),
        (*fixed, expand, ebias, reduce),
        [
            shaped((rows, width), bf16),
            shaped((rows, width), f32),
            shaped((rows, width), bf16),
            shaped((width, width), bf16),
            shaped((4 + steps, width), f32),
        ]
        + [shaped((steps // 2 * block_rows // 2, LANES), bf16)] * 4,
        "feed_forward",
        cost(12 * rows * width * units, 40 << 20, 2 * rows * units),
        scalars=(flag, count, side),
        grid=(steps,),
        specs=[resident(value.shape) for value in fixed]
        + [
            pl.BlockSpec((width, FF_BLOCK), lambda j, *_: (0, j)),
            pl.BlockSpec((1, FF_BLOCK), lambda j, *_: (0, j)),
            pl.BlockSpec((FF_BLOCK, width), lambda j, *_: (j, 0)),
        ],
        outs=[
            anywhere,
            anywhere,
            anywhere,
            resident((width, width)),
            resident((4 + steps, width)),
        ]
        + [anywhere] * 4,
        scratch=[
            pltpu.VMEM((rows, width), f32),
            pltpu.VMEM((rows, width), bf16),
            pltpu.VMEM((rows, width), bf16),
            pltpu.VMEM((rows, width), f32),
            pltpu.VMEM((rows, width), f32),
            pltpu.VMEM((rows, width), bf16),
            pltpu.VMEM((rows, width), bf16),
            pltpu.VMEM((steps, block_rows, LANES), bf16),
            pltpu.SemaphoreType.DMA((steps, 2)),
            pltpu.SemaphoreType.DMA((3, rows // 256)),
        ],
    )


def weight_kernel(
    spare,
    side_ref,
    normed_ref,
    image_ref,
    gq_ref,
    gk_ref,
    gv_ref,
    gik_ref,
    giv_ref,
    *refs,
):
    extra_ref = None if spare else refs[0]
    sums_ref, keep_ref, send_ref, keep, send, sems = refs[-6:]
    step = pl.program_id(0)
    width = normed_ref.shape[1]
    half = width // 2
    columns = gq_ref.shape[1] // LANES
    block = half * (columns if spare else columns + 1)

    def copies(part):
        span = pl.ds(part * block, block if part < 3 else spare)
        pairs = ((keep, keep_ref), (send, send_ref))
        return [
            pltpu.make_async_copy(here.at[span], there.at[span], sems.at[number, part])
            for number, (here, there) in enumerate(pairs)
        ]

    def store(part, total):
        if extra_ref is not None:
            more = extra_ref[:, part * LANES : (part + 1) * LANES].astype(f32)
            total = jnp.concatenate([total, more], axis=1)
        first = side_ref[0] == 0
        mine = jnp.where(first, total[:half], total[half:]).astype(bf16)
        other = jnp.where(first, total[half:], total[:half]).astype(bf16)
        for number in range(block // half):
            rows = slice(part * block + number * half, part * block + (number + 1) * half)
            cols = slice(number * LANES, (number + 1) * LANES)
            keep[rows, :] = mine[:, cols]
            send[rows, :] = other[:, cols]
        for copy in copies(part):
            copy.start()

    @pl.when(step == 0)
    def _():
        store(0, dot(normed_ref[...], gq_ref[...], TN))
        sums_ref[0:1] = column_sum(gq_ref[...].astype(f32))

    @pl.when(step == 1)
    def _():
        total = dot(normed_ref[...], gk_ref[...], TN)
        store(1, total + dot(image_ref[...], gik_ref[...], TN))

    @pl.when(step == 2)
    def _():
        total = dot(normed_ref[...], gv_ref[...], TN)
        store(2, total + dot(image_ref[...], giv_ref[...], TN))
        sums = column_sum(gv_ref[...].astype(f32)) + column_sum(giv_ref[...].astype(f32))
        sums_ref[1:2] = sums
        if spare:
            keep[3 * block :, :] = jnp.zeros((spare, LANES), bf16)
            send[3 * block :, :] = jnp.zeros((spare, LANES), bf16)
            for copy in copies(3):
                copy.start()
        for part in range(4 if spare else 3):
            for copy in copies(part):
                copy.wait()


def weight_grads(order, side, normed, image, grads, lanes, place, spare, extra):
    rows, width = normed.shape
    half_rows = 3 * (lanes // LANES + len(extra)) * width // 2 + spare
    column = lambda height: pl.BlockSpec((height, lanes), lambda *_: (0, place))
    anywhere = pl.BlockSpec(memory_space=pl.ANY)
    return call(
        order,
        functools.partial(weight_kernel, spare),
        (normed, image, *grads, *extra),
        [shaped((2, lanes), f32)] + [shaped((half_rows, LANES), bf16)] * 2,
        "weight_grads",
        weighed(cost(8 * rows * width * lanes, 12 << 20)),
        scalars=(side,),
        grid=(3,),
        specs=[resident(normed.shape), resident(image.shape)]
        + [column(value.shape[0]) for value in grads]
        + [resident(value.shape) for value in extra],
        outs=[resident((2, lanes)), anywhere, anywhere],
        scratch=[pltpu.VMEM((half_rows, LANES), bf16)] * 2 + [pltpu.SemaphoreType.DMA((2, 4))],
    )


def image_grad_kernel(keys_weight, values_weight, keys_ref, values_ref, out_ref):
    total = dot(keys_ref[...], keys_weight[...], NT) + dot(values_ref[...], values_weight[...], NT)
    out_ref[...] = total.astype(bf16)


def image_grads(order, weight, keys, values):
    rows, width = keys.shape
    part = lambda base: pl.BlockSpec((width, width), lambda *_: (0, base))
    return call(
        order,
        image_grad_kernel,
        (weight, weight, keys, values),
        [shaped((rows, width), bf16)],
        "image_grads",
        weighed(cost(4 * rows * width * width, 6 << 20)),
        grid=(1,),
        specs=[part(1), part(2), resident(keys.shape), resident(values.shape)],
        outs=[resident((rows, width))],
    )


def finish_kernel(
    flag_ref,
    hid_ref,
    gmid_ref,
    near_ref,
    far_ref,
    gq_ref,
    gk_ref,
    gv_ref,
    gain_ref,
    weight_ref,
    feed_sums_ref,
    first_sums_ref,
    last_sums_ref,
    _,
    out_ref,
    small_ref,
    sums,
):
    item, block = pl.program_id(0), pl.program_id(1)
    joined = jnp.concatenate([gq_ref[...], gk_ref[...], gv_ref[...]], axis=1)
    grad = dot(joined, weight_ref[...], NT)
    unit, scale = normalise(hid_ref[...].astype(f32))
    both = near_ref[...].astype(f32) + far_ref[...].astype(f32)
    grad = grad + jnp.where((flag_ref[0] == 0) & (block == 0), both, 0.0)
    total = gmid_ref[...] + norm_transpose(unit, scale, gain_ref[...], grad)
    out_ref[...] = total.astype(bf16)
    found = jnp.concatenate([column_sum(grad * unit), column_sum(grad)], axis=0)

    @pl.when((item == 0) & (block == 0))
    def _():
        sums[...] = jnp.zeros(sums.shape, f32)

    sums[0:2] += found

    @pl.when((item == pl.num_programs(0) - 1) & (block == pl.num_programs(1) - 1))
    def _():
        width = sums.shape[1]
        pad = lambda count: jnp.zeros((count, width), f32)
        own = [sums[0:2], feed_sums_ref[0:3], feed_sums_ref[4:8], pad(7)]
        own = jnp.concatenate(own, axis=0)
        bias_sums = jnp.concatenate([first_sums_ref[...], last_sums_ref[...]], axis=1)
        shared = [pad(9), feed_sums_ref[3:4], bias_sums, pad(4)]
        shared = jnp.concatenate(shared, axis=0)
        is_text = flag_ref[0] == 1
        first = jnp.where(is_text, 0.0, own) + shared
        rows = jnp.concatenate([first, jnp.where(is_text, own, 0.0)], axis=0).astype(bf16)
        count = rows.shape[0]
        for number in range(width // LANES):
            cols = slice(number * LANES, (number + 1) * LANES)
            small_ref[number * count : (number + 1) * count, :] = rows[:, cols]
        small_ref[width // LANES * count :, :] = jnp.zeros((SMALL - width // LANES * count, LANES), bf16)


def finish_rows(
    order, flag, hidden, gmid, near, far, grads, gain, weight, feed_sums, bias_sums, keep, item_rows
):
    rows, width = hidden.shape
    blocks = item_rows // IMG_PAD
    mine = pl.BlockSpec((IMG_PAD, width), lambda i, j, *_: (i * blocks + j, 0))
    image = pl.BlockSpec((IMG_PAD, width), lambda i, j, *_: (i, 0))
    fixed = (gain, weight, feed_sums, *bias_sums)
    place = keep.shape[0] // SMALL - 1
    return call(
        order,
        finish_kernel,
        (hidden, gmid, near, far, *grads, *fixed, keep),
        [shaped((rows, width), bf16), shaped(keep.shape, bf16)],
        "finish_rows",
        weighed(cost(6 * rows * width * width, 16 << 20)),
        scalars=(flag,),
        grid=(rows // item_rows, blocks),
        specs=[mine, mine, image, image, mine, mine, mine]
        + [resident(value.shape) for value in fixed]
        + [pl.BlockSpec(memory_space=pl.ANY)],
        outs=[mine, pl.BlockSpec((SMALL, LANES), lambda *_: (place, 0))],
        scratch=[pltpu.VMEM((8, width), f32)],
        aliases={13: 1},
    )


def expert_kernel(half_ref, value_ref, *refs):
    at = 0
    for out in refs[-2:]:
        tall = out.shape[0]
        for part in range(out.shape[1] // LANES):
            piece = value_ref[at : at + tall, :]
            out[:, part * LANES : (part + 1) * LANES] = piece.astype(f32)
            at += tall


def expert_outputs(order, half, first, value, width, units, earlier):
    tall = width // 2
    block_rows = 2 * width // LANES * tall
    return call(
        order,
        expert_kernel,
        (value, *earlier),
        [shaped((units, width), f32), shaped((width, units), f32)],
        "expert_outputs",
        cost(value.size, 6 * value.size),
        scalars=(half,),
        grid=(value.shape[0] // block_rows,),
        specs=[pl.BlockSpec((block_rows, LANES), lambda i, at: (i, 0))]
        + [pl.BlockSpec(memory_space=pl.ANY)] * len(earlier),
        outs=[
            pl.BlockSpec((tall, width), lambda i, at: (2 * (first + i) + at[0], 0)),
            pl.BlockSpec((tall, width), lambda i, at: (at[0], first + i)),
        ],
        aliases={2: 0, 3: 1} if earlier else None,
    )


def first_kernel(half_ref, value_ref, *refs):
    in_ref, out_ref, wide, narrow, sems = refs[-5:]
    tall = wide.shape[1]
    count = value_ref.shape[0] // tall // 3
    columns = in_ref.shape[1] // 3
    rows = pl.ds(pl.multiple_of(half_ref[0] * tall, tall), tall)
    copies = []
    for part in range(3):
        at = part * count * tall
        for number in range(count - 1):
            piece = value_ref[at + number * tall : at + (number + 1) * tall, :]
            wide[part, :, number * LANES : (number + 1) * LANES] = piece.astype(f32)
        piece = value_ref[at + (count - 1) * tall : at + count * tall, :]
        narrow[part] = piece.astype(f32)
        places = (
            (wide, in_ref.at[rows, pl.ds(part * columns, (count - 1) * LANES)]),
            (narrow, out_ref.at[rows, pl.ds(part * LANES, LANES)]),
        )
        for kind, (here, there) in enumerate(places):
            copy = pltpu.make_async_copy(here.at[part], there, sems.at[kind, part])
            copy.start()
            copies.append(copy)
    for copy in copies:
        copy.wait()


def first_outputs(order, half, value, width, earlier):
    tall = width // 2
    anywhere = pl.BlockSpec(memory_space=pl.ANY)
    return call(
        order,
        first_kernel,
        (value, *earlier),
        [shaped((width, 3 * width), f32), shaped((width, width), f32)],
        "first_outputs",
        cost(value.size, 6 * value.size),
        scalars=(half,),
        grid=(1,),
        specs=[resident(value.shape)] + [anywhere] * len(earlier),
        outs=[anywhere, anywhere],
        scratch=[
            pltpu.VMEM((3, tall, width - LANES), f32),
            pltpu.VMEM((3, tall, LANES), f32),
            pltpu.SemaphoreType.DMA((2, 3)),
        ],
        aliases={2: 0, 3: 1} if earlier else None,
    )


def last_kernel(side_ref, flag_ref, mine_ref, got_ref, *refs):
    in_ref, *vec_refs, expand_ref, pair_ref, project_ref, columns, sems = refs[1:]
    tall = columns.shape[2]
    width = in_ref.shape[1] // 3
    copies = []
    for number, ref in enumerate((mine_ref, got_ref)):
        half = side_ref[0] if number == 0 else 1 - side_ref[0]
        rows = pl.ds(pl.multiple_of(half * tall, tall), tall)
        for part in range(3):
            columns[number, part] = ref[part * tall : (part + 1) * tall, :].astype(f32)
            there = in_ref.at[rows, pl.ds((part + 1) * width - LANES, LANES)]
            copy = pltpu.make_async_copy(columns.at[number, part], there, sems.at[number, part])
            copy.start()
            copies.append(copy)
    both = mine_ref[3 * tall :, :].astype(f32) + got_ref[3 * tall :, :].astype(f32)
    rows = jnp.concatenate([both[at * 32 : (at + 1) * 32] for at in range(width // LANES)], axis=1)
    own = jnp.where(flag_ref[0] == 1, rows[16:], rows[:16])
    for number, ref in enumerate(vec_refs):
        ref[...] = own[number : number + 1]
    for number in range(expand_ref.shape[1] // width):
        cols = slice(number * width, (number + 1) * width)
        expand_ref[:, cols] = own[5 + number : 6 + number]
    project_ref[...] = rows[9:10]
    pair_ref[...] = rows[10:12]
    for copy in copies:
        copy.wait()


def last_outputs(order, side, flag, mine, got, width, units, earlier):
    vecs = [(1, width)] * 5 + [(1, units), (2, width), (1, width)]
    anywhere = pl.BlockSpec(memory_space=pl.ANY)
    return call(
        order,
        last_kernel,
        (mine, got, earlier),
        [shaped((width, 3 * width), f32)] + [shaped(shape, f32) for shape in vecs],
        "last_outputs",
        cost(got.size, 6 * got.size),
        scalars=(side, flag),
        grid=(1,),
        specs=[resident(mine.shape), resident(got.shape), anywhere],
        outs=[anywhere] + [resident(shape) for shape in vecs],
        scratch=[
            pltpu.VMEM((2, 3, width // 2, LANES), f32),
            pltpu.SemaphoreType.DMA((2, 3)),
        ],
        aliases={4: 0},
    )


def swap(value, axes, pair_of):
    count = 1
    for axis in axes:
        count *= lax.axis_size(axis)
    return lax.ppermute(value, axes, [(source, pair_of(source)) for source in range(count)])


def place_of(axes):
    place = 0
    for axis in axes:
        place = place * lax.axis_size(axis) + lax.axis_index(axis)
    return place


def late_stages(axes):
    stages = stage_bits(axes)
    if len(axes) == 2 and len(stages) == 5:
        return [stages[0], (0, 0), (2, 3), (3, 2), (4, 4)]
    return stages


def stage_bits(axes):
    count = 1
    for axis in axes:
        count *= lax.axis_size(axis)
    bits = count.bit_length() - 1
    core = len(axes) - 1
    others = [bit for bit in range(bits) if bit != core]
    if len(axes) == 1 and len(others) == 3:
        return [(core, core), (1, 2), (3, 1), (2, 3)]
    if len(axes) == 2 and len(others) == 4:
        return [(core, core), (0, 2), (2, 0), (3, 3), (4, 4)]
    return [(core, core)] + list(zip(others, others[1:] + others[:1]))


class Total:
    def __init__(self, order, axes, keep, send, stages=None):
        self.order = order
        self.axes = axes
        self.core = len(axes) - 1
        self.left = list(stages or stage_bits(axes))
        place = place_of(axes)
        second = ((place >> self.core) & 1) == 1
        sides = [(place >> jnp.where(second, pair[1], pair[0])) & 1 for pair in self.left]
        self.sides = dict(zip(self.left, sides))
        self.back = list(self.left)
        self.terms = (keep, self.exchange(send, self.left.pop(0)))
        self.mine = None

    def exchange(self, value, pair):
        other = lambda source: source ^ (1 << pair[(source >> self.core) & 1])
        self.got = swap(value, self.axes, other)
        return self.got

    def part(self, which, half):
        cut = lambda term: lax.dynamic_slice_in_dim(term, which * half, half, 0).astype(f32)
        return (cut(self.terms[0]) + cut(self.terms[1])).astype(bf16)

    def finish(self):
        while self.left or self.back:
            self.step()

    def step(self):
        if self.left:
            pair = self.left.pop(0)
            self.terms = self.order.after(*self.terms)
            half = self.terms[0].shape[0] // 2
            side = self.sides[pair]
            sent = self.part(1 - side, half)
            self.terms = (self.part(side, half), self.exchange(sent, pair))
            self.order.last = sent
            return
        pair = self.back.pop()
        if self.mine is None:
            self.terms = self.order.after(*self.terms)
            self.mine = (self.terms[0].astype(f32) + self.terms[1].astype(f32)).astype(bf16)
        else:
            mine, got = self.order.after(self.mine, self.got)
            low = jnp.where(self.last == 0, mine, got)
            high = jnp.where(self.last == 0, got, mine)
            self.mine = jnp.concatenate([low, high], axis=0)
        self.order.last = self.mine
        self.last = self.sides[pair]
        self.exchange(self.mine, pair)


def on_device(
    hidden_in,
    image_count,
    text_lengths,
    attend_gain,
    attend_shift,
    project_in,
    bias_pair,
    project_out,
    project_bias,
    feed_gain,
    feed_shift,
    expand_weight,
    expand_bias,
    reduce_weight,
    reduce_bias,
    cotangent,
):
    items, _, rows, width = hidden_in.shape
    units = expand_weight.shape[2]
    is_text = lax.axis_index("mod") == 1
    flag = is_text.astype(jnp.int32)[None]
    hidden = hidden_in.reshape(items * rows, width)
    to_text = lambda value: lax.ppermute(value, "mod", [(0, 1)])
    to_image = lambda value: lax.ppermute(value, "mod", [(1, 0)])

    far_rows = [to_text(hidden_in[item, 0, :IMG_PAD]) for item in range(items)]
    far_vecs = to_text(jnp.concatenate([attend_gain, attend_shift], axis=0))
    order = Order()
    normed, projected = project_rows(
        order, hidden, attend_gain, attend_shift, project_in, bias_pair
    )
    scalars = (flag, image_count, text_lengths)
    images, attended, lses = (), [], []
    for item in range(items):
        images = image_rows(
            order,
            flag,
            item,
            hidden,
            far_rows[item],
            attend_gain,
            attend_shift,
            far_vecs,
            project_in,
            bias_pair,
            rows,
            items,
            images,
        )
        out, lse = attend_forward(order, scalars, item, projected, images[1])
        attended.append(out)
        lses.append(lse)

    side = (lax.axis_index("dp") & 1)[None]
    (
        hidden_out,
        grad_middle,
        grad_attended,
        project_out_grad,
        feed_sums,
        keep0,
        send0,
        keep1,
        send1,
    ) = feed_forward(
        order,
        flag,
        image_count,
        side,
        attended[0],
        attended[1],
        project_out,
        hidden,
        cotangent.reshape(items * rows, width),
        (project_bias[None], feed_gain, feed_shift, reduce_bias),
        expand_weight[0],
        expand_bias,
        reduce_weight[0],
    )
    a = Total(order, ("dp",), keep0, send0)
    c = Total(order, ("dp",), keep1, send1)
    grads = ()

    def backward(item, start, pairs):
        return attend_backward(
            order,
            scalars,
            item,
            start,
            pairs,
            projected,
            images[1],
            attended[item],
            grad_attended,
            lses[item],
            grads,
        )

    def weights(lanes, place, spare, *extra):
        return weight_grads(
            order, side, normed, images[0], grads, lanes, place, spare, extra
        )

    def unpack(half, first, value, earlier=()):
        return expert_outputs(order, half, first, value, width, units, earlier)

    grads = backward(0, 0, 2)
    a.step()
    grads = backward(1, 0, 2)
    c.step()
    grads = backward(0, 2, 2)
    a.step()
    grads = backward(1, 2, 2)
    c.step()
    a.step()
    first_sums, keep, send = weights(2 * LANES, 0, 0, project_out_grad)
    s = Total(order, ("dp", "mod"), keep, send)
    a.step()
    grads = backward(0, 4, 2)
    s.step()
    c.step()
    a.step()
    grads = backward(1, 4, 2)
    c.step()
    s.step()
    near = image_grads(order, project_in, grads[3], grads[4])
    far = to_image(near)
    a.step()
    c.step()
    last_sums, keep, send = weights(LANES, 2, SMALL)
    p = Total(order, ("dp", "mod"), keep, send, late_stages(("dp", "mod")))
    s.step()
    (far,) = order.after(far)
    order.last = far
    grad_in, keep = finish_rows(
        order,
        flag,
        hidden,
        grad_middle,
        near,
        far,
        grads[:3],
        attend_gain,
        project_in,
        feed_sums,
        (first_sums, last_sums),
        keep,
        rows,
    )
    p.terms = (keep, p.got)
    c.step()
    p.step()
    a.step()
    a.finish()
    outputs = unpack(side, 0, a.mine)
    p.step()
    s.step()
    outputs = unpack(1 - side, 0, a.got, outputs)
    p.step()
    s.step()
    c.step()
    p.step()
    s.step()
    c.finish()
    outputs = unpack(side, 2, c.mine, outputs)
    p.step()
    s.step()
    reduce_grad, expand_grad = unpack(1 - side, 2, c.got, outputs)
    p.step()
    s.step()
    p.step()
    s.step()
    s.finish()
    projections = first_outputs(order, side, s.mine, width, ())
    p.step()
    project_in_grad, project_out_grad = first_outputs(order, 1 - side, s.got, width, projections)
    p.finish()
    (
        project_in_grad,
        attend_gain_grad,
        attend_shift_grad,
        feed_gain_grad,
        feed_shift_grad,
        reduce_bias_grad,
        expand_bias_grad,
        bias_pair_grad,
        project_bias_grad,
    ) = last_outputs(order, side, flag, p.mine, p.got, width, units, project_in_grad)
    return (
        hidden_out.reshape(hidden_in.shape),
        grad_in.reshape(hidden_in.shape),
        attend_gain_grad,
        attend_shift_grad,
        project_in_grad,
        bias_pair_grad,
        project_out_grad,
        project_bias_grad.reshape(-1),
        feed_gain_grad,
        feed_shift_grad,
        expand_grad[None],
        expand_bias_grad,
        reduce_grad[None],
        reduce_bias_grad,
    )


def solution(mesh):
    in_specs = (
        P("dp", "mod", None, None),
        P("dp"),
        P("dp", None),
        P("mod", None),
        P("mod", None),
        P(),
        P(),
        P(),
        P(),
        P("mod", None),
        P("mod", None),
        P("mod", None, None),
        P("mod", None),
        P("mod", None, None),
        P("mod", None),
        P("dp", "mod", None, None),
    )
    out_specs = (
        P("dp", "mod", None, None),
        P("dp", "mod", None, None),
        P("mod", None),
        P("mod", None),
        P(),
        P(),
        P(),
        P(),
        P("mod", None),
        P("mod", None),
        P("mod", None, None),
        P("mod", None),
        P("mod", None, None),
        P("mod", None),
    )
    return jax.shard_map(
        on_device, mesh=mesh, in_specs=in_specs, out_specs=out_specs, check_vma=False
    )
```

```python
import functools

import jax
import jax.numpy as jnp
from jax import lax
from jax.experimental import pallas as pl
from jax.experimental.pallas import tpu as pltpu
from jax.sharding import PartitionSpec as P

HEADS = 12
HEAD = 64
IMG_PAD = 256
PAIR = 2 * HEAD
PAIRS = HEADS // 2
GROUP_PAIRS = 2
GROUPS = PAIRS // GROUP_PAIRS
LANES = GROUP_PAIRS * PAIR
SMALL = 128
FF_BLOCK = 768

masked_value = -1e30
norm_eps = 1e-05

bf16 = jnp.bfloat16
f32 = jnp.float32

NN = (((1,), (0,)), ((), ()))
NT = (((1,), (1,)), ((), ()))
TN = (((0,), (0,)), ((), ()))
VMEM_BYTES = 56 << 20


def dot(left, right, dims=NN):
    return lax.dot_general(left, right, dims, preferred_element_type=f32)


def column_sum(values):
    return jnp.sum(values, axis=0, keepdims=True)


def row_mean(values):
    return jnp.mean(values, axis=1, keepdims=True)


def normalise(values):
    centred = values - row_mean(values)
    scale = lax.rsqrt(row_mean(centred * centred) + norm_eps)
    return centred * scale, scale


def norm_transpose(unit, scale, gain, grad):
    grad_unit = grad * gain
    return scale * (grad_unit - row_mean(grad_unit) - unit * row_mean(grad_unit * unit))


def cost(flops, moved, special=0):
    return pl.CostEstimate(flops=flops, bytes_accessed=moved, transcendentals=special)


def weighed(estimate):
    return pl.CostEstimate(
        flops=10 * estimate.flops,
        bytes_accessed=10 * estimate.bytes_accessed,
        transcendentals=10 * estimate.transcendentals,
    )


class Order:
    def __init__(self):
        self.last = None

    def after(self, *values):
        if self.last is None:
            return values
        *values, _ = lax.optimization_barrier((*values, self.last))
        return values


def call(order, kernel, inputs, out_shape, name, estimate, scalars=(), grid=(), specs=None, outs=None,
         scratch=(), aliases=None):
    inputs = (*order.after(inputs[0]), *inputs[1:])
    vmem = pl.BlockSpec(memory_space=pltpu.VMEM)
    found = pl.pallas_call(
        kernel,
        grid_spec=pltpu.PrefetchScalarGridSpec(
            num_scalar_prefetch=len(scalars),
            grid=grid,
            in_specs=[vmem] * len(inputs) if specs is None else list(specs),
            out_specs=[vmem] * len(out_shape) if outs is None else list(outs),
            scratch_shapes=list(scratch),
        ),
        out_shape=list(out_shape),
        input_output_aliases=aliases or {},
        compiler_params=pltpu.CompilerParams(vmem_limit_bytes=VMEM_BYTES),
        cost_estimate=estimate,
        name=name,
    )(*scalars, *inputs)
    order.last = found[-1]
    return found if len(found) > 1 else found[0]


def shaped(shape, dtype):
    return jax.ShapeDtypeStruct(shape, dtype)


def resident(shape):
    return pl.BlockSpec(shape, lambda *_: (0,) * len(shape), pipeline_mode=pl.Buffered(1))


def project_kernel(hid_ref, gain_ref, shift_ref, weight_ref, bias_ref, normed_ref, out_ref):
    unit, _ = normalise(hid_ref[...].astype(f32))
    normed = (unit * gain_ref[...] + shift_ref[...]).astype(bf16)
    normed_ref[...] = normed
    width = normed.shape[1]
    for part in range(3):
        cols = slice(part * width, (part + 1) * width)
        rows = dot(normed, weight_ref[:, cols])
        if part == 0:
            rows = (rows + bias_ref[0:1]).astype(bf16) * jnp.asarray(HEAD**-0.5, bf16)
        if part == 2:
            rows = rows + bias_ref[1:2]
        out_ref[:, cols] = rows.astype(bf16)


def project_rows(order, hidden, gain, shift, weight, bias):
    rows, width = hidden.shape
    block = 256
    blocked = lambda cols: pl.BlockSpec((block, cols), lambda r: (r, 0))
    inputs = (hidden, gain, shift, weight, bias)
    return call(
        order,
        project_kernel,
        inputs,
        [shaped((rows, width), bf16), shaped((rows, 3 * width), bf16)],
        "project_rows",
        cost(6 * rows * width * width, 10 * rows * width + 6 * width * width),
        grid=(rows // block,),
        specs=[blocked(width)] + [resident(value.shape) for value in inputs[1:]],
        outs=[blocked(width), blocked(3 * width)],
    )


def image_kernel(
    flag_ref,
    own_ref,
    far_ref,
    gain_ref,
    shift_ref,
    vec_ref,
    keys_ref,
    values_ref,
    bias_ref,
    *refs,
):
    normed_ref, out_ref = refs[-2:]
    is_text = flag_ref[0] == 1
    hidden = jnp.where(is_text, far_ref[...].astype(f32), own_ref[...].astype(f32))
    gain = jnp.where(is_text, vec_ref[0:1], gain_ref[...])
    shift = jnp.where(is_text, vec_ref[1:2], shift_ref[...])
    unit, _ = normalise(hidden)
    normed = (unit * gain + shift).astype(bf16)
    normed_ref[...] = normed
    width = normed.shape[1]
    out_ref[:, :width] = dot(normed, keys_ref[...]).astype(bf16)
    out_ref[:, width:] = (dot(normed, values_ref[...]) + bias_ref[1:2]).astype(bf16)


def image_rows(
    order, flag, item, hidden, far, gain, shift, vecs, weight, bias, item_rows, items, earlier
):
    width = hidden.shape[1]
    place = item * (item_rows // IMG_PAD)
    half = lambda base: pl.BlockSpec((width, width), lambda *_: (0, base))
    mine = lambda cols: pl.BlockSpec((IMG_PAD, cols), lambda *_: (item, 0))
    inputs = (hidden, far, gain, shift, vecs, weight, weight, bias, *earlier)
    return call(
        order,
        image_kernel,
        inputs,
        [shaped((items * IMG_PAD, width), bf16), shaped((items * IMG_PAD, 2 * width), bf16)],
        "image_rows",
        cost(4 * IMG_PAD * width * width, 6 << 20),
        scalars=(flag,),
        grid=(1,),
        specs=[
            pl.BlockSpec((IMG_PAD, width), lambda *_: (place, 0)),
            resident(far.shape),
            resident(gain.shape),
            resident(shift.shape),
            resident(vecs.shape),
            half(1),
            half(2),
            resident(bias.shape),
        ]
        + [pl.BlockSpec(memory_space=pl.ANY)] * len(earlier),
        outs=[mine(width), mine(2 * width)],
        aliases={9: 0, 10: 1} if earlier else None,
    )


def segments(shape, axis, lengths_ref, item):
    places = lax.broadcasted_iota(jnp.int32, shape, axis)
    total = jnp.zeros(shape, jnp.int32)
    end = 0
    for which in range(lengths_ref.shape[1]):
        end = end + lengths_ref[item, which]
        total += (places >= end).astype(jnp.int32)
    return total


def own_bias(rows, flag_ref, lengths_ref, item):
    shape = (rows, rows)
    same = segments(shape, 0, lengths_ref, item) == segments(shape, 1, lengths_ref, item)
    return jnp.where(same & (flag_ref[0] == 1), 0.0, masked_value).astype(f32)


def image_bias(shape, axis, count_ref, item):
    places = lax.broadcasted_iota(jnp.int32, shape, axis)
    return jnp.where(places < count_ref[item], 0.0, masked_value).astype(f32)


def forward_kernel(
    item,
    flag_ref,
    count_ref,
    lengths_ref,
    q_ref,
    k_ref,
    v_ref,
    ik_ref,
    iv_ref,
    out_ref,
    lse_ref,
    image_part,
    own_part,
):
    rows = q_ref.shape[0]

    @pl.when(pl.program_id(0) == 0)
    def _():
        image_part[...] = image_bias(image_part.shape, 1, count_ref, item)
        own_part[...] = own_bias(rows, flag_ref, lengths_ref, item)

    first = lax.broadcasted_iota(jnp.int32, (rows, PAIR), 1) < HEAD
    zero = jnp.zeros((), bf16)
    q = q_ref[...]
    image_keys, image_values = ik_ref[...], iv_ref[...]
    keys, values = k_ref[...], v_ref[...]
    outs, tops = [], []
    for head in range(2):
        q_head = jnp.where(first, q, zero) if head == 0 else jnp.where(first, zero, q)
        far = dot(q_head, image_keys, NT) + image_part[...]
        own = dot(q_head, keys, NT) + own_part[...]
        top = jnp.maximum(
            jnp.max(far, axis=1, keepdims=True), jnp.max(own, axis=1, keepdims=True)
        )
        far = jnp.exp(far - top)
        own = jnp.exp(own - top)
        total = jnp.sum(far, axis=1, keepdims=True) + jnp.sum(own, axis=1, keepdims=True)
        summed = dot(far.astype(bf16), image_values) + dot(own.astype(bf16), values)
        outs.append(summed / total)
        tops.append(top + jnp.log(total))
    out_ref[...] = jnp.where(first, outs[0], outs[1]).astype(bf16)
    turned = jnp.transpose(jnp.where(first, tops[0], tops[1]))
    lse_ref[0, 0:1, :] = turned[0:1]
    lse_ref[0, 1:2, :] = turned[HEAD : HEAD + 1]


def attend_forward(order, scalars, item, projected, image):
    rows = projected.shape[0] // 2
    spec = lambda base: pl.BlockSpec((rows, PAIR), lambda h, *_: (item, base + h))
    far = lambda base: pl.BlockSpec((IMG_PAD, PAIR), lambda h, *_: (item, base + h))
    keys = rows + IMG_PAD
    return call(
        order,
        functools.partial(forward_kernel, item),
        (projected, projected, projected, image, image),
        [shaped((rows, HEADS * HEAD), bf16), shaped((PAIRS, 2, rows), f32)],
        "attend_forward",
        cost(16 * HEADS * rows * keys * HEAD, 6 << 20, HEADS * rows * keys),
        scalars=scalars,
        grid=(PAIRS,),
        specs=[spec(0), spec(PAIRS), spec(2 * PAIRS), far(0), far(PAIRS)],
        outs=[
            pl.BlockSpec((rows, PAIR), lambda h, *_: (0, h)),
            pl.BlockSpec((1, 2, rows), lambda h, *_: (h, 0, 0)),
        ],
        scratch=[pltpu.VMEM((rows, IMG_PAD), f32), pltpu.VMEM((rows, rows), f32)],
    )


def backward_kernel(
    item,
    flag_ref,
    count_ref,
    lengths_ref,
    q_ref,
    k_ref,
    v_ref,
    ik_ref,
    iv_ref,
    out_ref,
    grad_ref,
    lse_ref,
    *refs,
):
    gq_ref, gk_ref, gv_ref, gik_ref, giv_ref, image_part, own_part = refs[-7:]
    rows = q_ref.shape[0]

    @pl.when(pl.program_id(0) == 0)
    def _():
        image_part[...] = image_bias(image_part.shape, 0, count_ref, item)
        own_part[...] = own_bias(rows, flag_ref, lengths_ref, item)

    first = lax.broadcasted_iota(jnp.int32, (rows, PAIR), 1) < HEAD
    zero = jnp.zeros((), bf16)
    q, grad = q_ref[...], grad_ref[...]
    products = grad.astype(f32) * out_ref[...].astype(f32)
    head_lanes = lax.broadcasted_iota(jnp.int32, (8, PAIR), 1) // HEAD
    head_rows = lax.broadcasted_iota(jnp.int32, (8, PAIR), 0)
    center = lax.dot_general(
        (head_lanes == head_rows).astype(f32),
        products,
        NT,
        preferred_element_type=f32,
        precision=lax.Precision.HIGHEST,
    )
    q_heads = [jnp.where(first, q, zero), jnp.where(first, zero, q)]
    grad_heads = [jnp.where(first, grad, zero), jnp.where(first, zero, grad)]
    lse = lse_ref[0]
    grad_query = [None, None]
    half = rows // 2
    pieces = (
        (ik_ref, iv_ref, gik_ref, giv_ref, image_part, 0, IMG_PAD),
        (k_ref, v_ref, gk_ref, gv_ref, own_part, 0, half),
        (k_ref, v_ref, gk_ref, gv_ref, own_part, half, half),
    )
    for keys_ref, values_ref, gk_out, gv_out, bias, start, count in pieces:
        piece = slice(start, start + count)
        keys, values = keys_ref[piece, :], values_ref[piece, :]
        low_lanes = lax.broadcasted_iota(jnp.int32, (count, PAIR), 1) < HEAD
        grad_keys, grad_values = [], []
        for head in range(2):
            scores = dot(keys, q_heads[head], NT) + bias[piece, :]
            probs = jnp.exp(scores - lse[head : head + 1])
            grad_probs = dot(values, grad_heads[head], NT)
            grad_scores = (probs * (grad_probs - center[head : head + 1])).astype(bf16)
            grad_values.append(dot(probs.astype(bf16), grad))
            grad_keys.append(dot(grad_scores, q))
            term = dot(grad_scores, keys, TN)
            grad_query[head] = term if grad_query[head] is None else grad_query[head] + term
        gk_out[piece, :] = jnp.where(low_lanes, grad_keys[0], grad_keys[1]).astype(bf16)
        gv_out[piece, :] = jnp.where(low_lanes, grad_values[0], grad_values[1]).astype(bf16)
    gq_ref[...] = (jnp.where(first, grad_query[0], grad_query[1]) * HEAD**-0.5).astype(bf16)


def attend_backward(order, scalars, item, start, pairs, projected, image, attended, grad, lse, earlier):
    rows, width = attended.shape
    spec = lambda base: pl.BlockSpec((rows, PAIR), lambda h, *_: (item, base + start + h))
    far = lambda base: pl.BlockSpec((IMG_PAD, PAIR), lambda h, *_: (item, base + start + h))
    own = pl.BlockSpec((rows, PAIR), lambda h, *_: (0, start + h))
    far_outs = pl.BlockSpec((IMG_PAD, PAIR), lambda h, *_: (item, start + h))
    keys = rows + IMG_PAD
    inputs = (projected, projected, projected, image, image, attended, grad, lse)
    first = len(scalars) + len(inputs)
    return call(
        order,
        functools.partial(backward_kernel, item),
        (*inputs, *earlier),
        [shaped((2 * rows, width), bf16)] * 3 + [shaped((2 * IMG_PAD, width), bf16)] * 2,
        "attend_backward",
        weighed(cost(80 * pairs * rows * keys * HEAD, pairs * 2 << 20, 2 * pairs * rows * keys)),
        scalars=scalars,
        grid=(pairs,),
        specs=[
            spec(0),
            spec(PAIRS),
            spec(2 * PAIRS),
            far(0),
            far(PAIRS),
            own,
            spec(0),
            pl.BlockSpec((1, 2, rows), lambda h, *_: (start + h, 0, 0)),
        ]
        + [pl.BlockSpec(memory_space=pl.ANY)] * len(earlier),
        outs=[spec(0), spec(0), spec(0), far_outs, far_outs],
        scratch=[pltpu.VMEM((IMG_PAD, rows), f32), pltpu.VMEM((rows, rows), f32)],
        aliases={first + at: at for at in range(len(earlier))},
    )


def gelu_pair(values):
    share = 0.5 * (1.0 + lax.erf(values * 0.7071067811865476))
    slope = share + values * jnp.exp(-0.5 * values * values) * 0.3989422804014327
    return values * share, slope


def feed_step(step, rows, item_rows, feed, top, result, gfeed, expand_ref, ebias_ref, reduce_ref):
    width = feed.shape[1]
    expand, reduce = expand_ref[...], reduce_ref[...]
    active_parts, gup_parts = [], []
    for start in range(0, rows, item_rows):
        here = slice(start, start + item_rows)
        upward = dot(feed[here, :], expand) + ebias_ref[...]
        gactive = dot(top[here, :], reduce, NT)
        active, slope = gelu_pair(upward)
        active = active.astype(bf16)
        gup = (gactive * slope).astype(bf16)
        result[here, :] += dot(active, reduce)
        gfeed[here, :] += dot(gup, expand, NT)
        active_parts.append(active)
        gup_parts.append(gup)
    active = jnp.concatenate(active_parts, axis=0)
    gup = jnp.concatenate(gup_parts, axis=0)
    greduce = dot(active, top[...], TN).astype(bf16)
    gexpand = dot(feed[...], gup, TN).astype(bf16)
    pieces = [greduce[:, at : at + LANES] for at in range(0, width, LANES)]
    pieces += [gexpand[:, at : at + LANES] for at in range(0, FF_BLOCK, LANES)]
    return pieces, column_sum(gup.astype(f32))


def store_pieces(out, pieces):
    at = 0
    for half in range(2):
        for piece in pieces:
            rows = piece.shape[0] // 2
            out[at : at + rows, :] = piece[half * rows : (half + 1) * rows]
            at += rows


def feed_kernel(
    flag_ref,
    count_ref,
    side_ref,
    att0_ref,
    att1_ref,
    project_ref,
    hid_ref,
    cot_ref,
    project_bias_ref,
    gain_ref,
    shift_ref,
    reduce_bias_ref,
    expand_ref,
    ebias_ref,
    reduce_ref,
    out_ref,
    gmid_ref,
    gatt_ref,
    gproject_ref,
    gvec_ref,
    keep0_ref,
    send0_ref,
    keep1_ref,
    send1_ref,
    middle,
    feed,
    top,
    result,
    gfeed,
    low_out,
    gatt,
    grads,
    grad_sems,
    row_sems,
    *,
    item_rows,
):
    step = pl.program_id(0)
    rows, width = hid_ref.shape
    block = 256
    att_refs = (att0_ref, att1_ref)
    half = grads.shape[1] // 2

    steps = grads.shape[0]

    def grad_copies(which):
        found = []
        chunk, place = divmod(which, steps // 2)
        outs = (keep1_ref, send1_ref) if chunk else (keep0_ref, send0_ref)
        for number, out in enumerate(outs):
            side = side_ref[0] if number == 0 else 1 - side_ref[0]
            here = grads.at[which, pl.ds(pl.multiple_of(side * half, half), half)]
            there = out.at[pl.ds(place * half, half)]
            found.append(pltpu.make_async_copy(here, there, grad_sems.at[which, number]))
        return found

    @pl.when(step == 0)
    def _():
        for start in range(0, rows, block):
            here = slice(start, start + block)
            inside = slice(start % item_rows, start % item_rows + block)
            att = att_refs[start // item_rows][inside, :]
            branch = dot(att, project_ref[...]) + project_bias_ref[...]
            x = hid_ref[here, :].astype(f32) + branch
            middle[here, :] = x
            unit, _ = normalise(x)
            feed[here, :] = (unit * gain_ref[...] + shift_ref[...]).astype(bf16)
            at = lax.broadcasted_iota(jnp.int32, (block, width), 0) + start % item_rows
            limit = jnp.where(flag_ref[0] == 1, item_rows, count_ref[start // item_rows])
            top[here, :] = jnp.where(at < limit, cot_ref[here, :].astype(f32), 0.0).astype(bf16)
            result[here, :] = x + reduce_bias_ref[...]
            gfeed[here, :] = jnp.zeros((block, width), f32)

    pieces, gvec_ref[pl.ds(4 + step, 1), :] = feed_step(
        step, rows, item_rows, feed, top, result, gfeed, expand_ref, ebias_ref, reduce_ref
    )
    store_pieces(grads.at[step], pieces)
    for which in range(steps):

        @pl.when(step == which)
        def _(which=which):
            for copy in grad_copies(which):
                copy.start()

    @pl.when(step == pl.num_programs(0) - 1)
    def _():
        copies = []
        sums = [jnp.zeros((1, width), f32)] * 4
        for number, start in enumerate(range(0, rows, block)):
            here = slice(start, start + block)
            low_out[here, :] = result[here, :].astype(bf16)
            unit, scale = normalise(middle[here, :])
            grad = gfeed[here, :]
            grad_top = top[here, :].astype(f32)
            gmid = grad_top + norm_transpose(unit, scale, gain_ref[...], grad)
            terms = (grad * unit, grad, grad_top, gmid)
            sums = [old + column_sum(new) for old, new in zip(sums, terms)]
            middle[here, :] = gmid
            gbranch = gmid.astype(bf16)
            feed[here, :] = gbranch
            gatt[here, :] = dot(gbranch, project_ref[...], NT).astype(bf16)
            for kind, (mine, there) in enumerate(
                ((low_out, out_ref), (middle, gmid_ref), (gatt, gatt_ref))
            ):
                span = pl.ds(start, block)
                copy = pltpu.make_async_copy(
                    mine.at[span, :], there.at[span, :], row_sems.at[kind, number]
                )
                copy.start()
                copies.append(copy)
        total = dot(att0_ref[...], feed[:item_rows, :], TN)
        total += dot(att1_ref[...], feed[item_rows:, :], TN)
        gproject_ref[...] = total.astype(bf16)
        gvec_ref[0:4, :] = jnp.concatenate(sums, axis=0)
        for copy in copies:
            copy.wait()
        for which in range(steps):
            for copy in grad_copies(which):
                copy.wait()


def feed_forward(order, flag, count, side, att0, att1, project, hidden, cotangent, vecs, expand, ebias, reduce):
    rows, width = hidden.shape
    item_rows = att0.shape[0]
    units = reduce.shape[0]
    steps = units // FF_BLOCK
    block_rows = 2 * width * FF_BLOCK // LANES
    fixed = (att0, att1, project, hidden, cotangent, *vecs)
    anywhere = pl.BlockSpec(memory_space=pl.ANY)
    return call(
        order,
        functools.partial(feed_kernel, item_rows=item_rows),
        (*fixed, expand, ebias, reduce),
        [
            shaped((rows, width), bf16),
            shaped((rows, width), f32),
            shaped((rows, width), bf16),
            shaped((width, width), bf16),
            shaped((4 + steps, width), f32),
        ]
        + [shaped((steps // 2 * block_rows // 2, LANES), bf16)] * 4,
        "feed_forward",
        cost(12 * rows * width * units, 40 << 20, 2 * rows * units),
        scalars=(flag, count, side),
        grid=(steps,),
        specs=[resident(value.shape) for value in fixed]
        + [
            pl.BlockSpec((width, FF_BLOCK), lambda j, *_: (0, j)),
            pl.BlockSpec((1, FF_BLOCK), lambda j, *_: (0, j)),
            pl.BlockSpec((FF_BLOCK, width), lambda j, *_: (j, 0)),
        ],
        outs=[
            anywhere,
            anywhere,
            anywhere,
            resident((width, width)),
            resident((4 + steps, width)),
        ]
        + [anywhere] * 4,
        scratch=[
            pltpu.VMEM((rows, width), f32),
            pltpu.VMEM((rows, width), bf16),
            pltpu.VMEM((rows, width), bf16),
            pltpu.VMEM((rows, width), f32),
            pltpu.VMEM((rows, width), f32),
            pltpu.VMEM((rows, width), bf16),
            pltpu.VMEM((rows, width), bf16),
            pltpu.VMEM((steps, block_rows, LANES), bf16),
            pltpu.SemaphoreType.DMA((steps, 2)),
            pltpu.SemaphoreType.DMA((3, rows // 256)),
        ],
    )


def weight_kernel(
    spare,
    side_ref,
    normed_ref,
    image_ref,
    gq_ref,
    gk_ref,
    gv_ref,
    gik_ref,
    giv_ref,
    *refs,
):
    extra_ref = None if spare else refs[0]
    sums_ref, keep_ref, send_ref, keep, send, sems = refs[-6:]
    step = pl.program_id(0)
    width = normed_ref.shape[1]
    half = width // 2
    columns = gq_ref.shape[1] // LANES
    block = half * (columns if spare else columns + 1)

    def copies(part):
        span = pl.ds(part * block, block if part < 3 else spare)
        pairs = ((keep, keep_ref), (send, send_ref))
        return [
            pltpu.make_async_copy(here.at[span], there.at[span], sems.at[number, part])
            for number, (here, there) in enumerate(pairs)
        ]

    def store(part, total):
        if extra_ref is not None:
            more = extra_ref[:, part * LANES : (part + 1) * LANES].astype(f32)
            total = jnp.concatenate([total, more], axis=1)
        first = side_ref[0] == 0
        mine = jnp.where(first, total[:half], total[half:]).astype(bf16)
        other = jnp.where(first, total[half:], total[:half]).astype(bf16)
        for number in range(block // half):
            rows = slice(part * block + number * half, part * block + (number + 1) * half)
            cols = slice(number * LANES, (number + 1) * LANES)
            keep[rows, :] = mine[:, cols]
            send[rows, :] = other[:, cols]
        for copy in copies(part):
            copy.start()

    @pl.when(step == 0)
    def _():
        store(0, dot(normed_ref[...], gq_ref[...], TN))
        sums_ref[0:1] = column_sum(gq_ref[...].astype(f32))

    @pl.when(step == 1)
    def _():
        total = dot(normed_ref[...], gk_ref[...], TN)
        store(1, total + dot(image_ref[...], gik_ref[...], TN))

    @pl.when(step == 2)
    def _():
        total = dot(normed_ref[...], gv_ref[...], TN)
        store(2, total + dot(image_ref[...], giv_ref[...], TN))
        sums = column_sum(gv_ref[...].astype(f32)) + column_sum(giv_ref[...].astype(f32))
        sums_ref[1:2] = sums
        if spare:
            keep[3 * block :, :] = jnp.zeros((spare, LANES), bf16)
            send[3 * block :, :] = jnp.zeros((spare, LANES), bf16)
            for copy in copies(3):
                copy.start()
        for part in range(4 if spare else 3):
            for copy in copies(part):
                copy.wait()


def weight_grads(order, side, normed, image, grads, lanes, place, spare, extra):
    rows, width = normed.shape
    half_rows = 3 * (lanes // LANES + len(extra)) * width // 2 + spare
    column = lambda height: pl.BlockSpec((height, lanes), lambda *_: (0, place))
    anywhere = pl.BlockSpec(memory_space=pl.ANY)
    return call(
        order,
        functools.partial(weight_kernel, spare),
        (normed, image, *grads, *extra),
        [shaped((2, lanes), f32)] + [shaped((half_rows, LANES), bf16)] * 2,
        "weight_grads",
        weighed(cost(8 * rows * width * lanes, 12 << 20)),
        scalars=(side,),
        grid=(3,),
        specs=[resident(normed.shape), resident(image.shape)]
        + [column(value.shape[0]) for value in grads]
        + [resident(value.shape) for value in extra],
        outs=[resident((2, lanes)), anywhere, anywhere],
        scratch=[pltpu.VMEM((half_rows, LANES), bf16)] * 2 + [pltpu.SemaphoreType.DMA((2, 4))],
    )


def image_grad_kernel(keys_weight, values_weight, keys_ref, values_ref, out_ref):
    total = dot(keys_ref[...], keys_weight[...], NT) + dot(values_ref[...], values_weight[...], NT)
    out_ref[...] = total.astype(bf16)


def image_grads(order, weight, keys, values):
    rows, width = keys.shape
    part = lambda base: pl.BlockSpec((width, width), lambda *_: (0, base))
    return call(
        order,
        image_grad_kernel,
        (weight, weight, keys, values),
        [shaped((rows, width), bf16)],
        "image_grads",
        weighed(cost(4 * rows * width * width, 6 << 20)),
        grid=(1,),
        specs=[part(1), part(2), resident(keys.shape), resident(values.shape)],
        outs=[resident((rows, width))],
    )


def finish_kernel(
    flag_ref,
    hid_ref,
    gmid_ref,
    near_ref,
    far_ref,
    gq_ref,
    gk_ref,
    gv_ref,
    gain_ref,
    weight_ref,
    feed_sums_ref,
    first_sums_ref,
    last_sums_ref,
    _,
    out_ref,
    small_ref,
    sums,
):
    item, block = pl.program_id(0), pl.program_id(1)
    joined = jnp.concatenate([gq_ref[...], gk_ref[...], gv_ref[...]], axis=1)
    grad = dot(joined, weight_ref[...], NT)
    unit, scale = normalise(hid_ref[...].astype(f32))
    both = near_ref[...].astype(f32) + far_ref[...].astype(f32)
    grad = grad + jnp.where((flag_ref[0] == 0) & (block == 0), both, 0.0)
    total = gmid_ref[...] + norm_transpose(unit, scale, gain_ref[...], grad)
    out_ref[...] = total.astype(bf16)
    found = jnp.concatenate([column_sum(grad * unit), column_sum(grad)], axis=0)

    @pl.when((item == 0) & (block == 0))
    def _():
        sums[...] = jnp.zeros(sums.shape, f32)

    sums[0:2] += found

    @pl.when((item == pl.num_programs(0) - 1) & (block == pl.num_programs(1) - 1))
    def _():
        width = sums.shape[1]
        pad = lambda count: jnp.zeros((count, width), f32)
        own = [sums[0:2], feed_sums_ref[0:3], feed_sums_ref[4:8], pad(7)]
        own = jnp.concatenate(own, axis=0)
        bias_sums = jnp.concatenate([first_sums_ref[...], last_sums_ref[...]], axis=1)
        shared = [pad(9), feed_sums_ref[3:4], bias_sums, pad(4)]
        shared = jnp.concatenate(shared, axis=0)
        is_text = flag_ref[0] == 1
        first = jnp.where(is_text, 0.0, own) + shared
        rows = jnp.concatenate([first, jnp.where(is_text, own, 0.0)], axis=0).astype(bf16)
        count = rows.shape[0]
        for number in range(width // LANES):
            cols = slice(number * LANES, (number + 1) * LANES)
            small_ref[number * count : (number + 1) * count, :] = rows[:, cols]
        small_ref[width // LANES * count :, :] = jnp.zeros((SMALL - width // LANES * count, LANES), bf16)


def finish_rows(
    order, flag, hidden, gmid, near, far, grads, gain, weight, feed_sums, bias_sums, keep, item_rows
):
    rows, width = hidden.shape
    blocks = item_rows // IMG_PAD
    mine = pl.BlockSpec((IMG_PAD, width), lambda i, j, *_: (i * blocks + j, 0))
    image = pl.BlockSpec((IMG_PAD, width), lambda i, j, *_: (i, 0))
    fixed = (gain, weight, feed_sums, *bias_sums)
    place = keep.shape[0] // SMALL - 1
    return call(
        order,
        finish_kernel,
        (hidden, gmid, near, far, *grads, *fixed, keep),
        [shaped((rows, width), bf16), shaped(keep.shape, bf16)],
        "finish_rows",
        weighed(cost(6 * rows * width * width, 16 << 20)),
        scalars=(flag,),
        grid=(rows // item_rows, blocks),
        specs=[mine, mine, image, image, mine, mine, mine]
        + [resident(value.shape) for value in fixed]
        + [pl.BlockSpec(memory_space=pl.ANY)],
        outs=[mine, pl.BlockSpec((SMALL, LANES), lambda *_: (place, 0))],
        scratch=[pltpu.VMEM((8, width), f32)],
        aliases={13: 1},
    )


def expert_kernel(half_ref, value_ref, *refs):
    at = 0
    for out in refs[-2:]:
        tall = out.shape[0]
        for part in range(out.shape[1] // LANES):
            piece = value_ref[at : at + tall, :]
            out[:, part * LANES : (part + 1) * LANES] = piece.astype(f32)
            at += tall


def expert_outputs(order, half, first, value, width, units, earlier):
    tall = width // 2
    block_rows = 2 * width // LANES * tall
    return call(
        order,
        expert_kernel,
        (value, *earlier),
        [shaped((units, width), f32), shaped((width, units), f32)],
        "expert_outputs",
        cost(value.size, 6 * value.size),
        scalars=(half,),
        grid=(value.shape[0] // block_rows,),
        specs=[pl.BlockSpec((block_rows, LANES), lambda i, at: (i, 0))]
        + [pl.BlockSpec(memory_space=pl.ANY)] * len(earlier),
        outs=[
            pl.BlockSpec((tall, width), lambda i, at: (2 * (first + i) + at[0], 0)),
            pl.BlockSpec((tall, width), lambda i, at: (at[0], first + i)),
        ],
        aliases={2: 0, 3: 1} if earlier else None,
    )


def first_kernel(half_ref, value_ref, *refs):
    in_ref, out_ref, wide, narrow, sems = refs[-5:]
    tall = wide.shape[1]
    count = value_ref.shape[0] // tall // 3
    columns = in_ref.shape[1] // 3
    rows = pl.ds(pl.multiple_of(half_ref[0] * tall, tall), tall)
    copies = []
    for part in range(3):
        at = part * count * tall
        for number in range(count - 1):
            piece = value_ref[at + number * tall : at + (number + 1) * tall, :]
            wide[part, :, number * LANES : (number + 1) * LANES] = piece.astype(f32)
        piece = value_ref[at + (count - 1) * tall : at + count * tall, :]
        narrow[part] = piece.astype(f32)
        places = (
            (wide, in_ref.at[rows, pl.ds(part * columns, (count - 1) * LANES)]),
            (narrow, out_ref.at[rows, pl.ds(part * LANES, LANES)]),
        )
        for kind, (here, there) in enumerate(places):
            copy = pltpu.make_async_copy(here.at[part], there, sems.at[kind, part])
            copy.start()
            copies.append(copy)
    for copy in copies:
        copy.wait()


def first_outputs(order, half, value, width, earlier):
    tall = width // 2
    anywhere = pl.BlockSpec(memory_space=pl.ANY)
    return call(
        order,
        first_kernel,
        (value, *earlier),
        [shaped((width, 3 * width), f32), shaped((width, width), f32)],
        "first_outputs",
        cost(value.size, 6 * value.size),
        scalars=(half,),
        grid=(1,),
        specs=[resident(value.shape)] + [anywhere] * len(earlier),
        outs=[anywhere, anywhere],
        scratch=[
            pltpu.VMEM((3, tall, width - LANES), f32),
            pltpu.VMEM((3, tall, LANES), f32),
            pltpu.SemaphoreType.DMA((2, 3)),
        ],
        aliases={2: 0, 3: 1} if earlier else None,
    )


def last_kernel(side_ref, flag_ref, mine_ref, got_ref, *refs):
    in_ref, *vec_refs, expand_ref, pair_ref, project_ref, columns, sems = refs[1:]
    tall = columns.shape[2]
    width = in_ref.shape[1] // 3
    copies = []
    for number, ref in enumerate((mine_ref, got_ref)):
        half = side_ref[0] if number == 0 else 1 - side_ref[0]
        rows = pl.ds(pl.multiple_of(half * tall, tall), tall)
        for part in range(3):
            columns[number, part] = ref[part * tall : (part + 1) * tall, :].astype(f32)
            there = in_ref.at[rows, pl.ds((part + 1) * width - LANES, LANES)]
            copy = pltpu.make_async_copy(columns.at[number, part], there, sems.at[number, part])
            copy.start()
            copies.append(copy)
    both = mine_ref[3 * tall :, :].astype(f32) + got_ref[3 * tall :, :].astype(f32)
    rows = jnp.concatenate([both[at * 32 : (at + 1) * 32] for at in range(width // LANES)], axis=1)
    own = jnp.where(flag_ref[0] == 1, rows[16:], rows[:16])
    for number, ref in enumerate(vec_refs):
        ref[...] = own[number : number + 1]
    for number in range(expand_ref.shape[1] // width):
        cols = slice(number * width, (number + 1) * width)
        expand_ref[:, cols] = own[5 + number : 6 + number]
    project_ref[...] = rows[9]
    pair_ref[...] = rows[10:12]
    for copy in copies:
        copy.wait()


def last_outputs(order, side, flag, mine, got, width, units, earlier):
    vecs = [(1, width)] * 5 + [(1, units), (2, width), (width,)]
    anywhere = pl.BlockSpec(memory_space=pl.ANY)
    return call(
        order,
        last_kernel,
        (mine, got, earlier),
        [shaped((width, 3 * width), f32)] + [shaped(shape, f32) for shape in vecs],
        "last_outputs",
        cost(got.size, 6 * got.size),
        scalars=(side, flag),
        grid=(1,),
        specs=[resident(mine.shape), resident(got.shape), anywhere],
        outs=[anywhere] + [resident(shape) for shape in vecs],
        scratch=[
            pltpu.VMEM((2, 3, width // 2, LANES), f32),
            pltpu.SemaphoreType.DMA((2, 3)),
        ],
        aliases={4: 0},
    )


def swap(value, axes, pair_of):
    count = 1
    for axis in axes:
        count *= lax.axis_size(axis)
    return lax.ppermute(value, axes, [(source, pair_of(source)) for source in range(count)])


def place_of(axes):
    place = 0
    for axis in axes:
        place = place * lax.axis_size(axis) + lax.axis_index(axis)
    return place


def late_stages(axes):
    stages = stage_bits(axes)
    if len(axes) == 2 and len(stages) == 5:
        return [stages[0], (0, 0), (2, 3), (3, 2), (4, 4)]
    return stages


def stage_bits(axes):
    count = 1
    for axis in axes:
        count *= lax.axis_size(axis)
    bits = count.bit_length() - 1
    core = len(axes) - 1
    others = [bit for bit in range(bits) if bit != core]
    if len(axes) == 1 and len(others) == 3:
        return [(core, core), (1, 2), (3, 1), (2, 3)]
    if len(axes) == 2 and len(others) == 4:
        return [(core, core), (0, 2), (2, 0), (3, 3), (4, 4)]
    return [(core, core)] + list(zip(others, others[1:] + others[:1]))


class Total:
    def __init__(self, order, axes, keep, send, stages=None):
        self.order = order
        self.axes = axes
        self.core = len(axes) - 1
        self.left = list(stages or stage_bits(axes))
        place = place_of(axes)
        second = ((place >> self.core) & 1) == 1
        sides = [(place >> jnp.where(second, pair[1], pair[0])) & 1 for pair in self.left]
        self.sides = dict(zip(self.left, sides))
        self.back = list(self.left)
        self.terms = (keep, self.exchange(send, self.left.pop(0)))
        self.mine = None

    def exchange(self, value, pair):
        other = lambda source: source ^ (1 << pair[(source >> self.core) & 1])
        self.got = swap(value, self.axes, other)
        return self.got

    def part(self, which, half):
        cut = lambda term: lax.dynamic_slice_in_dim(term, which * half, half, 0).astype(f32)
        return (cut(self.terms[0]) + cut(self.terms[1])).astype(bf16)

    def finish(self):
        while self.left or self.back:
            self.step()

    def step(self):
        if self.left:
            pair = self.left.pop(0)
            self.terms = self.order.after(*self.terms)
            half = self.terms[0].shape[0] // 2
            side = self.sides[pair]
            sent = self.part(1 - side, half)
            self.terms = (self.part(side, half), self.exchange(sent, pair))
            self.order.last = sent
            return
        pair = self.back.pop()
        if self.mine is None:
            self.terms = self.order.after(*self.terms)
            self.mine = (self.terms[0].astype(f32) + self.terms[1].astype(f32)).astype(bf16)
        else:
            mine, got = self.order.after(self.mine, self.got)
            low = jnp.where(self.last == 0, mine, got)
            high = jnp.where(self.last == 0, got, mine)
            self.mine = jnp.concatenate([low, high], axis=0)
        self.order.last = self.mine
        self.last = self.sides[pair]
        self.exchange(self.mine, pair)


def on_device(
    hidden_in,
    image_count,
    text_lengths,
    attend_gain,
    attend_shift,
    project_in,
    bias_pair,
    project_out,
    project_bias,
    feed_gain,
    feed_shift,
    expand_weight,
    expand_bias,
    reduce_weight,
    reduce_bias,
    cotangent,
):
    items, _, rows, width = hidden_in.shape
    units = expand_weight.shape[2]
    is_text = lax.axis_index("mod") == 1
    flag = is_text.astype(jnp.int32)[None]
    hidden = hidden_in.reshape(items * rows, width)
    to_text = lambda value: lax.ppermute(value, "mod", [(0, 1)])
    to_image = lambda value: lax.ppermute(value, "mod", [(1, 0)])

    far_rows = [to_text(hidden_in[item, 0, :IMG_PAD]) for item in range(items)]
    far_vecs = to_text(jnp.concatenate([attend_gain, attend_shift], axis=0))
    order = Order()
    normed, projected = project_rows(
        order, hidden, attend_gain, attend_shift, project_in, bias_pair
    )
    scalars = (flag, image_count, text_lengths)
    images, attended, lses = (), [], []
    for item in range(items):
        images = image_rows(
            order,
            flag,
            item,
            hidden,
            far_rows[item],
            attend_gain,
            attend_shift,
            far_vecs,
            project_in,
            bias_pair,
            rows,
            items,
            images,
        )
        out, lse = attend_forward(order, scalars, item, projected, images[1])
        attended.append(out)
        lses.append(lse)

    side = (lax.axis_index("dp") & 1)[None]
    (
        hidden_out,
        grad_middle,
        grad_attended,
        project_out_grad,
        feed_sums,
        keep0,
        send0,
        keep1,
        send1,
    ) = feed_forward(
        order,
        flag,
        image_count,
        side,
        attended[0],
        attended[1],
        project_out,
        hidden,
        cotangent.reshape(items * rows, width),
        (project_bias[None], feed_gain, feed_shift, reduce_bias),
        expand_weight[0],
        expand_bias,
        reduce_weight[0],
    )
    a = Total(order, ("dp",), keep0, send0)
    c = Total(order, ("dp",), keep1, send1)
    grads = ()

    def backward(item, start, pairs):
        return attend_backward(
            order,
            scalars,
            item,
            start,
            pairs,
            projected,
            images[1],
            attended[item],
            grad_attended,
            lses[item],
            grads,
        )

    def weights(lanes, place, spare, *extra):
        return weight_grads(
            order, side, normed, images[0], grads, lanes, place, spare, extra
        )

    def unpack(half, first, value, earlier=()):
        return expert_outputs(order, half, first, value, width, units, earlier)

    grads = backward(0, 0, 2)
    a.step()
    grads = backward(1, 0, 2)
    c.step()
    grads = backward(0, 2, 2)
    a.step()
    grads = backward(1, 2, 2)
    c.step()
    first_sums, keep, send = weights(2 * LANES, 0, 0, project_out_grad)
    s = Total(order, ("dp", "mod"), keep, send)
    a.step()
    grads = backward(0, 4, 2)
    s.step()
    a.step()
    grads = backward(1, 4, 2)
    c.step()
    s.step()
    near = image_grads(order, project_in, grads[3], grads[4])
    far = to_image(near)
    c.step()
    a.step()
    last_sums, keep, send = weights(LANES, 2, SMALL)
    p = Total(order, ("dp", "mod"), keep, send, late_stages(("dp", "mod")))
    s.step()
    c.step()
    a.step()
    (far,) = order.after(far)
    order.last = far
    grad_in, keep = finish_rows(
        order,
        flag,
        hidden,
        grad_middle,
        near,
        far,
        grads[:3],
        attend_gain,
        project_in,
        feed_sums,
        (first_sums, last_sums),
        keep,
        rows,
    )
    p.terms = (keep, p.got)
    p.step()
    s.step()
    a.step()
    p.step()
    c.step()
    p.step()
    s.step()
    a.finish()
    outputs = unpack(side, 0, a.mine)
    p.step()
    s.step()
    p.step()
    outputs = unpack(1 - side, 0, a.got, outputs)
    p.step()
    s.step()
    c.step()
    p.step()
    s.step()
    c.finish()
    outputs = unpack(side, 2, c.mine, outputs)
    p.step()
    s.step()
    reduce_grad, expand_grad = unpack(1 - side, 2, c.got, outputs)
    s.finish()
    projections = first_outputs(order, side, s.mine, width, ())
    project_in_grad, project_out_grad = first_outputs(order, 1 - side, s.got, width, projections)
    p.finish()
    (
        project_in_grad,
        attend_gain_grad,
        attend_shift_grad,
        feed_gain_grad,
        feed_shift_grad,
        reduce_bias_grad,
        expand_bias_grad,
        bias_pair_grad,
        project_bias_grad,
    ) = last_outputs(order, side, flag, p.mine, p.got, width, units, project_in_grad)
    return (
        hidden_out.reshape(hidden_in.shape),
        grad_in.reshape(hidden_in.shape),
        attend_gain_grad,
        attend_shift_grad,
        project_in_grad,
        bias_pair_grad,
        project_out_grad,
        project_bias_grad,
        feed_gain_grad,
        feed_shift_grad,
        expand_grad[None],
        expand_bias_grad,
        reduce_grad[None],
        reduce_bias_grad,
    )


def solution(mesh):
    in_specs = (
        P("dp", "mod", None, None),
        P("dp"),
        P("dp", None),
        P("mod", None),
        P("mod", None),
        P(),
        P(),
        P(),
        P(),
        P("mod", None),
        P("mod", None),
        P("mod", None, None),
        P("mod", None),
        P("mod", None, None),
        P("mod", None),
        P("dp", "mod", None, None),
    )
    out_specs = (
        P("dp", "mod", None, None),
        P("dp", "mod", None, None),
        P("mod", None),
        P("mod", None),
        P(),
        P(),
        P(),
        P(),
        P("mod", None),
        P("mod", None),
        P("mod", None, None),
        P("mod", None),
        P("mod", None, None),
        P("mod", None),
    )
    return jax.shard_map(
        on_device, mesh=mesh, in_specs=in_specs, out_specs=out_specs, check_vma=False
    )
```

```python
import functools

import jax
import jax.numpy as jnp
from jax import lax
from jax.experimental import pallas as pl
from jax.experimental.pallas import tpu as pltpu
from jax.sharding import PartitionSpec as P

HEADS = 12
HEAD = 64
IMG_PAD = 256
PAIR = 2 * HEAD
PAIRS = HEADS // 2
GROUP_PAIRS = 2
GROUPS = PAIRS // GROUP_PAIRS
LANES = GROUP_PAIRS * PAIR
SMALL = 128
FF_BLOCK = 768

masked_value = -1e30
norm_eps = 1e-05

bf16 = jnp.bfloat16
f32 = jnp.float32

NN = (((1,), (0,)), ((), ()))
NT = (((1,), (1,)), ((), ()))
TN = (((0,), (0,)), ((), ()))
VMEM_BYTES = 56 << 20


def dot(left, right, dims=NN):
    return lax.dot_general(left, right, dims, preferred_element_type=f32)


def column_sum(values):
    return jnp.sum(values, axis=0, keepdims=True)


def row_mean(values):
    return jnp.mean(values, axis=1, keepdims=True)


def normalise(values):
    centred = values - row_mean(values)
    scale = lax.rsqrt(row_mean(centred * centred) + norm_eps)
    return centred * scale, scale


def norm_transpose(unit, scale, gain, grad):
    grad_unit = grad * gain
    return scale * (grad_unit - row_mean(grad_unit) - unit * row_mean(grad_unit * unit))


def cost(flops, moved, special=0):
    return pl.CostEstimate(flops=flops, bytes_accessed=moved, transcendentals=special)


def weighed(estimate):
    return pl.CostEstimate(
        flops=10 * estimate.flops,
        bytes_accessed=10 * estimate.bytes_accessed,
        transcendentals=10 * estimate.transcendentals,
    )


class Order:
    def __init__(self):
        self.last = None

    def after(self, *values):
        if self.last is None:
            return values
        *values, _ = lax.optimization_barrier((*values, self.last))
        return values


def call(order, kernel, inputs, out_shape, name, estimate, scalars=(), grid=(), specs=None, outs=None,
         scratch=(), aliases=None):
    inputs = (*order.after(inputs[0]), *inputs[1:])
    vmem = pl.BlockSpec(memory_space=pltpu.VMEM)
    found = pl.pallas_call(
        kernel,
        grid_spec=pltpu.PrefetchScalarGridSpec(
            num_scalar_prefetch=len(scalars),
            grid=grid,
            in_specs=[vmem] * len(inputs) if specs is None else list(specs),
            out_specs=[vmem] * len(out_shape) if outs is None else list(outs),
            scratch_shapes=list(scratch),
        ),
        out_shape=list(out_shape),
        input_output_aliases=aliases or {},
        compiler_params=pltpu.CompilerParams(vmem_limit_bytes=VMEM_BYTES),
        cost_estimate=estimate,
        name=name,
    )(*scalars, *inputs)
    order.last = found[-1]
    return found if len(found) > 1 else found[0]


def shaped(shape, dtype):
    return jax.ShapeDtypeStruct(shape, dtype)


def resident(shape):
    return pl.BlockSpec(shape, lambda *_: (0,) * len(shape), pipeline_mode=pl.Buffered(1))


def project_kernel(hid_ref, gain_ref, shift_ref, weight_ref, bias_ref, normed_ref, out_ref):
    unit, _ = normalise(hid_ref[...].astype(f32))
    normed = (unit * gain_ref[...] + shift_ref[...]).astype(bf16)
    normed_ref[...] = normed
    width = normed.shape[1]
    for part in range(3):
        cols = slice(part * width, (part + 1) * width)
        rows = dot(normed, weight_ref[:, cols])
        if part == 0:
            rows = (rows + bias_ref[0:1]).astype(bf16) * jnp.asarray(HEAD**-0.5, bf16)
        if part == 2:
            rows = rows + bias_ref[1:2]
        out_ref[:, cols] = rows.astype(bf16)


def project_rows(order, hidden, gain, shift, weight, bias):
    rows, width = hidden.shape
    block = 256
    blocked = lambda cols: pl.BlockSpec((block, cols), lambda r: (r, 0))
    inputs = (hidden, gain, shift, weight, bias)
    return call(
        order,
        project_kernel,
        inputs,
        [shaped((rows, width), bf16), shaped((rows, 3 * width), bf16)],
        "project_rows",
        cost(6 * rows * width * width, 10 * rows * width + 6 * width * width),
        grid=(rows // block,),
        specs=[blocked(width)] + [resident(value.shape) for value in inputs[1:]],
        outs=[blocked(width), blocked(3 * width)],
    )


def image_kernel(
    flag_ref,
    own_ref,
    far_ref,
    gain_ref,
    shift_ref,
    vec_ref,
    keys_ref,
    values_ref,
    bias_ref,
    *refs,
):
    normed_ref, out_ref = refs[-2:]
    is_text = flag_ref[0] == 1
    hidden = jnp.where(is_text, far_ref[...].astype(f32), own_ref[...].astype(f32))
    gain = jnp.where(is_text, vec_ref[0:1], gain_ref[...])
    shift = jnp.where(is_text, vec_ref[1:2], shift_ref[...])
    unit, _ = normalise(hidden)
    normed = (unit * gain + shift).astype(bf16)
    normed_ref[...] = normed
    width = normed.shape[1]
    out_ref[:, :width] = dot(normed, keys_ref[...]).astype(bf16)
    out_ref[:, width:] = (dot(normed, values_ref[...]) + bias_ref[1:2]).astype(bf16)


def image_rows(
    order, flag, item, hidden, far, gain, shift, vecs, weight, bias, item_rows, items, earlier
):
    width = hidden.shape[1]
    place = item * (item_rows // IMG_PAD)
    half = lambda base: pl.BlockSpec((width, width), lambda *_: (0, base))
    mine = lambda cols: pl.BlockSpec((IMG_PAD, cols), lambda *_: (item, 0))
    inputs = (hidden, far, gain, shift, vecs, weight, weight, bias, *earlier)
    return call(
        order,
        image_kernel,
        inputs,
        [shaped((items * IMG_PAD, width), bf16), shaped((items * IMG_PAD, 2 * width), bf16)],
        "image_rows",
        cost(4 * IMG_PAD * width * width, 6 << 20),
        scalars=(flag,),
        grid=(1,),
        specs=[
            pl.BlockSpec((IMG_PAD, width), lambda *_: (place, 0)),
            resident(far.shape),
            resident(gain.shape),
            resident(shift.shape),
            resident(vecs.shape),
            half(1),
            half(2),
            resident(bias.shape),
        ]
        + [pl.BlockSpec(memory_space=pl.ANY)] * len(earlier),
        outs=[mine(width), mine(2 * width)],
        aliases={9: 0, 10: 1} if earlier else None,
    )


def segments(shape, axis, lengths_ref, item):
    places = lax.broadcasted_iota(jnp.int32, shape, axis)
    total = jnp.zeros(shape, jnp.int32)
    end = 0
    for which in range(lengths_ref.shape[1]):
        end = end + lengths_ref[item, which]
        total += (places >= end).astype(jnp.int32)
    return total


def own_bias(rows, flag_ref, lengths_ref, item):
    shape = (rows, rows)
    same = segments(shape, 0, lengths_ref, item) == segments(shape, 1, lengths_ref, item)
    return jnp.where(same & (flag_ref[0] == 1), 0.0, masked_value).astype(f32)


def image_bias(shape, axis, count_ref, item):
    places = lax.broadcasted_iota(jnp.int32, shape, axis)
    return jnp.where(places < count_ref[item], 0.0, masked_value).astype(f32)


def forward_kernel(
    item,
    flag_ref,
    count_ref,
    lengths_ref,
    q_ref,
    k_ref,
    v_ref,
    ik_ref,
    iv_ref,
    out_ref,
    lse_ref,
    image_part,
    own_part,
):
    rows = q_ref.shape[0]

    @pl.when(pl.program_id(0) == 0)
    def _():
        image_part[...] = image_bias(image_part.shape, 1, count_ref, item)
        own_part[...] = own_bias(rows, flag_ref, lengths_ref, item)

    first = lax.broadcasted_iota(jnp.int32, (rows, PAIR), 1) < HEAD
    zero = jnp.zeros((), bf16)
    q = q_ref[...]
    image_keys, image_values = ik_ref[...], iv_ref[...]
    keys, values = k_ref[...], v_ref[...]
    outs, tops = [], []
    for head in range(2):
        q_head = jnp.where(first, q, zero) if head == 0 else jnp.where(first, zero, q)
        far = dot(q_head, image_keys, NT) + image_part[...]
        own = dot(q_head, keys, NT) + own_part[...]
        top = jnp.maximum(
            jnp.max(far, axis=1, keepdims=True), jnp.max(own, axis=1, keepdims=True)
        )
        far = jnp.exp(far - top)
        own = jnp.exp(own - top)
        total = jnp.sum(far, axis=1, keepdims=True) + jnp.sum(own, axis=1, keepdims=True)
        summed = dot(far.astype(bf16), image_values) + dot(own.astype(bf16), values)
        outs.append(summed / total)
        tops.append(top + jnp.log(total))
    out_ref[...] = jnp.where(first, outs[0], outs[1]).astype(bf16)
    turned = jnp.transpose(jnp.where(first, tops[0], tops[1]))
    lse_ref[0, 0:1, :] = turned[0:1]
    lse_ref[0, 1:2, :] = turned[HEAD : HEAD + 1]


def attend_forward(order, scalars, item, projected, image):
    rows = projected.shape[0] // 2
    spec = lambda base: pl.BlockSpec((rows, PAIR), lambda h, *_: (item, base + h))
    far = lambda base: pl.BlockSpec((IMG_PAD, PAIR), lambda h, *_: (item, base + h))
    keys = rows + IMG_PAD
    return call(
        order,
        functools.partial(forward_kernel, item),
        (projected, projected, projected, image, image),
        [shaped((rows, HEADS * HEAD), bf16), shaped((PAIRS, 2, rows), f32)],
        "attend_forward",
        cost(16 * HEADS * rows * keys * HEAD, 6 << 20, HEADS * rows * keys),
        scalars=scalars,
        grid=(PAIRS,),
        specs=[spec(0), spec(PAIRS), spec(2 * PAIRS), far(0), far(PAIRS)],
        outs=[
            pl.BlockSpec((rows, PAIR), lambda h, *_: (0, h)),
            pl.BlockSpec((1, 2, rows), lambda h, *_: (h, 0, 0)),
        ],
        scratch=[pltpu.VMEM((rows, IMG_PAD), f32), pltpu.VMEM((rows, rows), f32)],
    )


def backward_kernel(
    item,
    flag_ref,
    count_ref,
    lengths_ref,
    q_ref,
    k_ref,
    v_ref,
    ik_ref,
    iv_ref,
    out_ref,
    grad_ref,
    lse_ref,
    *refs,
):
    gq_ref, gk_ref, gv_ref, gik_ref, giv_ref, image_part, own_part = refs[-7:]
    rows = q_ref.shape[0]

    @pl.when(pl.program_id(0) == 0)
    def _():
        image_part[...] = image_bias(image_part.shape, 0, count_ref, item)
        own_part[...] = own_bias(rows, flag_ref, lengths_ref, item)

    first = lax.broadcasted_iota(jnp.int32, (rows, PAIR), 1) < HEAD
    zero = jnp.zeros((), bf16)
    q, grad = q_ref[...], grad_ref[...]
    products = grad.astype(f32) * out_ref[...].astype(f32)
    head_lanes = lax.broadcasted_iota(jnp.int32, (8, PAIR), 1) // HEAD
    head_rows = lax.broadcasted_iota(jnp.int32, (8, PAIR), 0)
    center = lax.dot_general(
        (head_lanes == head_rows).astype(f32),
        products,
        NT,
        preferred_element_type=f32,
        precision=lax.Precision.HIGHEST,
    )
    q_heads = [jnp.where(first, q, zero), jnp.where(first, zero, q)]
    grad_heads = [jnp.where(first, grad, zero), jnp.where(first, zero, grad)]
    lse = lse_ref[0]
    grad_query = [None, None]
    half = rows // 2
    pieces = (
        (ik_ref, iv_ref, gik_ref, giv_ref, image_part, 0, IMG_PAD),
        (k_ref, v_ref, gk_ref, gv_ref, own_part, 0, half),
        (k_ref, v_ref, gk_ref, gv_ref, own_part, half, half),
    )
    for keys_ref, values_ref, gk_out, gv_out, bias, start, count in pieces:
        piece = slice(start, start + count)
        keys, values = keys_ref[piece, :], values_ref[piece, :]
        low_lanes = lax.broadcasted_iota(jnp.int32, (count, PAIR), 1) < HEAD
        grad_keys, grad_values = [], []
        for head in range(2):
            scores = dot(keys, q_heads[head], NT) + bias[piece, :]
            probs = jnp.exp(scores - lse[head : head + 1])
            grad_probs = dot(values, grad_heads[head], NT)
            grad_scores = (probs * (grad_probs - center[head : head + 1])).astype(bf16)
            grad_values.append(dot(probs.astype(bf16), grad))
            grad_keys.append(dot(grad_scores, q))
            term = dot(grad_scores, keys, TN)
            grad_query[head] = term if grad_query[head] is None else grad_query[head] + term
        gk_out[piece, :] = jnp.where(low_lanes, grad_keys[0], grad_keys[1]).astype(bf16)
        gv_out[piece, :] = jnp.where(low_lanes, grad_values[0], grad_values[1]).astype(bf16)
    gq_ref[...] = (jnp.where(first, grad_query[0], grad_query[1]) * HEAD**-0.5).astype(bf16)


def attend_backward(order, scalars, item, start, pairs, projected, image, attended, grad, lse, earlier):
    rows, width = attended.shape
    spec = lambda base: pl.BlockSpec((rows, PAIR), lambda h, *_: (item, base + start + h))
    far = lambda base: pl.BlockSpec((IMG_PAD, PAIR), lambda h, *_: (item, base + start + h))
    own = pl.BlockSpec((rows, PAIR), lambda h, *_: (0, start + h))
    far_outs = pl.BlockSpec((IMG_PAD, PAIR), lambda h, *_: (item, start + h))
    keys = rows + IMG_PAD
    inputs = (projected, projected, projected, image, image, attended, grad, lse)
    first = len(scalars) + len(inputs)
    return call(
        order,
        functools.partial(backward_kernel, item),
        (*inputs, *earlier),
        [shaped((2 * rows, width), bf16)] * 3 + [shaped((2 * IMG_PAD, width), bf16)] * 2,
        "attend_backward",
        weighed(cost(80 * pairs * rows * keys * HEAD, pairs * 2 << 20, 2 * pairs * rows * keys)),
        scalars=scalars,
        grid=(pairs,),
        specs=[
            spec(0),
            spec(PAIRS),
            spec(2 * PAIRS),
            far(0),
            far(PAIRS),
            own,
            spec(0),
            pl.BlockSpec((1, 2, rows), lambda h, *_: (start + h, 0, 0)),
        ]
        + [pl.BlockSpec(memory_space=pl.ANY)] * len(earlier),
        outs=[spec(0), spec(0), spec(0), far_outs, far_outs],
        scratch=[pltpu.VMEM((IMG_PAD, rows), f32), pltpu.VMEM((rows, rows), f32)],
        aliases={first + at: at for at in range(len(earlier))},
    )


def gelu_pair(values):
    share = 0.5 * (1.0 + lax.erf(values * 0.7071067811865476))
    slope = share + values * jnp.exp(-0.5 * values * values) * 0.3989422804014327
    return values * share, slope


def feed_step(step, rows, item_rows, feed, top, result, gfeed, expand_ref, ebias_ref, reduce_ref):
    width = feed.shape[1]
    expand, reduce = expand_ref[...], reduce_ref[...]
    active_parts, gup_parts = [], []
    for start in range(0, rows, item_rows):
        here = slice(start, start + item_rows)
        upward = dot(feed[here, :], expand) + ebias_ref[...]
        gactive = dot(top[here, :], reduce, NT)
        active, slope = gelu_pair(upward)
        active = active.astype(bf16)
        gup = (gactive * slope).astype(bf16)
        result[here, :] += dot(active, reduce)
        gfeed[here, :] += dot(gup, expand, NT)
        active_parts.append(active)
        gup_parts.append(gup)
    active = jnp.concatenate(active_parts, axis=0)
    gup = jnp.concatenate(gup_parts, axis=0)
    greduce = dot(active, top[...], TN).astype(bf16)
    gexpand = dot(feed[...], gup, TN).astype(bf16)
    pieces = [greduce[:, at : at + LANES] for at in range(0, width, LANES)]
    pieces += [gexpand[:, at : at + LANES] for at in range(0, FF_BLOCK, LANES)]
    return pieces, column_sum(gup.astype(f32))


def store_pieces(out, pieces):
    at = 0
    for half in range(2):
        for piece in pieces:
            rows = piece.shape[0] // 2
            out[at : at + rows, :] = piece[half * rows : (half + 1) * rows]
            at += rows


def feed_kernel(
    flag_ref,
    count_ref,
    side_ref,
    att0_ref,
    att1_ref,
    project_ref,
    hid_ref,
    cot_ref,
    project_bias_ref,
    gain_ref,
    shift_ref,
    reduce_bias_ref,
    expand_ref,
    ebias_ref,
    reduce_ref,
    out_ref,
    gmid_ref,
    gatt_ref,
    gproject_ref,
    gvec_ref,
    keep0_ref,
    send0_ref,
    keep1_ref,
    send1_ref,
    middle,
    feed,
    top,
    result,
    gfeed,
    low_out,
    gatt,
    grads,
    grad_sems,
    row_sems,
    *,
    item_rows,
):
    step = pl.program_id(0)
    rows, width = hid_ref.shape
    block = 256
    att_refs = (att0_ref, att1_ref)
    half = grads.shape[1] // 2

    steps = grads.shape[0]

    def grad_copies(which):
        found = []
        chunk, place = divmod(which, steps // 2)
        outs = (keep1_ref, send1_ref) if chunk else (keep0_ref, send0_ref)
        for number, out in enumerate(outs):
            side = side_ref[0] if number == 0 else 1 - side_ref[0]
            here = grads.at[which, pl.ds(pl.multiple_of(side * half, half), half)]
            there = out.at[pl.ds(place * half, half)]
            found.append(pltpu.make_async_copy(here, there, grad_sems.at[which, number]))
        return found

    @pl.when(step == 0)
    def _():
        for start in range(0, rows, block):
            here = slice(start, start + block)
            inside = slice(start % item_rows, start % item_rows + block)
            att = att_refs[start // item_rows][inside, :]
            branch = dot(att, project_ref[...]) + project_bias_ref[...]
            x = hid_ref[here, :].astype(f32) + branch
            middle[here, :] = x
            unit, _ = normalise(x)
            feed[here, :] = (unit * gain_ref[...] + shift_ref[...]).astype(bf16)
            at = lax.broadcasted_iota(jnp.int32, (block, width), 0) + start % item_rows
            limit = jnp.where(flag_ref[0] == 1, item_rows, count_ref[start // item_rows])
            top[here, :] = jnp.where(at < limit, cot_ref[here, :].astype(f32), 0.0).astype(bf16)
            result[here, :] = x + reduce_bias_ref[...]
            gfeed[here, :] = jnp.zeros((block, width), f32)

    pieces, gvec_ref[pl.ds(4 + step, 1), :] = feed_step(
        step, rows, item_rows, feed, top, result, gfeed, expand_ref, ebias_ref, reduce_ref
    )
    store_pieces(grads.at[step], pieces)
    for which in range(steps):

        @pl.when(step == which)
        def _(which=which):
            for copy in grad_copies(which):
                copy.start()

    @pl.when(step == pl.num_programs(0) - 1)
    def _():
        copies = []
        sums = [jnp.zeros((1, width), f32)] * 4
        for number, start in enumerate(range(0, rows, block)):
            here = slice(start, start + block)
            low_out[here, :] = result[here, :].astype(bf16)
            unit, scale = normalise(middle[here, :])
            grad = gfeed[here, :]
            grad_top = top[here, :].astype(f32)
            gmid = grad_top + norm_transpose(unit, scale, gain_ref[...], grad)
            terms = (grad * unit, grad, grad_top, gmid)
            sums = [old + column_sum(new) for old, new in zip(sums, terms)]
            middle[here, :] = gmid
            gbranch = gmid.astype(bf16)
            feed[here, :] = gbranch
            gatt[here, :] = dot(gbranch, project_ref[...], NT).astype(bf16)
            for kind, (mine, there) in enumerate(
                ((low_out, out_ref), (middle, gmid_ref), (gatt, gatt_ref))
            ):
                span = pl.ds(start, block)
                copy = pltpu.make_async_copy(
                    mine.at[span, :], there.at[span, :], row_sems.at[kind, number]
                )
                copy.start()
                copies.append(copy)
        total = dot(att0_ref[...], feed[:item_rows, :], TN)
        total += dot(att1_ref[...], feed[item_rows:, :], TN)
        gproject_ref[...] = total.astype(bf16)
        gvec_ref[0:4, :] = jnp.concatenate(sums, axis=0)
        for copy in copies:
            copy.wait()
        for which in range(steps):
            for copy in grad_copies(which):
                copy.wait()


def feed_forward(order, flag, count, side, att0, att1, project, hidden, cotangent, vecs, expand, ebias, reduce):
    rows, width = hidden.shape
    item_rows = att0.shape[0]
    units = reduce.shape[0]
    steps = units // FF_BLOCK
    block_rows = 2 * width * FF_BLOCK // LANES
    fixed = (att0, att1, project, hidden, cotangent, *vecs)
    anywhere = pl.BlockSpec(memory_space=pl.ANY)
    return call(
        order,
        functools.partial(feed_kernel, item_rows=item_rows),
        (*fixed, expand, ebias, reduce),
        [
            shaped((rows, width), bf16),
            shaped((rows, width), f32),
            shaped((rows, width), bf16),
            shaped((width, width), bf16),
            shaped((4 + steps, width), f32),
        ]
        + [shaped((steps // 2 * block_rows // 2, LANES), bf16)] * 4,
        "feed_forward",
        cost(12 * rows * width * units, 40 << 20, 2 * rows * units),
        scalars=(flag, count, side),
        grid=(steps,),
        specs=[resident(value.shape) for value in fixed]
        + [
            pl.BlockSpec((width, FF_BLOCK), lambda j, *_: (0, j)),
            pl.BlockSpec((1, FF_BLOCK), lambda j, *_: (0, j)),
            pl.BlockSpec((FF_BLOCK, width), lambda j, *_: (j, 0)),
        ],
        outs=[
            anywhere,
            anywhere,
            anywhere,
            resident((width, width)),
            resident((4 + steps, width)),
        ]
        + [anywhere] * 4,
        scratch=[
            pltpu.VMEM((rows, width), f32),
            pltpu.VMEM((rows, width), bf16),
            pltpu.VMEM((rows, width), bf16),
            pltpu.VMEM((rows, width), f32),
            pltpu.VMEM((rows, width), f32),
            pltpu.VMEM((rows, width), bf16),
            pltpu.VMEM((rows, width), bf16),
            pltpu.VMEM((steps, block_rows, LANES), bf16),
            pltpu.SemaphoreType.DMA((steps, 2)),
            pltpu.SemaphoreType.DMA((3, rows // 256)),
        ],
    )


def weight_kernel(
    spare,
    side_ref,
    normed_ref,
    image_ref,
    gq_ref,
    gk_ref,
    gv_ref,
    gik_ref,
    giv_ref,
    *refs,
):
    extra_ref = None if spare else refs[0]
    sums_ref, keep_ref, send_ref, keep, send, sems = refs[-6:]
    step = pl.program_id(0)
    width = normed_ref.shape[1]
    half = width // 2
    columns = gq_ref.shape[1] // LANES
    block = half * (columns if spare else columns + 1)

    def copies(part):
        span = pl.ds(part * block, block if part < 3 else spare)
        pairs = ((keep, keep_ref), (send, send_ref))
        return [
            pltpu.make_async_copy(here.at[span], there.at[span], sems.at[number, part])
            for number, (here, there) in enumerate(pairs)
        ]

    def store(part, total):
        if extra_ref is not None:
            more = extra_ref[:, part * LANES : (part + 1) * LANES].astype(f32)
            total = jnp.concatenate([total, more], axis=1)
        first = side_ref[0] == 0
        mine = jnp.where(first, total[:half], total[half:]).astype(bf16)
        other = jnp.where(first, total[half:], total[:half]).astype(bf16)
        for number in range(block // half):
            rows = slice(part * block + number * half, part * block + (number + 1) * half)
            cols = slice(number * LANES, (number + 1) * LANES)
            keep[rows, :] = mine[:, cols]
            send[rows, :] = other[:, cols]
        for copy in copies(part):
            copy.start()

    @pl.when(step == 0)
    def _():
        store(0, dot(normed_ref[...], gq_ref[...], TN))
        sums_ref[0:1] = column_sum(gq_ref[...].astype(f32))

    @pl.when(step == 1)
    def _():
        total = dot(normed_ref[...], gk_ref[...], TN)
        store(1, total + dot(image_ref[...], gik_ref[...], TN))

    @pl.when(step == 2)
    def _():
        total = dot(normed_ref[...], gv_ref[...], TN)
        store(2, total + dot(image_ref[...], giv_ref[...], TN))
        sums = column_sum(gv_ref[...].astype(f32)) + column_sum(giv_ref[...].astype(f32))
        sums_ref[1:2] = sums
        if spare:
            keep[3 * block :, :] = jnp.zeros((spare, LANES), bf16)
            send[3 * block :, :] = jnp.zeros((spare, LANES), bf16)
            for copy in copies(3):
                copy.start()
        for part in range(4 if spare else 3):
            for copy in copies(part):
                copy.wait()


def weight_grads(order, side, normed, image, grads, lanes, place, spare, extra):
    rows, width = normed.shape
    half_rows = 3 * (lanes // LANES + len(extra)) * width // 2 + spare
    column = lambda height: pl.BlockSpec((height, lanes), lambda *_: (0, place))
    anywhere = pl.BlockSpec(memory_space=pl.ANY)
    return call(
        order,
        functools.partial(weight_kernel, spare),
        (normed, image, *grads, *extra),
        [shaped((2, lanes), f32)] + [shaped((half_rows, LANES), bf16)] * 2,
        "weight_grads",
        weighed(cost(8 * rows * width * lanes, 12 << 20)),
        scalars=(side,),
        grid=(3,),
        specs=[resident(normed.shape), resident(image.shape)]
        + [column(value.shape[0]) for value in grads]
        + [resident(value.shape) for value in extra],
        outs=[resident((2, lanes)), anywhere, anywhere],
        scratch=[pltpu.VMEM((half_rows, LANES), bf16)] * 2 + [pltpu.SemaphoreType.DMA((2, 4))],
    )


def image_grad_kernel(keys_weight, values_weight, keys_ref, values_ref, out_ref):
    total = dot(keys_ref[...], keys_weight[...], NT) + dot(values_ref[...], values_weight[...], NT)
    out_ref[...] = total.astype(bf16)


def image_grads(order, weight, keys, values):
    rows, width = keys.shape
    part = lambda base: pl.BlockSpec((width, width), lambda *_: (0, base))
    return call(
        order,
        image_grad_kernel,
        (weight, weight, keys, values),
        [shaped((rows, width), bf16)],
        "image_grads",
        weighed(cost(4 * rows * width * width, 6 << 20)),
        grid=(1,),
        specs=[part(1), part(2), resident(keys.shape), resident(values.shape)],
        outs=[resident((rows, width))],
    )


def finish_kernel(
    flag_ref,
    hid_ref,
    gmid_ref,
    near_ref,
    far_ref,
    gq_ref,
    gk_ref,
    gv_ref,
    gain_ref,
    weight_ref,
    feed_sums_ref,
    first_sums_ref,
    last_sums_ref,
    _,
    out_ref,
    small_ref,
    sums,
):
    item, block = pl.program_id(0), pl.program_id(1)
    joined = jnp.concatenate([gq_ref[...], gk_ref[...], gv_ref[...]], axis=1)
    grad = dot(joined, weight_ref[...], NT)
    unit, scale = normalise(hid_ref[...].astype(f32))
    both = near_ref[...].astype(f32) + far_ref[...].astype(f32)
    grad = grad + jnp.where((flag_ref[0] == 0) & (block == 0), both, 0.0)
    total = gmid_ref[...] + norm_transpose(unit, scale, gain_ref[...], grad)
    out_ref[...] = total.astype(bf16)
    found = jnp.concatenate([column_sum(grad * unit), column_sum(grad)], axis=0)

    @pl.when((item == 0) & (block == 0))
    def _():
        sums[...] = jnp.zeros(sums.shape, f32)

    sums[0:2] += found

    @pl.when((item == pl.num_programs(0) - 1) & (block == pl.num_programs(1) - 1))
    def _():
        width = sums.shape[1]
        pad = lambda count: jnp.zeros((count, width), f32)
        own = [sums[0:2], feed_sums_ref[0:3], feed_sums_ref[4:8], pad(7)]
        own = jnp.concatenate(own, axis=0)
        bias_sums = jnp.concatenate([first_sums_ref[...], last_sums_ref[...]], axis=1)
        shared = [pad(9), feed_sums_ref[3:4], bias_sums, pad(4)]
        shared = jnp.concatenate(shared, axis=0)
        is_text = flag_ref[0] == 1
        first = jnp.where(is_text, 0.0, own) + shared
        rows = jnp.concatenate([first, jnp.where(is_text, own, 0.0)], axis=0).astype(bf16)
        count = rows.shape[0]
        for number in range(width // LANES):
            cols = slice(number * LANES, (number + 1) * LANES)
            small_ref[number * count : (number + 1) * count, :] = rows[:, cols]
        small_ref[width // LANES * count :, :] = jnp.zeros((SMALL - width // LANES * count, LANES), bf16)


def finish_rows(
    order, flag, hidden, gmid, near, far, grads, gain, weight, feed_sums, bias_sums, keep, item_rows
):
    rows, width = hidden.shape
    blocks = item_rows // IMG_PAD
    mine = pl.BlockSpec((IMG_PAD, width), lambda i, j, *_: (i * blocks + j, 0))
    image = pl.BlockSpec((IMG_PAD, width), lambda i, j, *_: (i, 0))
    fixed = (gain, weight, feed_sums, *bias_sums)
    place = keep.shape[0] // SMALL - 1
    return call(
        order,
        finish_kernel,
        (hidden, gmid, near, far, *grads, *fixed, keep),
        [shaped((rows, width), bf16), shaped(keep.shape, bf16)],
        "finish_rows",
        weighed(cost(6 * rows * width * width, 16 << 20)),
        scalars=(flag,),
        grid=(rows // item_rows, blocks),
        specs=[mine, mine, image, image, mine, mine, mine]
        + [resident(value.shape) for value in fixed]
        + [pl.BlockSpec(memory_space=pl.ANY)],
        outs=[mine, pl.BlockSpec((SMALL, LANES), lambda *_: (place, 0))],
        scratch=[pltpu.VMEM((8, width), f32)],
        aliases={13: 1},
    )


def expert_kernel(half_ref, value_ref, *refs):
    at = 0
    for out in refs[-2:]:
        tall = out.shape[0]
        for part in range(out.shape[1] // LANES):
            piece = value_ref[at : at + tall, :]
            out[:, part * LANES : (part + 1) * LANES] = piece.astype(f32)
            at += tall


def expert_outputs(order, half, first, value, width, units, earlier):
    tall = width // 2
    block_rows = 2 * width // LANES * tall
    return call(
        order,
        expert_kernel,
        (value, *earlier),
        [shaped((units, width), f32), shaped((width, units), f32)],
        "expert_outputs",
        cost(value.size, 6 * value.size),
        scalars=(half,),
        grid=(value.shape[0] // block_rows,),
        specs=[pl.BlockSpec((block_rows, LANES), lambda i, at: (i, 0))]
        + [pl.BlockSpec(memory_space=pl.ANY)] * len(earlier),
        outs=[
            pl.BlockSpec((tall, width), lambda i, at: (2 * (first + i) + at[0], 0)),
            pl.BlockSpec((tall, width), lambda i, at: (at[0], first + i)),
        ],
        aliases={2: 0, 3: 1} if earlier else None,
    )


def first_kernel(half_ref, value_ref, *refs):
    in_ref, out_ref, wide, narrow, sems = refs[-5:]
    tall = wide.shape[1]
    count = value_ref.shape[0] // tall // 3
    columns = in_ref.shape[1] // 3
    rows = pl.ds(pl.multiple_of(half_ref[0] * tall, tall), tall)
    copies = []
    for part in range(3):
        at = part * count * tall
        for number in range(count - 1):
            piece = value_ref[at + number * tall : at + (number + 1) * tall, :]
            wide[part, :, number * LANES : (number + 1) * LANES] = piece.astype(f32)
        piece = value_ref[at + (count - 1) * tall : at + count * tall, :]
        narrow[part] = piece.astype(f32)
        places = (
            (wide, in_ref.at[rows, pl.ds(part * columns, (count - 1) * LANES)]),
            (narrow, out_ref.at[rows, pl.ds(part * LANES, LANES)]),
        )
        for kind, (here, there) in enumerate(places):
            copy = pltpu.make_async_copy(here.at[part], there, sems.at[kind, part])
            copy.start()
            copies.append(copy)
    for copy in copies:
        copy.wait()


def first_outputs(order, half, value, width, earlier):
    tall = width // 2
    anywhere = pl.BlockSpec(memory_space=pl.ANY)
    return call(
        order,
        first_kernel,
        (value, *earlier),
        [shaped((width, 3 * width), f32), shaped((width, width), f32)],
        "first_outputs",
        cost(value.size, 6 * value.size),
        scalars=(half,),
        grid=(1,),
        specs=[resident(value.shape)] + [anywhere] * len(earlier),
        outs=[anywhere, anywhere],
        scratch=[
            pltpu.VMEM((3, tall, width - LANES), f32),
            pltpu.VMEM((3, tall, LANES), f32),
            pltpu.SemaphoreType.DMA((2, 3)),
        ],
        aliases={2: 0, 3: 1} if earlier else None,
    )


def last_kernel(side_ref, flag_ref, mine_ref, got_ref, *refs):
    in_ref, *vec_refs, expand_ref, pair_ref, project_ref, columns, sems = refs[1:]
    tall = columns.shape[2]
    width = in_ref.shape[1] // 3
    copies = []
    for number, ref in enumerate((mine_ref, got_ref)):
        half = side_ref[0] if number == 0 else 1 - side_ref[0]
        rows = pl.ds(pl.multiple_of(half * tall, tall), tall)
        for part in range(3):
            columns[number, part] = ref[part * tall : (part + 1) * tall, :].astype(f32)
            there = in_ref.at[rows, pl.ds((part + 1) * width - LANES, LANES)]
            copy = pltpu.make_async_copy(columns.at[number, part], there, sems.at[number, part])
            copy.start()
            copies.append(copy)
    both = mine_ref[3 * tall :, :].astype(f32) + got_ref[3 * tall :, :].astype(f32)
    rows = jnp.concatenate([both[at * 32 : (at + 1) * 32] for at in range(width // LANES)], axis=1)
    own = jnp.where(flag_ref[0] == 1, rows[16:], rows[:16])
    for number, ref in enumerate(vec_refs):
        ref[...] = own[number : number + 1]
    for number in range(expand_ref.shape[1] // width):
        cols = slice(number * width, (number + 1) * width)
        expand_ref[:, cols] = own[5 + number : 6 + number]
    project_ref[...] = rows[9]
    pair_ref[...] = rows[10:12]
    for copy in copies:
        copy.wait()


def last_outputs(order, side, flag, mine, got, width, units, earlier):
    vecs = [(1, width)] * 5 + [(1, units), (2, width), (width,)]
    anywhere = pl.BlockSpec(memory_space=pl.ANY)
    return call(
        order,
        last_kernel,
        (mine, got, earlier),
        [shaped((width, 3 * width), f32)] + [shaped(shape, f32) for shape in vecs],
        "last_outputs",
        cost(got.size, 6 * got.size),
        scalars=(side, flag),
        grid=(1,),
        specs=[resident(mine.shape), resident(got.shape), anywhere],
        outs=[anywhere] + [resident(shape) for shape in vecs],
        scratch=[
            pltpu.VMEM((2, 3, width // 2, LANES), f32),
            pltpu.SemaphoreType.DMA((2, 3)),
        ],
        aliases={4: 0},
    )


def swap(value, axes, pair_of):
    count = 1
    for axis in axes:
        count *= lax.axis_size(axis)
    return lax.ppermute(value, axes, [(source, pair_of(source)) for source in range(count)])


def place_of(axes):
    place = 0
    for axis in axes:
        place = place * lax.axis_size(axis) + lax.axis_index(axis)
    return place


def late_stages(axes):
    stages = stage_bits(axes)
    if len(axes) == 2 and len(stages) == 5:
        return [stages[0], (0, 0), (2, 3), (3, 2), (4, 4)]
    return stages


def stage_bits(axes):
    count = 1
    for axis in axes:
        count *= lax.axis_size(axis)
    bits = count.bit_length() - 1
    core = len(axes) - 1
    others = [bit for bit in range(bits) if bit != core]
    if len(axes) == 1 and len(others) == 3:
        return [(core, core), (1, 2), (3, 1), (2, 3)]
    if len(axes) == 2 and len(others) == 4:
        return [(core, core), (0, 2), (2, 0), (3, 3), (4, 4)]
    return [(core, core)] + list(zip(others, others[1:] + others[:1]))


class Total:
    def __init__(self, order, axes, keep, send, stages=None):
        self.order = order
        self.axes = axes
        self.core = len(axes) - 1
        self.left = list(stages or stage_bits(axes))
        place = place_of(axes)
        second = ((place >> self.core) & 1) == 1
        sides = [(place >> jnp.where(second, pair[1], pair[0])) & 1 for pair in self.left]
        self.sides = dict(zip(self.left, sides))
        self.back = list(self.left)
        self.terms = (keep, self.exchange(send, self.left.pop(0)))
        self.mine = None

    def exchange(self, value, pair):
        other = lambda source: source ^ (1 << pair[(source >> self.core) & 1])
        self.got = swap(value, self.axes, other)
        return self.got

    def part(self, which, half):
        cut = lambda term: lax.dynamic_slice_in_dim(term, which * half, half, 0).astype(f32)
        return (cut(self.terms[0]) + cut(self.terms[1])).astype(bf16)

    def finish(self):
        while self.left or self.back:
            self.step()

    def step(self):
        if self.left:
            pair = self.left.pop(0)
            self.terms = self.order.after(*self.terms)
            half = self.terms[0].shape[0] // 2
            side = self.sides[pair]
            sent = self.part(1 - side, half)
            self.terms = (self.part(side, half), self.exchange(sent, pair))
            self.order.last = sent
            return
        pair = self.back.pop()
        if self.mine is None:
            self.terms = self.order.after(*self.terms)
            self.mine = (self.terms[0].astype(f32) + self.terms[1].astype(f32)).astype(bf16)
        else:
            mine, got = self.order.after(self.mine, self.got)
            low = jnp.where(self.last == 0, mine, got)
            high = jnp.where(self.last == 0, got, mine)
            self.mine = jnp.concatenate([low, high], axis=0)
        self.order.last = self.mine
        self.last = self.sides[pair]
        self.exchange(self.mine, pair)


def on_device(
    hidden_in,
    image_count,
    text_lengths,
    attend_gain,
    attend_shift,
    project_in,
    bias_pair,
    project_out,
    project_bias,
    feed_gain,
    feed_shift,
    expand_weight,
    expand_bias,
    reduce_weight,
    reduce_bias,
    cotangent,
):
    items, _, rows, width = hidden_in.shape
    units = expand_weight.shape[2]
    is_text = lax.axis_index("mod") == 1
    flag = is_text.astype(jnp.int32)[None]
    hidden = hidden_in.reshape(items * rows, width)
    to_text = lambda value: lax.ppermute(value, "mod", [(0, 1)])
    to_image = lambda value: lax.ppermute(value, "mod", [(1, 0)])

    far_rows = [to_text(hidden_in[item, 0, :IMG_PAD]) for item in range(items)]
    far_vecs = to_text(jnp.concatenate([attend_gain, attend_shift], axis=0))
    order = Order()
    normed, projected = project_rows(
        order, hidden, attend_gain, attend_shift, project_in, bias_pair
    )
    scalars = (flag, image_count, text_lengths)
    images, attended, lses = (), [], []
    for item in range(items):
        images = image_rows(
            order,
            flag,
            item,
            hidden,
            far_rows[item],
            attend_gain,
            attend_shift,
            far_vecs,
            project_in,
            bias_pair,
            rows,
            items,
            images,
        )
        out, lse = attend_forward(order, scalars, item, projected, images[1])
        attended.append(out)
        lses.append(lse)

    side = (lax.axis_index("dp") & 1)[None]
    (
        hidden_out,
        grad_middle,
        grad_attended,
        project_out_grad,
        feed_sums,
        keep0,
        send0,
        keep1,
        send1,
    ) = feed_forward(
        order,
        flag,
        image_count,
        side,
        attended[0],
        attended[1],
        project_out,
        hidden,
        cotangent.reshape(items * rows, width),
        (project_bias[None], feed_gain, feed_shift, reduce_bias),
        expand_weight[0],
        expand_bias,
        reduce_weight[0],
    )
    a = Total(order, ("dp",), keep0, send0)
    c = Total(order, ("dp",), keep1, send1)
    grads = ()

    def backward(item, start, pairs):
        return attend_backward(
            order,
            scalars,
            item,
            start,
            pairs,
            projected,
            images[1],
            attended[item],
            grad_attended,
            lses[item],
            grads,
        )

    def weights(lanes, place, spare, *extra):
        return weight_grads(
            order, side, normed, images[0], grads, lanes, place, spare, extra
        )

    def unpack(half, first, value, earlier=()):
        return expert_outputs(order, half, first, value, width, units, earlier)

    grads = backward(0, 0, 2)
    a.step()
    grads = backward(1, 0, 2)
    c.step()
    grads = backward(0, 2, 2)
    a.step()
    grads = backward(1, 2, 2)
    c.step()
    first_sums, keep, send = weights(2 * LANES, 0, 0, project_out_grad)
    s = Total(order, ("dp", "mod"), keep, send)
    a.step()
    grads = backward(0, 4, 2)
    s.step()
    a.step()
    grads = backward(1, 4, 2)
    a.step()
    c.step()
    s.step()
    near = image_grads(order, project_in, grads[3], grads[4])
    far = to_image(near)
    c.step()
    a.step()
    last_sums, keep, send = weights(LANES, 2, SMALL)
    p = Total(order, ("dp", "mod"), keep, send, late_stages(("dp", "mod")))
    s.step()
    c.step()
    (far,) = order.after(far)
    order.last = far
    grad_in, keep = finish_rows(
        order,
        flag,
        hidden,
        grad_middle,
        near,
        far,
        grads[:3],
        attend_gain,
        project_in,
        feed_sums,
        (first_sums, last_sums),
        keep,
        rows,
    )
    p.terms = (keep, p.got)
    p.step()
    a.step()
    c.step()
    p.step()
    a.finish()
    outputs = unpack(side, 0, a.mine)
    s.step()
    p.step()
    s.step()
    outputs = unpack(1 - side, 0, a.got, outputs)
    p.step()
    c.step()
    s.step()
    p.step()
    c.finish()
    outputs = unpack(side, 2, c.mine, outputs)
    s.step()
    p.step()
    s.step()
    reduce_grad, expand_grad = unpack(1 - side, 2, c.got, outputs)
    p.step()
    s.step()
    s.finish()
    projections = first_outputs(order, side, s.mine, width, ())
    project_in_grad, project_out_grad = first_outputs(order, 1 - side, s.got, width, projections)
    p.finish()
    (
        project_in_grad,
        attend_gain_grad,
        attend_shift_grad,
        feed_gain_grad,
        feed_shift_grad,
        reduce_bias_grad,
        expand_bias_grad,
        bias_pair_grad,
        project_bias_grad,
    ) = last_outputs(order, side, flag, p.mine, p.got, width, units, project_in_grad)
    return (
        hidden_out.reshape(hidden_in.shape),
        grad_in.reshape(hidden_in.shape),
        attend_gain_grad,
        attend_shift_grad,
        project_in_grad,
        bias_pair_grad,
        project_out_grad,
        project_bias_grad,
        feed_gain_grad,
        feed_shift_grad,
        expand_grad[None],
        expand_bias_grad,
        reduce_grad[None],
        reduce_bias_grad,
    )


def solution(mesh):
    in_specs = (
        P("dp", "mod", None, None),
        P("dp"),
        P("dp", None),
        P("mod", None),
        P("mod", None),
        P(),
        P(),
        P(),
        P(),
        P("mod", None),
        P("mod", None),
        P("mod", None, None),
        P("mod", None),
        P("mod", None, None),
        P("mod", None),
        P("dp", "mod", None, None),
    )
    out_specs = (
        P("dp", "mod", None, None),
        P("dp", "mod", None, None),
        P("mod", None),
        P("mod", None),
        P(),
        P(),
        P(),
        P(),
        P("mod", None),
        P("mod", None),
        P("mod", None, None),
        P("mod", None),
        P("mod", None, None),
        P("mod", None),
    )
    return jax.shard_map(
        on_device, mesh=mesh, in_specs=in_specs, out_specs=out_specs, check_vma=False
    )
```

```python
import functools

import jax
import jax.numpy as jnp
from jax import lax
from jax.experimental import pallas as pl
from jax.experimental.pallas import tpu as pltpu
from jax.sharding import PartitionSpec as P

HEADS = 12
HEAD = 64
IMG_PAD = 256
PAIR = 2 * HEAD
PAIRS = HEADS // 2
GROUP_PAIRS = 2
GROUPS = PAIRS // GROUP_PAIRS
LANES = GROUP_PAIRS * PAIR
SMALL = 128
FF_BLOCK = 768

masked_value = -1e30
norm_eps = 1e-05

bf16 = jnp.bfloat16
f32 = jnp.float32

NN = (((1,), (0,)), ((), ()))
NT = (((1,), (1,)), ((), ()))
TN = (((0,), (0,)), ((), ()))
VMEM_BYTES = 56 << 20


def dot(left, right, dims=NN):
    return lax.dot_general(left, right, dims, preferred_element_type=f32)


def column_sum(values):
    return jnp.sum(values, axis=0, keepdims=True)


def row_mean(values):
    return jnp.mean(values, axis=1, keepdims=True)


def normalise(values):
    centred = values - row_mean(values)
    scale = lax.rsqrt(row_mean(centred * centred) + norm_eps)
    return centred * scale, scale


def norm_transpose(unit, scale, gain, grad):
    grad_unit = grad * gain
    return scale * (grad_unit - row_mean(grad_unit) - unit * row_mean(grad_unit * unit))


def cost(flops, moved, special=0):
    return pl.CostEstimate(flops=flops, bytes_accessed=moved, transcendentals=special)


def weighed(estimate):
    return pl.CostEstimate(
        flops=10 * estimate.flops,
        bytes_accessed=10 * estimate.bytes_accessed,
        transcendentals=10 * estimate.transcendentals,
    )


class Order:
    def __init__(self):
        self.last = None

    def after(self, *values):
        if self.last is None:
            return values
        *values, _ = lax.optimization_barrier((*values, self.last))
        return values


def call(order, kernel, inputs, out_shape, name, estimate, scalars=(), grid=(), specs=None, outs=None,
         scratch=(), aliases=None):
    inputs = (*order.after(inputs[0]), *inputs[1:])
    vmem = pl.BlockSpec(memory_space=pltpu.VMEM)
    found = pl.pallas_call(
        kernel,
        grid_spec=pltpu.PrefetchScalarGridSpec(
            num_scalar_prefetch=len(scalars),
            grid=grid,
            in_specs=[vmem] * len(inputs) if specs is None else list(specs),
            out_specs=[vmem] * len(out_shape) if outs is None else list(outs),
            scratch_shapes=list(scratch),
        ),
        out_shape=list(out_shape),
        input_output_aliases=aliases or {},
        compiler_params=pltpu.CompilerParams(vmem_limit_bytes=VMEM_BYTES),
        cost_estimate=estimate,
        name=name,
    )(*scalars, *inputs)
    order.last = found[-1]
    return found if len(found) > 1 else found[0]


def shaped(shape, dtype):
    return jax.ShapeDtypeStruct(shape, dtype)


def resident(shape):
    return pl.BlockSpec(shape, lambda *_: (0,) * len(shape), pipeline_mode=pl.Buffered(1))


def project_kernel(hid_ref, gain_ref, shift_ref, weight_ref, bias_ref, normed_ref, out_ref):
    unit, _ = normalise(hid_ref[...].astype(f32))
    normed = (unit * gain_ref[...] + shift_ref[...]).astype(bf16)
    normed_ref[...] = normed
    width = normed.shape[1]
    for part in range(3):
        cols = slice(part * width, (part + 1) * width)
        rows = dot(normed, weight_ref[:, cols])
        if part == 0:
            rows = (rows + bias_ref[0:1]).astype(bf16) * jnp.asarray(HEAD**-0.5, bf16)
        if part == 2:
            rows = rows + bias_ref[1:2]
        out_ref[:, cols] = rows.astype(bf16)


def project_rows(order, hidden, gain, shift, weight, bias):
    rows, width = hidden.shape
    block = 256
    blocked = lambda cols: pl.BlockSpec((block, cols), lambda r: (r, 0))
    inputs = (hidden, gain, shift, weight, bias)
    return call(
        order,
        project_kernel,
        inputs,
        [shaped((rows, width), bf16), shaped((rows, 3 * width), bf16)],
        "project_rows",
        cost(6 * rows * width * width, 10 * rows * width + 6 * width * width),
        grid=(rows // block,),
        specs=[blocked(width)] + [resident(value.shape) for value in inputs[1:]],
        outs=[blocked(width), blocked(3 * width)],
    )


def image_kernel(
    flag_ref,
    own_ref,
    far_ref,
    gain_ref,
    shift_ref,
    vec_ref,
    keys_ref,
    values_ref,
    bias_ref,
    *refs,
):
    normed_ref, out_ref = refs[-2:]
    is_text = flag_ref[0] == 1
    hidden = jnp.where(is_text, far_ref[...].astype(f32), own_ref[...].astype(f32))
    gain = jnp.where(is_text, vec_ref[0:1], gain_ref[...])
    shift = jnp.where(is_text, vec_ref[1:2], shift_ref[...])
    unit, _ = normalise(hidden)
    normed = (unit * gain + shift).astype(bf16)
    normed_ref[...] = normed
    width = normed.shape[1]
    out_ref[:, :width] = dot(normed, keys_ref[...]).astype(bf16)
    out_ref[:, width:] = (dot(normed, values_ref[...]) + bias_ref[1:2]).astype(bf16)


def image_rows(
    order, flag, item, hidden, far, gain, shift, vecs, weight, bias, item_rows, items, earlier
):
    width = hidden.shape[1]
    place = item * (item_rows // IMG_PAD)
    half = lambda base: pl.BlockSpec((width, width), lambda *_: (0, base))
    mine = lambda cols: pl.BlockSpec((IMG_PAD, cols), lambda *_: (item, 0))
    inputs = (hidden, far, gain, shift, vecs, weight, weight, bias, *earlier)
    return call(
        order,
        image_kernel,
        inputs,
        [shaped((items * IMG_PAD, width), bf16), shaped((items * IMG_PAD, 2 * width), bf16)],
        "image_rows",
        cost(4 * IMG_PAD * width * width, 6 << 20),
        scalars=(flag,),
        grid=(1,),
        specs=[
            pl.BlockSpec((IMG_PAD, width), lambda *_: (place, 0)),
            resident(far.shape),
            resident(gain.shape),
            resident(shift.shape),
            resident(vecs.shape),
            half(1),
            half(2),
            resident(bias.shape),
        ]
        + [pl.BlockSpec(memory_space=pl.ANY)] * len(earlier),
        outs=[mine(width), mine(2 * width)],
        aliases={9: 0, 10: 1} if earlier else None,
    )


def segments(shape, axis, lengths_ref, item):
    places = lax.broadcasted_iota(jnp.int32, shape, axis)
    total = jnp.zeros(shape, jnp.int32)
    end = 0
    for which in range(lengths_ref.shape[1]):
        end = end + lengths_ref[item, which]
        total += (places >= end).astype(jnp.int32)
    return total


def own_bias(rows, flag_ref, lengths_ref, item):
    shape = (rows, rows)
    same = segments(shape, 0, lengths_ref, item) == segments(shape, 1, lengths_ref, item)
    return jnp.where(same & (flag_ref[0] == 1), 0.0, masked_value).astype(f32)


def image_bias(shape, axis, count_ref, item):
    places = lax.broadcasted_iota(jnp.int32, shape, axis)
    return jnp.where(places < count_ref[item], 0.0, masked_value).astype(f32)


def forward_kernel(
    item,
    flag_ref,
    count_ref,
    lengths_ref,
    q_ref,
    k_ref,
    v_ref,
    ik_ref,
    iv_ref,
    out_ref,
    lse_ref,
    image_part,
    own_part,
):
    rows = q_ref.shape[0]

    @pl.when(pl.program_id(0) == 0)
    def _():
        image_part[...] = image_bias(image_part.shape, 1, count_ref, item)
        own_part[...] = own_bias(rows, flag_ref, lengths_ref, item)

    first = lax.broadcasted_iota(jnp.int32, (rows, PAIR), 1) < HEAD
    zero = jnp.zeros((), bf16)
    q = q_ref[...]
    image_keys, image_values = ik_ref[...], iv_ref[...]
    keys, values = k_ref[...], v_ref[...]
    outs, tops = [], []
    for head in range(2):
        q_head = jnp.where(first, q, zero) if head == 0 else jnp.where(first, zero, q)
        far = dot(q_head, image_keys, NT) + image_part[...]
        own = dot(q_head, keys, NT) + own_part[...]
        top = jnp.maximum(
            jnp.max(far, axis=1, keepdims=True), jnp.max(own, axis=1, keepdims=True)
        )
        far = jnp.exp(far - top)
        own = jnp.exp(own - top)
        total = jnp.sum(far, axis=1, keepdims=True) + jnp.sum(own, axis=1, keepdims=True)
        summed = dot(far.astype(bf16), image_values) + dot(own.astype(bf16), values)
        outs.append(summed / total)
        tops.append(top + jnp.log(total))
    out_ref[...] = jnp.where(first, outs[0], outs[1]).astype(bf16)
    turned = jnp.transpose(jnp.where(first, tops[0], tops[1]))
    lse_ref[0, 0:1, :] = turned[0:1]
    lse_ref[0, 1:2, :] = turned[HEAD : HEAD + 1]


def attend_forward(order, scalars, item, projected, image):
    rows = projected.shape[0] // 2
    spec = lambda base: pl.BlockSpec((rows, PAIR), lambda h, *_: (item, base + h))
    far = lambda base: pl.BlockSpec((IMG_PAD, PAIR), lambda h, *_: (item, base + h))
    keys = rows + IMG_PAD
    return call(
        order,
        functools.partial(forward_kernel, item),
        (projected, projected, projected, image, image),
        [shaped((rows, HEADS * HEAD), bf16), shaped((PAIRS, 2, rows), f32)],
        "attend_forward",
        cost(16 * HEADS * rows * keys * HEAD, 6 << 20, HEADS * rows * keys),
        scalars=scalars,
        grid=(PAIRS,),
        specs=[spec(0), spec(PAIRS), spec(2 * PAIRS), far(0), far(PAIRS)],
        outs=[
            pl.BlockSpec((rows, PAIR), lambda h, *_: (0, h)),
            pl.BlockSpec((1, 2, rows), lambda h, *_: (h, 0, 0)),
        ],
        scratch=[pltpu.VMEM((rows, IMG_PAD), f32), pltpu.VMEM((rows, rows), f32)],
    )


def backward_kernel(
    item,
    flag_ref,
    count_ref,
    lengths_ref,
    q_ref,
    k_ref,
    v_ref,
    ik_ref,
    iv_ref,
    out_ref,
    grad_ref,
    lse_ref,
    *refs,
):
    gq_ref, gk_ref, gv_ref, gik_ref, giv_ref, image_part, own_part = refs[-7:]
    rows = q_ref.shape[0]

    @pl.when(pl.program_id(0) == 0)
    def _():
        image_part[...] = image_bias(image_part.shape, 0, count_ref, item)
        own_part[...] = own_bias(rows, flag_ref, lengths_ref, item)

    first = lax.broadcasted_iota(jnp.int32, (rows, PAIR), 1) < HEAD
    zero = jnp.zeros((), bf16)
    q, grad = q_ref[...], grad_ref[...]
    products = grad.astype(f32) * out_ref[...].astype(f32)
    head_lanes = lax.broadcasted_iota(jnp.int32, (8, PAIR), 1) // HEAD
    head_rows = lax.broadcasted_iota(jnp.int32, (8, PAIR), 0)
    center = lax.dot_general(
        (head_lanes == head_rows).astype(f32),
        products,
        NT,
        preferred_element_type=f32,
        precision=lax.Precision.HIGHEST,
    )
    q_heads = [jnp.where(first, q, zero), jnp.where(first, zero, q)]
    grad_heads = [jnp.where(first, grad, zero), jnp.where(first, zero, grad)]
    lse = lse_ref[0]
    grad_query = [None, None]
    half = rows // 2
    pieces = (
        (ik_ref, iv_ref, gik_ref, giv_ref, image_part, 0, IMG_PAD),
        (k_ref, v_ref, gk_ref, gv_ref, own_part, 0, half),
        (k_ref, v_ref, gk_ref, gv_ref, own_part, half, half),
    )
    for keys_ref, values_ref, gk_out, gv_out, bias, start, count in pieces:
        piece = slice(start, start + count)
        keys, values = keys_ref[piece, :], values_ref[piece, :]
        low_lanes = lax.broadcasted_iota(jnp.int32, (count, PAIR), 1) < HEAD
        grad_keys, grad_values = [], []
        for head in range(2):
            scores = dot(keys, q_heads[head], NT) + bias[piece, :]
            probs = jnp.exp(scores - lse[head : head + 1])
            grad_probs = dot(values, grad_heads[head], NT)
            grad_scores = (probs * (grad_probs - center[head : head + 1])).astype(bf16)
            grad_values.append(dot(probs.astype(bf16), grad))
            grad_keys.append(dot(grad_scores, q))
            term = dot(grad_scores, keys, TN)
            grad_query[head] = term if grad_query[head] is None else grad_query[head] + term
        gk_out[piece, :] = jnp.where(low_lanes, grad_keys[0], grad_keys[1]).astype(bf16)
        gv_out[piece, :] = jnp.where(low_lanes, grad_values[0], grad_values[1]).astype(bf16)
    gq_ref[...] = (jnp.where(first, grad_query[0], grad_query[1]) * HEAD**-0.5).astype(bf16)


def attend_backward(order, scalars, item, start, pairs, projected, image, attended, grad, lse, earlier):
    rows, width = attended.shape
    spec = lambda base: pl.BlockSpec((rows, PAIR), lambda h, *_: (item, base + start + h))
    far = lambda base: pl.BlockSpec((IMG_PAD, PAIR), lambda h, *_: (item, base + start + h))
    own = pl.BlockSpec((rows, PAIR), lambda h, *_: (0, start + h))
    far_outs = pl.BlockSpec((IMG_PAD, PAIR), lambda h, *_: (item, start + h))
    keys = rows + IMG_PAD
    inputs = (projected, projected, projected, image, image, attended, grad, lse)
    first = len(scalars) + len(inputs)
    return call(
        order,
        functools.partial(backward_kernel, item),
        (*inputs, *earlier),
        [shaped((2 * rows, width), bf16)] * 3 + [shaped((2 * IMG_PAD, width), bf16)] * 2,
        "attend_backward",
        weighed(cost(80 * pairs * rows * keys * HEAD, pairs * 2 << 20, 2 * pairs * rows * keys)),
        scalars=scalars,
        grid=(pairs,),
        specs=[
            spec(0),
            spec(PAIRS),
            spec(2 * PAIRS),
            far(0),
            far(PAIRS),
            own,
            spec(0),
            pl.BlockSpec((1, 2, rows), lambda h, *_: (start + h, 0, 0)),
        ]
        + [pl.BlockSpec(memory_space=pl.ANY)] * len(earlier),
        outs=[spec(0), spec(0), spec(0), far_outs, far_outs],
        scratch=[pltpu.VMEM((IMG_PAD, rows), f32), pltpu.VMEM((rows, rows), f32)],
        aliases={first + at: at for at in range(len(earlier))},
    )


def gelu_pair(values):
    share = 0.5 * (1.0 + lax.erf(values * 0.7071067811865476))
    slope = share + values * jnp.exp(-0.5 * values * values) * 0.3989422804014327
    return values * share, slope


def feed_step(step, rows, item_rows, feed, top, result, gfeed, expand_ref, ebias_ref, reduce_ref):
    width = feed.shape[1]
    expand, reduce = expand_ref[...], reduce_ref[...]
    active_parts, gup_parts = [], []
    for start in range(0, rows, item_rows):
        here = slice(start, start + item_rows)
        upward = dot(feed[here, :], expand) + ebias_ref[...]
        gactive = dot(top[here, :], reduce, NT)
        active, slope = gelu_pair(upward)
        active = active.astype(bf16)
        gup = (gactive * slope).astype(bf16)
        result[here, :] += dot(active, reduce)
        gfeed[here, :] += dot(gup, expand, NT)
        active_parts.append(active)
        gup_parts.append(gup)
    active = jnp.concatenate(active_parts, axis=0)
    gup = jnp.concatenate(gup_parts, axis=0)
    greduce = dot(active, top[...], TN).astype(bf16)
    gexpand = dot(feed[...], gup, TN).astype(bf16)
    pieces = [greduce[:, at : at + LANES] for at in range(0, width, LANES)]
    pieces += [gexpand[:, at : at + LANES] for at in range(0, FF_BLOCK, LANES)]
    return pieces, column_sum(gup.astype(f32))


def store_pieces(out, pieces):
    at = 0
    for half in range(2):
        for piece in pieces:
            rows = piece.shape[0] // 2
            out[at : at + rows, :] = piece[half * rows : (half + 1) * rows]
            at += rows


def feed_kernel(
    flag_ref,
    count_ref,
    side_ref,
    att0_ref,
    att1_ref,
    project_ref,
    hid_ref,
    cot_ref,
    project_bias_ref,
    gain_ref,
    shift_ref,
    reduce_bias_ref,
    expand_ref,
    ebias_ref,
    reduce_ref,
    out_ref,
    gmid_ref,
    gatt_ref,
    gproject_ref,
    gvec_ref,
    keep0_ref,
    send0_ref,
    keep1_ref,
    send1_ref,
    middle,
    feed,
    top,
    result,
    gfeed,
    low_out,
    gatt,
    grads,
    grad_sems,
    row_sems,
    *,
    item_rows,
):
    step = pl.program_id(0)
    rows, width = hid_ref.shape
    block = 256
    att_refs = (att0_ref, att1_ref)
    half = grads.shape[1] // 2

    steps = grads.shape[0]

    def grad_copies(which):
        found = []
        chunk, place = divmod(which, steps // 2)
        outs = (keep1_ref, send1_ref) if chunk else (keep0_ref, send0_ref)
        for number, out in enumerate(outs):
            side = side_ref[0] if number == 0 else 1 - side_ref[0]
            here = grads.at[which, pl.ds(pl.multiple_of(side * half, half), half)]
            there = out.at[pl.ds(place * half, half)]
            found.append(pltpu.make_async_copy(here, there, grad_sems.at[which, number]))
        return found

    @pl.when(step == 0)
    def _():
        for start in range(0, rows, block):
            here = slice(start, start + block)
            inside = slice(start % item_rows, start % item_rows + block)
            att = att_refs[start // item_rows][inside, :]
            branch = dot(att, project_ref[...]) + project_bias_ref[...]
            x = hid_ref[here, :].astype(f32) + branch
            middle[here, :] = x
            unit, _ = normalise(x)
            feed[here, :] = (unit * gain_ref[...] + shift_ref[...]).astype(bf16)
            at = lax.broadcasted_iota(jnp.int32, (block, width), 0) + start % item_rows
            limit = jnp.where(flag_ref[0] == 1, item_rows, count_ref[start // item_rows])
            top[here, :] = jnp.where(at < limit, cot_ref[here, :].astype(f32), 0.0).astype(bf16)
            result[here, :] = x + reduce_bias_ref[...]
            gfeed[here, :] = jnp.zeros((block, width), f32)

    pieces, gvec_ref[pl.ds(4 + step, 1), :] = feed_step(
        step, rows, item_rows, feed, top, result, gfeed, expand_ref, ebias_ref, reduce_ref
    )
    store_pieces(grads.at[step], pieces)
    for which in range(steps):

        @pl.when(step == which)
        def _(which=which):
            for copy in grad_copies(which):
                copy.start()

    @pl.when(step == pl.num_programs(0) - 1)
    def _():
        copies = []
        sums = [jnp.zeros((1, width), f32)] * 4
        for number, start in enumerate(range(0, rows, block)):
            here = slice(start, start + block)
            low_out[here, :] = result[here, :].astype(bf16)
            unit, scale = normalise(middle[here, :])
            grad = gfeed[here, :]
            grad_top = top[here, :].astype(f32)
            gmid = grad_top + norm_transpose(unit, scale, gain_ref[...], grad)
            terms = (grad * unit, grad, grad_top, gmid)
            sums = [old + column_sum(new) for old, new in zip(sums, terms)]
            middle[here, :] = gmid
            gbranch = gmid.astype(bf16)
            feed[here, :] = gbranch
            gatt[here, :] = dot(gbranch, project_ref[...], NT).astype(bf16)
            for kind, (mine, there) in enumerate(
                ((low_out, out_ref), (middle, gmid_ref), (gatt, gatt_ref))
            ):
                span = pl.ds(start, block)
                copy = pltpu.make_async_copy(
                    mine.at[span, :], there.at[span, :], row_sems.at[kind, number]
                )
                copy.start()
                copies.append(copy)
        total = dot(att0_ref[...], feed[:item_rows, :], TN)
        total += dot(att1_ref[...], feed[item_rows:, :], TN)
        gproject_ref[...] = total.astype(bf16)
        gvec_ref[0:4, :] = jnp.concatenate(sums, axis=0)
        for copy in copies:
            copy.wait()
        for which in range(steps):
            for copy in grad_copies(which):
                copy.wait()


def feed_forward(order, flag, count, side, att0, att1, project, hidden, cotangent, vecs, expand, ebias, reduce):
    rows, width = hidden.shape
    item_rows = att0.shape[0]
    units = reduce.shape[0]
    steps = units // FF_BLOCK
    block_rows = 2 * width * FF_BLOCK // LANES
    fixed = (att0, att1, project, hidden, cotangent, *vecs)
    anywhere = pl.BlockSpec(memory_space=pl.ANY)
    return call(
        order,
        functools.partial(feed_kernel, item_rows=item_rows),
        (*fixed, expand, ebias, reduce),
        [
            shaped((rows, width), bf16),
            shaped((rows, width), f32),
            shaped((rows, width), bf16),
            shaped((width, width), bf16),
            shaped((4 + steps, width), f32),
        ]
        + [shaped((steps // 2 * block_rows // 2, LANES), bf16)] * 4,
        "feed_forward",
        cost(12 * rows * width * units, 40 << 20, 2 * rows * units),
        scalars=(flag, count, side),
        grid=(steps,),
        specs=[resident(value.shape) for value in fixed]
        + [
            pl.BlockSpec((width, FF_BLOCK), lambda j, *_: (0, j)),
            pl.BlockSpec((1, FF_BLOCK), lambda j, *_: (0, j)),
            pl.BlockSpec((FF_BLOCK, width), lambda j, *_: (j, 0)),
        ],
        outs=[
            anywhere,
            anywhere,
            anywhere,
            resident((width, width)),
            resident((4 + steps, width)),
        ]
        + [anywhere] * 4,
        scratch=[
            pltpu.VMEM((rows, width), f32),
            pltpu.VMEM((rows, width), bf16),
            pltpu.VMEM((rows, width), bf16),
            pltpu.VMEM((rows, width), f32),
            pltpu.VMEM((rows, width), f32),
            pltpu.VMEM((rows, width), bf16),
            pltpu.VMEM((rows, width), bf16),
            pltpu.VMEM((steps, block_rows, LANES), bf16),
            pltpu.SemaphoreType.DMA((steps, 2)),
            pltpu.SemaphoreType.DMA((3, rows // 256)),
        ],
    )


def weight_kernel(
    spare,
    side_ref,
    normed_ref,
    image_ref,
    gq_ref,
    gk_ref,
    gv_ref,
    gik_ref,
    giv_ref,
    *refs,
):
    extra_ref = None if spare else refs[0]
    sums_ref, keep_ref, send_ref, keep, send, sems = refs[-6:]
    step = pl.program_id(0)
    width = normed_ref.shape[1]
    half = width // 2
    columns = gq_ref.shape[1] // LANES
    block = half * (columns if spare else columns + 1)

    def copies(part):
        span = pl.ds(part * block, block if part < 3 else spare)
        pairs = ((keep, keep_ref), (send, send_ref))
        return [
            pltpu.make_async_copy(here.at[span], there.at[span], sems.at[number, part])
            for number, (here, there) in enumerate(pairs)
        ]

    def store(part, total):
        if extra_ref is not None:
            more = extra_ref[:, part * LANES : (part + 1) * LANES].astype(f32)
            total = jnp.concatenate([total, more], axis=1)
        first = side_ref[0] == 0
        mine = jnp.where(first, total[:half], total[half:]).astype(bf16)
        other = jnp.where(first, total[half:], total[:half]).astype(bf16)
        for number in range(block // half):
            rows = slice(part * block + number * half, part * block + (number + 1) * half)
            cols = slice(number * LANES, (number + 1) * LANES)
            keep[rows, :] = mine[:, cols]
            send[rows, :] = other[:, cols]
        for copy in copies(part):
            copy.start()

    @pl.when(step == 0)
    def _():
        store(0, dot(normed_ref[...], gq_ref[...], TN))
        sums_ref[0:1] = column_sum(gq_ref[...].astype(f32))

    @pl.when(step == 1)
    def _():
        total = dot(normed_ref[...], gk_ref[...], TN)
        store(1, total + dot(image_ref[...], gik_ref[...], TN))

    @pl.when(step == 2)
    def _():
        total = dot(normed_ref[...], gv_ref[...], TN)
        store(2, total + dot(image_ref[...], giv_ref[...], TN))
        sums = column_sum(gv_ref[...].astype(f32)) + column_sum(giv_ref[...].astype(f32))
        sums_ref[1:2] = sums
        if spare:
            keep[3 * block :, :] = jnp.zeros((spare, LANES), bf16)
            send[3 * block :, :] = jnp.zeros((spare, LANES), bf16)
            for copy in copies(3):
                copy.start()
        for part in range(4 if spare else 3):
            for copy in copies(part):
                copy.wait()


def weight_grads(order, side, normed, image, grads, lanes, place, spare, extra):
    rows, width = normed.shape
    half_rows = 3 * (lanes // LANES + len(extra)) * width // 2 + spare
    column = lambda height: pl.BlockSpec((height, lanes), lambda *_: (0, place))
    anywhere = pl.BlockSpec(memory_space=pl.ANY)
    return call(
        order,
        functools.partial(weight_kernel, spare),
        (normed, image, *grads, *extra),
        [shaped((2, lanes), f32)] + [shaped((half_rows, LANES), bf16)] * 2,
        "weight_grads",
        weighed(cost(8 * rows * width * lanes, 12 << 20)),
        scalars=(side,),
        grid=(3,),
        specs=[resident(normed.shape), resident(image.shape)]
        + [column(value.shape[0]) for value in grads]
        + [resident(value.shape) for value in extra],
        outs=[resident((2, lanes)), anywhere, anywhere],
        scratch=[pltpu.VMEM((half_rows, LANES), bf16)] * 2 + [pltpu.SemaphoreType.DMA((2, 4))],
    )


def image_grad_kernel(keys_weight, values_weight, keys_ref, values_ref, out_ref):
    total = dot(keys_ref[...], keys_weight[...], NT) + dot(values_ref[...], values_weight[...], NT)
    out_ref[...] = total.astype(bf16)


def image_grads(order, weight, keys, values):
    rows, width = keys.shape
    part = lambda base: pl.BlockSpec((width, width), lambda *_: (0, base))
    return call(
        order,
        image_grad_kernel,
        (weight, weight, keys, values),
        [shaped((rows, width), bf16)],
        "image_grads",
        weighed(cost(4 * rows * width * width, 6 << 20)),
        grid=(1,),
        specs=[part(1), part(2), resident(keys.shape), resident(values.shape)],
        outs=[resident((rows, width))],
    )


def finish_kernel(
    flag_ref,
    hid_ref,
    gmid_ref,
    near_ref,
    far_ref,
    gq_ref,
    gk_ref,
    gv_ref,
    gain_ref,
    weight_ref,
    feed_sums_ref,
    first_sums_ref,
    last_sums_ref,
    _,
    out_ref,
    small_ref,
    sums,
):
    item, block = pl.program_id(0), pl.program_id(1)
    joined = jnp.concatenate([gq_ref[...], gk_ref[...], gv_ref[...]], axis=1)
    grad = dot(joined, weight_ref[...], NT)
    unit, scale = normalise(hid_ref[...].astype(f32))
    both = near_ref[...].astype(f32) + far_ref[...].astype(f32)
    grad = grad + jnp.where((flag_ref[0] == 0) & (block == 0), both, 0.0)
    total = gmid_ref[...] + norm_transpose(unit, scale, gain_ref[...], grad)
    out_ref[...] = total.astype(bf16)
    found = jnp.concatenate([column_sum(grad * unit), column_sum(grad)], axis=0)

    @pl.when((item == 0) & (block == 0))
    def _():
        sums[...] = jnp.zeros(sums.shape, f32)

    sums[0:2] += found

    @pl.when((item == pl.num_programs(0) - 1) & (block == pl.num_programs(1) - 1))
    def _():
        width = sums.shape[1]
        pad = lambda count: jnp.zeros((count, width), f32)
        own = [sums[0:2], feed_sums_ref[0:3], feed_sums_ref[4:8], pad(7)]
        own = jnp.concatenate(own, axis=0)
        bias_sums = jnp.concatenate([first_sums_ref[...], last_sums_ref[...]], axis=1)
        shared = [pad(9), feed_sums_ref[3:4], bias_sums, pad(4)]
        shared = jnp.concatenate(shared, axis=0)
        is_text = flag_ref[0] == 1
        first = jnp.where(is_text, 0.0, own) + shared
        rows = jnp.concatenate([first, jnp.where(is_text, own, 0.0)], axis=0).astype(bf16)
        count = rows.shape[0]
        for number in range(width // LANES):
            cols = slice(number * LANES, (number + 1) * LANES)
            small_ref[number * count : (number + 1) * count, :] = rows[:, cols]
        small_ref[width // LANES * count :, :] = jnp.zeros((SMALL - width // LANES * count, LANES), bf16)


def finish_rows(
    order, flag, hidden, gmid, near, far, grads, gain, weight, feed_sums, bias_sums, keep, item_rows
):
    rows, width = hidden.shape
    blocks = item_rows // IMG_PAD
    mine = pl.BlockSpec((IMG_PAD, width), lambda i, j, *_: (i * blocks + j, 0))
    image = pl.BlockSpec((IMG_PAD, width), lambda i, j, *_: (i, 0))
    fixed = (gain, weight, feed_sums, *bias_sums)
    place = keep.shape[0] // SMALL - 1
    return call(
        order,
        finish_kernel,
        (hidden, gmid, near, far, *grads, *fixed, keep),
        [shaped((rows, width), bf16), shaped(keep.shape, bf16)],
        "finish_rows",
        weighed(cost(6 * rows * width * width, 16 << 20)),
        scalars=(flag,),
        grid=(rows // item_rows, blocks),
        specs=[mine, mine, image, image, mine, mine, mine]
        + [resident(value.shape) for value in fixed]
        + [pl.BlockSpec(memory_space=pl.ANY)],
        outs=[mine, pl.BlockSpec((SMALL, LANES), lambda *_: (place, 0))],
        scratch=[pltpu.VMEM((8, width), f32)],
        aliases={13: 1},
    )


def expert_kernel(half_ref, value_ref, *refs):
    at = 0
    for out in refs[-2:]:
        tall = out.shape[0]
        for part in range(out.shape[1] // LANES):
            piece = value_ref[at : at + tall, :]
            out[:, part * LANES : (part + 1) * LANES] = piece.astype(f32)
            at += tall


def expert_outputs(order, half, first, value, width, units, earlier):
    tall = width // 2
    block_rows = 2 * width // LANES * tall
    return call(
        order,
        expert_kernel,
        (value, *earlier),
        [shaped((units, width), f32), shaped((width, units), f32)],
        "expert_outputs",
        cost(value.size, 6 * value.size),
        scalars=(half,),
        grid=(value.shape[0] // block_rows,),
        specs=[pl.BlockSpec((block_rows, LANES), lambda i, at: (i, 0))]
        + [pl.BlockSpec(memory_space=pl.ANY)] * len(earlier),
        outs=[
            pl.BlockSpec((tall, width), lambda i, at: (2 * (first + i) + at[0], 0)),
            pl.BlockSpec((tall, width), lambda i, at: (at[0], first + i)),
        ],
        aliases={2: 0, 3: 1} if earlier else None,
    )


def first_kernel(half_ref, value_ref, *refs):
    in_ref, out_ref, wide, narrow, sems = refs[-5:]
    tall = wide.shape[1]
    count = value_ref.shape[0] // tall // 3
    columns = in_ref.shape[1] // 3
    rows = pl.ds(pl.multiple_of(half_ref[0] * tall, tall), tall)
    copies = []
    for part in range(3):
        at = part * count * tall
        for number in range(count - 1):
            piece = value_ref[at + number * tall : at + (number + 1) * tall, :]
            wide[part, :, number * LANES : (number + 1) * LANES] = piece.astype(f32)
        piece = value_ref[at + (count - 1) * tall : at + count * tall, :]
        narrow[part] = piece.astype(f32)
        places = (
            (wide, in_ref.at[rows, pl.ds(part * columns, (count - 1) * LANES)]),
            (narrow, out_ref.at[rows, pl.ds(part * LANES, LANES)]),
        )
        for kind, (here, there) in enumerate(places):
            copy = pltpu.make_async_copy(here.at[part], there, sems.at[kind, part])
            copy.start()
            copies.append(copy)
    for copy in copies:
        copy.wait()


def first_outputs(order, half, value, width, earlier):
    tall = width // 2
    anywhere = pl.BlockSpec(memory_space=pl.ANY)
    return call(
        order,
        first_kernel,
        (value, *earlier),
        [shaped((width, 3 * width), f32), shaped((width, width), f32)],
        "first_outputs",
        cost(value.size, 6 * value.size),
        scalars=(half,),
        grid=(1,),
        specs=[resident(value.shape)] + [anywhere] * len(earlier),
        outs=[anywhere, anywhere],
        scratch=[
            pltpu.VMEM((3, tall, width - LANES), f32),
            pltpu.VMEM((3, tall, LANES), f32),
            pltpu.SemaphoreType.DMA((2, 3)),
        ],
        aliases={2: 0, 3: 1} if earlier else None,
    )


def last_kernel(side_ref, flag_ref, mine_ref, got_ref, *refs):
    in_ref, *vec_refs, expand_ref, pair_ref, project_ref, columns, sems = refs[1:]
    tall = columns.shape[2]
    width = in_ref.shape[1] // 3
    copies = []
    for number, ref in enumerate((mine_ref, got_ref)):
        half = side_ref[0] if number == 0 else 1 - side_ref[0]
        rows = pl.ds(pl.multiple_of(half * tall, tall), tall)
        for part in range(3):
            columns[number, part] = ref[part * tall : (part + 1) * tall, :].astype(f32)
            there = in_ref.at[rows, pl.ds((part + 1) * width - LANES, LANES)]
            copy = pltpu.make_async_copy(columns.at[number, part], there, sems.at[number, part])
            copy.start()
            copies.append(copy)
    both = mine_ref[3 * tall :, :].astype(f32) + got_ref[3 * tall :, :].astype(f32)
    rows = jnp.concatenate([both[at * 32 : (at + 1) * 32] for at in range(width // LANES)], axis=1)
    own = jnp.where(flag_ref[0] == 1, rows[16:], rows[:16])
    for number, ref in enumerate(vec_refs):
        ref[...] = own[number : number + 1]
    for number in range(expand_ref.shape[1] // width):
        cols = slice(number * width, (number + 1) * width)
        expand_ref[:, cols] = own[5 + number : 6 + number]
    project_ref[...] = rows[9]
    pair_ref[...] = rows[10:12]
    for copy in copies:
        copy.wait()


def last_outputs(order, side, flag, mine, got, width, units, earlier):
    vecs = [(1, width)] * 5 + [(1, units), (2, width), (width,)]
    anywhere = pl.BlockSpec(memory_space=pl.ANY)
    return call(
        order,
        last_kernel,
        (mine, got, earlier),
        [shaped((width, 3 * width), f32)] + [shaped(shape, f32) for shape in vecs],
        "last_outputs",
        cost(got.size, 6 * got.size),
        scalars=(side, flag),
        grid=(1,),
        specs=[resident(mine.shape), resident(got.shape), anywhere],
        outs=[anywhere] + [resident(shape) for shape in vecs],
        scratch=[
            pltpu.VMEM((2, 3, width // 2, LANES), f32),
            pltpu.SemaphoreType.DMA((2, 3)),
        ],
        aliases={4: 0},
    )


def swap(value, axes, pair_of):
    count = 1
    for axis in axes:
        count *= lax.axis_size(axis)
    return lax.ppermute(value, axes, [(source, pair_of(source)) for source in range(count)])


def place_of(axes):
    place = 0
    for axis in axes:
        place = place * lax.axis_size(axis) + lax.axis_index(axis)
    return place


def late_stages(axes):
    stages = stage_bits(axes)
    if len(axes) == 2 and len(stages) == 5:
        return [stages[0], (0, 0), (2, 3), (3, 2), (4, 4)]
    return stages


def stage_bits(axes):
    count = 1
    for axis in axes:
        count *= lax.axis_size(axis)
    bits = count.bit_length() - 1
    core = len(axes) - 1
    others = [bit for bit in range(bits) if bit != core]
    if len(axes) == 1 and len(others) == 3:
        return [(core, core), (1, 2), (3, 1), (2, 3)]
    if len(axes) == 2 and len(others) == 4:
        return [(core, core), (0, 2), (2, 0), (3, 3), (4, 4)]
    return [(core, core)] + list(zip(others, others[1:] + others[:1]))


class Total:
    def __init__(self, order, axes, keep, send, stages=None):
        self.order = order
        self.axes = axes
        self.core = len(axes) - 1
        self.left = list(stages or stage_bits(axes))
        place = place_of(axes)
        second = ((place >> self.core) & 1) == 1
        sides = [(place >> jnp.where(second, pair[1], pair[0])) & 1 for pair in self.left]
        self.sides = dict(zip(self.left, sides))
        self.back = list(self.left)
        self.terms = (keep, self.exchange(send, self.left.pop(0)))
        self.mine = None

    def exchange(self, value, pair):
        other = lambda source: source ^ (1 << pair[(source >> self.core) & 1])
        self.got = swap(value, self.axes, other)
        return self.got

    def part(self, which, half):
        cut = lambda term: lax.dynamic_slice_in_dim(term, which * half, half, 0).astype(f32)
        return (cut(self.terms[0]) + cut(self.terms[1])).astype(bf16)

    def finish(self):
        while self.left or self.back:
            self.step()

    def step(self):
        if self.left:
            pair = self.left.pop(0)
            self.terms = self.order.after(*self.terms)
            half = self.terms[0].shape[0] // 2
            side = self.sides[pair]
            sent = self.part(1 - side, half)
            self.terms = (self.part(side, half), self.exchange(sent, pair))
            self.order.last = sent
            return
        pair = self.back.pop()
        if self.mine is None:
            self.terms = self.order.after(*self.terms)
            self.mine = (self.terms[0].astype(f32) + self.terms[1].astype(f32)).astype(bf16)
        else:
            mine, got = self.order.after(self.mine, self.got)
            low = jnp.where(self.last == 0, mine, got)
            high = jnp.where(self.last == 0, got, mine)
            self.mine = jnp.concatenate([low, high], axis=0)
        self.order.last = self.mine
        self.last = self.sides[pair]
        self.exchange(self.mine, pair)


def on_device(
    hidden_in,
    image_count,
    text_lengths,
    attend_gain,
    attend_shift,
    project_in,
    bias_pair,
    project_out,
    project_bias,
    feed_gain,
    feed_shift,
    expand_weight,
    expand_bias,
    reduce_weight,
    reduce_bias,
    cotangent,
):
    items, _, rows, width = hidden_in.shape
    units = expand_weight.shape[2]
    is_text = lax.axis_index("mod") == 1
    flag = is_text.astype(jnp.int32)[None]
    hidden = hidden_in.reshape(items * rows, width)
    to_text = lambda value: lax.ppermute(value, "mod", [(0, 1)])
    to_image = lambda value: lax.ppermute(value, "mod", [(1, 0)])

    far_rows = [to_text(hidden_in[item, 0, :IMG_PAD]) for item in range(items)]
    far_vecs = to_text(jnp.concatenate([attend_gain, attend_shift], axis=0))
    order = Order()
    normed, projected = project_rows(
        order, hidden, attend_gain, attend_shift, project_in, bias_pair
    )
    scalars = (flag, image_count, text_lengths)
    images, attended, lses = (), [], []
    for item in range(items):
        images = image_rows(
            order,
            flag,
            item,
            hidden,
            far_rows[item],
            attend_gain,
            attend_shift,
            far_vecs,
            project_in,
            bias_pair,
            rows,
            items,
            images,
        )
        out, lse = attend_forward(order, scalars, item, projected, images[1])
        attended.append(out)
        lses.append(lse)

    side = (lax.axis_index("dp") & 1)[None]
    (
        hidden_out,
        grad_middle,
        grad_attended,
        project_out_grad,
        feed_sums,
        keep0,
        send0,
        keep1,
        send1,
    ) = feed_forward(
        order,
        flag,
        image_count,
        side,
        attended[0],
        attended[1],
        project_out,
        hidden,
        cotangent.reshape(items * rows, width),
        (project_bias[None], feed_gain, feed_shift, reduce_bias),
        expand_weight[0],
        expand_bias,
        reduce_weight[0],
    )
    a = Total(order, ("dp",), keep0, send0)
    c = Total(order, ("dp",), keep1, send1)
    grads = ()

    def backward(item, start, pairs):
        return attend_backward(
            order,
            scalars,
            item,
            start,
            pairs,
            projected,
            images[1],
            attended[item],
            grad_attended,
            lses[item],
            grads,
        )

    def weights(lanes, place, spare, *extra):
        return weight_grads(
            order, side, normed, images[0], grads, lanes, place, spare, extra
        )

    def unpack(half, first, value, earlier=()):
        return expert_outputs(order, half, first, value, width, units, earlier)

    grads = backward(0, 0, 2)
    a.step()
    grads = backward(1, 0, 2)
    c.step()
    grads = backward(0, 2, 2)
    a.step()
    grads = backward(1, 2, 2)
    c.step()
    first_sums, keep, send = weights(2 * LANES, 0, 0, project_out_grad)
    s = Total(order, ("dp", "mod"), keep, send)
    a.step()
    grads = backward(0, 4, 2)
    s.step()
    a.step()
    grads = backward(1, 4, 2)
    c.step()
    s.step()
    near = image_grads(order, project_in, grads[3], grads[4])
    far = to_image(near)
    c.step()
    a.step()
    last_sums, keep, send = weights(LANES, 2, SMALL)
    p = Total(order, ("dp", "mod"), keep, send, late_stages(("dp", "mod")))
    s.step()
    c.step()
    a.step()
    (far,) = order.after(far)
    order.last = far
    grad_in, keep = finish_rows(
        order,
        flag,
        hidden,
        grad_middle,
        near,
        far,
        grads[:3],
        attend_gain,
        project_in,
        feed_sums,
        (first_sums, last_sums),
        keep,
        rows,
    )
    p.terms = (keep, p.got)
    p.step()
    s.step()
    a.step()
    p.step()
    c.step()
    p.step()
    s.step()
    a.finish()
    outputs = unpack(side, 0, a.mine)
    p.step()
    s.step()
    p.step()
    outputs = unpack(1 - side, 0, a.got, outputs)
    p.step()
    s.step()
    c.step()
    p.step()
    s.step()
    c.finish()
    outputs = unpack(side, 2, c.mine, outputs)
    p.step()
    reduce_grad, expand_grad = unpack(1 - side, 2, c.got, outputs)
    p.finish()
    s.step()
    s.finish()
    projections = first_outputs(order, side, s.mine, width, ())
    project_in_grad, project_out_grad = first_outputs(order, 1 - side, s.got, width, projections)
    p.finish()
    (
        project_in_grad,
        attend_gain_grad,
        attend_shift_grad,
        feed_gain_grad,
        feed_shift_grad,
        reduce_bias_grad,
        expand_bias_grad,
        bias_pair_grad,
        project_bias_grad,
    ) = last_outputs(order, side, flag, p.mine, p.got, width, units, project_in_grad)
    return (
        hidden_out.reshape(hidden_in.shape),
        grad_in.reshape(hidden_in.shape),
        attend_gain_grad,
        attend_shift_grad,
        project_in_grad,
        bias_pair_grad,
        project_out_grad,
        project_bias_grad,
        feed_gain_grad,
        feed_shift_grad,
        expand_grad[None],
        expand_bias_grad,
        reduce_grad[None],
        reduce_bias_grad,
    )


def solution(mesh):
    in_specs = (
        P("dp", "mod", None, None),
        P("dp"),
        P("dp", None),
        P("mod", None),
        P("mod", None),
        P(),
        P(),
        P(),
        P(),
        P("mod", None),
        P("mod", None),
        P("mod", None, None),
        P("mod", None),
        P("mod", None, None),
        P("mod", None),
        P("dp", "mod", None, None),
    )
    out_specs = (
        P("dp", "mod", None, None),
        P("dp", "mod", None, None),
        P("mod", None),
        P("mod", None),
        P(),
        P(),
        P(),
        P(),
        P("mod", None),
        P("mod", None),
        P("mod", None, None),
        P("mod", None),
        P("mod", None, None),
        P("mod", None),
    )
    return jax.shard_map(
        on_device, mesh=mesh, in_specs=in_specs, out_specs=out_specs, check_vma=False
    )
```

```python
import functools

import jax
import jax.numpy as jnp
from jax import lax
from jax.experimental import pallas as pl
from jax.experimental.pallas import tpu as pltpu
from jax.sharding import PartitionSpec as P

HEADS = 12
HEAD = 64
IMG_PAD = 256
PAIR = 2 * HEAD
PAIRS = HEADS // 2
GROUP_PAIRS = 2
GROUPS = PAIRS // GROUP_PAIRS
LANES = GROUP_PAIRS * PAIR
SMALL = 128
FF_BLOCK = 768

masked_value = -1e30
norm_eps = 1e-05

bf16 = jnp.bfloat16
f32 = jnp.float32

NN = (((1,), (0,)), ((), ()))
NT = (((1,), (1,)), ((), ()))
TN = (((0,), (0,)), ((), ()))
VMEM_BYTES = 56 << 20


def dot(left, right, dims=NN):
    return lax.dot_general(left, right, dims, preferred_element_type=f32)


def column_sum(values):
    return jnp.sum(values, axis=0, keepdims=True)


def row_mean(values):
    return jnp.mean(values, axis=1, keepdims=True)


def normalise(values):
    centred = values - row_mean(values)
    scale = lax.rsqrt(row_mean(centred * centred) + norm_eps)
    return centred * scale, scale


def norm_transpose(unit, scale, gain, grad):
    grad_unit = grad * gain
    return scale * (grad_unit - row_mean(grad_unit) - unit * row_mean(grad_unit * unit))


def cost(flops, moved, special=0):
    return pl.CostEstimate(flops=flops, bytes_accessed=moved, transcendentals=special)


def weighed(estimate):
    return pl.CostEstimate(
        flops=10 * estimate.flops,
        bytes_accessed=10 * estimate.bytes_accessed,
        transcendentals=10 * estimate.transcendentals,
    )


class Order:
    def __init__(self):
        self.last = None

    def after(self, *values):
        if self.last is None:
            return values
        *values, _ = lax.optimization_barrier((*values, self.last))
        return values


def call(order, kernel, inputs, out_shape, name, estimate, scalars=(), grid=(), specs=None, outs=None,
         scratch=(), aliases=None):
    inputs = (*order.after(inputs[0]), *inputs[1:])
    vmem = pl.BlockSpec(memory_space=pltpu.VMEM)
    found = pl.pallas_call(
        kernel,
        grid_spec=pltpu.PrefetchScalarGridSpec(
            num_scalar_prefetch=len(scalars),
            grid=grid,
            in_specs=[vmem] * len(inputs) if specs is None else list(specs),
            out_specs=[vmem] * len(out_shape) if outs is None else list(outs),
            scratch_shapes=list(scratch),
        ),
        out_shape=list(out_shape),
        input_output_aliases=aliases or {},
        compiler_params=pltpu.CompilerParams(vmem_limit_bytes=VMEM_BYTES),
        cost_estimate=estimate,
        name=name,
    )(*scalars, *inputs)
    order.last = found[-1]
    return found if len(found) > 1 else found[0]


def shaped(shape, dtype):
    return jax.ShapeDtypeStruct(shape, dtype)


def resident(shape):
    return pl.BlockSpec(shape, lambda *_: (0,) * len(shape), pipeline_mode=pl.Buffered(1))


def project_kernel(hid_ref, gain_ref, shift_ref, weight_ref, bias_ref, normed_ref, out_ref):
    unit, _ = normalise(hid_ref[...].astype(f32))
    normed = (unit * gain_ref[...] + shift_ref[...]).astype(bf16)
    normed_ref[...] = normed
    width = normed.shape[1]
    for part in range(3):
        cols = slice(part * width, (part + 1) * width)
        rows = dot(normed, weight_ref[:, cols])
        if part == 0:
            rows = (rows + bias_ref[0:1]).astype(bf16) * jnp.asarray(HEAD**-0.5, bf16)
        if part == 2:
            rows = rows + bias_ref[1:2]
        out_ref[:, cols] = rows.astype(bf16)


def project_rows(order, hidden, gain, shift, weight, bias):
    rows, width = hidden.shape
    block = 256
    blocked = lambda cols: pl.BlockSpec((block, cols), lambda r: (r, 0))
    inputs = (hidden, gain, shift, weight, bias)
    return call(
        order,
        project_kernel,
        inputs,
        [shaped((rows, width), bf16), shaped((rows, 3 * width), bf16)],
        "project_rows",
        cost(6 * rows * width * width, 10 * rows * width + 6 * width * width),
        grid=(rows // block,),
        specs=[blocked(width)] + [resident(value.shape) for value in inputs[1:]],
        outs=[blocked(width), blocked(3 * width)],
    )


def image_kernel(
    flag_ref,
    own_ref,
    far_ref,
    gain_ref,
    shift_ref,
    vec_ref,
    keys_ref,
    values_ref,
    bias_ref,
    *refs,
):
    normed_ref, out_ref = refs[-2:]
    is_text = flag_ref[0] == 1
    hidden = jnp.where(is_text, far_ref[...].astype(f32), own_ref[...].astype(f32))
    gain = jnp.where(is_text, vec_ref[0:1], gain_ref[...])
    shift = jnp.where(is_text, vec_ref[1:2], shift_ref[...])
    unit, _ = normalise(hidden)
    normed = (unit * gain + shift).astype(bf16)
    normed_ref[...] = normed
    width = normed.shape[1]
    out_ref[:, :width] = dot(normed, keys_ref[...]).astype(bf16)
    out_ref[:, width:] = (dot(normed, values_ref[...]) + bias_ref[1:2]).astype(bf16)


def image_rows(
    order, flag, item, hidden, far, gain, shift, vecs, weight, bias, item_rows, items, earlier
):
    width = hidden.shape[1]
    place = item * (item_rows // IMG_PAD)
    half = lambda base: pl.BlockSpec((width, width), lambda *_: (0, base))
    mine = lambda cols: pl.BlockSpec((IMG_PAD, cols), lambda *_: (item, 0))
    inputs = (hidden, far, gain, shift, vecs, weight, weight, bias, *earlier)
    return call(
        order,
        image_kernel,
        inputs,
        [shaped((items * IMG_PAD, width), bf16), shaped((items * IMG_PAD, 2 * width), bf16)],
        "image_rows",
        cost(4 * IMG_PAD * width * width, 6 << 20),
        scalars=(flag,),
        grid=(1,),
        specs=[
            pl.BlockSpec((IMG_PAD, width), lambda *_: (place, 0)),
            resident(far.shape),
            resident(gain.shape),
            resident(shift.shape),
            resident(vecs.shape),
            half(1),
            half(2),
            resident(bias.shape),
        ]
        + [pl.BlockSpec(memory_space=pl.ANY)] * len(earlier),
        outs=[mine(width), mine(2 * width)],
        aliases={9: 0, 10: 1} if earlier else None,
    )


def segments(shape, axis, lengths_ref, item):
    places = lax.broadcasted_iota(jnp.int32, shape, axis)
    total = jnp.zeros(shape, jnp.int32)
    end = 0
    for which in range(lengths_ref.shape[1]):
        end = end + lengths_ref[item, which]
        total += (places >= end).astype(jnp.int32)
    return total


def own_bias(rows, flag_ref, lengths_ref, item):
    shape = (rows, rows)
    same = segments(shape, 0, lengths_ref, item) == segments(shape, 1, lengths_ref, item)
    return jnp.where(same & (flag_ref[0] == 1), 0.0, masked_value).astype(f32)


def image_bias(shape, axis, count_ref, item):
    places = lax.broadcasted_iota(jnp.int32, shape, axis)
    return jnp.where(places < count_ref[item], 0.0, masked_value).astype(f32)


def forward_kernel(
    item,
    flag_ref,
    count_ref,
    lengths_ref,
    q_ref,
    k_ref,
    v_ref,
    ik_ref,
    iv_ref,
    out_ref,
    lse_ref,
    image_part,
    own_part,
):
    rows = q_ref.shape[0]

    @pl.when(pl.program_id(0) == 0)
    def _():
        image_part[...] = image_bias(image_part.shape, 1, count_ref, item)
        own_part[...] = own_bias(rows, flag_ref, lengths_ref, item)

    first = lax.broadcasted_iota(jnp.int32, (rows, PAIR), 1) < HEAD
    zero = jnp.zeros((), bf16)
    q = q_ref[...]
    image_keys, image_values = ik_ref[...], iv_ref[...]
    keys, values = k_ref[...], v_ref[...]
    outs, tops = [], []
    for head in range(2):
        q_head = jnp.where(first, q, zero) if head == 0 else jnp.where(first, zero, q)
        far = dot(q_head, image_keys, NT) + image_part[...]
        own = dot(q_head, keys, NT) + own_part[...]
        top = jnp.maximum(
            jnp.max(far, axis=1, keepdims=True), jnp.max(own, axis=1, keepdims=True)
        )
        far = jnp.exp(far - top)
        own = jnp.exp(own - top)
        total = jnp.sum(far, axis=1, keepdims=True) + jnp.sum(own, axis=1, keepdims=True)
        summed = dot(far.astype(bf16), image_values) + dot(own.astype(bf16), values)
        outs.append(summed / total)
        tops.append(top + jnp.log(total))
    out_ref[...] = jnp.where(first, outs[0], outs[1]).astype(bf16)
    turned = jnp.transpose(jnp.where(first, tops[0], tops[1]))
    lse_ref[0, 0:1, :] = turned[0:1]
    lse_ref[0, 1:2, :] = turned[HEAD : HEAD + 1]


def attend_forward(order, scalars, item, projected, image):
    rows = projected.shape[0] // 2
    spec = lambda base: pl.BlockSpec((rows, PAIR), lambda h, *_: (item, base + h))
    far = lambda base: pl.BlockSpec((IMG_PAD, PAIR), lambda h, *_: (item, base + h))
    keys = rows + IMG_PAD
    return call(
        order,
        functools.partial(forward_kernel, item),
        (projected, projected, projected, image, image),
        [shaped((rows, HEADS * HEAD), bf16), shaped((PAIRS, 2, rows), f32)],
        "attend_forward",
        cost(16 * HEADS * rows * keys * HEAD, 6 << 20, HEADS * rows * keys),
        scalars=scalars,
        grid=(PAIRS,),
        specs=[spec(0), spec(PAIRS), spec(2 * PAIRS), far(0), far(PAIRS)],
        outs=[
            pl.BlockSpec((rows, PAIR), lambda h, *_: (0, h)),
            pl.BlockSpec((1, 2, rows), lambda h, *_: (h, 0, 0)),
        ],
        scratch=[pltpu.VMEM((rows, IMG_PAD), f32), pltpu.VMEM((rows, rows), f32)],
    )


def backward_kernel(
    item,
    flag_ref,
    count_ref,
    lengths_ref,
    q_ref,
    k_ref,
    v_ref,
    ik_ref,
    iv_ref,
    out_ref,
    grad_ref,
    lse_ref,
    *refs,
):
    gq_ref, gk_ref, gv_ref, gik_ref, giv_ref, image_part, own_part = refs[-7:]
    rows = q_ref.shape[0]

    @pl.when(pl.program_id(0) == 0)
    def _():
        image_part[...] = image_bias(image_part.shape, 0, count_ref, item)
        own_part[...] = own_bias(rows, flag_ref, lengths_ref, item)

    first = lax.broadcasted_iota(jnp.int32, (rows, PAIR), 1) < HEAD
    zero = jnp.zeros((), bf16)
    q, grad = q_ref[...], grad_ref[...]
    products = grad.astype(f32) * out_ref[...].astype(f32)
    head_lanes = lax.broadcasted_iota(jnp.int32, (8, PAIR), 1) // HEAD
    head_rows = lax.broadcasted_iota(jnp.int32, (8, PAIR), 0)
    center = lax.dot_general(
        (head_lanes == head_rows).astype(f32),
        products,
        NT,
        preferred_element_type=f32,
        precision=lax.Precision.HIGHEST,
    )
    q_heads = [jnp.where(first, q, zero), jnp.where(first, zero, q)]
    grad_heads = [jnp.where(first, grad, zero), jnp.where(first, zero, grad)]
    lse = lse_ref[0]
    grad_query = [None, None]
    half = rows // 2
    pieces = (
        (ik_ref, iv_ref, gik_ref, giv_ref, image_part, 0, IMG_PAD),
        (k_ref, v_ref, gk_ref, gv_ref, own_part, 0, half),
        (k_ref, v_ref, gk_ref, gv_ref, own_part, half, half),
    )
    for keys_ref, values_ref, gk_out, gv_out, bias, start, count in pieces:
        piece = slice(start, start + count)
        keys, values = keys_ref[piece, :], values_ref[piece, :]
        low_lanes = lax.broadcasted_iota(jnp.int32, (count, PAIR), 1) < HEAD
        grad_keys, grad_values = [], []
        for head in range(2):
            scores = dot(keys, q_heads[head], NT) + bias[piece, :]
            probs = jnp.exp(scores - lse[head : head + 1])
            grad_probs = dot(values, grad_heads[head], NT)
            grad_scores = (probs * (grad_probs - center[head : head + 1])).astype(bf16)
            grad_values.append(dot(probs.astype(bf16), grad))
            grad_keys.append(dot(grad_scores, q))
            term = dot(grad_scores, keys, TN)
            grad_query[head] = term if grad_query[head] is None else grad_query[head] + term
        gk_out[piece, :] = jnp.where(low_lanes, grad_keys[0], grad_keys[1]).astype(bf16)
        gv_out[piece, :] = jnp.where(low_lanes, grad_values[0], grad_values[1]).astype(bf16)
    gq_ref[...] = (jnp.where(first, grad_query[0], grad_query[1]) * HEAD**-0.5).astype(bf16)


def attend_backward(order, scalars, item, start, pairs, projected, image, attended, grad, lse, earlier):
    rows, width = attended.shape
    spec = lambda base: pl.BlockSpec((rows, PAIR), lambda h, *_: (item, base + start + h))
    far = lambda base: pl.BlockSpec((IMG_PAD, PAIR), lambda h, *_: (item, base + start + h))
    own = pl.BlockSpec((rows, PAIR), lambda h, *_: (0, start + h))
    far_outs = pl.BlockSpec((IMG_PAD, PAIR), lambda h, *_: (item, start + h))
    keys = rows + IMG_PAD
    inputs = (projected, projected, projected, image, image, attended, grad, lse)
    first = len(scalars) + len(inputs)
    return call(
        order,
        functools.partial(backward_kernel, item),
        (*inputs, *earlier),
        [shaped((2 * rows, width), bf16)] * 3 + [shaped((2 * IMG_PAD, width), bf16)] * 2,
        "attend_backward",
        weighed(cost(80 * pairs * rows * keys * HEAD, pairs * 2 << 20, 2 * pairs * rows * keys)),
        scalars=scalars,
        grid=(pairs,),
        specs=[
            spec(0),
            spec(PAIRS),
            spec(2 * PAIRS),
            far(0),
            far(PAIRS),
            own,
            spec(0),
            pl.BlockSpec((1, 2, rows), lambda h, *_: (start + h, 0, 0)),
        ]
        + [pl.BlockSpec(memory_space=pl.ANY)] * len(earlier),
        outs=[spec(0), spec(0), spec(0), far_outs, far_outs],
        scratch=[pltpu.VMEM((IMG_PAD, rows), f32), pltpu.VMEM((rows, rows), f32)],
        aliases={first + at: at for at in range(len(earlier))},
    )


def gelu_pair(values):
    share = 0.5 * (1.0 + lax.erf(values * 0.7071067811865476))
    slope = share + values * jnp.exp(-0.5 * values * values) * 0.3989422804014327
    return values * share, slope


def feed_step(step, rows, item_rows, feed, top, result, gfeed, expand_ref, ebias_ref, reduce_ref):
    width = feed.shape[1]
    expand, reduce = expand_ref[...], reduce_ref[...]
    active_parts, gup_parts = [], []
    for start in range(0, rows, item_rows):
        here = slice(start, start + item_rows)
        upward = dot(feed[here, :], expand) + ebias_ref[...]
        gactive = dot(top[here, :], reduce, NT)
        active, slope = gelu_pair(upward)
        active = active.astype(bf16)
        gup = (gactive * slope).astype(bf16)
        result[here, :] += dot(active, reduce)
        gfeed[here, :] += dot(gup, expand, NT)
        active_parts.append(active)
        gup_parts.append(gup)
    active = jnp.concatenate(active_parts, axis=0)
    gup = jnp.concatenate(gup_parts, axis=0)
    greduce = dot(active, top[...], TN).astype(bf16)
    gexpand = dot(feed[...], gup, TN).astype(bf16)
    pieces = [greduce[:, at : at + LANES] for at in range(0, width, LANES)]
    pieces += [gexpand[:, at : at + LANES] for at in range(0, FF_BLOCK, LANES)]
    return pieces, column_sum(gup.astype(f32))


def store_pieces(out, pieces):
    at = 0
    for half in range(2):
        for piece in pieces:
            rows = piece.shape[0] // 2
            out[at : at + rows, :] = piece[half * rows : (half + 1) * rows]
            at += rows


def feed_kernel(
    flag_ref,
    count_ref,
    side_ref,
    att0_ref,
    att1_ref,
    project_ref,
    hid_ref,
    cot_ref,
    project_bias_ref,
    gain_ref,
    shift_ref,
    reduce_bias_ref,
    expand_ref,
    ebias_ref,
    reduce_ref,
    out_ref,
    gmid_ref,
    gatt_ref,
    gproject_ref,
    gvec_ref,
    keep0_ref,
    send0_ref,
    keep1_ref,
    send1_ref,
    middle,
    feed,
    top,
    result,
    gfeed,
    low_out,
    gatt,
    grads,
    grad_sems,
    row_sems,
    *,
    item_rows,
):
    step = pl.program_id(0)
    rows, width = hid_ref.shape
    block = 256
    att_refs = (att0_ref, att1_ref)
    half = grads.shape[1] // 2

    steps = grads.shape[0]

    def grad_copies(which):
        found = []
        chunk, place = divmod(which, steps // 2)
        outs = (keep1_ref, send1_ref) if chunk else (keep0_ref, send0_ref)
        for number, out in enumerate(outs):
            side = side_ref[0] if number == 0 else 1 - side_ref[0]
            here = grads.at[which, pl.ds(pl.multiple_of(side * half, half), half)]
            there = out.at[pl.ds(place * half, half)]
            found.append(pltpu.make_async_copy(here, there, grad_sems.at[which, number]))
        return found

    @pl.when(step == 0)
    def _():
        for start in range(0, rows, block):
            here = slice(start, start + block)
            inside = slice(start % item_rows, start % item_rows + block)
            att = att_refs[start // item_rows][inside, :]
            branch = dot(att, project_ref[...]) + project_bias_ref[...]
            x = hid_ref[here, :].astype(f32) + branch
            middle[here, :] = x
            unit, _ = normalise(x)
            feed[here, :] = (unit * gain_ref[...] + shift_ref[...]).astype(bf16)
            at = lax.broadcasted_iota(jnp.int32, (block, width), 0) + start % item_rows
            limit = jnp.where(flag_ref[0] == 1, item_rows, count_ref[start // item_rows])
            top[here, :] = jnp.where(at < limit, cot_ref[here, :].astype(f32), 0.0).astype(bf16)
            result[here, :] = x + reduce_bias_ref[...]
            gfeed[here, :] = jnp.zeros((block, width), f32)

    pieces, gvec_ref[pl.ds(4 + step, 1), :] = feed_step(
        step, rows, item_rows, feed, top, result, gfeed, expand_ref, ebias_ref, reduce_ref
    )
    store_pieces(grads.at[step], pieces)
    for which in range(steps):

        @pl.when(step == which)
        def _(which=which):
            for copy in grad_copies(which):
                copy.start()

    @pl.when(step == pl.num_programs(0) - 1)
    def _():
        copies = []
        sums = [jnp.zeros((1, width), f32)] * 4
        for number, start in enumerate(range(0, rows, block)):
            here = slice(start, start + block)
            low_out[here, :] = result[here, :].astype(bf16)
            unit, scale = normalise(middle[here, :])
            grad = gfeed[here, :]
            grad_top = top[here, :].astype(f32)
            gmid = grad_top + norm_transpose(unit, scale, gain_ref[...], grad)
            terms = (grad * unit, grad, grad_top, gmid)
            sums = [old + column_sum(new) for old, new in zip(sums, terms)]
            middle[here, :] = gmid
            gbranch = gmid.astype(bf16)
            feed[here, :] = gbranch
            gatt[here, :] = dot(gbranch, project_ref[...], NT).astype(bf16)
            for kind, (mine, there) in enumerate(
                ((low_out, out_ref), (middle, gmid_ref), (gatt, gatt_ref))
            ):
                span = pl.ds(start, block)
                copy = pltpu.make_async_copy(
                    mine.at[span, :], there.at[span, :], row_sems.at[kind, number]
                )
                copy.start()
                copies.append(copy)
        total = dot(att0_ref[...], feed[:item_rows, :], TN)
        total += dot(att1_ref[...], feed[item_rows:, :], TN)
        gproject_ref[...] = total.astype(bf16)
        gvec_ref[0:4, :] = jnp.concatenate(sums, axis=0)
        for copy in copies:
            copy.wait()
        for which in range(steps):
            for copy in grad_copies(which):
                copy.wait()


def feed_forward(order, flag, count, side, att0, att1, project, hidden, cotangent, vecs, expand, ebias, reduce):
    rows, width = hidden.shape
    item_rows = att0.shape[0]
    units = reduce.shape[0]
    steps = units // FF_BLOCK
    block_rows = 2 * width * FF_BLOCK // LANES
    fixed = (att0, att1, project, hidden, cotangent, *vecs)
    anywhere = pl.BlockSpec(memory_space=pl.ANY)
    return call(
        order,
        functools.partial(feed_kernel, item_rows=item_rows),
        (*fixed, expand, ebias, reduce),
        [
            shaped((rows, width), bf16),
            shaped((rows, width), f32),
            shaped((rows, width), bf16),
            shaped((width, width), bf16),
            shaped((4 + steps, width), f32),
        ]
        + [shaped((steps // 2 * block_rows // 2, LANES), bf16)] * 4,
        "feed_forward",
        cost(12 * rows * width * units, 40 << 20, 2 * rows * units),
        scalars=(flag, count, side),
        grid=(steps,),
        specs=[resident(value.shape) for value in fixed]
        + [
            pl.BlockSpec((width, FF_BLOCK), lambda j, *_: (0, j)),
            pl.BlockSpec((1, FF_BLOCK), lambda j, *_: (0, j)),
            pl.BlockSpec((FF_BLOCK, width), lambda j, *_: (j, 0)),
        ],
        outs=[
            anywhere,
            anywhere,
            anywhere,
            resident((width, width)),
            resident((4 + steps, width)),
        ]
        + [anywhere] * 4,
        scratch=[
            pltpu.VMEM((rows, width), f32),
            pltpu.VMEM((rows, width), bf16),
            pltpu.VMEM((rows, width), bf16),
            pltpu.VMEM((rows, width), f32),
            pltpu.VMEM((rows, width), f32),
            pltpu.VMEM((rows, width), bf16),
            pltpu.VMEM((rows, width), bf16),
            pltpu.VMEM((steps, block_rows, LANES), bf16),
            pltpu.SemaphoreType.DMA((steps, 2)),
            pltpu.SemaphoreType.DMA((3, rows // 256)),
        ],
    )


def weight_kernel(
    spare,
    side_ref,
    normed_ref,
    image_ref,
    gq_ref,
    gk_ref,
    gv_ref,
    gik_ref,
    giv_ref,
    *refs,
):
    extra_ref = None if spare else refs[0]
    sums_ref, keep_ref, send_ref, keep, send, sems = refs[-6:]
    step = pl.program_id(0)
    width = normed_ref.shape[1]
    half = width // 2
    columns = gq_ref.shape[1] // LANES
    block = half * (columns if spare else columns + 1)

    def copies(part):
        span = pl.ds(part * block, block if part < 3 else spare)
        pairs = ((keep, keep_ref), (send, send_ref))
        return [
            pltpu.make_async_copy(here.at[span], there.at[span], sems.at[number, part])
            for number, (here, there) in enumerate(pairs)
        ]

    def store(part, total):
        if extra_ref is not None:
            more = extra_ref[:, part * LANES : (part + 1) * LANES].astype(f32)
            total = jnp.concatenate([total, more], axis=1)
        first = side_ref[0] == 0
        mine = jnp.where(first, total[:half], total[half:]).astype(bf16)
        other = jnp.where(first, total[half:], total[:half]).astype(bf16)
        for number in range(block // half):
            rows = slice(part * block + number * half, part * block + (number + 1) * half)
            cols = slice(number * LANES, (number + 1) * LANES)
            keep[rows, :] = mine[:, cols]
            send[rows, :] = other[:, cols]
        for copy in copies(part):
            copy.start()

    @pl.when(step == 0)
    def _():
        store(0, dot(normed_ref[...], gq_ref[...], TN))
        sums_ref[0:1] = column_sum(gq_ref[...].astype(f32))

    @pl.when(step == 1)
    def _():
        total = dot(normed_ref[...], gk_ref[...], TN)
        store(1, total + dot(image_ref[...], gik_ref[...], TN))

    @pl.when(step == 2)
    def _():
        total = dot(normed_ref[...], gv_ref[...], TN)
        store(2, total + dot(image_ref[...], giv_ref[...], TN))
        sums = column_sum(gv_ref[...].astype(f32)) + column_sum(giv_ref[...].astype(f32))
        sums_ref[1:2] = sums
        if spare:
            keep[3 * block :, :] = jnp.zeros((spare, LANES), bf16)
            send[3 * block :, :] = jnp.zeros((spare, LANES), bf16)
            for copy in copies(3):
                copy.start()
        for part in range(4 if spare else 3):
            for copy in copies(part):
                copy.wait()


def weight_grads(order, side, normed, image, grads, lanes, place, spare, extra):
    rows, width = normed.shape
    half_rows = 3 * (lanes // LANES + len(extra)) * width // 2 + spare
    column = lambda height: pl.BlockSpec((height, lanes), lambda *_: (0, place))
    anywhere = pl.BlockSpec(memory_space=pl.ANY)
    return call(
        order,
        functools.partial(weight_kernel, spare),
        (normed, image, *grads, *extra),
        [shaped((2, lanes), f32)] + [shaped((half_rows, LANES), bf16)] * 2,
        "weight_grads",
        weighed(cost(8 * rows * width * lanes, 12 << 20)),
        scalars=(side,),
        grid=(3,),
        specs=[resident(normed.shape), resident(image.shape)]
        + [column(value.shape[0]) for value in grads]
        + [resident(value.shape) for value in extra],
        outs=[resident((2, lanes)), anywhere, anywhere],
        scratch=[pltpu.VMEM((half_rows, LANES), bf16)] * 2 + [pltpu.SemaphoreType.DMA((2, 4))],
    )


def image_grad_kernel(keys_weight, values_weight, keys_ref, values_ref, out_ref):
    total = dot(keys_ref[...], keys_weight[...], NT) + dot(values_ref[...], values_weight[...], NT)
    out_ref[...] = total.astype(bf16)


def image_grads(order, weight, keys, values):
    rows, width = keys.shape
    part = lambda base: pl.BlockSpec((width, width), lambda *_: (0, base))
    return call(
        order,
        image_grad_kernel,
        (weight, weight, keys, values),
        [shaped((rows, width), bf16)],
        "image_grads",
        weighed(cost(4 * rows * width * width, 6 << 20)),
        grid=(1,),
        specs=[part(1), part(2), resident(keys.shape), resident(values.shape)],
        outs=[resident((rows, width))],
    )


def finish_kernel(
    flag_ref,
    hid_ref,
    gmid_ref,
    near_ref,
    far_ref,
    gq_ref,
    gk_ref,
    gv_ref,
    gain_ref,
    weight_ref,
    feed_sums_ref,
    first_sums_ref,
    last_sums_ref,
    _,
    out_ref,
    small_ref,
    sums,
):
    item, block = pl.program_id(0), pl.program_id(1)
    joined = jnp.concatenate([gq_ref[...], gk_ref[...], gv_ref[...]], axis=1)
    grad = dot(joined, weight_ref[...], NT)
    unit, scale = normalise(hid_ref[...].astype(f32))
    both = near_ref[...].astype(f32) + far_ref[...].astype(f32)
    grad = grad + jnp.where((flag_ref[0] == 0) & (block == 0), both, 0.0)
    total = gmid_ref[...] + norm_transpose(unit, scale, gain_ref[...], grad)
    out_ref[...] = total.astype(bf16)
    found = jnp.concatenate([column_sum(grad * unit), column_sum(grad)], axis=0)

    @pl.when((item == 0) & (block == 0))
    def _():
        sums[...] = jnp.zeros(sums.shape, f32)

    sums[0:2] += found

    @pl.when((item == pl.num_programs(0) - 1) & (block == pl.num_programs(1) - 1))
    def _():
        width = sums.shape[1]
        pad = lambda count: jnp.zeros((count, width), f32)
        own = [sums[0:2], feed_sums_ref[0:3], feed_sums_ref[4:8], pad(7)]
        own = jnp.concatenate(own, axis=0)
        bias_sums = jnp.concatenate([first_sums_ref[...], last_sums_ref[...]], axis=1)
        shared = [pad(9), feed_sums_ref[3:4], bias_sums, pad(4)]
        shared = jnp.concatenate(shared, axis=0)
        is_text = flag_ref[0] == 1
        first = jnp.where(is_text, 0.0, own) + shared
        rows = jnp.concatenate([first, jnp.where(is_text, own, 0.0)], axis=0).astype(bf16)
        count = rows.shape[0]
        for number in range(width // LANES):
            cols = slice(number * LANES, (number + 1) * LANES)
            small_ref[number * count : (number + 1) * count, :] = rows[:, cols]
        small_ref[width // LANES * count :, :] = jnp.zeros((SMALL - width // LANES * count, LANES), bf16)


def finish_rows(
    order, flag, hidden, gmid, near, far, grads, gain, weight, feed_sums, bias_sums, keep, item_rows
):
    rows, width = hidden.shape
    blocks = item_rows // IMG_PAD
    mine = pl.BlockSpec((IMG_PAD, width), lambda i, j, *_: (i * blocks + j, 0))
    image = pl.BlockSpec((IMG_PAD, width), lambda i, j, *_: (i, 0))
    fixed = (gain, weight, feed_sums, *bias_sums)
    place = keep.shape[0] // SMALL - 1
    return call(
        order,
        finish_kernel,
        (hidden, gmid, near, far, *grads, *fixed, keep),
        [shaped((rows, width), bf16), shaped(keep.shape, bf16)],
        "finish_rows",
        weighed(cost(6 * rows * width * width, 16 << 20)),
        scalars=(flag,),
        grid=(rows // item_rows, blocks),
        specs=[mine, mine, image, image, mine, mine, mine]
        + [resident(value.shape) for value in fixed]
        + [pl.BlockSpec(memory_space=pl.ANY)],
        outs=[mine, pl.BlockSpec((SMALL, LANES), lambda *_: (place, 0))],
        scratch=[pltpu.VMEM((8, width), f32)],
        aliases={13: 1},
    )


def expert_kernel(half_ref, value_ref, *refs):
    at = 0
    for out in refs[-2:]:
        tall = out.shape[0]
        for part in range(out.shape[1] // LANES):
            piece = value_ref[at : at + tall, :]
            out[:, part * LANES : (part + 1) * LANES] = piece.astype(f32)
            at += tall


def expert_outputs(order, half, first, value, width, units, earlier):
    tall = width // 2
    block_rows = 2 * width // LANES * tall
    return call(
        order,
        expert_kernel,
        (value, *earlier),
        [shaped((units, width), f32), shaped((width, units), f32)],
        "expert_outputs",
        cost(value.size, 6 * value.size),
        scalars=(half,),
        grid=(value.shape[0] // block_rows,),
        specs=[pl.BlockSpec((block_rows, LANES), lambda i, at: (i, 0))]
        + [pl.BlockSpec(memory_space=pl.ANY)] * len(earlier),
        outs=[
            pl.BlockSpec((tall, width), lambda i, at: (2 * (first + i) + at[0], 0)),
            pl.BlockSpec((tall, width), lambda i, at: (at[0], first + i)),
        ],
        aliases={2: 0, 3: 1} if earlier else None,
    )


def first_kernel(half_ref, value_ref, *refs):
    in_ref, out_ref, wide, narrow, sems = refs[-5:]
    tall = wide.shape[1]
    count = value_ref.shape[0] // tall // 3
    columns = in_ref.shape[1] // 3
    rows = pl.ds(pl.multiple_of(half_ref[0] * tall, tall), tall)
    copies = []
    for part in range(3):
        at = part * count * tall
        for number in range(count - 1):
            piece = value_ref[at + number * tall : at + (number + 1) * tall, :]
            wide[part, :, number * LANES : (number + 1) * LANES] = piece.astype(f32)
        piece = value_ref[at + (count - 1) * tall : at + count * tall, :]
        narrow[part] = piece.astype(f32)
        places = (
            (wide, in_ref.at[rows, pl.ds(part * columns, (count - 1) * LANES)]),
            (narrow, out_ref.at[rows, pl.ds(part * LANES, LANES)]),
        )
        for kind, (here, there) in enumerate(places):
            copy = pltpu.make_async_copy(here.at[part], there, sems.at[kind, part])
            copy.start()
            copies.append(copy)
    for copy in copies:
        copy.wait()


def first_outputs(order, half, value, width, earlier):
    tall = width // 2
    anywhere = pl.BlockSpec(memory_space=pl.ANY)
    return call(
        order,
        first_kernel,
        (value, *earlier),
        [shaped((width, 3 * width), f32), shaped((width, width), f32)],
        "first_outputs",
        cost(value.size, 6 * value.size),
        scalars=(half,),
        grid=(1,),
        specs=[resident(value.shape)] + [anywhere] * len(earlier),
        outs=[anywhere, anywhere],
        scratch=[
            pltpu.VMEM((3, tall, width - LANES), f32),
            pltpu.VMEM((3, tall, LANES), f32),
            pltpu.SemaphoreType.DMA((2, 3)),
        ],
        aliases={2: 0, 3: 1} if earlier else None,
    )


def last_kernel(side_ref, flag_ref, mine_ref, got_ref, *refs):
    in_ref, *vec_refs, expand_ref, pair_ref, project_ref, columns, sems = refs[1:]
    tall = columns.shape[2]
    width = in_ref.shape[1] // 3
    copies = []
    for number, ref in enumerate((mine_ref, got_ref)):
        half = side_ref[0] if number == 0 else 1 - side_ref[0]
        rows = pl.ds(pl.multiple_of(half * tall, tall), tall)
        for part in range(3):
            columns[number, part] = ref[part * tall : (part + 1) * tall, :].astype(f32)
            there = in_ref.at[rows, pl.ds((part + 1) * width - LANES, LANES)]
            copy = pltpu.make_async_copy(columns.at[number, part], there, sems.at[number, part])
            copy.start()
            copies.append(copy)
    both = mine_ref[3 * tall :, :].astype(f32) + got_ref[3 * tall :, :].astype(f32)
    rows = jnp.concatenate([both[at * 32 : (at + 1) * 32] for at in range(width // LANES)], axis=1)
    own = jnp.where(flag_ref[0] == 1, rows[16:], rows[:16])
    for number, ref in enumerate(vec_refs):
        ref[...] = own[number : number + 1]
    for number in range(expand_ref.shape[1] // width):
        cols = slice(number * width, (number + 1) * width)
        expand_ref[:, cols] = own[5 + number : 6 + number]
    project_ref[...] = rows[9]
    pair_ref[...] = rows[10:12]
    for copy in copies:
        copy.wait()


def last_outputs(order, side, flag, mine, got, width, units, earlier):
    vecs = [(1, width)] * 5 + [(1, units), (2, width), (width,)]
    anywhere = pl.BlockSpec(memory_space=pl.ANY)
    return call(
        order,
        last_kernel,
        (mine, got, earlier),
        [shaped((width, 3 * width), f32)] + [shaped(shape, f32) for shape in vecs],
        "last_outputs",
        cost(got.size, 6 * got.size),
        scalars=(side, flag),
        grid=(1,),
        specs=[resident(mine.shape), resident(got.shape), anywhere],
        outs=[anywhere] + [resident(shape) for shape in vecs],
        scratch=[
            pltpu.VMEM((2, 3, width // 2, LANES), f32),
            pltpu.SemaphoreType.DMA((2, 3)),
        ],
        aliases={4: 0},
    )


def swap(value, axes, pair_of):
    count = 1
    for axis in axes:
        count *= lax.axis_size(axis)
    return lax.ppermute(value, axes, [(source, pair_of(source)) for source in range(count)])


def place_of(axes):
    place = 0
    for axis in axes:
        place = place * lax.axis_size(axis) + lax.axis_index(axis)
    return place


def late_stages(axes):
    stages = stage_bits(axes)
    if len(axes) == 2 and len(stages) == 5:
        return [stages[0], (0, 0), (2, 3), (3, 2), (4, 4)]
    return stages


def stage_bits(axes):
    count = 1
    for axis in axes:
        count *= lax.axis_size(axis)
    bits = count.bit_length() - 1
    core = len(axes) - 1
    others = [bit for bit in range(bits) if bit != core]
    if len(axes) == 1 and len(others) == 3:
        return [(core, core), (1, 2), (3, 1), (2, 3)]
    if len(axes) == 2 and len(others) == 4:
        return [(core, core), (0, 2), (2, 0), (3, 3), (4, 4)]
    return [(core, core)] + list(zip(others, others[1:] + others[:1]))


class Total:
    def __init__(self, order, axes, keep, send, stages=None):
        self.order = order
        self.axes = axes
        self.core = len(axes) - 1
        self.left = list(stages or stage_bits(axes))
        place = place_of(axes)
        second = ((place >> self.core) & 1) == 1
        sides = [(place >> jnp.where(second, pair[1], pair[0])) & 1 for pair in self.left]
        self.sides = dict(zip(self.left, sides))
        self.back = list(self.left)
        self.terms = (keep, self.exchange(send, self.left.pop(0)))
        self.mine = None

    def exchange(self, value, pair):
        other = lambda source: source ^ (1 << pair[(source >> self.core) & 1])
        self.got = swap(value, self.axes, other)
        return self.got

    def part(self, which, half):
        cut = lambda term: lax.dynamic_slice_in_dim(term, which * half, half, 0).astype(f32)
        return (cut(self.terms[0]) + cut(self.terms[1])).astype(bf16)

    def finish(self):
        while self.left or self.back:
            self.step()

    def step(self):
        if self.left:
            pair = self.left.pop(0)
            self.terms = self.order.after(*self.terms)
            half = self.terms[0].shape[0] // 2
            side = self.sides[pair]
            sent = self.part(1 - side, half)
            self.terms = (self.part(side, half), self.exchange(sent, pair))
            self.order.last = sent
            return
        pair = self.back.pop()
        if self.mine is None:
            self.terms = self.order.after(*self.terms)
            self.mine = (self.terms[0].astype(f32) + self.terms[1].astype(f32)).astype(bf16)
        else:
            mine, got = self.order.after(self.mine, self.got)
            low = jnp.where(self.last == 0, mine, got)
            high = jnp.where(self.last == 0, got, mine)
            self.mine = jnp.concatenate([low, high], axis=0)
        self.order.last = self.mine
        self.last = self.sides[pair]
        self.exchange(self.mine, pair)


def on_device(
    hidden_in,
    image_count,
    text_lengths,
    attend_gain,
    attend_shift,
    project_in,
    bias_pair,
    project_out,
    project_bias,
    feed_gain,
    feed_shift,
    expand_weight,
    expand_bias,
    reduce_weight,
    reduce_bias,
    cotangent,
):
    items, _, rows, width = hidden_in.shape
    units = expand_weight.shape[2]
    is_text = lax.axis_index("mod") == 1
    flag = is_text.astype(jnp.int32)[None]
    hidden = hidden_in.reshape(items * rows, width)
    to_text = lambda value: lax.ppermute(value, "mod", [(0, 1)])
    to_image = lambda value: lax.ppermute(value, "mod", [(1, 0)])

    far_rows = [to_text(hidden_in[item, 0, :IMG_PAD]) for item in range(items)]
    far_vecs = to_text(jnp.concatenate([attend_gain, attend_shift], axis=0))
    order = Order()
    normed, projected = project_rows(
        order, hidden, attend_gain, attend_shift, project_in, bias_pair
    )
    scalars = (flag, image_count, text_lengths)
    images, attended, lses = (), [], []
    for item in range(items):
        images = image_rows(
            order,
            flag,
            item,
            hidden,
            far_rows[item],
            attend_gain,
            attend_shift,
            far_vecs,
            project_in,
            bias_pair,
            rows,
            items,
            images,
        )
        out, lse = attend_forward(order, scalars, item, projected, images[1])
        attended.append(out)
        lses.append(lse)

    side = (lax.axis_index("dp") & 1)[None]
    (
        hidden_out,
        grad_middle,
        grad_attended,
        project_out_grad,
        feed_sums,
        keep0,
        send0,
        keep1,
        send1,
    ) = feed_forward(
        order,
        flag,
        image_count,
        side,
        attended[0],
        attended[1],
        project_out,
        hidden,
        cotangent.reshape(items * rows, width),
        (project_bias[None], feed_gain, feed_shift, reduce_bias),
        expand_weight[0],
        expand_bias,
        reduce_weight[0],
    )
    a = Total(order, ("dp",), keep0, send0)
    c = Total(order, ("dp",), keep1, send1)
    grads = ()

    def backward(item, start, pairs):
        return attend_backward(
            order,
            scalars,
            item,
            start,
            pairs,
            projected,
            images[1],
            attended[item],
            grad_attended,
            lses[item],
            grads,
        )

    def weights(lanes, place, spare, *extra):
        return weight_grads(
            order, side, normed, images[0], grads, lanes, place, spare, extra
        )

    def unpack(half, first, value, earlier=()):
        return expert_outputs(order, half, first, value, width, units, earlier)

    grads = backward(0, 0, 2)
    a.step()
    grads = backward(1, 0, 2)
    c.step()
    grads = backward(0, 2, 2)
    a.step()
    grads = backward(1, 2, 2)
    c.step()
    first_sums, keep, send = weights(2 * LANES, 0, 0, project_out_grad)
    s = Total(order, ("dp", "mod"), keep, send)
    a.step()
    grads = backward(0, 4, 2)
    s.step()
    a.step()
    grads = backward(1, 4, 2)
    c.step()
    s.step()
    near = image_grads(order, project_in, grads[3], grads[4])
    far = to_image(near)
    c.step()
    a.step()
    last_sums, keep, send = weights(LANES, 2, SMALL)
    p = Total(order, ("dp", "mod"), keep, send, late_stages(("dp", "mod")))
    s.step()
    c.step()
    a.step()
    (far,) = order.after(far)
    order.last = far
    grad_in, keep = finish_rows(
        order,
        flag,
        hidden,
        grad_middle,
        near,
        far,
        grads[:3],
        attend_gain,
        project_in,
        feed_sums,
        (first_sums, last_sums),
        keep,
        rows,
    )
    p.terms = (keep, p.got)
    p.step()
    s.step()
    a.step()
    p.step()
    c.step()
    p.step()
    s.step()
    a.finish()
    outputs = unpack(side, 0, a.mine)
    p.step()
    s.step()
    p.step()
    outputs = unpack(1 - side, 0, a.got, outputs)
    p.step()
    s.step()
    p.step()
    c.step()
    s.step()
    p.step()
    c.finish()
    outputs = unpack(side, 2, c.mine, outputs)
    reduce_grad, expand_grad = unpack(1 - side, 2, c.got, outputs)
    p.finish()
    s.step()
    s.finish()
    projections = first_outputs(order, side, s.mine, width, ())
    project_in_grad, project_out_grad = first_outputs(order, 1 - side, s.got, width, projections)
    p.finish()
    (
        project_in_grad,
        attend_gain_grad,
        attend_shift_grad,
        feed_gain_grad,
        feed_shift_grad,
        reduce_bias_grad,
        expand_bias_grad,
        bias_pair_grad,
        project_bias_grad,
    ) = last_outputs(order, side, flag, p.mine, p.got, width, units, project_in_grad)
    return (
        hidden_out.reshape(hidden_in.shape),
        grad_in.reshape(hidden_in.shape),
        attend_gain_grad,
        attend_shift_grad,
        project_in_grad,
        bias_pair_grad,
        project_out_grad,
        project_bias_grad,
        feed_gain_grad,
        feed_shift_grad,
        expand_grad[None],
        expand_bias_grad,
        reduce_grad[None],
        reduce_bias_grad,
    )


def solution(mesh):
    in_specs = (
        P("dp", "mod", None, None),
        P("dp"),
        P("dp", None),
        P("mod", None),
        P("mod", None),
        P(),
        P(),
        P(),
        P(),
        P("mod", None),
        P("mod", None),
        P("mod", None, None),
        P("mod", None),
        P("mod", None, None),
        P("mod", None),
        P("dp", "mod", None, None),
    )
    out_specs = (
        P("dp", "mod", None, None),
        P("dp", "mod", None, None),
        P("mod", None),
        P("mod", None),
        P(),
        P(),
        P(),
        P(),
        P("mod", None),
        P("mod", None),
        P("mod", None, None),
        P("mod", None),
        P("mod", None, None),
        P("mod", None),
    )
    return jax.shard_map(
        on_device, mesh=mesh, in_specs=in_specs, out_specs=out_specs, check_vma=False
    )
```

```python
import functools

import jax
import jax.numpy as jnp
from jax import lax
from jax.experimental import pallas as pl
from jax.experimental.pallas import tpu as pltpu
from jax.sharding import PartitionSpec as P

HEADS = 12
HEAD = 64
IMG_PAD = 256
PAIR = 2 * HEAD
PAIRS = HEADS // 2
GROUP_PAIRS = 2
GROUPS = PAIRS // GROUP_PAIRS
LANES = GROUP_PAIRS * PAIR
SMALL = 128
FF_BLOCK = 768

masked_value = -1e30
norm_eps = 1e-05

bf16 = jnp.bfloat16
f32 = jnp.float32

NN = (((1,), (0,)), ((), ()))
NT = (((1,), (1,)), ((), ()))
TN = (((0,), (0,)), ((), ()))
VMEM_BYTES = 56 << 20


def dot(left, right, dims=NN):
    return lax.dot_general(left, right, dims, preferred_element_type=f32)


def column_sum(values):
    return jnp.sum(values, axis=0, keepdims=True)


def row_mean(values):
    return jnp.mean(values, axis=1, keepdims=True)


def normalise(values):
    centred = values - row_mean(values)
    scale = lax.rsqrt(row_mean(centred * centred) + norm_eps)
    return centred * scale, scale


def norm_transpose(unit, scale, gain, grad):
    grad_unit = grad * gain
    return scale * (grad_unit - row_mean(grad_unit) - unit * row_mean(grad_unit * unit))


def cost(flops, moved, special=0):
    return pl.CostEstimate(flops=flops, bytes_accessed=moved, transcendentals=special)


def weighed(estimate):
    return pl.CostEstimate(
        flops=10 * estimate.flops,
        bytes_accessed=10 * estimate.bytes_accessed,
        transcendentals=10 * estimate.transcendentals,
    )


class Order:
    def __init__(self):
        self.last = None

    def after(self, *values):
        if self.last is None:
            return values
        *values, _ = lax.optimization_barrier((*values, self.last))
        return values


def call(order, kernel, inputs, out_shape, name, estimate, scalars=(), grid=(), specs=None, outs=None,
         scratch=(), aliases=None):
    inputs = (*order.after(inputs[0]), *inputs[1:])
    vmem = pl.BlockSpec(memory_space=pltpu.VMEM)
    found = pl.pallas_call(
        kernel,
        grid_spec=pltpu.PrefetchScalarGridSpec(
            num_scalar_prefetch=len(scalars),
            grid=grid,
            in_specs=[vmem] * len(inputs) if specs is None else list(specs),
            out_specs=[vmem] * len(out_shape) if outs is None else list(outs),
            scratch_shapes=list(scratch),
        ),
        out_shape=list(out_shape),
        input_output_aliases=aliases or {},
        compiler_params=pltpu.CompilerParams(vmem_limit_bytes=VMEM_BYTES),
        cost_estimate=estimate,
        name=name,
    )(*scalars, *inputs)
    order.last = found[-1]
    return found if len(found) > 1 else found[0]


def shaped(shape, dtype):
    return jax.ShapeDtypeStruct(shape, dtype)


def resident(shape):
    return pl.BlockSpec(shape, lambda *_: (0,) * len(shape), pipeline_mode=pl.Buffered(1))


def project_kernel(hid_ref, gain_ref, shift_ref, weight_ref, bias_ref, normed_ref, out_ref):
    unit, _ = normalise(hid_ref[...].astype(f32))
    normed = (unit * gain_ref[...] + shift_ref[...]).astype(bf16)
    normed_ref[...] = normed
    width = normed.shape[1]
    for part in range(3):
        cols = slice(part * width, (part + 1) * width)
        rows = dot(normed, weight_ref[:, cols])
        if part == 0:
            rows = (rows + bias_ref[0:1]).astype(bf16) * jnp.asarray(HEAD**-0.5, bf16)
        if part == 2:
            rows = rows + bias_ref[1:2]
        out_ref[:, cols] = rows.astype(bf16)


def project_rows(order, hidden, gain, shift, weight, bias):
    rows, width = hidden.shape
    block = 256
    blocked = lambda cols: pl.BlockSpec((block, cols), lambda r: (r, 0))
    inputs = (hidden, gain, shift, weight, bias)
    return call(
        order,
        project_kernel,
        inputs,
        [shaped((rows, width), bf16), shaped((rows, 3 * width), bf16)],
        "project_rows",
        cost(6 * rows * width * width, 10 * rows * width + 6 * width * width),
        grid=(rows // block,),
        specs=[blocked(width)] + [resident(value.shape) for value in inputs[1:]],
        outs=[blocked(width), blocked(3 * width)],
    )


def image_kernel(
    flag_ref,
    own_ref,
    far_ref,
    gain_ref,
    shift_ref,
    vec_ref,
    keys_ref,
    values_ref,
    bias_ref,
    *refs,
):
    normed_ref, out_ref = refs[-2:]
    is_text = flag_ref[0] == 1
    hidden = jnp.where(is_text, far_ref[...].astype(f32), own_ref[...].astype(f32))
    gain = jnp.where(is_text, vec_ref[0:1], gain_ref[...])
    shift = jnp.where(is_text, vec_ref[1:2], shift_ref[...])
    unit, _ = normalise(hidden)
    normed = (unit * gain + shift).astype(bf16)
    normed_ref[...] = normed
    width = normed.shape[1]
    out_ref[:, :width] = dot(normed, keys_ref[...]).astype(bf16)
    out_ref[:, width:] = (dot(normed, values_ref[...]) + bias_ref[1:2]).astype(bf16)


def image_rows(
    order, flag, item, hidden, far, gain, shift, vecs, weight, bias, item_rows, items, earlier
):
    width = hidden.shape[1]
    place = item * (item_rows // IMG_PAD)
    half = lambda base: pl.BlockSpec((width, width), lambda *_: (0, base))
    mine = lambda cols: pl.BlockSpec((IMG_PAD, cols), lambda *_: (item, 0))
    inputs = (hidden, far, gain, shift, vecs, weight, weight, bias, *earlier)
    return call(
        order,
        image_kernel,
        inputs,
        [shaped((items * IMG_PAD, width), bf16), shaped((items * IMG_PAD, 2 * width), bf16)],
        "image_rows",
        cost(4 * IMG_PAD * width * width, 6 << 20),
        scalars=(flag,),
        grid=(1,),
        specs=[
            pl.BlockSpec((IMG_PAD, width), lambda *_: (place, 0)),
            resident(far.shape),
            resident(gain.shape),
            resident(shift.shape),
            resident(vecs.shape),
            half(1),
            half(2),
            resident(bias.shape),
        ]
        + [pl.BlockSpec(memory_space=pl.ANY)] * len(earlier),
        outs=[mine(width), mine(2 * width)],
        aliases={9: 0, 10: 1} if earlier else None,
    )


def segments(shape, axis, lengths_ref, item):
    places = lax.broadcasted_iota(jnp.int32, shape, axis)
    total = jnp.zeros(shape, jnp.int32)
    end = 0
    for which in range(lengths_ref.shape[1]):
        end = end + lengths_ref[item, which]
        total += (places >= end).astype(jnp.int32)
    return total


def own_bias(rows, flag_ref, lengths_ref, item):
    shape = (rows, rows)
    same = segments(shape, 0, lengths_ref, item) == segments(shape, 1, lengths_ref, item)
    return jnp.where(same & (flag_ref[0] == 1), 0.0, masked_value).astype(f32)


def image_bias(shape, axis, count_ref, item):
    places = lax.broadcasted_iota(jnp.int32, shape, axis)
    return jnp.where(places < count_ref[item], 0.0, masked_value).astype(f32)


def forward_kernel(
    item,
    flag_ref,
    count_ref,
    lengths_ref,
    q_ref,
    k_ref,
    v_ref,
    ik_ref,
    iv_ref,
    out_ref,
    lse_ref,
    image_part,
    own_part,
):
    rows = q_ref.shape[0]

    @pl.when(pl.program_id(0) == 0)
    def _():
        image_part[...] = image_bias(image_part.shape, 1, count_ref, item)
        own_part[...] = own_bias(rows, flag_ref, lengths_ref, item)

    first = lax.broadcasted_iota(jnp.int32, (rows, PAIR), 1) < HEAD
    zero = jnp.zeros((), bf16)
    q = q_ref[...]
    image_keys, image_values = ik_ref[...], iv_ref[...]
    keys, values = k_ref[...], v_ref[...]
    outs, tops = [], []
    for head in range(2):
        q_head = jnp.where(first, q, zero) if head == 0 else jnp.where(first, zero, q)
        far = dot(q_head, image_keys, NT) + image_part[...]
        own = dot(q_head, keys, NT) + own_part[...]
        top = jnp.maximum(
            jnp.max(far, axis=1, keepdims=True), jnp.max(own, axis=1, keepdims=True)
        )
        far = jnp.exp(far - top)
        own = jnp.exp(own - top)
        total = jnp.sum(far, axis=1, keepdims=True) + jnp.sum(own, axis=1, keepdims=True)
        summed = dot(far.astype(bf16), image_values) + dot(own.astype(bf16), values)
        outs.append(summed / total)
        tops.append(top + jnp.log(total))
    out_ref[...] = jnp.where(first, outs[0], outs[1]).astype(bf16)
    turned = jnp.transpose(jnp.where(first, tops[0], tops[1]))
    lse_ref[0, 0:1, :] = turned[0:1]
    lse_ref[0, 1:2, :] = turned[HEAD : HEAD + 1]


def attend_forward(order, scalars, item, projected, image):
    rows = projected.shape[0] // 2
    spec = lambda base: pl.BlockSpec((rows, PAIR), lambda h, *_: (item, base + h))
    far = lambda base: pl.BlockSpec((IMG_PAD, PAIR), lambda h, *_: (item, base + h))
    keys = rows + IMG_PAD
    return call(
        order,
        functools.partial(forward_kernel, item),
        (projected, projected, projected, image, image),
        [shaped((rows, HEADS * HEAD), bf16), shaped((PAIRS, 2, rows), f32)],
        "attend_forward",
        cost(16 * HEADS * rows * keys * HEAD, 6 << 20, HEADS * rows * keys),
        scalars=scalars,
        grid=(PAIRS,),
        specs=[spec(0), spec(PAIRS), spec(2 * PAIRS), far(0), far(PAIRS)],
        outs=[
            pl.BlockSpec((rows, PAIR), lambda h, *_: (0, h)),
            pl.BlockSpec((1, 2, rows), lambda h, *_: (h, 0, 0)),
        ],
        scratch=[pltpu.VMEM((rows, IMG_PAD), f32), pltpu.VMEM((rows, rows), f32)],
    )


def backward_kernel(
    item,
    flag_ref,
    count_ref,
    lengths_ref,
    q_ref,
    k_ref,
    v_ref,
    ik_ref,
    iv_ref,
    out_ref,
    grad_ref,
    lse_ref,
    *refs,
):
    gq_ref, gk_ref, gv_ref, gik_ref, giv_ref, image_part, own_part = refs[-7:]
    rows = q_ref.shape[0]

    @pl.when(pl.program_id(0) == 0)
    def _():
        image_part[...] = image_bias(image_part.shape, 0, count_ref, item)
        own_part[...] = own_bias(rows, flag_ref, lengths_ref, item)

    first = lax.broadcasted_iota(jnp.int32, (rows, PAIR), 1) < HEAD
    zero = jnp.zeros((), bf16)
    q, grad = q_ref[...], grad_ref[...]
    products = grad.astype(f32) * out_ref[...].astype(f32)
    head_lanes = lax.broadcasted_iota(jnp.int32, (8, PAIR), 1) // HEAD
    head_rows = lax.broadcasted_iota(jnp.int32, (8, PAIR), 0)
    center = lax.dot_general(
        (head_lanes == head_rows).astype(f32),
        products,
        NT,
        preferred_element_type=f32,
        precision=lax.Precision.HIGHEST,
    )
    q_heads = [jnp.where(first, q, zero), jnp.where(first, zero, q)]
    grad_heads = [jnp.where(first, grad, zero), jnp.where(first, zero, grad)]
    lse = lse_ref[0]
    grad_query = [None, None]
    half = rows // 2
    pieces = (
        (ik_ref, iv_ref, gik_ref, giv_ref, image_part, 0, IMG_PAD),
        (k_ref, v_ref, gk_ref, gv_ref, own_part, 0, half),
        (k_ref, v_ref, gk_ref, gv_ref, own_part, half, half),
    )
    for keys_ref, values_ref, gk_out, gv_out, bias, start, count in pieces:
        piece = slice(start, start + count)
        keys, values = keys_ref[piece, :], values_ref[piece, :]
        low_lanes = lax.broadcasted_iota(jnp.int32, (count, PAIR), 1) < HEAD
        grad_keys, grad_values = [], []
        for head in range(2):
            scores = dot(keys, q_heads[head], NT) + bias[piece, :]
            probs = jnp.exp(scores - lse[head : head + 1])
            grad_probs = dot(values, grad_heads[head], NT)
            grad_scores = (probs * (grad_probs - center[head : head + 1])).astype(bf16)
            grad_values.append(dot(probs.astype(bf16), grad))
            grad_keys.append(dot(grad_scores, q))
            term = dot(grad_scores, keys, TN)
            grad_query[head] = term if grad_query[head] is None else grad_query[head] + term
        gk_out[piece, :] = jnp.where(low_lanes, grad_keys[0], grad_keys[1]).astype(bf16)
        gv_out[piece, :] = jnp.where(low_lanes, grad_values[0], grad_values[1]).astype(bf16)
    gq_ref[...] = (jnp.where(first, grad_query[0], grad_query[1]) * HEAD**-0.5).astype(bf16)


def attend_backward(order, scalars, item, start, pairs, projected, image, attended, grad, lse, earlier):
    rows, width = attended.shape
    spec = lambda base: pl.BlockSpec((rows, PAIR), lambda h, *_: (item, base + start + h))
    far = lambda base: pl.BlockSpec((IMG_PAD, PAIR), lambda h, *_: (item, base + start + h))
    own = pl.BlockSpec((rows, PAIR), lambda h, *_: (0, start + h))
    far_outs = pl.BlockSpec((IMG_PAD, PAIR), lambda h, *_: (item, start + h))
    keys = rows + IMG_PAD
    inputs = (projected, projected, projected, image, image, attended, grad, lse)
    first = len(scalars) + len(inputs)
    return call(
        order,
        functools.partial(backward_kernel, item),
        (*inputs, *earlier),
        [shaped((2 * rows, width), bf16)] * 3 + [shaped((2 * IMG_PAD, width), bf16)] * 2,
        "attend_backward",
        weighed(cost(80 * pairs * rows * keys * HEAD, pairs * 2 << 20, 2 * pairs * rows * keys)),
        scalars=scalars,
        grid=(pairs,),
        specs=[
            spec(0),
            spec(PAIRS),
            spec(2 * PAIRS),
            far(0),
            far(PAIRS),
            own,
            spec(0),
            pl.BlockSpec((1, 2, rows), lambda h, *_: (start + h, 0, 0)),
        ]
        + [pl.BlockSpec(memory_space=pl.ANY)] * len(earlier),
        outs=[spec(0), spec(0), spec(0), far_outs, far_outs],
        scratch=[pltpu.VMEM((IMG_PAD, rows), f32), pltpu.VMEM((rows, rows), f32)],
        aliases={first + at: at for at in range(len(earlier))},
    )


def gelu_pair(values):
    share = 0.5 * (1.0 + lax.erf(values * 0.7071067811865476))
    slope = share + values * jnp.exp(-0.5 * values * values) * 0.3989422804014327
    return values * share, slope


def feed_step(step, rows, item_rows, feed, top, result, gfeed, expand_ref, ebias_ref, reduce_ref):
    width = feed.shape[1]
    expand, reduce = expand_ref[...], reduce_ref[...]
    active_parts, gup_parts = [], []
    for start in range(0, rows, item_rows):
        here = slice(start, start + item_rows)
        upward = dot(feed[here, :], expand) + ebias_ref[...]
        gactive = dot(top[here, :], reduce, NT)
        active, slope = gelu_pair(upward)
        active = active.astype(bf16)
        gup = (gactive * slope).astype(bf16)
        result[here, :] += dot(active, reduce)
        gfeed[here, :] += dot(gup, expand, NT)
        active_parts.append(active)
        gup_parts.append(gup)
    active = jnp.concatenate(active_parts, axis=0)
    gup = jnp.concatenate(gup_parts, axis=0)
    greduce = dot(active, top[...], TN).astype(bf16)
    gexpand = dot(feed[...], gup, TN).astype(bf16)
    pieces = [greduce[:, at : at + LANES] for at in range(0, width, LANES)]
    pieces += [gexpand[:, at : at + LANES] for at in range(0, FF_BLOCK, LANES)]
    return pieces, column_sum(gup.astype(f32))


def store_pieces(out, pieces):
    at = 0
    for half in range(2):
        for piece in pieces:
            rows = piece.shape[0] // 2
            out[at : at + rows, :] = piece[half * rows : (half + 1) * rows]
            at += rows


def feed_kernel(
    flag_ref,
    count_ref,
    side_ref,
    att0_ref,
    att1_ref,
    project_ref,
    hid_ref,
    cot_ref,
    project_bias_ref,
    gain_ref,
    shift_ref,
    reduce_bias_ref,
    expand_ref,
    ebias_ref,
    reduce_ref,
    out_ref,
    gmid_ref,
    gatt_ref,
    gproject_ref,
    gvec_ref,
    keep0_ref,
    send0_ref,
    keep1_ref,
    send1_ref,
    middle,
    feed,
    top,
    result,
    gfeed,
    low_out,
    gatt,
    grads,
    grad_sems,
    row_sems,
    *,
    item_rows,
):
    step = pl.program_id(0)
    rows, width = hid_ref.shape
    block = 256
    att_refs = (att0_ref, att1_ref)
    half = grads.shape[1] // 2

    steps = grads.shape[0]

    def grad_copies(which):
        found = []
        chunk, place = divmod(which, steps // 2)
        outs = (keep1_ref, send1_ref) if chunk else (keep0_ref, send0_ref)
        for number, out in enumerate(outs):
            side = side_ref[0] if number == 0 else 1 - side_ref[0]
            here = grads.at[which, pl.ds(pl.multiple_of(side * half, half), half)]
            there = out.at[pl.ds(place * half, half)]
            found.append(pltpu.make_async_copy(here, there, grad_sems.at[which, number]))
        return found

    @pl.when(step == 0)
    def _():
        for start in range(0, rows, block):
            here = slice(start, start + block)
            inside = slice(start % item_rows, start % item_rows + block)
            att = att_refs[start // item_rows][inside, :]
            branch = dot(att, project_ref[...]) + project_bias_ref[...]
            x = hid_ref[here, :].astype(f32) + branch
            middle[here, :] = x
            unit, _ = normalise(x)
            feed[here, :] = (unit * gain_ref[...] + shift_ref[...]).astype(bf16)
            at = lax.broadcasted_iota(jnp.int32, (block, width), 0) + start % item_rows
            limit = jnp.where(flag_ref[0] == 1, item_rows, count_ref[start // item_rows])
            top[here, :] = jnp.where(at < limit, cot_ref[here, :].astype(f32), 0.0).astype(bf16)
            result[here, :] = x + reduce_bias_ref[...]
            gfeed[here, :] = jnp.zeros((block, width), f32)

    pieces, gvec_ref[pl.ds(4 + step, 1), :] = feed_step(
        step, rows, item_rows, feed, top, result, gfeed, expand_ref, ebias_ref, reduce_ref
    )
    store_pieces(grads.at[step], pieces)
    for which in range(steps):

        @pl.when(step == which)
        def _(which=which):
            for copy in grad_copies(which):
                copy.start()

    @pl.when(step == pl.num_programs(0) - 1)
    def _():
        copies = []
        sums = [jnp.zeros((1, width), f32)] * 4
        for number, start in enumerate(range(0, rows, block)):
            here = slice(start, start + block)
            low_out[here, :] = result[here, :].astype(bf16)
            unit, scale = normalise(middle[here, :])
            grad = gfeed[here, :]
            grad_top = top[here, :].astype(f32)
            gmid = grad_top + norm_transpose(unit, scale, gain_ref[...], grad)
            terms = (grad * unit, grad, grad_top, gmid)
            sums = [old + column_sum(new) for old, new in zip(sums, terms)]
            middle[here, :] = gmid
            gbranch = gmid.astype(bf16)
            feed[here, :] = gbranch
            gatt[here, :] = dot(gbranch, project_ref[...], NT).astype(bf16)
            for kind, (mine, there) in enumerate(
                ((low_out, out_ref), (middle, gmid_ref), (gatt, gatt_ref))
            ):
                span = pl.ds(start, block)
                copy = pltpu.make_async_copy(
                    mine.at[span, :], there.at[span, :], row_sems.at[kind, number]
                )
                copy.start()
                copies.append(copy)
        total = dot(att0_ref[...], feed[:item_rows, :], TN)
        total += dot(att1_ref[...], feed[item_rows:, :], TN)
        gproject_ref[...] = total.astype(bf16)
        gvec_ref[0:4, :] = jnp.concatenate(sums, axis=0)
        for copy in copies:
            copy.wait()
        for which in range(steps):
            for copy in grad_copies(which):
                copy.wait()


def feed_forward(order, flag, count, side, att0, att1, project, hidden, cotangent, vecs, expand, ebias, reduce):
    rows, width = hidden.shape
    item_rows = att0.shape[0]
    units = reduce.shape[0]
    steps = units // FF_BLOCK
    block_rows = 2 * width * FF_BLOCK // LANES
    fixed = (att0, att1, project, hidden, cotangent, *vecs)
    anywhere = pl.BlockSpec(memory_space=pl.ANY)
    return call(
        order,
        functools.partial(feed_kernel, item_rows=item_rows),
        (*fixed, expand, ebias, reduce),
        [
            shaped((rows, width), bf16),
            shaped((rows, width), f32),
            shaped((rows, width), bf16),
            shaped((width, width), bf16),
            shaped((4 + steps, width), f32),
        ]
        + [shaped((steps // 2 * block_rows // 2, LANES), bf16)] * 4,
        "feed_forward",
        cost(12 * rows * width * units, 40 << 20, 2 * rows * units),
        scalars=(flag, count, side),
        grid=(steps,),
        specs=[resident(value.shape) for value in fixed]
        + [
            pl.BlockSpec((width, FF_BLOCK), lambda j, *_: (0, j)),
            pl.BlockSpec((1, FF_BLOCK), lambda j, *_: (0, j)),
            pl.BlockSpec((FF_BLOCK, width), lambda j, *_: (j, 0)),
        ],
        outs=[
            anywhere,
            anywhere,
            anywhere,
            resident((width, width)),
            resident((4 + steps, width)),
        ]
        + [anywhere] * 4,
        scratch=[
            pltpu.VMEM((rows, width), f32),
            pltpu.VMEM((rows, width), bf16),
            pltpu.VMEM((rows, width), bf16),
            pltpu.VMEM((rows, width), f32),
            pltpu.VMEM((rows, width), f32),
            pltpu.VMEM((rows, width), bf16),
            pltpu.VMEM((rows, width), bf16),
            pltpu.VMEM((steps, block_rows, LANES), bf16),
            pltpu.SemaphoreType.DMA((steps, 2)),
            pltpu.SemaphoreType.DMA((3, rows // 256)),
        ],
    )


def weight_kernel(
    spare,
    side_ref,
    normed_ref,
    image_ref,
    gq_ref,
    gk_ref,
    gv_ref,
    gik_ref,
    giv_ref,
    *refs,
):
    extra_ref = None if spare else refs[0]
    sums_ref, keep_ref, send_ref, keep, send, sems = refs[-6:]
    step = pl.program_id(0)
    width = normed_ref.shape[1]
    half = width // 2
    columns = gq_ref.shape[1] // LANES
    block = half * (columns if spare else columns + 1)

    def copies(part):
        span = pl.ds(part * block, block if part < 3 else spare)
        pairs = ((keep, keep_ref), (send, send_ref))
        return [
            pltpu.make_async_copy(here.at[span], there.at[span], sems.at[number, part])
            for number, (here, there) in enumerate(pairs)
        ]

    def store(part, total):
        if extra_ref is not None:
            more = extra_ref[:, part * LANES : (part + 1) * LANES].astype(f32)
            total = jnp.concatenate([total, more], axis=1)
        first = side_ref[0] == 0
        mine = jnp.where(first, total[:half], total[half:]).astype(bf16)
        other = jnp.where(first, total[half:], total[:half]).astype(bf16)
        for number in range(block // half):
            rows = slice(part * block + number * half, part * block + (number + 1) * half)
            cols = slice(number * LANES, (number + 1) * LANES)
            keep[rows, :] = mine[:, cols]
            send[rows, :] = other[:, cols]
        for copy in copies(part):
            copy.start()

    @pl.when(step == 0)
    def _():
        store(0, dot(normed_ref[...], gq_ref[...], TN))
        sums_ref[0:1] = column_sum(gq_ref[...].astype(f32))

    @pl.when(step == 1)
    def _():
        total = dot(normed_ref[...], gk_ref[...], TN)
        store(1, total + dot(image_ref[...], gik_ref[...], TN))

    @pl.when(step == 2)
    def _():
        total = dot(normed_ref[...], gv_ref[...], TN)
        store(2, total + dot(image_ref[...], giv_ref[...], TN))
        sums = column_sum(gv_ref[...].astype(f32)) + column_sum(giv_ref[...].astype(f32))
        sums_ref[1:2] = sums
        if spare:
            keep[3 * block :, :] = jnp.zeros((spare, LANES), bf16)
            send[3 * block :, :] = jnp.zeros((spare, LANES), bf16)
            for copy in copies(3):
                copy.start()
        for part in range(4 if spare else 3):
            for copy in copies(part):
                copy.wait()


def weight_grads(order, side, normed, image, grads, lanes, place, spare, extra):
    rows, width = normed.shape
    half_rows = 3 * (lanes // LANES + len(extra)) * width // 2 + spare
    column = lambda height: pl.BlockSpec((height, lanes), lambda *_: (0, place))
    anywhere = pl.BlockSpec(memory_space=pl.ANY)
    return call(
        order,
        functools.partial(weight_kernel, spare),
        (normed, image, *grads, *extra),
        [shaped((2, lanes), f32)] + [shaped((half_rows, LANES), bf16)] * 2,
        "weight_grads",
        weighed(cost(8 * rows * width * lanes, 12 << 20)),
        scalars=(side,),
        grid=(3,),
        specs=[resident(normed.shape), resident(image.shape)]
        + [column(value.shape[0]) for value in grads]
        + [resident(value.shape) for value in extra],
        outs=[resident((2, lanes)), anywhere, anywhere],
        scratch=[pltpu.VMEM((half_rows, LANES), bf16)] * 2 + [pltpu.SemaphoreType.DMA((2, 4))],
    )


def image_grad_kernel(keys_weight, values_weight, keys_ref, values_ref, out_ref):
    total = dot(keys_ref[...], keys_weight[...], NT) + dot(values_ref[...], values_weight[...], NT)
    out_ref[...] = total.astype(bf16)


def image_grads(order, weight, keys, values):
    rows, width = keys.shape
    part = lambda base: pl.BlockSpec((width, width), lambda *_: (0, base))
    return call(
        order,
        image_grad_kernel,
        (weight, weight, keys, values),
        [shaped((rows, width), bf16)],
        "image_grads",
        weighed(cost(4 * rows * width * width, 6 << 20)),
        grid=(1,),
        specs=[part(1), part(2), resident(keys.shape), resident(values.shape)],
        outs=[resident((rows, width))],
    )


def finish_kernel(
    flag_ref,
    hid_ref,
    gmid_ref,
    near_ref,
    far_ref,
    gq_ref,
    gk_ref,
    gv_ref,
    gain_ref,
    weight_ref,
    feed_sums_ref,
    first_sums_ref,
    last_sums_ref,
    _,
    out_ref,
    small_ref,
    sums,
):
    item, block = pl.program_id(0), pl.program_id(1)
    joined = jnp.concatenate([gq_ref[...], gk_ref[...], gv_ref[...]], axis=1)
    grad = dot(joined, weight_ref[...], NT)
    unit, scale = normalise(hid_ref[...].astype(f32))
    both = near_ref[...].astype(f32) + far_ref[...].astype(f32)
    grad = grad + jnp.where((flag_ref[0] == 0) & (block == 0), both, 0.0)
    total = gmid_ref[...] + norm_transpose(unit, scale, gain_ref[...], grad)
    out_ref[...] = total.astype(bf16)
    found = jnp.concatenate([column_sum(grad * unit), column_sum(grad)], axis=0)

    @pl.when((item == 0) & (block == 0))
    def _():
        sums[...] = jnp.zeros(sums.shape, f32)

    sums[0:2] += found

    @pl.when((item == pl.num_programs(0) - 1) & (block == pl.num_programs(1) - 1))
    def _():
        width = sums.shape[1]
        pad = lambda count: jnp.zeros((count, width), f32)
        own = [sums[0:2], feed_sums_ref[0:3], feed_sums_ref[4:8], pad(7)]
        own = jnp.concatenate(own, axis=0)
        bias_sums = jnp.concatenate([first_sums_ref[...], last_sums_ref[...]], axis=1)
        shared = [pad(9), feed_sums_ref[3:4], bias_sums, pad(4)]
        shared = jnp.concatenate(shared, axis=0)
        is_text = flag_ref[0] == 1
        first = jnp.where(is_text, 0.0, own) + shared
        rows = jnp.concatenate([first, jnp.where(is_text, own, 0.0)], axis=0).astype(bf16)
        count = rows.shape[0]
        for number in range(width // LANES):
            cols = slice(number * LANES, (number + 1) * LANES)
            small_ref[number * count : (number + 1) * count, :] = rows[:, cols]
        small_ref[width // LANES * count :, :] = jnp.zeros((SMALL - width // LANES * count, LANES), bf16)


def finish_rows(
    order, flag, hidden, gmid, near, far, grads, gain, weight, feed_sums, bias_sums, keep, item_rows
):
    rows, width = hidden.shape
    blocks = item_rows // IMG_PAD
    mine = pl.BlockSpec((IMG_PAD, width), lambda i, j, *_: (i * blocks + j, 0))
    image = pl.BlockSpec((IMG_PAD, width), lambda i, j, *_: (i, 0))
    fixed = (gain, weight, feed_sums, *bias_sums)
    place = keep.shape[0] // SMALL - 1
    return call(
        order,
        finish_kernel,
        (hidden, gmid, near, far, *grads, *fixed, keep),
        [shaped((rows, width), bf16), shaped(keep.shape, bf16)],
        "finish_rows",
        weighed(cost(6 * rows * width * width, 16 << 20)),
        scalars=(flag,),
        grid=(rows // item_rows, blocks),
        specs=[mine, mine, image, image, mine, mine, mine]
        + [resident(value.shape) for value in fixed]
        + [pl.BlockSpec(memory_space=pl.ANY)],
        outs=[mine, pl.BlockSpec((SMALL, LANES), lambda *_: (place, 0))],
        scratch=[pltpu.VMEM((8, width), f32)],
        aliases={13: 1},
    )


def expert_kernel(half_ref, value_ref, *refs):
    at = 0
    for out in refs[-2:]:
        tall = out.shape[0]
        for part in range(out.shape[1] // LANES):
            piece = value_ref[at : at + tall, :]
            out[:, part * LANES : (part + 1) * LANES] = piece.astype(f32)
            at += tall


def expert_outputs(order, half, first, value, width, units, earlier):
    tall = width // 2
    block_rows = 2 * width // LANES * tall
    return call(
        order,
        expert_kernel,
        (value, *earlier),
        [shaped((units, width), f32), shaped((width, units), f32)],
        "expert_outputs",
        cost(value.size, 6 * value.size),
        scalars=(half,),
        grid=(value.shape[0] // block_rows,),
        specs=[pl.BlockSpec((block_rows, LANES), lambda i, at: (i, 0))]
        + [pl.BlockSpec(memory_space=pl.ANY)] * len(earlier),
        outs=[
            pl.BlockSpec((tall, width), lambda i, at: (2 * (first + i) + at[0], 0)),
            pl.BlockSpec((tall, width), lambda i, at: (at[0], first + i)),
        ],
        aliases={2: 0, 3: 1} if earlier else None,
    )


def first_kernel(half_ref, value_ref, *refs):
    in_ref, out_ref, wide, narrow, sems = refs[-5:]
    tall = wide.shape[1]
    count = value_ref.shape[0] // tall // 3
    columns = in_ref.shape[1] // 3
    rows = pl.ds(pl.multiple_of(half_ref[0] * tall, tall), tall)
    copies = []
    for part in range(3):
        at = part * count * tall
        for number in range(count - 1):
            piece = value_ref[at + number * tall : at + (number + 1) * tall, :]
            wide[part, :, number * LANES : (number + 1) * LANES] = piece.astype(f32)
        piece = value_ref[at + (count - 1) * tall : at + count * tall, :]
        narrow[part] = piece.astype(f32)
        places = (
            (wide, in_ref.at[rows, pl.ds(part * columns, (count - 1) * LANES)]),
            (narrow, out_ref.at[rows, pl.ds(part * LANES, LANES)]),
        )
        for kind, (here, there) in enumerate(places):
            copy = pltpu.make_async_copy(here.at[part], there, sems.at[kind, part])
            copy.start()
            copies.append(copy)
    for copy in copies:
        copy.wait()


def first_outputs(order, half, value, width, earlier):
    tall = width // 2
    anywhere = pl.BlockSpec(memory_space=pl.ANY)
    return call(
        order,
        first_kernel,
        (value, *earlier),
        [shaped((width, 3 * width), f32), shaped((width, width), f32)],
        "first_outputs",
        cost(value.size, 6 * value.size),
        scalars=(half,),
        grid=(1,),
        specs=[resident(value.shape)] + [anywhere] * len(earlier),
        outs=[anywhere, anywhere],
        scratch=[
            pltpu.VMEM((3, tall, width - LANES), f32),
            pltpu.VMEM((3, tall, LANES), f32),
            pltpu.SemaphoreType.DMA((2, 3)),
        ],
        aliases={2: 0, 3: 1} if earlier else None,
    )


def last_kernel(side_ref, flag_ref, mine_ref, got_ref, *refs):
    in_ref, *vec_refs, expand_ref, pair_ref, project_ref, columns, sems = refs[1:]
    tall = columns.shape[2]
    width = in_ref.shape[1] // 3
    copies = []
    for number, ref in enumerate((mine_ref, got_ref)):
        half = side_ref[0] if number == 0 else 1 - side_ref[0]
        rows = pl.ds(pl.multiple_of(half * tall, tall), tall)
        for part in range(3):
            columns[number, part] = ref[part * tall : (part + 1) * tall, :].astype(f32)
            there = in_ref.at[rows, pl.ds((part + 1) * width - LANES, LANES)]
            copy = pltpu.make_async_copy(columns.at[number, part], there, sems.at[number, part])
            copy.start()
            copies.append(copy)
    both = mine_ref[3 * tall :, :].astype(f32) + got_ref[3 * tall :, :].astype(f32)
    rows = jnp.concatenate([both[at * 32 : (at + 1) * 32] for at in range(width // LANES)], axis=1)
    own = jnp.where(flag_ref[0] == 1, rows[16:], rows[:16])
    for number, ref in enumerate(vec_refs):
        ref[...] = own[number : number + 1]
    for number in range(expand_ref.shape[1] // width):
        cols = slice(number * width, (number + 1) * width)
        expand_ref[:, cols] = own[5 + number : 6 + number]
    project_ref[...] = rows[9]
    pair_ref[...] = rows[10:12]
    for copy in copies:
        copy.wait()


def last_outputs(order, side, flag, mine, got, width, units, earlier):
    vecs = [(1, width)] * 5 + [(1, units), (2, width), (width,)]
    anywhere = pl.BlockSpec(memory_space=pl.ANY)
    return call(
        order,
        last_kernel,
        (mine, got, earlier),
        [shaped((width, 3 * width), f32)] + [shaped(shape, f32) for shape in vecs],
        "last_outputs",
        cost(got.size, 6 * got.size),
        scalars=(side, flag),
        grid=(1,),
        specs=[resident(mine.shape), resident(got.shape), anywhere],
        outs=[anywhere] + [resident(shape) for shape in vecs],
        scratch=[
            pltpu.VMEM((2, 3, width // 2, LANES), f32),
            pltpu.SemaphoreType.DMA((2, 3)),
        ],
        aliases={4: 0},
    )


def swap(value, axes, pair_of):
    count = 1
    for axis in axes:
        count *= lax.axis_size(axis)
    return lax.ppermute(value, axes, [(source, pair_of(source)) for source in range(count)])


def place_of(axes):
    place = 0
    for axis in axes:
        place = place * lax.axis_size(axis) + lax.axis_index(axis)
    return place


def late_stages(axes):
    stages = stage_bits(axes)
    if len(axes) == 2 and len(stages) == 5:
        return [stages[0], (3, 3), (0, 2), (2, 0), (4, 4)]
    return stages


def stage_bits(axes):
    count = 1
    for axis in axes:
        count *= lax.axis_size(axis)
    bits = count.bit_length() - 1
    core = len(axes) - 1
    others = [bit for bit in range(bits) if bit != core]
    if len(axes) == 1 and len(others) == 3:
        return [(core, core), (1, 2), (3, 1), (2, 3)]
    if len(axes) == 2 and len(others) == 4:
        return [(core, core), (0, 2), (2, 0), (3, 3), (4, 4)]
    return [(core, core)] + list(zip(others, others[1:] + others[:1]))


class Total:
    def __init__(self, order, axes, keep, send, stages=None):
        self.order = order
        self.axes = axes
        self.core = len(axes) - 1
        self.left = list(stages or stage_bits(axes))
        place = place_of(axes)
        second = ((place >> self.core) & 1) == 1
        sides = [(place >> jnp.where(second, pair[1], pair[0])) & 1 for pair in self.left]
        self.sides = dict(zip(self.left, sides))
        self.back = list(self.left)
        self.terms = (keep, self.exchange(send, self.left.pop(0)))
        self.mine = None

    def exchange(self, value, pair):
        other = lambda source: source ^ (1 << pair[(source >> self.core) & 1])
        self.got = swap(value, self.axes, other)
        return self.got

    def part(self, which, half):
        cut = lambda term: lax.dynamic_slice_in_dim(term, which * half, half, 0).astype(f32)
        return (cut(self.terms[0]) + cut(self.terms[1])).astype(bf16)

    def finish(self):
        while self.left or self.back:
            self.step()

    def step(self):
        if self.left:
            pair = self.left.pop(0)
            self.terms = self.order.after(*self.terms)
            half = self.terms[0].shape[0] // 2
            side = self.sides[pair]
            sent = self.part(1 - side, half)
            self.terms = (self.part(side, half), self.exchange(sent, pair))
            self.order.last = sent
            return
        pair = self.back.pop()
        if self.mine is None:
            self.terms = self.order.after(*self.terms)
            self.mine = (self.terms[0].astype(f32) + self.terms[1].astype(f32)).astype(bf16)
        else:
            mine, got = self.order.after(self.mine, self.got)
            low = jnp.where(self.last == 0, mine, got)
            high = jnp.where(self.last == 0, got, mine)
            self.mine = jnp.concatenate([low, high], axis=0)
        self.order.last = self.mine
        self.last = self.sides[pair]
        self.exchange(self.mine, pair)


def on_device(
    hidden_in,
    image_count,
    text_lengths,
    attend_gain,
    attend_shift,
    project_in,
    bias_pair,
    project_out,
    project_bias,
    feed_gain,
    feed_shift,
    expand_weight,
    expand_bias,
    reduce_weight,
    reduce_bias,
    cotangent,
):
    items, _, rows, width = hidden_in.shape
    units = expand_weight.shape[2]
    is_text = lax.axis_index("mod") == 1
    flag = is_text.astype(jnp.int32)[None]
    hidden = hidden_in.reshape(items * rows, width)
    to_text = lambda value: lax.ppermute(value, "mod", [(0, 1)])
    to_image = lambda value: lax.ppermute(value, "mod", [(1, 0)])

    far_rows = [to_text(hidden_in[item, 0, :IMG_PAD]) for item in range(items)]
    far_vecs = to_text(jnp.concatenate([attend_gain, attend_shift], axis=0))
    order = Order()
    normed, projected = project_rows(
        order, hidden, attend_gain, attend_shift, project_in, bias_pair
    )
    scalars = (flag, image_count, text_lengths)
    images, attended, lses = (), [], []
    for item in range(items):
        images = image_rows(
            order,
            flag,
            item,
            hidden,
            far_rows[item],
            attend_gain,
            attend_shift,
            far_vecs,
            project_in,
            bias_pair,
            rows,
            items,
            images,
        )
        out, lse = attend_forward(order, scalars, item, projected, images[1])
        attended.append(out)
        lses.append(lse)

    side = (lax.axis_index("dp") & 1)[None]
    (
        hidden_out,
        grad_middle,
        grad_attended,
        project_out_grad,
        feed_sums,
        keep0,
        send0,
        keep1,
        send1,
    ) = feed_forward(
        order,
        flag,
        image_count,
        side,
        attended[0],
        attended[1],
        project_out,
        hidden,
        cotangent.reshape(items * rows, width),
        (project_bias[None], feed_gain, feed_shift, reduce_bias),
        expand_weight[0],
        expand_bias,
        reduce_weight[0],
    )
    a = Total(order, ("dp",), keep0, send0)
    c = Total(order, ("dp",), keep1, send1)
    grads = ()

    def backward(item, start, pairs):
        return attend_backward(
            order,
            scalars,
            item,
            start,
            pairs,
            projected,
            images[1],
            attended[item],
            grad_attended,
            lses[item],
            grads,
        )

    def weights(lanes, place, spare, *extra):
        return weight_grads(
            order, side, normed, images[0], grads, lanes, place, spare, extra
        )

    def unpack(half, first, value, earlier=()):
        return expert_outputs(order, half, first, value, width, units, earlier)

    grads = backward(0, 0, 2)
    a.step()
    grads = backward(1, 0, 2)
    c.step()
    grads = backward(0, 2, 2)
    a.step()
    grads = backward(1, 2, 2)
    c.step()
    first_sums, keep, send = weights(2 * LANES, 0, 0, project_out_grad)
    s = Total(order, ("dp", "mod"), keep, send)
    a.step()
    grads = backward(0, 4, 2)
    s.step()
    a.step()
    grads = backward(1, 4, 2)
    c.step()
    s.step()
    near = image_grads(order, project_in, grads[3], grads[4])
    far = to_image(near)
    c.step()
    a.step()
    last_sums, keep, send = weights(LANES, 2, SMALL)
    p = Total(order, ("dp", "mod"), keep, send, late_stages(("dp", "mod")))
    s.step()
    c.step()
    a.step()
    (far,) = order.after(far)
    order.last = far
    grad_in, keep = finish_rows(
        order,
        flag,
        hidden,
        grad_middle,
        near,
        far,
        grads[:3],
        attend_gain,
        project_in,
        feed_sums,
        (first_sums, last_sums),
        keep,
        rows,
    )
    p.terms = (keep, p.got)
    p.step()
    s.step()
    a.step()
    p.step()
    c.step()
    p.step()
    s.step()
    a.finish()
    outputs = unpack(side, 0, a.mine)
    p.step()
    s.step()
    p.step()
    outputs = unpack(1 - side, 0, a.got, outputs)
    p.step()
    s.step()
    p.step()
    c.step()
    s.step()
    p.step()
    c.finish()
    outputs = unpack(side, 2, c.mine, outputs)
    reduce_grad, expand_grad = unpack(1 - side, 2, c.got, outputs)
    p.finish()
    s.step()
    s.finish()
    projections = first_outputs(order, side, s.mine, width, ())
    project_in_grad, project_out_grad = first_outputs(order, 1 - side, s.got, width, projections)
    p.finish()
    (
        project_in_grad,
        attend_gain_grad,
        attend_shift_grad,
        feed_gain_grad,
        feed_shift_grad,
        reduce_bias_grad,
        expand_bias_grad,
        bias_pair_grad,
        project_bias_grad,
    ) = last_outputs(order, side, flag, p.mine, p.got, width, units, project_in_grad)
    return (
        hidden_out.reshape(hidden_in.shape),
        grad_in.reshape(hidden_in.shape),
        attend_gain_grad,
        attend_shift_grad,
        project_in_grad,
        bias_pair_grad,
        project_out_grad,
        project_bias_grad,
        feed_gain_grad,
        feed_shift_grad,
        expand_grad[None],
        expand_bias_grad,
        reduce_grad[None],
        reduce_bias_grad,
    )


def solution(mesh):
    in_specs = (
        P("dp", "mod", None, None),
        P("dp"),
        P("dp", None),
        P("mod", None),
        P("mod", None),
        P(),
        P(),
        P(),
        P(),
        P("mod", None),
        P("mod", None),
        P("mod", None, None),
        P("mod", None),
        P("mod", None, None),
        P("mod", None),
        P("dp", "mod", None, None),
    )
    out_specs = (
        P("dp", "mod", None, None),
        P("dp", "mod", None, None),
        P("mod", None),
        P("mod", None),
        P(),
        P(),
        P(),
        P(),
        P("mod", None),
        P("mod", None),
        P("mod", None, None),
        P("mod", None),
        P("mod", None, None),
        P("mod", None),
    )
    return jax.shard_map(
        on_device, mesh=mesh, in_specs=in_specs, out_specs=out_specs, check_vma=False
    )
```

```python
import functools

import jax
import jax.numpy as jnp
from jax import lax
from jax.experimental import pallas as pl
from jax.experimental.pallas import tpu as pltpu
from jax.sharding import PartitionSpec as P

HEADS = 12
HEAD = 64
IMG_PAD = 256
PAIR = 2 * HEAD
PAIRS = HEADS // 2
GROUP_PAIRS = 2
GROUPS = PAIRS // GROUP_PAIRS
LANES = GROUP_PAIRS * PAIR
SMALL = 128
FF_BLOCK = 768

masked_value = -1e30
norm_eps = 1e-05

bf16 = jnp.bfloat16
f32 = jnp.float32

NN = (((1,), (0,)), ((), ()))
NT = (((1,), (1,)), ((), ()))
TN = (((0,), (0,)), ((), ()))
VMEM_BYTES = 56 << 20


def dot(left, right, dims=NN):
    return lax.dot_general(left, right, dims, preferred_element_type=f32)


def column_sum(values):
    return jnp.sum(values, axis=0, keepdims=True)


def row_mean(values):
    return jnp.mean(values, axis=1, keepdims=True)


def normalise(values):
    centred = values - row_mean(values)
    scale = lax.rsqrt(row_mean(centred * centred) + norm_eps)
    return centred * scale, scale


def norm_transpose(unit, scale, gain, grad):
    grad_unit = grad * gain
    return scale * (grad_unit - row_mean(grad_unit) - unit * row_mean(grad_unit * unit))


def cost(flops, moved, special=0):
    return pl.CostEstimate(flops=flops, bytes_accessed=moved, transcendentals=special)


def weighed(estimate):
    return pl.CostEstimate(
        flops=10 * estimate.flops,
        bytes_accessed=10 * estimate.bytes_accessed,
        transcendentals=10 * estimate.transcendentals,
    )


class Order:
    def __init__(self):
        self.last = None

    def after(self, *values):
        if self.last is None:
            return values
        *values, _ = lax.optimization_barrier((*values, self.last))
        return values


def call(order, kernel, inputs, out_shape, name, estimate, scalars=(), grid=(), specs=None, outs=None,
         scratch=(), aliases=None):
    inputs = (*order.after(inputs[0]), *inputs[1:])
    vmem = pl.BlockSpec(memory_space=pltpu.VMEM)
    found = pl.pallas_call(
        kernel,
        grid_spec=pltpu.PrefetchScalarGridSpec(
            num_scalar_prefetch=len(scalars),
            grid=grid,
            in_specs=[vmem] * len(inputs) if specs is None else list(specs),
            out_specs=[vmem] * len(out_shape) if outs is None else list(outs),
            scratch_shapes=list(scratch),
        ),
        out_shape=list(out_shape),
        input_output_aliases=aliases or {},
        compiler_params=pltpu.CompilerParams(vmem_limit_bytes=VMEM_BYTES),
        cost_estimate=estimate,
        name=name,
    )(*scalars, *inputs)
    order.last = found[-1]
    return found if len(found) > 1 else found[0]


def shaped(shape, dtype):
    return jax.ShapeDtypeStruct(shape, dtype)


def resident(shape):
    return pl.BlockSpec(shape, lambda *_: (0,) * len(shape), pipeline_mode=pl.Buffered(1))


def project_kernel(hid_ref, gain_ref, shift_ref, weight_ref, bias_ref, normed_ref, out_ref):
    unit, _ = normalise(hid_ref[...].astype(f32))
    normed = (unit * gain_ref[...] + shift_ref[...]).astype(bf16)
    normed_ref[...] = normed
    width = normed.shape[1]
    for part in range(3):
        cols = slice(part * width, (part + 1) * width)
        rows = dot(normed, weight_ref[:, cols])
        if part == 0:
            rows = (rows + bias_ref[0:1]).astype(bf16) * jnp.asarray(HEAD**-0.5, bf16)
        if part == 2:
            rows = rows + bias_ref[1:2]
        out_ref[:, cols] = rows.astype(bf16)


def project_rows(order, hidden, gain, shift, weight, bias):
    rows, width = hidden.shape
    block = 256
    blocked = lambda cols: pl.BlockSpec((block, cols), lambda r: (r, 0))
    inputs = (hidden, gain, shift, weight, bias)
    return call(
        order,
        project_kernel,
        inputs,
        [shaped((rows, width), bf16), shaped((rows, 3 * width), bf16)],
        "project_rows",
        cost(6 * rows * width * width, 10 * rows * width + 6 * width * width),
        grid=(rows // block,),
        specs=[blocked(width)] + [resident(value.shape) for value in inputs[1:]],
        outs=[blocked(width), blocked(3 * width)],
    )


def image_kernel(
    flag_ref,
    own_ref,
    far_ref,
    gain_ref,
    shift_ref,
    vec_ref,
    keys_ref,
    values_ref,
    bias_ref,
    *refs,
):
    normed_ref, out_ref = refs[-2:]
    is_text = flag_ref[0] == 1
    hidden = jnp.where(is_text, far_ref[...].astype(f32), own_ref[...].astype(f32))
    gain = jnp.where(is_text, vec_ref[0:1], gain_ref[...])
    shift = jnp.where(is_text, vec_ref[1:2], shift_ref[...])
    unit, _ = normalise(hidden)
    normed = (unit * gain + shift).astype(bf16)
    normed_ref[...] = normed
    width = normed.shape[1]
    out_ref[:, :width] = dot(normed, keys_ref[...]).astype(bf16)
    out_ref[:, width:] = (dot(normed, values_ref[...]) + bias_ref[1:2]).astype(bf16)


def image_rows(
    order, flag, item, hidden, far, gain, shift, vecs, weight, bias, item_rows, items, earlier
):
    width = hidden.shape[1]
    place = item * (item_rows // IMG_PAD)
    half = lambda base: pl.BlockSpec((width, width), lambda *_: (0, base))
    mine = lambda cols: pl.BlockSpec((IMG_PAD, cols), lambda *_: (item, 0))
    inputs = (hidden, far, gain, shift, vecs, weight, weight, bias, *earlier)
    return call(
        order,
        image_kernel,
        inputs,
        [shaped((items * IMG_PAD, width), bf16), shaped((items * IMG_PAD, 2 * width), bf16)],
        "image_rows",
        cost(4 * IMG_PAD * width * width, 6 << 20),
        scalars=(flag,),
        grid=(1,),
        specs=[
            pl.BlockSpec((IMG_PAD, width), lambda *_: (place, 0)),
            resident(far.shape),
            resident(gain.shape),
            resident(shift.shape),
            resident(vecs.shape),
            half(1),
            half(2),
            resident(bias.shape),
        ]
        + [pl.BlockSpec(memory_space=pl.ANY)] * len(earlier),
        outs=[mine(width), mine(2 * width)],
        aliases={9: 0, 10: 1} if earlier else None,
    )


def segments(shape, axis, lengths_ref, item):
    places = lax.broadcasted_iota(jnp.int32, shape, axis)
    total = jnp.zeros(shape, jnp.int32)
    end = 0
    for which in range(lengths_ref.shape[1]):
        end = end + lengths_ref[item, which]
        total += (places >= end).astype(jnp.int32)
    return total


def own_bias(rows, flag_ref, lengths_ref, item):
    shape = (rows, rows)
    same = segments(shape, 0, lengths_ref, item) == segments(shape, 1, lengths_ref, item)
    return jnp.where(same & (flag_ref[0] == 1), 0.0, masked_value).astype(f32)


def image_bias(shape, axis, count_ref, item):
    places = lax.broadcasted_iota(jnp.int32, shape, axis)
    return jnp.where(places < count_ref[item], 0.0, masked_value).astype(f32)


def forward_kernel(
    item,
    flag_ref,
    count_ref,
    lengths_ref,
    q_ref,
    k_ref,
    v_ref,
    ik_ref,
    iv_ref,
    out_ref,
    lse_ref,
    image_part,
    own_part,
):
    rows = q_ref.shape[0]

    @pl.when(pl.program_id(0) == 0)
    def _():
        image_part[...] = image_bias(image_part.shape, 1, count_ref, item)
        own_part[...] = own_bias(rows, flag_ref, lengths_ref, item)

    first = lax.broadcasted_iota(jnp.int32, (rows, PAIR), 1) < HEAD
    zero = jnp.zeros((), bf16)
    q = q_ref[...]
    image_keys, image_values = ik_ref[...], iv_ref[...]
    keys, values = k_ref[...], v_ref[...]
    outs, tops = [], []
    for head in range(2):
        q_head = jnp.where(first, q, zero) if head == 0 else jnp.where(first, zero, q)
        far = dot(q_head, image_keys, NT) + image_part[...]
        own = dot(q_head, keys, NT) + own_part[...]
        top = jnp.maximum(
            jnp.max(far, axis=1, keepdims=True), jnp.max(own, axis=1, keepdims=True)
        )
        far = jnp.exp(far - top)
        own = jnp.exp(own - top)
        total = jnp.sum(far, axis=1, keepdims=True) + jnp.sum(own, axis=1, keepdims=True)
        summed = dot(far.astype(bf16), image_values) + dot(own.astype(bf16), values)
        outs.append(summed / total)
        tops.append(top + jnp.log(total))
    out_ref[...] = jnp.where(first, outs[0], outs[1]).astype(bf16)
    turned = jnp.transpose(jnp.where(first, tops[0], tops[1]))
    lse_ref[0, 0:1, :] = turned[0:1]
    lse_ref[0, 1:2, :] = turned[HEAD : HEAD + 1]


def attend_forward(order, scalars, item, projected, image):
    rows = projected.shape[0] // 2
    spec = lambda base: pl.BlockSpec((rows, PAIR), lambda h, *_: (item, base + h))
    far = lambda base: pl.BlockSpec((IMG_PAD, PAIR), lambda h, *_: (item, base + h))
    keys = rows + IMG_PAD
    return call(
        order,
        functools.partial(forward_kernel, item),
        (projected, projected, projected, image, image),
        [shaped((rows, HEADS * HEAD), bf16), shaped((PAIRS, 2, rows), f32)],
        "attend_forward",
        cost(16 * HEADS * rows * keys * HEAD, 6 << 20, HEADS * rows * keys),
        scalars=scalars,
        grid=(PAIRS,),
        specs=[spec(0), spec(PAIRS), spec(2 * PAIRS), far(0), far(PAIRS)],
        outs=[
            pl.BlockSpec((rows, PAIR), lambda h, *_: (0, h)),
            pl.BlockSpec((1, 2, rows), lambda h, *_: (h, 0, 0)),
        ],
        scratch=[pltpu.VMEM((rows, IMG_PAD), f32), pltpu.VMEM((rows, rows), f32)],
    )


def backward_kernel(
    item,
    flag_ref,
    count_ref,
    lengths_ref,
    q_ref,
    k_ref,
    v_ref,
    ik_ref,
    iv_ref,
    out_ref,
    grad_ref,
    lse_ref,
    *refs,
):
    gq_ref, gk_ref, gv_ref, gik_ref, giv_ref, image_part, own_part = refs[-7:]
    rows = q_ref.shape[0]

    @pl.when(pl.program_id(0) == 0)
    def _():
        image_part[...] = image_bias(image_part.shape, 0, count_ref, item)
        own_part[...] = own_bias(rows, flag_ref, lengths_ref, item)

    first = lax.broadcasted_iota(jnp.int32, (rows, PAIR), 1) < HEAD
    zero = jnp.zeros((), bf16)
    q, grad = q_ref[...], grad_ref[...]
    products = grad.astype(f32) * out_ref[...].astype(f32)
    head_lanes = lax.broadcasted_iota(jnp.int32, (8, PAIR), 1) // HEAD
    head_rows = lax.broadcasted_iota(jnp.int32, (8, PAIR), 0)
    center = lax.dot_general(
        (head_lanes == head_rows).astype(f32),
        products,
        NT,
        preferred_element_type=f32,
        precision=lax.Precision.HIGHEST,
    )
    q_heads = [jnp.where(first, q, zero), jnp.where(first, zero, q)]
    grad_heads = [jnp.where(first, grad, zero), jnp.where(first, zero, grad)]
    lse = lse_ref[0]
    grad_query = [None, None]
    half = rows // 2
    pieces = (
        (ik_ref, iv_ref, gik_ref, giv_ref, image_part, 0, IMG_PAD),
        (k_ref, v_ref, gk_ref, gv_ref, own_part, 0, half),
        (k_ref, v_ref, gk_ref, gv_ref, own_part, half, half),
    )
    for keys_ref, values_ref, gk_out, gv_out, bias, start, count in pieces:
        piece = slice(start, start + count)
        keys, values = keys_ref[piece, :], values_ref[piece, :]
        low_lanes = lax.broadcasted_iota(jnp.int32, (count, PAIR), 1) < HEAD
        grad_keys, grad_values = [], []
        for head in range(2):
            scores = dot(keys, q_heads[head], NT) + bias[piece, :]
            probs = jnp.exp(scores - lse[head : head + 1])
            grad_probs = dot(values, grad_heads[head], NT)
            grad_scores = (probs * (grad_probs - center[head : head + 1])).astype(bf16)
            grad_values.append(dot(probs.astype(bf16), grad))
            grad_keys.append(dot(grad_scores, q))
            term = dot(grad_scores, keys, TN)
            grad_query[head] = term if grad_query[head] is None else grad_query[head] + term
        gk_out[piece, :] = jnp.where(low_lanes, grad_keys[0], grad_keys[1]).astype(bf16)
        gv_out[piece, :] = jnp.where(low_lanes, grad_values[0], grad_values[1]).astype(bf16)
    gq_ref[...] = (jnp.where(first, grad_query[0], grad_query[1]) * HEAD**-0.5).astype(bf16)


def attend_backward(order, scalars, item, start, pairs, projected, image, attended, grad, lse, earlier):
    rows, width = attended.shape
    spec = lambda base: pl.BlockSpec((rows, PAIR), lambda h, *_: (item, base + start + h))
    far = lambda base: pl.BlockSpec((IMG_PAD, PAIR), lambda h, *_: (item, base + start + h))
    own = pl.BlockSpec((rows, PAIR), lambda h, *_: (0, start + h))
    far_outs = pl.BlockSpec((IMG_PAD, PAIR), lambda h, *_: (item, start + h))
    keys = rows + IMG_PAD
    inputs = (projected, projected, projected, image, image, attended, grad, lse)
    first = len(scalars) + len(inputs)
    return call(
        order,
        functools.partial(backward_kernel, item),
        (*inputs, *earlier),
        [shaped((2 * rows, width), bf16)] * 3 + [shaped((2 * IMG_PAD, width), bf16)] * 2,
        "attend_backward",
        weighed(cost(80 * pairs * rows * keys * HEAD, pairs * 2 << 20, 2 * pairs * rows * keys)),
        scalars=scalars,
        grid=(pairs,),
        specs=[
            spec(0),
            spec(PAIRS),
            spec(2 * PAIRS),
            far(0),
            far(PAIRS),
            own,
            spec(0),
            pl.BlockSpec((1, 2, rows), lambda h, *_: (start + h, 0, 0)),
        ]
        + [pl.BlockSpec(memory_space=pl.ANY)] * len(earlier),
        outs=[spec(0), spec(0), spec(0), far_outs, far_outs],
        scratch=[pltpu.VMEM((IMG_PAD, rows), f32), pltpu.VMEM((rows, rows), f32)],
        aliases={first + at: at for at in range(len(earlier))},
    )


def gelu_pair(values):
    share = 0.5 * (1.0 + lax.erf(values * 0.7071067811865476))
    slope = share + values * jnp.exp(-0.5 * values * values) * 0.3989422804014327
    return values * share, slope


def feed_step(step, rows, item_rows, feed, top, result, gfeed, expand_ref, ebias_ref, reduce_ref):
    width = feed.shape[1]
    expand, reduce = expand_ref[...], reduce_ref[...]
    active_parts, gup_parts = [], []
    for start in range(0, rows, item_rows):
        here = slice(start, start + item_rows)
        upward = dot(feed[here, :], expand) + ebias_ref[...]
        gactive = dot(top[here, :], reduce, NT)
        active, slope = gelu_pair(upward)
        active = active.astype(bf16)
        gup = (gactive * slope).astype(bf16)
        result[here, :] += dot(active, reduce)
        gfeed[here, :] += dot(gup, expand, NT)
        active_parts.append(active)
        gup_parts.append(gup)
    active = jnp.concatenate(active_parts, axis=0)
    gup = jnp.concatenate(gup_parts, axis=0)
    greduce = dot(active, top[...], TN).astype(bf16)
    gexpand = dot(feed[...], gup, TN).astype(bf16)
    pieces = [greduce[:, at : at + LANES] for at in range(0, width, LANES)]
    pieces += [gexpand[:, at : at + LANES] for at in range(0, FF_BLOCK, LANES)]
    return pieces, column_sum(gup.astype(f32))


def store_pieces(out, pieces):
    at = 0
    for half in range(2):
        for piece in pieces:
            rows = piece.shape[0] // 2
            out[at : at + rows, :] = piece[half * rows : (half + 1) * rows]
            at += rows


def feed_kernel(
    flag_ref,
    count_ref,
    side_ref,
    att0_ref,
    att1_ref,
    project_ref,
    hid_ref,
    cot_ref,
    project_bias_ref,
    gain_ref,
    shift_ref,
    reduce_bias_ref,
    expand_ref,
    ebias_ref,
    reduce_ref,
    out_ref,
    gmid_ref,
    gatt_ref,
    gproject_ref,
    gvec_ref,
    keep0_ref,
    send0_ref,
    keep1_ref,
    send1_ref,
    middle,
    feed,
    top,
    result,
    gfeed,
    low_out,
    gatt,
    grads,
    grad_sems,
    row_sems,
    *,
    item_rows,
):
    step = pl.program_id(0)
    rows, width = hid_ref.shape
    block = 256
    att_refs = (att0_ref, att1_ref)
    half = grads.shape[1] // 2

    steps = grads.shape[0]

    def grad_copies(which):
        found = []
        chunk, place = divmod(which, steps // 2)
        outs = (keep1_ref, send1_ref) if chunk else (keep0_ref, send0_ref)
        for number, out in enumerate(outs):
            side = side_ref[0] if number == 0 else 1 - side_ref[0]
            here = grads.at[which, pl.ds(pl.multiple_of(side * half, half), half)]
            there = out.at[pl.ds(place * half, half)]
            found.append(pltpu.make_async_copy(here, there, grad_sems.at[which, number]))
        return found

    @pl.when(step == 0)
    def _():
        for start in range(0, rows, block):
            here = slice(start, start + block)
            inside = slice(start % item_rows, start % item_rows + block)
            att = att_refs[start // item_rows][inside, :]
            branch = dot(att, project_ref[...]) + project_bias_ref[...]
            x = hid_ref[here, :].astype(f32) + branch
            middle[here, :] = x
            unit, _ = normalise(x)
            feed[here, :] = (unit * gain_ref[...] + shift_ref[...]).astype(bf16)
            at = lax.broadcasted_iota(jnp.int32, (block, width), 0) + start % item_rows
            limit = jnp.where(flag_ref[0] == 1, item_rows, count_ref[start // item_rows])
            top[here, :] = jnp.where(at < limit, cot_ref[here, :].astype(f32), 0.0).astype(bf16)
            result[here, :] = x + reduce_bias_ref[...]
            gfeed[here, :] = jnp.zeros((block, width), f32)

    pieces, gvec_ref[pl.ds(4 + step, 1), :] = feed_step(
        step, rows, item_rows, feed, top, result, gfeed, expand_ref, ebias_ref, reduce_ref
    )
    store_pieces(grads.at[step], pieces)
    for which in range(steps):

        @pl.when(step == which)
        def _(which=which):
            for copy in grad_copies(which):
                copy.start()

    @pl.when(step == pl.num_programs(0) - 1)
    def _():
        copies = []
        sums = [jnp.zeros((1, width), f32)] * 4
        for number, start in enumerate(range(0, rows, block)):
            here = slice(start, start + block)
            low_out[here, :] = result[here, :].astype(bf16)
            unit, scale = normalise(middle[here, :])
            grad = gfeed[here, :]
            grad_top = top[here, :].astype(f32)
            gmid = grad_top + norm_transpose(unit, scale, gain_ref[...], grad)
            terms = (grad * unit, grad, grad_top, gmid)
            sums = [old + column_sum(new) for old, new in zip(sums, terms)]
            middle[here, :] = gmid
            gbranch = gmid.astype(bf16)
            feed[here, :] = gbranch
            gatt[here, :] = dot(gbranch, project_ref[...], NT).astype(bf16)
            for kind, (mine, there) in enumerate(
                ((low_out, out_ref), (middle, gmid_ref), (gatt, gatt_ref))
            ):
                span = pl.ds(start, block)
                copy = pltpu.make_async_copy(
                    mine.at[span, :], there.at[span, :], row_sems.at[kind, number]
                )
                copy.start()
                copies.append(copy)
        total = dot(att0_ref[...], feed[:item_rows, :], TN)
        total += dot(att1_ref[...], feed[item_rows:, :], TN)
        gproject_ref[...] = total.astype(bf16)
        gvec_ref[0:4, :] = jnp.concatenate(sums, axis=0)
        for copy in copies:
            copy.wait()
        for which in range(steps):
            for copy in grad_copies(which):
                copy.wait()


def feed_forward(order, flag, count, side, att0, att1, project, hidden, cotangent, vecs, expand, ebias, reduce):
    rows, width = hidden.shape
    item_rows = att0.shape[0]
    units = reduce.shape[0]
    steps = units // FF_BLOCK
    block_rows = 2 * width * FF_BLOCK // LANES
    fixed = (att0, att1, project, hidden, cotangent, *vecs)
    anywhere = pl.BlockSpec(memory_space=pl.ANY)
    return call(
        order,
        functools.partial(feed_kernel, item_rows=item_rows),
        (*fixed, expand, ebias, reduce),
        [
            shaped((rows, width), bf16),
            shaped((rows, width), f32),
            shaped((rows, width), bf16),
            shaped((width, width), bf16),
            shaped((4 + steps, width), f32),
        ]
        + [shaped((steps // 2 * block_rows // 2, LANES), bf16)] * 4,
        "feed_forward",
        cost(12 * rows * width * units, 40 << 20, 2 * rows * units),
        scalars=(flag, count, side),
        grid=(steps,),
        specs=[resident(value.shape) for value in fixed]
        + [
            pl.BlockSpec((width, FF_BLOCK), lambda j, *_: (0, j)),
            pl.BlockSpec((1, FF_BLOCK), lambda j, *_: (0, j)),
            pl.BlockSpec((FF_BLOCK, width), lambda j, *_: (j, 0)),
        ],
        outs=[
            anywhere,
            anywhere,
            anywhere,
            resident((width, width)),
            resident((4 + steps, width)),
        ]
        + [anywhere] * 4,
        scratch=[
            pltpu.VMEM((rows, width), f32),
            pltpu.VMEM((rows, width), bf16),
            pltpu.VMEM((rows, width), bf16),
            pltpu.VMEM((rows, width), f32),
            pltpu.VMEM((rows, width), f32),
            pltpu.VMEM((rows, width), bf16),
            pltpu.VMEM((rows, width), bf16),
            pltpu.VMEM((steps, block_rows, LANES), bf16),
            pltpu.SemaphoreType.DMA((steps, 2)),
            pltpu.SemaphoreType.DMA((3, rows // 256)),
        ],
    )


def weight_kernel(
    spare,
    side_ref,
    normed_ref,
    image_ref,
    gq_ref,
    gk_ref,
    gv_ref,
    gik_ref,
    giv_ref,
    *refs,
):
    extra_ref = None if spare else refs[0]
    sums_ref, keep_ref, send_ref, keep, send, sems = refs[-6:]
    step = pl.program_id(0)
    width = normed_ref.shape[1]
    half = width // 2
    columns = gq_ref.shape[1] // LANES
    block = half * (columns if spare else columns + 1)

    def copies(part):
        span = pl.ds(part * block, block if part < 3 else spare)
        pairs = ((keep, keep_ref), (send, send_ref))
        return [
            pltpu.make_async_copy(here.at[span], there.at[span], sems.at[number, part])
            for number, (here, there) in enumerate(pairs)
        ]

    def store(part, total):
        if extra_ref is not None:
            more = extra_ref[:, part * LANES : (part + 1) * LANES].astype(f32)
            total = jnp.concatenate([total, more], axis=1)
        first = side_ref[0] == 0
        mine = jnp.where(first, total[:half], total[half:]).astype(bf16)
        other = jnp.where(first, total[half:], total[:half]).astype(bf16)
        for number in range(block // half):
            rows = slice(part * block + number * half, part * block + (number + 1) * half)
            cols = slice(number * LANES, (number + 1) * LANES)
            keep[rows, :] = mine[:, cols]
            send[rows, :] = other[:, cols]
        for copy in copies(part):
            copy.start()

    @pl.when(step == 0)
    def _():
        store(0, dot(normed_ref[...], gq_ref[...], TN))
        sums_ref[0:1] = column_sum(gq_ref[...].astype(f32))

    @pl.when(step == 1)
    def _():
        total = dot(normed_ref[...], gk_ref[...], TN)
        store(1, total + dot(image_ref[...], gik_ref[...], TN))

    @pl.when(step == 2)
    def _():
        total = dot(normed_ref[...], gv_ref[...], TN)
        store(2, total + dot(image_ref[...], giv_ref[...], TN))
        sums = column_sum(gv_ref[...].astype(f32)) + column_sum(giv_ref[...].astype(f32))
        sums_ref[1:2] = sums
        if spare:
            keep[3 * block :, :] = jnp.zeros((spare, LANES), bf16)
            send[3 * block :, :] = jnp.zeros((spare, LANES), bf16)
            for copy in copies(3):
                copy.start()
        for part in range(4 if spare else 3):
            for copy in copies(part):
                copy.wait()


def weight_grads(order, side, normed, image, grads, lanes, place, spare, extra):
    rows, width = normed.shape
    half_rows = 3 * (lanes // LANES + len(extra)) * width // 2 + spare
    column = lambda height: pl.BlockSpec((height, lanes), lambda *_: (0, place))
    anywhere = pl.BlockSpec(memory_space=pl.ANY)
    return call(
        order,
        functools.partial(weight_kernel, spare),
        (normed, image, *grads, *extra),
        [shaped((2, lanes), f32)] + [shaped((half_rows, LANES), bf16)] * 2,
        "weight_grads",
        weighed(cost(8 * rows * width * lanes, 12 << 20)),
        scalars=(side,),
        grid=(3,),
        specs=[resident(normed.shape), resident(image.shape)]
        + [column(value.shape[0]) for value in grads]
        + [resident(value.shape) for value in extra],
        outs=[resident((2, lanes)), anywhere, anywhere],
        scratch=[pltpu.VMEM((half_rows, LANES), bf16)] * 2 + [pltpu.SemaphoreType.DMA((2, 4))],
    )


def image_grad_kernel(keys_weight, values_weight, keys_ref, values_ref, out_ref):
    total = dot(keys_ref[...], keys_weight[...], NT) + dot(values_ref[...], values_weight[...], NT)
    out_ref[...] = total.astype(bf16)


def image_grads(order, weight, keys, values):
    rows, width = keys.shape
    part = lambda base: pl.BlockSpec((width, width), lambda *_: (0, base))
    return call(
        order,
        image_grad_kernel,
        (weight, weight, keys, values),
        [shaped((rows, width), bf16)],
        "image_grads",
        weighed(cost(4 * rows * width * width, 6 << 20)),
        grid=(1,),
        specs=[part(1), part(2), resident(keys.shape), resident(values.shape)],
        outs=[resident((rows, width))],
    )


def finish_kernel(
    flag_ref,
    hid_ref,
    gmid_ref,
    near_ref,
    far_ref,
    gq_ref,
    gk_ref,
    gv_ref,
    gain_ref,
    weight_ref,
    feed_sums_ref,
    first_sums_ref,
    last_sums_ref,
    _,
    out_ref,
    small_ref,
    sums,
):
    item, block = pl.program_id(0), pl.program_id(1)
    joined = jnp.concatenate([gq_ref[...], gk_ref[...], gv_ref[...]], axis=1)
    grad = dot(joined, weight_ref[...], NT)
    unit, scale = normalise(hid_ref[...].astype(f32))
    both = near_ref[...].astype(f32) + far_ref[...].astype(f32)
    grad = grad + jnp.where((flag_ref[0] == 0) & (block == 0), both, 0.0)
    total = gmid_ref[...] + norm_transpose(unit, scale, gain_ref[...], grad)
    out_ref[...] = total.astype(bf16)
    found = jnp.concatenate([column_sum(grad * unit), column_sum(grad)], axis=0)

    @pl.when((item == 0) & (block == 0))
    def _():
        sums[...] = jnp.zeros(sums.shape, f32)

    sums[0:2] += found

    @pl.when((item == pl.num_programs(0) - 1) & (block == pl.num_programs(1) - 1))
    def _():
        width = sums.shape[1]
        pad = lambda count: jnp.zeros((count, width), f32)
        own = [sums[0:2], feed_sums_ref[0:3], feed_sums_ref[4:8], pad(7)]
        own = jnp.concatenate(own, axis=0)
        bias_sums = jnp.concatenate([first_sums_ref[...], last_sums_ref[...]], axis=1)
        shared = [pad(9), feed_sums_ref[3:4], bias_sums, pad(4)]
        shared = jnp.concatenate(shared, axis=0)
        is_text = flag_ref[0] == 1
        first = jnp.where(is_text, 0.0, own) + shared
        rows = jnp.concatenate([first, jnp.where(is_text, own, 0.0)], axis=0).astype(bf16)
        count = rows.shape[0]
        for number in range(width // LANES):
            cols = slice(number * LANES, (number + 1) * LANES)
            small_ref[number * count : (number + 1) * count, :] = rows[:, cols]
        small_ref[width // LANES * count :, :] = jnp.zeros((SMALL - width // LANES * count, LANES), bf16)


def finish_rows(
    order, flag, hidden, gmid, near, far, grads, gain, weight, feed_sums, bias_sums, keep, item_rows
):
    rows, width = hidden.shape
    blocks = item_rows // IMG_PAD
    mine = pl.BlockSpec((IMG_PAD, width), lambda i, j, *_: (i * blocks + j, 0))
    image = pl.BlockSpec((IMG_PAD, width), lambda i, j, *_: (i, 0))
    fixed = (gain, weight, feed_sums, *bias_sums)
    place = keep.shape[0] // SMALL - 1
    return call(
        order,
        finish_kernel,
        (hidden, gmid, near, far, *grads, *fixed, keep),
        [shaped((rows, width), bf16), shaped(keep.shape, bf16)],
        "finish_rows",
        weighed(cost(6 * rows * width * width, 16 << 20)),
        scalars=(flag,),
        grid=(rows // item_rows, blocks),
        specs=[mine, mine, image, image, mine, mine, mine]
        + [resident(value.shape) for value in fixed]
        + [pl.BlockSpec(memory_space=pl.ANY)],
        outs=[mine, pl.BlockSpec((SMALL, LANES), lambda *_: (place, 0))],
        scratch=[pltpu.VMEM((8, width), f32)],
        aliases={13: 1},
    )


def expert_kernel(half_ref, value_ref, *refs):
    at = 0
    for out in refs[-2:]:
        tall = out.shape[0]
        for part in range(out.shape[1] // LANES):
            piece = value_ref[at : at + tall, :]
            out[:, part * LANES : (part + 1) * LANES] = piece.astype(f32)
            at += tall


def expert_outputs(order, half, first, value, width, units, earlier):
    tall = width // 2
    block_rows = 2 * width // LANES * tall
    return call(
        order,
        expert_kernel,
        (value, *earlier),
        [shaped((units, width), f32), shaped((width, units), f32)],
        "expert_outputs",
        cost(value.size, 6 * value.size),
        scalars=(half,),
        grid=(value.shape[0] // block_rows,),
        specs=[pl.BlockSpec((block_rows, LANES), lambda i, at: (i, 0))]
        + [pl.BlockSpec(memory_space=pl.ANY)] * len(earlier),
        outs=[
            pl.BlockSpec((tall, width), lambda i, at: (2 * (first + i) + at[0], 0)),
            pl.BlockSpec((tall, width), lambda i, at: (at[0], first + i)),
        ],
        aliases={2: 0, 3: 1} if earlier else None,
    )


def first_kernel(half_ref, value_ref, *refs):
    in_ref, out_ref, wide, narrow, sems = refs[-5:]
    tall = wide.shape[1]
    count = value_ref.shape[0] // tall // 3
    columns = in_ref.shape[1] // 3
    rows = pl.ds(pl.multiple_of(half_ref[0] * tall, tall), tall)
    copies = []
    for part in range(3):
        at = part * count * tall
        for number in range(count - 1):
            piece = value_ref[at + number * tall : at + (number + 1) * tall, :]
            wide[part, :, number * LANES : (number + 1) * LANES] = piece.astype(f32)
        piece = value_ref[at + (count - 1) * tall : at + count * tall, :]
        narrow[part] = piece.astype(f32)
        places = (
            (wide, in_ref.at[rows, pl.ds(part * columns, (count - 1) * LANES)]),
            (narrow, out_ref.at[rows, pl.ds(part * LANES, LANES)]),
        )
        for kind, (here, there) in enumerate(places):
            copy = pltpu.make_async_copy(here.at[part], there, sems.at[kind, part])
            copy.start()
            copies.append(copy)
    for copy in copies:
        copy.wait()


def first_outputs(order, half, value, width, earlier):
    tall = width // 2
    anywhere = pl.BlockSpec(memory_space=pl.ANY)
    return call(
        order,
        first_kernel,
        (value, *earlier),
        [shaped((width, 3 * width), f32), shaped((width, width), f32)],
        "first_outputs",
        cost(value.size, 6 * value.size),
        scalars=(half,),
        grid=(1,),
        specs=[resident(value.shape)] + [anywhere] * len(earlier),
        outs=[anywhere, anywhere],
        scratch=[
            pltpu.VMEM((3, tall, width - LANES), f32),
            pltpu.VMEM((3, tall, LANES), f32),
            pltpu.SemaphoreType.DMA((2, 3)),
        ],
        aliases={2: 0, 3: 1} if earlier else None,
    )


def last_kernel(side_ref, flag_ref, mine_ref, got_ref, *refs):
    in_ref, *vec_refs, expand_ref, pair_ref, project_ref, columns, sems = refs[1:]
    tall = columns.shape[2]
    width = in_ref.shape[1] // 3
    copies = []
    for number, ref in enumerate((mine_ref, got_ref)):
        half = side_ref[0] if number == 0 else 1 - side_ref[0]
        rows = pl.ds(pl.multiple_of(half * tall, tall), tall)
        for part in range(3):
            columns[number, part] = ref[part * tall : (part + 1) * tall, :].astype(f32)
            there = in_ref.at[rows, pl.ds((part + 1) * width - LANES, LANES)]
            copy = pltpu.make_async_copy(columns.at[number, part], there, sems.at[number, part])
            copy.start()
            copies.append(copy)
    both = mine_ref[3 * tall :, :].astype(f32) + got_ref[3 * tall :, :].astype(f32)
    rows = jnp.concatenate([both[at * 32 : (at + 1) * 32] for at in range(width // LANES)], axis=1)
    own = jnp.where(flag_ref[0] == 1, rows[16:], rows[:16])
    for number, ref in enumerate(vec_refs):
        ref[...] = own[number : number + 1]
    for number in range(expand_ref.shape[1] // width):
        cols = slice(number * width, (number + 1) * width)
        expand_ref[:, cols] = own[5 + number : 6 + number]
    project_ref[...] = rows[9]
    pair_ref[...] = rows[10:12]
    for copy in copies:
        copy.wait()


def last_outputs(order, side, flag, mine, got, width, units, earlier):
    vecs = [(1, width)] * 5 + [(1, units), (2, width), (width,)]
    anywhere = pl.BlockSpec(memory_space=pl.ANY)
    return call(
        order,
        last_kernel,
        (mine, got, earlier),
        [shaped((width, 3 * width), f32)] + [shaped(shape, f32) for shape in vecs],
        "last_outputs",
        cost(got.size, 6 * got.size),
        scalars=(side, flag),
        grid=(1,),
        specs=[resident(mine.shape), resident(got.shape), anywhere],
        outs=[anywhere] + [resident(shape) for shape in vecs],
        scratch=[
            pltpu.VMEM((2, 3, width // 2, LANES), f32),
            pltpu.SemaphoreType.DMA((2, 3)),
        ],
        aliases={4: 0},
    )


def swap(value, axes, pair_of):
    count = 1
    for axis in axes:
        count *= lax.axis_size(axis)
    return lax.ppermute(value, axes, [(source, pair_of(source)) for source in range(count)])


def place_of(axes):
    place = 0
    for axis in axes:
        place = place * lax.axis_size(axis) + lax.axis_index(axis)
    return place


def late_stages(axes):
    stages = stage_bits(axes)
    if len(axes) == 2 and len(stages) == 5:
        return [stages[0], (0, 0), (2, 3), (3, 2), (4, 4)]
    return stages


def stage_bits(axes):
    count = 1
    for axis in axes:
        count *= lax.axis_size(axis)
    bits = count.bit_length() - 1
    core = len(axes) - 1
    others = [bit for bit in range(bits) if bit != core]
    if len(axes) == 1 and len(others) == 3:
        return [(core, core), (1, 2), (3, 1), (2, 3)]
    if len(axes) == 2 and len(others) == 4:
        return [(core, core), (0, 2), (2, 0), (3, 3), (4, 4)]
    return [(core, core)] + list(zip(others, others[1:] + others[:1]))


class Total:
    def __init__(self, order, axes, keep, send, stages=None):
        self.order = order
        self.axes = axes
        self.core = len(axes) - 1
        self.left = list(stages or stage_bits(axes))
        place = place_of(axes)
        second = ((place >> self.core) & 1) == 1
        sides = [(place >> jnp.where(second, pair[1], pair[0])) & 1 for pair in self.left]
        self.sides = dict(zip(self.left, sides))
        self.back = list(self.left)
        self.terms = (keep, self.exchange(send, self.left.pop(0)))
        self.mine = None

    def exchange(self, value, pair):
        other = lambda source: source ^ (1 << pair[(source >> self.core) & 1])
        self.got = swap(value, self.axes, other)
        return self.got

    def part(self, which, half):
        cut = lambda term: lax.dynamic_slice_in_dim(term, which * half, half, 0).astype(f32)
        return (cut(self.terms[0]) + cut(self.terms[1])).astype(bf16)

    def finish(self):
        while self.left or self.back:
            self.step()

    def step(self):
        if self.left:
            pair = self.left.pop(0)
            self.terms = self.order.after(*self.terms)
            half = self.terms[0].shape[0] // 2
            side = self.sides[pair]
            sent = self.part(1 - side, half)
            self.terms = (self.part(side, half), self.exchange(sent, pair))
            self.order.last = sent
            return
        pair = self.back.pop()
        if self.mine is None:
            self.terms = self.order.after(*self.terms)
            self.mine = (self.terms[0].astype(f32) + self.terms[1].astype(f32)).astype(bf16)
        else:
            mine, got = self.order.after(self.mine, self.got)
            low = jnp.where(self.last == 0, mine, got)
            high = jnp.where(self.last == 0, got, mine)
            self.mine = jnp.concatenate([low, high], axis=0)
        self.order.last = self.mine
        self.last = self.sides[pair]
        self.exchange(self.mine, pair)


def on_device(
    hidden_in,
    image_count,
    text_lengths,
    attend_gain,
    attend_shift,
    project_in,
    bias_pair,
    project_out,
    project_bias,
    feed_gain,
    feed_shift,
    expand_weight,
    expand_bias,
    reduce_weight,
    reduce_bias,
    cotangent,
):
    items, _, rows, width = hidden_in.shape
    units = expand_weight.shape[2]
    is_text = lax.axis_index("mod") == 1
    flag = is_text.astype(jnp.int32)[None]
    hidden = hidden_in.reshape(items * rows, width)
    to_text = lambda value: lax.ppermute(value, "mod", [(0, 1)])
    to_image = lambda value: lax.ppermute(value, "mod", [(1, 0)])

    far_rows = [to_text(hidden_in[item, 0, :IMG_PAD]) for item in range(items)]
    far_vecs = to_text(jnp.concatenate([attend_gain, attend_shift], axis=0))
    order = Order()
    normed, projected = project_rows(
        order, hidden, attend_gain, attend_shift, project_in, bias_pair
    )
    scalars = (flag, image_count, text_lengths)
    images, attended, lses = (), [], []
    for item in range(items):
        images = image_rows(
            order,
            flag,
            item,
            hidden,
            far_rows[item],
            attend_gain,
            attend_shift,
            far_vecs,
            project_in,
            bias_pair,
            rows,
            items,
            images,
        )
        out, lse = attend_forward(order, scalars, item, projected, images[1])
        attended.append(out)
        lses.append(lse)

    side = (lax.axis_index("dp") & 1)[None]
    (
        hidden_out,
        grad_middle,
        grad_attended,
        project_out_grad,
        feed_sums,
        keep0,
        send0,
        keep1,
        send1,
    ) = feed_forward(
        order,
        flag,
        image_count,
        side,
        attended[0],
        attended[1],
        project_out,
        hidden,
        cotangent.reshape(items * rows, width),
        (project_bias[None], feed_gain, feed_shift, reduce_bias),
        expand_weight[0],
        expand_bias,
        reduce_weight[0],
    )
    a = Total(order, ("dp",), keep0, send0)
    c = Total(order, ("dp",), keep1, send1)
    grads = ()

    def backward(item, start, pairs):
        return attend_backward(
            order,
            scalars,
            item,
            start,
            pairs,
            projected,
            images[1],
            attended[item],
            grad_attended,
            lses[item],
            grads,
        )

    def weights(lanes, place, spare, *extra):
        return weight_grads(
            order, side, normed, images[0], grads, lanes, place, spare, extra
        )

    def unpack(half, first, value, earlier=()):
        return expert_outputs(order, half, first, value, width, units, earlier)

    grads = backward(0, 0, 2)
    a.step()
    grads = backward(1, 0, 2)
    c.step()
    grads = backward(0, 2, 2)
    a.step()
    grads = backward(1, 2, 2)
    c.step()
    first_sums, keep, send = weights(2 * LANES, 0, 0, project_out_grad)
    s = Total(order, ("dp", "mod"), keep, send)
    a.step()
    grads = backward(0, 4, 2)
    s.step()
    a.step()
    grads = backward(1, 4, 2)
    c.step()
    s.step()
    near = image_grads(order, project_in, grads[3], grads[4])
    far = to_image(near)
    c.step()
    a.step()
    last_sums, keep, send = weights(LANES, 2, SMALL)
    p = Total(order, ("dp", "mod"), keep, send)
    s.step()
    c.step()
    a.step()
    (far,) = order.after(far)
    order.last = far
    grad_in, keep = finish_rows(
        order,
        flag,
        hidden,
        grad_middle,
        near,
        far,
        grads[:3],
        attend_gain,
        project_in,
        feed_sums,
        (first_sums, last_sums),
        keep,
        rows,
    )
    p.terms = (keep, p.got)
    p.step()
    s.step()
    a.step()
    p.step()
    c.step()
    p.step()
    s.step()
    a.finish()
    outputs = unpack(side, 0, a.mine)
    p.step()
    s.step()
    p.step()
    outputs = unpack(1 - side, 0, a.got, outputs)
    p.step()
    s.step()
    c.step()
    p.step()
    s.step()
    c.finish()
    outputs = unpack(side, 2, c.mine, outputs)
    p.step()
    s.step()
    reduce_grad, expand_grad = unpack(1 - side, 2, c.got, outputs)
    s.finish()
    projections = first_outputs(order, side, s.mine, width, ())
    project_in_grad, project_out_grad = first_outputs(order, 1 - side, s.got, width, projections)
    p.finish()
    (
        project_in_grad,
        attend_gain_grad,
        attend_shift_grad,
        feed_gain_grad,
        feed_shift_grad,
        reduce_bias_grad,
        expand_bias_grad,
        bias_pair_grad,
        project_bias_grad,
    ) = last_outputs(order, side, flag, p.mine, p.got, width, units, project_in_grad)
    return (
        hidden_out.reshape(hidden_in.shape),
        grad_in.reshape(hidden_in.shape),
        attend_gain_grad,
        attend_shift_grad,
        project_in_grad,
        bias_pair_grad,
        project_out_grad,
        project_bias_grad,
        feed_gain_grad,
        feed_shift_grad,
        expand_grad[None],
        expand_bias_grad,
        reduce_grad[None],
        reduce_bias_grad,
    )


def solution(mesh):
    in_specs = (
        P("dp", "mod", None, None),
        P("dp"),
        P("dp", None),
        P("mod", None),
        P("mod", None),
        P(),
        P(),
        P(),
        P(),
        P("mod", None),
        P("mod", None),
        P("mod", None, None),
        P("mod", None),
        P("mod", None, None),
        P("mod", None),
        P("dp", "mod", None, None),
    )
    out_specs = (
        P("dp", "mod", None, None),
        P("dp", "mod", None, None),
        P("mod", None),
        P("mod", None),
        P(),
        P(),
        P(),
        P(),
        P("mod", None),
        P("mod", None),
        P("mod", None, None),
        P("mod", None),
        P("mod", None, None),
        P("mod", None),
    )
    return jax.shard_map(
        on_device, mesh=mesh, in_specs=in_specs, out_specs=out_specs, check_vma=False
    )
```

```python
import functools

import jax
import jax.numpy as jnp
from jax import lax
from jax.experimental import pallas as pl
from jax.experimental.pallas import tpu as pltpu
from jax.sharding import PartitionSpec as P

HEADS = 12
HEAD = 64
IMG_PAD = 256
PAIR = 2 * HEAD
PAIRS = HEADS // 2
GROUP_PAIRS = 2
GROUPS = PAIRS // GROUP_PAIRS
LANES = GROUP_PAIRS * PAIR
SMALL = 128
FF_BLOCK = 768

masked_value = -1e30
norm_eps = 1e-05

bf16 = jnp.bfloat16
f32 = jnp.float32

NN = (((1,), (0,)), ((), ()))
NT = (((1,), (1,)), ((), ()))
TN = (((0,), (0,)), ((), ()))
VMEM_BYTES = 56 << 20


def dot(left, right, dims=NN):
    return lax.dot_general(left, right, dims, preferred_element_type=f32)


def column_sum(values):
    return jnp.sum(values, axis=0, keepdims=True)


def row_mean(values):
    return jnp.mean(values, axis=1, keepdims=True)


def normalise(values):
    centred = values - row_mean(values)
    scale = lax.rsqrt(row_mean(centred * centred) + norm_eps)
    return centred * scale, scale


def norm_transpose(unit, scale, gain, grad):
    grad_unit = grad * gain
    return scale * (grad_unit - row_mean(grad_unit) - unit * row_mean(grad_unit * unit))


def cost(flops, moved, special=0):
    return pl.CostEstimate(flops=flops, bytes_accessed=moved, transcendentals=special)


def weighed(estimate):
    return pl.CostEstimate(
        flops=10 * estimate.flops,
        bytes_accessed=10 * estimate.bytes_accessed,
        transcendentals=10 * estimate.transcendentals,
    )


class Order:
    def __init__(self):
        self.last = None

    def after(self, *values):
        if self.last is None:
            return values
        *values, _ = lax.optimization_barrier((*values, self.last))
        return values


def call(order, kernel, inputs, out_shape, name, estimate, scalars=(), grid=(), specs=None, outs=None,
         scratch=(), aliases=None):
    inputs = (*order.after(inputs[0]), *inputs[1:])
    vmem = pl.BlockSpec(memory_space=pltpu.VMEM)
    found = pl.pallas_call(
        kernel,
        grid_spec=pltpu.PrefetchScalarGridSpec(
            num_scalar_prefetch=len(scalars),
            grid=grid,
            in_specs=[vmem] * len(inputs) if specs is None else list(specs),
            out_specs=[vmem] * len(out_shape) if outs is None else list(outs),
            scratch_shapes=list(scratch),
        ),
        out_shape=list(out_shape),
        input_output_aliases=aliases or {},
        compiler_params=pltpu.CompilerParams(vmem_limit_bytes=VMEM_BYTES),
        cost_estimate=estimate,
        name=name,
    )(*scalars, *inputs)
    order.last = found[-1]
    return found if len(found) > 1 else found[0]


def shaped(shape, dtype):
    return jax.ShapeDtypeStruct(shape, dtype)


def resident(shape):
    return pl.BlockSpec(shape, lambda *_: (0,) * len(shape), pipeline_mode=pl.Buffered(1))


def project_kernel(hid_ref, gain_ref, shift_ref, weight_ref, bias_ref, normed_ref, out_ref):
    unit, _ = normalise(hid_ref[...].astype(f32))
    normed = (unit * gain_ref[...] + shift_ref[...]).astype(bf16)
    normed_ref[...] = normed
    width = normed.shape[1]
    for part in range(3):
        cols = slice(part * width, (part + 1) * width)
        rows = dot(normed, weight_ref[:, cols])
        if part == 0:
            rows = (rows + bias_ref[0:1]).astype(bf16) * jnp.asarray(HEAD**-0.5, bf16)
        if part == 2:
            rows = rows + bias_ref[1:2]
        out_ref[:, cols] = rows.astype(bf16)


def project_rows(order, hidden, gain, shift, weight, bias):
    rows, width = hidden.shape
    block = 256
    blocked = lambda cols: pl.BlockSpec((block, cols), lambda r: (r, 0))
    inputs = (hidden, gain, shift, weight, bias)
    return call(
        order,
        project_kernel,
        inputs,
        [shaped((rows, width), bf16), shaped((rows, 3 * width), bf16)],
        "project_rows",
        cost(6 * rows * width * width, 10 * rows * width + 6 * width * width),
        grid=(rows // block,),
        specs=[blocked(width)] + [resident(value.shape) for value in inputs[1:]],
        outs=[blocked(width), blocked(3 * width)],
    )


def image_kernel(
    flag_ref,
    own_ref,
    far_ref,
    gain_ref,
    shift_ref,
    vec_ref,
    keys_ref,
    values_ref,
    bias_ref,
    *refs,
):
    normed_ref, out_ref = refs[-2:]
    is_text = flag_ref[0] == 1
    hidden = jnp.where(is_text, far_ref[...].astype(f32), own_ref[...].astype(f32))
    gain = jnp.where(is_text, vec_ref[0:1], gain_ref[...])
    shift = jnp.where(is_text, vec_ref[1:2], shift_ref[...])
    unit, _ = normalise(hidden)
    normed = (unit * gain + shift).astype(bf16)
    normed_ref[...] = normed
    width = normed.shape[1]
    out_ref[:, :width] = dot(normed, keys_ref[...]).astype(bf16)
    out_ref[:, width:] = (dot(normed, values_ref[...]) + bias_ref[1:2]).astype(bf16)


def image_rows(
    order, flag, item, hidden, far, gain, shift, vecs, weight, bias, item_rows, items, earlier
):
    width = hidden.shape[1]
    place = item * (item_rows // IMG_PAD)
    half = lambda base: pl.BlockSpec((width, width), lambda *_: (0, base))
    mine = lambda cols: pl.BlockSpec((IMG_PAD, cols), lambda *_: (item, 0))
    inputs = (hidden, far, gain, shift, vecs, weight, weight, bias, *earlier)
    return call(
        order,
        image_kernel,
        inputs,
        [shaped((items * IMG_PAD, width), bf16), shaped((items * IMG_PAD, 2 * width), bf16)],
        "image_rows",
        cost(4 * IMG_PAD * width * width, 6 << 20),
        scalars=(flag,),
        grid=(1,),
        specs=[
            pl.BlockSpec((IMG_PAD, width), lambda *_: (place, 0)),
            resident(far.shape),
            resident(gain.shape),
            resident(shift.shape),
            resident(vecs.shape),
            half(1),
            half(2),
            resident(bias.shape),
        ]
        + [pl.BlockSpec(memory_space=pl.ANY)] * len(earlier),
        outs=[mine(width), mine(2 * width)],
        aliases={9: 0, 10: 1} if earlier else None,
    )


def segments(shape, axis, lengths_ref, item):
    places = lax.broadcasted_iota(jnp.int32, shape, axis)
    total = jnp.zeros(shape, jnp.int32)
    end = 0
    for which in range(lengths_ref.shape[1]):
        end = end + lengths_ref[item, which]
        total += (places >= end).astype(jnp.int32)
    return total


def own_bias(rows, flag_ref, lengths_ref, item):
    shape = (rows, rows)
    same = segments(shape, 0, lengths_ref, item) == segments(shape, 1, lengths_ref, item)
    return jnp.where(same & (flag_ref[0] == 1), 0.0, masked_value).astype(f32)


def image_bias(shape, axis, count_ref, item):
    places = lax.broadcasted_iota(jnp.int32, shape, axis)
    return jnp.where(places < count_ref[item], 0.0, masked_value).astype(f32)


def forward_kernel(
    item,
    flag_ref,
    count_ref,
    lengths_ref,
    q_ref,
    k_ref,
    v_ref,
    ik_ref,
    iv_ref,
    out_ref,
    lse_ref,
    image_part,
    own_part,
):
    rows = q_ref.shape[0]

    @pl.when(pl.program_id(0) == 0)
    def _():
        image_part[...] = image_bias(image_part.shape, 1, count_ref, item)
        own_part[...] = own_bias(rows, flag_ref, lengths_ref, item)

    first = lax.broadcasted_iota(jnp.int32, (rows, PAIR), 1) < HEAD
    zero = jnp.zeros((), bf16)
    q = q_ref[...]
    image_keys, image_values = ik_ref[...], iv_ref[...]
    keys, values = k_ref[...], v_ref[...]
    outs, tops = [], []
    for head in range(2):
        q_head = jnp.where(first, q, zero) if head == 0 else jnp.where(first, zero, q)
        far = dot(q_head, image_keys, NT) + image_part[...]
        own = dot(q_head, keys, NT) + own_part[...]
        top = jnp.maximum(
            jnp.max(far, axis=1, keepdims=True), jnp.max(own, axis=1, keepdims=True)
        )
        far = jnp.exp(far - top)
        own = jnp.exp(own - top)
        total = jnp.sum(far, axis=1, keepdims=True) + jnp.sum(own, axis=1, keepdims=True)
        summed = dot(far.astype(bf16), image_values) + dot(own.astype(bf16), values)
        outs.append(summed / total)
        tops.append(top + jnp.log(total))
    out_ref[...] = jnp.where(first, outs[0], outs[1]).astype(bf16)
    turned = jnp.transpose(jnp.where(first, tops[0], tops[1]))
    lse_ref[0, 0:1, :] = turned[0:1]
    lse_ref[0, 1:2, :] = turned[HEAD : HEAD + 1]


def attend_forward(order, scalars, item, projected, image):
    rows = projected.shape[0] // 2
    spec = lambda base: pl.BlockSpec((rows, PAIR), lambda h, *_: (item, base + h))
    far = lambda base: pl.BlockSpec((IMG_PAD, PAIR), lambda h, *_: (item, base + h))
    keys = rows + IMG_PAD
    return call(
        order,
        functools.partial(forward_kernel, item),
        (projected, projected, projected, image, image),
        [shaped((rows, HEADS * HEAD), bf16), shaped((PAIRS, 2, rows), f32)],
        "attend_forward",
        cost(16 * HEADS * rows * keys * HEAD, 6 << 20, HEADS * rows * keys),
        scalars=scalars,
        grid=(PAIRS,),
        specs=[spec(0), spec(PAIRS), spec(2 * PAIRS), far(0), far(PAIRS)],
        outs=[
            pl.BlockSpec((rows, PAIR), lambda h, *_: (0, h)),
            pl.BlockSpec((1, 2, rows), lambda h, *_: (h, 0, 0)),
        ],
        scratch=[pltpu.VMEM((rows, IMG_PAD), f32), pltpu.VMEM((rows, rows), f32)],
    )


def backward_kernel(
    item,
    flag_ref,
    count_ref,
    lengths_ref,
    q_ref,
    k_ref,
    v_ref,
    ik_ref,
    iv_ref,
    out_ref,
    grad_ref,
    lse_ref,
    *refs,
):
    gq_ref, gk_ref, gv_ref, gik_ref, giv_ref, image_part, own_part = refs[-7:]
    rows = q_ref.shape[0]

    @pl.when(pl.program_id(0) == 0)
    def _():
        image_part[...] = image_bias(image_part.shape, 0, count_ref, item)
        own_part[...] = own_bias(rows, flag_ref, lengths_ref, item)

    first = lax.broadcasted_iota(jnp.int32, (rows, PAIR), 1) < HEAD
    zero = jnp.zeros((), bf16)
    q, grad = q_ref[...], grad_ref[...]
    products = grad.astype(f32) * out_ref[...].astype(f32)
    head_lanes = lax.broadcasted_iota(jnp.int32, (8, PAIR), 1) // HEAD
    head_rows = lax.broadcasted_iota(jnp.int32, (8, PAIR), 0)
    center = lax.dot_general(
        (head_lanes == head_rows).astype(f32),
        products,
        NT,
        preferred_element_type=f32,
        precision=lax.Precision.HIGHEST,
    )
    q_heads = [jnp.where(first, q, zero), jnp.where(first, zero, q)]
    grad_heads = [jnp.where(first, grad, zero), jnp.where(first, zero, grad)]
    lse = lse_ref[0]
    grad_query = [None, None]
    half = rows // 2
    pieces = (
        (ik_ref, iv_ref, gik_ref, giv_ref, image_part, 0, IMG_PAD),
        (k_ref, v_ref, gk_ref, gv_ref, own_part, 0, half),
        (k_ref, v_ref, gk_ref, gv_ref, own_part, half, half),
    )
    for keys_ref, values_ref, gk_out, gv_out, bias, start, count in pieces:
        piece = slice(start, start + count)
        keys, values = keys_ref[piece, :], values_ref[piece, :]
        low_lanes = lax.broadcasted_iota(jnp.int32, (count, PAIR), 1) < HEAD
        grad_keys, grad_values = [], []
        for head in range(2):
            scores = dot(keys, q_heads[head], NT) + bias[piece, :]
            probs = jnp.exp(scores - lse[head : head + 1])
            grad_probs = dot(values, grad_heads[head], NT)
            grad_scores = (probs * (grad_probs - center[head : head + 1])).astype(bf16)
            grad_values.append(dot(probs.astype(bf16), grad))
            grad_keys.append(dot(grad_scores, q))
            term = dot(grad_scores, keys, TN)
            grad_query[head] = term if grad_query[head] is None else grad_query[head] + term
        gk_out[piece, :] = jnp.where(low_lanes, grad_keys[0], grad_keys[1]).astype(bf16)
        gv_out[piece, :] = jnp.where(low_lanes, grad_values[0], grad_values[1]).astype(bf16)
    gq_ref[...] = (jnp.where(first, grad_query[0], grad_query[1]) * HEAD**-0.5).astype(bf16)


def attend_backward(order, scalars, item, start, pairs, projected, image, attended, grad, lse, earlier):
    rows, width = attended.shape
    spec = lambda base: pl.BlockSpec((rows, PAIR), lambda h, *_: (item, base + start + h))
    far = lambda base: pl.BlockSpec((IMG_PAD, PAIR), lambda h, *_: (item, base + start + h))
    own = pl.BlockSpec((rows, PAIR), lambda h, *_: (0, start + h))
    far_outs = pl.BlockSpec((IMG_PAD, PAIR), lambda h, *_: (item, start + h))
    keys = rows + IMG_PAD
    inputs = (projected, projected, projected, image, image, attended, grad, lse)
    first = len(scalars) + len(inputs)
    return call(
        order,
        functools.partial(backward_kernel, item),
        (*inputs, *earlier),
        [shaped((2 * rows, width), bf16)] * 3 + [shaped((2 * IMG_PAD, width), bf16)] * 2,
        "attend_backward",
        weighed(cost(80 * pairs * rows * keys * HEAD, pairs * 2 << 20, 2 * pairs * rows * keys)),
        scalars=scalars,
        grid=(pairs,),
        specs=[
            spec(0),
            spec(PAIRS),
            spec(2 * PAIRS),
            far(0),
            far(PAIRS),
            own,
            spec(0),
            pl.BlockSpec((1, 2, rows), lambda h, *_: (start + h, 0, 0)),
        ]
        + [pl.BlockSpec(memory_space=pl.ANY)] * len(earlier),
        outs=[spec(0), spec(0), spec(0), far_outs, far_outs],
        scratch=[pltpu.VMEM((IMG_PAD, rows), f32), pltpu.VMEM((rows, rows), f32)],
        aliases={first + at: at for at in range(len(earlier))},
    )


def gelu_pair(values):
    share = 0.5 * (1.0 + lax.erf(values * 0.7071067811865476))
    slope = share + values * jnp.exp(-0.5 * values * values) * 0.3989422804014327
    return values * share, slope


def feed_step(step, rows, item_rows, feed, top, result, gfeed, expand_ref, ebias_ref, reduce_ref):
    width = feed.shape[1]
    expand, reduce = expand_ref[...], reduce_ref[...]
    active_parts, gup_parts = [], []
    for start in range(0, rows, item_rows):
        here = slice(start, start + item_rows)
        upward = dot(feed[here, :], expand) + ebias_ref[...]
        gactive = dot(top[here, :], reduce, NT)
        active, slope = gelu_pair(upward)
        active = active.astype(bf16)
        gup = (gactive * slope).astype(bf16)
        result[here, :] += dot(active, reduce)
        gfeed[here, :] += dot(gup, expand, NT)
        active_parts.append(active)
        gup_parts.append(gup)
    active = jnp.concatenate(active_parts, axis=0)
    gup = jnp.concatenate(gup_parts, axis=0)
    greduce = dot(active, top[...], TN).astype(bf16)
    gexpand = dot(feed[...], gup, TN).astype(bf16)
    pieces = [greduce[:, at : at + LANES] for at in range(0, width, LANES)]
    pieces += [gexpand[:, at : at + LANES] for at in range(0, FF_BLOCK, LANES)]
    return pieces, column_sum(gup.astype(f32))


def store_pieces(out, pieces):
    at = 0
    for half in range(2):
        for piece in pieces:
            rows = piece.shape[0] // 2
            out[at : at + rows, :] = piece[half * rows : (half + 1) * rows]
            at += rows


def feed_kernel(
    flag_ref,
    count_ref,
    side_ref,
    att0_ref,
    att1_ref,
    project_ref,
    hid_ref,
    cot_ref,
    project_bias_ref,
    gain_ref,
    shift_ref,
    reduce_bias_ref,
    expand_ref,
    ebias_ref,
    reduce_ref,
    out_ref,
    gmid_ref,
    gatt_ref,
    gproject_ref,
    gvec_ref,
    keep0_ref,
    send0_ref,
    keep1_ref,
    send1_ref,
    middle,
    feed,
    top,
    result,
    gfeed,
    low_out,
    gatt,
    grads,
    grad_sems,
    row_sems,
    *,
    item_rows,
):
    step = pl.program_id(0)
    rows, width = hid_ref.shape
    block = 256
    att_refs = (att0_ref, att1_ref)
    half = grads.shape[1] // 2

    steps = grads.shape[0]

    def grad_copies(which):
        found = []
        chunk, place = divmod(which, steps // 2)
        outs = (keep1_ref, send1_ref) if chunk else (keep0_ref, send0_ref)
        for number, out in enumerate(outs):
            side = side_ref[0] if number == 0 else 1 - side_ref[0]
            here = grads.at[which, pl.ds(pl.multiple_of(side * half, half), half)]
            there = out.at[pl.ds(place * half, half)]
            found.append(pltpu.make_async_copy(here, there, grad_sems.at[which, number]))
        return found

    @pl.when(step == 0)
    def _():
        for start in range(0, rows, block):
            here = slice(start, start + block)
            inside = slice(start % item_rows, start % item_rows + block)
            att = att_refs[start // item_rows][inside, :]
            branch = dot(att, project_ref[...]) + project_bias_ref[...]
            x = hid_ref[here, :].astype(f32) + branch
            middle[here, :] = x
            unit, _ = normalise(x)
            feed[here, :] = (unit * gain_ref[...] + shift_ref[...]).astype(bf16)
            at = lax.broadcasted_iota(jnp.int32, (block, width), 0) + start % item_rows
            limit = jnp.where(flag_ref[0] == 1, item_rows, count_ref[start // item_rows])
            top[here, :] = jnp.where(at < limit, cot_ref[here, :].astype(f32), 0.0).astype(bf16)
            result[here, :] = x + reduce_bias_ref[...]
            gfeed[here, :] = jnp.zeros((block, width), f32)

    pieces, gvec_ref[pl.ds(4 + step, 1), :] = feed_step(
        step, rows, item_rows, feed, top, result, gfeed, expand_ref, ebias_ref, reduce_ref
    )
    store_pieces(grads.at[step], pieces)
    for which in range(steps):

        @pl.when(step == which)
        def _(which=which):
            for copy in grad_copies(which):
                copy.start()

    @pl.when(step == pl.num_programs(0) - 1)
    def _():
        copies = []
        sums = [jnp.zeros((1, width), f32)] * 4
        for number, start in enumerate(range(0, rows, block)):
            here = slice(start, start + block)
            low_out[here, :] = result[here, :].astype(bf16)
            unit, scale = normalise(middle[here, :])
            grad = gfeed[here, :]
            grad_top = top[here, :].astype(f32)
            gmid = grad_top + norm_transpose(unit, scale, gain_ref[...], grad)
            terms = (grad * unit, grad, grad_top, gmid)
            sums = [old + column_sum(new) for old, new in zip(sums, terms)]
            middle[here, :] = gmid
            gbranch = gmid.astype(bf16)
            feed[here, :] = gbranch
            gatt[here, :] = dot(gbranch, project_ref[...], NT).astype(bf16)
            for kind, (mine, there) in enumerate(
                ((low_out, out_ref), (middle, gmid_ref), (gatt, gatt_ref))
            ):
                span = pl.ds(start, block)
                copy = pltpu.make_async_copy(
                    mine.at[span, :], there.at[span, :], row_sems.at[kind, number]
                )
                copy.start()
                copies.append(copy)
        total = dot(att0_ref[...], feed[:item_rows, :], TN)
        total += dot(att1_ref[...], feed[item_rows:, :], TN)
        gproject_ref[...] = total.astype(bf16)
        gvec_ref[0:4, :] = jnp.concatenate(sums, axis=0)
        for copy in copies:
            copy.wait()
        for which in range(steps):
            for copy in grad_copies(which):
                copy.wait()


def feed_forward(order, flag, count, side, att0, att1, project, hidden, cotangent, vecs, expand, ebias, reduce):
    rows, width = hidden.shape
    item_rows = att0.shape[0]
    units = reduce.shape[0]
    steps = units // FF_BLOCK
    block_rows = 2 * width * FF_BLOCK // LANES
    fixed = (att0, att1, project, hidden, cotangent, *vecs)
    anywhere = pl.BlockSpec(memory_space=pl.ANY)
    return call(
        order,
        functools.partial(feed_kernel, item_rows=item_rows),
        (*fixed, expand, ebias, reduce),
        [
            shaped((rows, width), bf16),
            shaped((rows, width), f32),
            shaped((rows, width), bf16),
            shaped((width, width), bf16),
            shaped((4 + steps, width), f32),
        ]
        + [shaped((steps // 2 * block_rows // 2, LANES), bf16)] * 4,
        "feed_forward",
        cost(12 * rows * width * units, 40 << 20, 2 * rows * units),
        scalars=(flag, count, side),
        grid=(steps,),
        specs=[resident(value.shape) for value in fixed]
        + [
            pl.BlockSpec((width, FF_BLOCK), lambda j, *_: (0, j)),
            pl.BlockSpec((1, FF_BLOCK), lambda j, *_: (0, j)),
            pl.BlockSpec((FF_BLOCK, width), lambda j, *_: (j, 0)),
        ],
        outs=[
            anywhere,
            anywhere,
            anywhere,
            resident((width, width)),
            resident((4 + steps, width)),
        ]
        + [anywhere] * 4,
        scratch=[
            pltpu.VMEM((rows, width), f32),
            pltpu.VMEM((rows, width), bf16),
            pltpu.VMEM((rows, width), bf16),
            pltpu.VMEM((rows, width), f32),
            pltpu.VMEM((rows, width), f32),
            pltpu.VMEM((rows, width), bf16),
            pltpu.VMEM((rows, width), bf16),
            pltpu.VMEM((steps, block_rows, LANES), bf16),
            pltpu.SemaphoreType.DMA((steps, 2)),
            pltpu.SemaphoreType.DMA((3, rows // 256)),
        ],
    )


def weight_kernel(
    spare,
    side_ref,
    normed_ref,
    image_ref,
    gq_ref,
    gk_ref,
    gv_ref,
    gik_ref,
    giv_ref,
    *refs,
):
    extra_ref = None if spare else refs[0]
    sums_ref, keep_ref, send_ref, keep, send, sems = refs[-6:]
    step = pl.program_id(0)
    width = normed_ref.shape[1]
    half = width // 2
    columns = gq_ref.shape[1] // LANES
    block = half * (columns if spare else columns + 1)

    def copies(part):
        span = pl.ds(part * block, block if part < 3 else spare)
        pairs = ((keep, keep_ref), (send, send_ref))
        return [
            pltpu.make_async_copy(here.at[span], there.at[span], sems.at[number, part])
            for number, (here, there) in enumerate(pairs)
        ]

    def store(part, total):
        if extra_ref is not None:
            more = extra_ref[:, part * LANES : (part + 1) * LANES].astype(f32)
            total = jnp.concatenate([total, more], axis=1)
        first = side_ref[0] == 0
        mine = jnp.where(first, total[:half], total[half:]).astype(bf16)
        other = jnp.where(first, total[half:], total[:half]).astype(bf16)
        for number in range(block // half):
            rows = slice(part * block + number * half, part * block + (number + 1) * half)
            cols = slice(number * LANES, (number + 1) * LANES)
            keep[rows, :] = mine[:, cols]
            send[rows, :] = other[:, cols]
        for copy in copies(part):
            copy.start()

    @pl.when(step == 0)
    def _():
        store(0, dot(normed_ref[...], gq_ref[...], TN))
        sums_ref[0:1] = column_sum(gq_ref[...].astype(f32))

    @pl.when(step == 1)
    def _():
        total = dot(normed_ref[...], gk_ref[...], TN)
        store(1, total + dot(image_ref[...], gik_ref[...], TN))

    @pl.when(step == 2)
    def _():
        total = dot(normed_ref[...], gv_ref[...], TN)
        store(2, total + dot(image_ref[...], giv_ref[...], TN))
        sums = column_sum(gv_ref[...].astype(f32)) + column_sum(giv_ref[...].astype(f32))
        sums_ref[1:2] = sums
        if spare:
            keep[3 * block :, :] = jnp.zeros((spare, LANES), bf16)
            send[3 * block :, :] = jnp.zeros((spare, LANES), bf16)
            for copy in copies(3):
                copy.start()
        for part in range(4 if spare else 3):
            for copy in copies(part):
                copy.wait()


def weight_grads(order, side, normed, image, grads, lanes, place, spare, extra):
    rows, width = normed.shape
    half_rows = 3 * (lanes // LANES + len(extra)) * width // 2 + spare
    column = lambda height: pl.BlockSpec((height, lanes), lambda *_: (0, place))
    anywhere = pl.BlockSpec(memory_space=pl.ANY)
    return call(
        order,
        functools.partial(weight_kernel, spare),
        (normed, image, *grads, *extra),
        [shaped((2, lanes), f32)] + [shaped((half_rows, LANES), bf16)] * 2,
        "weight_grads",
        weighed(cost(8 * rows * width * lanes, 12 << 20)),
        scalars=(side,),
        grid=(3,),
        specs=[resident(normed.shape), resident(image.shape)]
        + [column(value.shape[0]) for value in grads]
        + [resident(value.shape) for value in extra],
        outs=[resident((2, lanes)), anywhere, anywhere],
        scratch=[pltpu.VMEM((half_rows, LANES), bf16)] * 2 + [pltpu.SemaphoreType.DMA((2, 4))],
    )


def image_grad_kernel(keys_weight, values_weight, keys_ref, values_ref, out_ref):
    total = dot(keys_ref[...], keys_weight[...], NT) + dot(values_ref[...], values_weight[...], NT)
    out_ref[...] = total.astype(bf16)


def image_grads(order, weight, keys, values):
    rows, width = keys.shape
    part = lambda base: pl.BlockSpec((width, width), lambda *_: (0, base))
    return call(
        order,
        image_grad_kernel,
        (weight, weight, keys, values),
        [shaped((rows, width), bf16)],
        "image_grads",
        weighed(cost(4 * rows * width * width, 6 << 20)),
        grid=(1,),
        specs=[part(1), part(2), resident(keys.shape), resident(values.shape)],
        outs=[resident((rows, width))],
    )


def finish_kernel(
    flag_ref,
    hid_ref,
    gmid_ref,
    near_ref,
    far_ref,
    gq_ref,
    gk_ref,
    gv_ref,
    gain_ref,
    weight_ref,
    feed_sums_ref,
    first_sums_ref,
    last_sums_ref,
    _,
    out_ref,
    small_ref,
    sums,
):
    item, block = pl.program_id(0), pl.program_id(1)
    joined = jnp.concatenate([gq_ref[...], gk_ref[...], gv_ref[...]], axis=1)
    grad = dot(joined, weight_ref[...], NT)
    unit, scale = normalise(hid_ref[...].astype(f32))
    both = near_ref[...].astype(f32) + far_ref[...].astype(f32)
    grad = grad + jnp.where((flag_ref[0] == 0) & (block == 0), both, 0.0)
    total = gmid_ref[...] + norm_transpose(unit, scale, gain_ref[...], grad)
    out_ref[...] = total.astype(bf16)
    found = jnp.concatenate([column_sum(grad * unit), column_sum(grad)], axis=0)

    @pl.when((item == 0) & (block == 0))
    def _():
        sums[...] = jnp.zeros(sums.shape, f32)

    sums[0:2] += found

    @pl.when((item == pl.num_programs(0) - 1) & (block == pl.num_programs(1) - 1))
    def _():
        width = sums.shape[1]
        pad = lambda count: jnp.zeros((count, width), f32)
        own = [sums[0:2], feed_sums_ref[0:3], feed_sums_ref[4:8], pad(7)]
        own = jnp.concatenate(own, axis=0)
        bias_sums = jnp.concatenate([first_sums_ref[...], last_sums_ref[...]], axis=1)
        shared = [pad(9), feed_sums_ref[3:4], bias_sums, pad(4)]
        shared = jnp.concatenate(shared, axis=0)
        is_text = flag_ref[0] == 1
        first = jnp.where(is_text, 0.0, own) + shared
        rows = jnp.concatenate([first, jnp.where(is_text, own, 0.0)], axis=0).astype(bf16)
        count = rows.shape[0]
        for number in range(width // LANES):
            cols = slice(number * LANES, (number + 1) * LANES)
            small_ref[number * count : (number + 1) * count, :] = rows[:, cols]
        small_ref[width // LANES * count :, :] = jnp.zeros((SMALL - width // LANES * count, LANES), bf16)


def finish_rows(
    order, flag, hidden, gmid, near, far, grads, gain, weight, feed_sums, bias_sums, keep, item_rows
):
    rows, width = hidden.shape
    blocks = item_rows // IMG_PAD
    mine = pl.BlockSpec((IMG_PAD, width), lambda i, j, *_: (i * blocks + j, 0))
    image = pl.BlockSpec((IMG_PAD, width), lambda i, j, *_: (i, 0))
    fixed = (gain, weight, feed_sums, *bias_sums)
    place = keep.shape[0] // SMALL - 1
    return call(
        order,
        finish_kernel,
        (hidden, gmid, near, far, *grads, *fixed, keep),
        [shaped((rows, width), bf16), shaped(keep.shape, bf16)],
        "finish_rows",
        weighed(cost(6 * rows * width * width, 16 << 20)),
        scalars=(flag,),
        grid=(rows // item_rows, blocks),
        specs=[mine, mine, image, image, mine, mine, mine]
        + [resident(value.shape) for value in fixed]
        + [pl.BlockSpec(memory_space=pl.ANY)],
        outs=[mine, pl.BlockSpec((SMALL, LANES), lambda *_: (place, 0))],
        scratch=[pltpu.VMEM((8, width), f32)],
        aliases={13: 1},
    )


def expert_kernel(half_ref, value_ref, *refs):
    at = 0
    for out in refs[-2:]:
        tall = out.shape[0]
        for part in range(out.shape[1] // LANES):
            piece = value_ref[at : at + tall, :]
            out[:, part * LANES : (part + 1) * LANES] = piece.astype(f32)
            at += tall


def expert_outputs(order, half, first, value, width, units, earlier):
    tall = width // 2
    block_rows = 2 * width // LANES * tall
    return call(
        order,
        expert_kernel,
        (value, *earlier),
        [shaped((units, width), f32), shaped((width, units), f32)],
        "expert_outputs",
        cost(value.size, 6 * value.size),
        scalars=(half,),
        grid=(value.shape[0] // block_rows,),
        specs=[pl.BlockSpec((block_rows, LANES), lambda i, at: (i, 0))]
        + [pl.BlockSpec(memory_space=pl.ANY)] * len(earlier),
        outs=[
            pl.BlockSpec((tall, width), lambda i, at: (2 * (first + i) + at[0], 0)),
            pl.BlockSpec((tall, width), lambda i, at: (at[0], first + i)),
        ],
        aliases={2: 0, 3: 1} if earlier else None,
    )


def first_kernel(half_ref, value_ref, *refs):
    in_ref, out_ref, wide, narrow, sems = refs[-5:]
    tall = wide.shape[1]
    count = value_ref.shape[0] // tall // 3
    columns = in_ref.shape[1] // 3
    rows = pl.ds(pl.multiple_of(half_ref[0] * tall, tall), tall)
    copies = []
    for part in range(3):
        at = part * count * tall
        for number in range(count - 1):
            piece = value_ref[at + number * tall : at + (number + 1) * tall, :]
            wide[part, :, number * LANES : (number + 1) * LANES] = piece.astype(f32)
        piece = value_ref[at + (count - 1) * tall : at + count * tall, :]
        narrow[part] = piece.astype(f32)
        places = (
            (wide, in_ref.at[rows, pl.ds(part * columns, (count - 1) * LANES)]),
            (narrow, out_ref.at[rows, pl.ds(part * LANES, LANES)]),
        )
        for kind, (here, there) in enumerate(places):
            copy = pltpu.make_async_copy(here.at[part], there, sems.at[kind, part])
            copy.start()
            copies.append(copy)
    for copy in copies:
        copy.wait()


def first_outputs(order, half, value, width, earlier):
    tall = width // 2
    anywhere = pl.BlockSpec(memory_space=pl.ANY)
    return call(
        order,
        first_kernel,
        (value, *earlier),
        [shaped((width, 3 * width), f32), shaped((width, width), f32)],
        "first_outputs",
        cost(value.size, 6 * value.size),
        scalars=(half,),
        grid=(1,),
        specs=[resident(value.shape)] + [anywhere] * len(earlier),
        outs=[anywhere, anywhere],
        scratch=[
            pltpu.VMEM((3, tall, width - LANES), f32),
            pltpu.VMEM((3, tall, LANES), f32),
            pltpu.SemaphoreType.DMA((2, 3)),
        ],
        aliases={2: 0, 3: 1} if earlier else None,
    )


def last_kernel(side_ref, flag_ref, mine_ref, got_ref, *refs):
    in_ref, *vec_refs, expand_ref, pair_ref, project_ref, columns, sems = refs[1:]
    tall = columns.shape[2]
    width = in_ref.shape[1] // 3
    copies = []
    for number, ref in enumerate((mine_ref, got_ref)):
        half = side_ref[0] if number == 0 else 1 - side_ref[0]
        rows = pl.ds(pl.multiple_of(half * tall, tall), tall)
        for part in range(3):
            columns[number, part] = ref[part * tall : (part + 1) * tall, :].astype(f32)
            there = in_ref.at[rows, pl.ds((part + 1) * width - LANES, LANES)]
            copy = pltpu.make_async_copy(columns.at[number, part], there, sems.at[number, part])
            copy.start()
            copies.append(copy)
    both = mine_ref[3 * tall :, :].astype(f32) + got_ref[3 * tall :, :].astype(f32)
    rows = jnp.concatenate([both[at * 32 : (at + 1) * 32] for at in range(width // LANES)], axis=1)
    own = jnp.where(flag_ref[0] == 1, rows[16:], rows[:16])
    for number, ref in enumerate(vec_refs):
        ref[...] = own[number : number + 1]
    for number in range(expand_ref.shape[1] // width):
        cols = slice(number * width, (number + 1) * width)
        expand_ref[:, cols] = own[5 + number : 6 + number]
    project_ref[...] = rows[9]
    pair_ref[...] = rows[10:12]
    for copy in copies:
        copy.wait()


def last_outputs(order, side, flag, mine, got, width, units, earlier):
    vecs = [(1, width)] * 5 + [(1, units), (2, width), (width,)]
    anywhere = pl.BlockSpec(memory_space=pl.ANY)
    return call(
        order,
        last_kernel,
        (mine, got, earlier),
        [shaped((width, 3 * width), f32)] + [shaped(shape, f32) for shape in vecs],
        "last_outputs",
        cost(got.size, 6 * got.size),
        scalars=(side, flag),
        grid=(1,),
        specs=[resident(mine.shape), resident(got.shape), anywhere],
        outs=[anywhere] + [resident(shape) for shape in vecs],
        scratch=[
            pltpu.VMEM((2, 3, width // 2, LANES), f32),
            pltpu.SemaphoreType.DMA((2, 3)),
        ],
        aliases={4: 0},
    )


def swap(value, axes, pair_of):
    count = 1
    for axis in axes:
        count *= lax.axis_size(axis)
    return lax.ppermute(value, axes, [(source, pair_of(source)) for source in range(count)])


def place_of(axes):
    place = 0
    for axis in axes:
        place = place * lax.axis_size(axis) + lax.axis_index(axis)
    return place


def late_stages(axes):
    stages = stage_bits(axes)
    if len(axes) == 2 and len(stages) == 5:
        return [stages[0], (0, 0), (2, 3), (3, 2), (4, 4)]
    return stages


def stage_bits(axes):
    count = 1
    for axis in axes:
        count *= lax.axis_size(axis)
    bits = count.bit_length() - 1
    core = len(axes) - 1
    others = [bit for bit in range(bits) if bit != core]
    if len(axes) == 1 and len(others) == 3:
        return [(core, core), (1, 2), (3, 1), (2, 3)]
    if len(axes) == 2 and len(others) == 4:
        return [(core, core), (0, 2), (2, 0), (3, 3), (4, 4)]
    return [(core, core)] + list(zip(others, others[1:] + others[:1]))


class Total:
    def __init__(self, order, axes, keep, send, stages=None):
        self.order = order
        self.axes = axes
        self.core = len(axes) - 1
        self.left = list(stages or stage_bits(axes))
        place = place_of(axes)
        second = ((place >> self.core) & 1) == 1
        sides = [(place >> jnp.where(second, pair[1], pair[0])) & 1 for pair in self.left]
        self.sides = dict(zip(self.left, sides))
        self.back = list(self.left)
        self.terms = (keep, self.exchange(send, self.left.pop(0)))
        self.mine = None

    def exchange(self, value, pair):
        other = lambda source: source ^ (1 << pair[(source >> self.core) & 1])
        self.got = swap(value, self.axes, other)
        return self.got

    def part(self, which, half):
        cut = lambda term: lax.dynamic_slice_in_dim(term, which * half, half, 0).astype(f32)
        return (cut(self.terms[0]) + cut(self.terms[1])).astype(bf16)

    def finish(self):
        while self.left or self.back:
            self.step()

    def step(self):
        if self.left:
            pair = self.left.pop(0)
            self.terms = self.order.after(*self.terms)
            half = self.terms[0].shape[0] // 2
            side = self.sides[pair]
            sent = self.part(1 - side, half)
            self.terms = (self.part(side, half), self.exchange(sent, pair))
            self.order.last = sent
            return
        pair = self.back.pop()
        if self.mine is None:
            self.terms = self.order.after(*self.terms)
            self.mine = (self.terms[0].astype(f32) + self.terms[1].astype(f32)).astype(bf16)
        else:
            mine, got = self.order.after(self.mine, self.got)
            low = jnp.where(self.last == 0, mine, got)
            high = jnp.where(self.last == 0, got, mine)
            self.mine = jnp.concatenate([low, high], axis=0)
        self.order.last = self.mine
        self.last = self.sides[pair]
        self.exchange(self.mine, pair)


def on_device(
    hidden_in,
    image_count,
    text_lengths,
    attend_gain,
    attend_shift,
    project_in,
    bias_pair,
    project_out,
    project_bias,
    feed_gain,
    feed_shift,
    expand_weight,
    expand_bias,
    reduce_weight,
    reduce_bias,
    cotangent,
):
    items, _, rows, width = hidden_in.shape
    units = expand_weight.shape[2]
    is_text = lax.axis_index("mod") == 1
    flag = is_text.astype(jnp.int32)[None]
    hidden = hidden_in.reshape(items * rows, width)
    to_text = lambda value: lax.ppermute(value, "mod", [(0, 1)])
    to_image = lambda value: lax.ppermute(value, "mod", [(1, 0)])

    far_rows = [to_text(hidden_in[item, 0, :IMG_PAD]) for item in range(items)]
    far_vecs = to_text(jnp.concatenate([attend_gain, attend_shift], axis=0))
    order = Order()
    normed, projected = project_rows(
        order, hidden, attend_gain, attend_shift, project_in, bias_pair
    )
    scalars = (flag, image_count, text_lengths)
    images, attended, lses = (), [], []
    for item in range(items):
        images = image_rows(
            order,
            flag,
            item,
            hidden,
            far_rows[item],
            attend_gain,
            attend_shift,
            far_vecs,
            project_in,
            bias_pair,
            rows,
            items,
            images,
        )
        out, lse = attend_forward(order, scalars, item, projected, images[1])
        attended.append(out)
        lses.append(lse)

    side = (lax.axis_index("dp") & 1)[None]
    (
        hidden_out,
        grad_middle,
        grad_attended,
        project_out_grad,
        feed_sums,
        keep0,
        send0,
        keep1,
        send1,
    ) = feed_forward(
        order,
        flag,
        image_count,
        side,
        attended[0],
        attended[1],
        project_out,
        hidden,
        cotangent.reshape(items * rows, width),
        (project_bias[None], feed_gain, feed_shift, reduce_bias),
        expand_weight[0],
        expand_bias,
        reduce_weight[0],
    )
    a = Total(order, ("dp",), keep0, send0)
    c = Total(order, ("dp",), keep1, send1)
    grads = ()

    def backward(item, start, pairs):
        return attend_backward(
            order,
            scalars,
            item,
            start,
            pairs,
            projected,
            images[1],
            attended[item],
            grad_attended,
            lses[item],
            grads,
        )

    def weights(lanes, place, spare, *extra):
        return weight_grads(
            order, side, normed, images[0], grads, lanes, place, spare, extra
        )

    def unpack(half, first, value, earlier=()):
        return expert_outputs(order, half, first, value, width, units, earlier)

    grads = backward(0, 0, 2)
    a.step()
    grads = backward(1, 0, 2)
    c.step()
    grads = backward(0, 2, 2)
    a.step()
    grads = backward(1, 2, 2)
    c.step()
    first_sums, keep, send = weights(2 * LANES, 0, 0, project_out_grad)
    s = Total(order, ("dp", "mod"), keep, send)
    a.step()
    grads = backward(0, 4, 2)
    s.step()
    a.step()
    grads = backward(1, 4, 2)
    c.step()
    s.step()
    near = image_grads(order, project_in, grads[3], grads[4])
    far = to_image(near)
    c.step()
    a.step()
    last_sums, keep, send = weights(LANES, 2, SMALL)
    p = Total(order, ("dp", "mod"), keep, send, late_stages(("dp", "mod")))
    s.step()
    c.step()
    a.step()
    (far,) = order.after(far)
    order.last = far
    grad_in, keep = finish_rows(
        order,
        flag,
        hidden,
        grad_middle,
        near,
        far,
        grads[:3],
        attend_gain,
        project_in,
        feed_sums,
        (first_sums, last_sums),
        keep,
        rows,
    )
    p.terms = (keep, p.got)
    p.step()
    s.step()
    a.step()
    p.step()
    c.step()
    p.step()
    s.step()
    a.finish()
    outputs = unpack(side, 0, a.mine)
    p.step()
    s.step()
    p.step()
    outputs = unpack(1 - side, 0, a.got, outputs)
    p.step()
    s.step()
    c.step()
    p.step()
    s.step()
    p.step()
    c.finish()
    outputs = unpack(side, 2, c.mine, outputs)
    p.finish()
    s.step()
    reduce_grad, expand_grad = unpack(1 - side, 2, c.got, outputs)
    s.finish()
    projections = first_outputs(order, side, s.mine, width, ())
    project_in_grad, project_out_grad = first_outputs(order, 1 - side, s.got, width, projections)
    p.finish()
    (
        project_in_grad,
        attend_gain_grad,
        attend_shift_grad,
        feed_gain_grad,
        feed_shift_grad,
        reduce_bias_grad,
        expand_bias_grad,
        bias_pair_grad,
        project_bias_grad,
    ) = last_outputs(order, side, flag, p.mine, p.got, width, units, project_in_grad)
    return (
        hidden_out.reshape(hidden_in.shape),
        grad_in.reshape(hidden_in.shape),
        attend_gain_grad,
        attend_shift_grad,
        project_in_grad,
        bias_pair_grad,
        project_out_grad,
        project_bias_grad,
        feed_gain_grad,
        feed_shift_grad,
        expand_grad[None],
        expand_bias_grad,
        reduce_grad[None],
        reduce_bias_grad,
    )


def solution(mesh):
    in_specs = (
        P("dp", "mod", None, None),
        P("dp"),
        P("dp", None),
        P("mod", None),
        P("mod", None),
        P(),
        P(),
        P(),
        P(),
        P("mod", None),
        P("mod", None),
        P("mod", None, None),
        P("mod", None),
        P("mod", None, None),
        P("mod", None),
        P("dp", "mod", None, None),
    )
    out_specs = (
        P("dp", "mod", None, None),
        P("dp", "mod", None, None),
        P("mod", None),
        P("mod", None),
        P(),
        P(),
        P(),
        P(),
        P("mod", None),
        P("mod", None),
        P("mod", None, None),
        P("mod", None),
        P("mod", None, None),
        P("mod", None),
    )
    return jax.shard_map(
        on_device, mesh=mesh, in_specs=in_specs, out_specs=out_specs, check_vma=False
    )
```
